32 devices in a mesh: ctx: 8 (over z, x), fsdp: 4 (over y, core).
Axes of the slice: x: 2, y: 2, z: 4, core: 2. Of those that a mesh axis runs over, the one named last changes fastest.
Arguments:
- tokens: bfloat16 [4, 2048, 1024], P('fsdp', 'ctx'), may hold values from -6 to 6
- cotangent: bfloat16 [4, 2048, 1024], P('fsdp', 'ctx'), may hold values from -6 to 6
- block_map: int32 [8, 2], replicated, may hold values from 0 to 15, as said below
- positions: int32 [4, 2048], P('fsdp', 'ctx'), may hold values from 0 to 4094, as said below
- attn_gain: float32 [1024], P('fsdp'), may hold values from 0.1 to 1.9
- query_weight: float32 [1024, 2048], P('fsdp'), may hold values from -0.1875 to 0.1875
- key_weight: float32 [1024, 1024], P('fsdp'), may hold values from -0.1875 to 0.1875
- value_weight: float32 [1024, 1024], P('fsdp'), may hold values from -0.1875 to 0.1875
- query_gain: float32 [128], P('fsdp'), may hold values from 1 to 2
- key_gain: float32 [128], P('fsdp'), may hold values from 1 to 2
- out_weight: float32 [2048, 1024], P('fsdp'), may hold values from -1 to 1
- mlp_gain: float32 [1024], P('fsdp'), may hold values from 0.1 to 1.9
- gate_weight: float32 [1024, 3072], P('fsdp'), may hold values from -0.1875 to 0.1875
- up_weight: float32 [1024, 3072], P('fsdp'), may hold values from -0.1875 to 0.1875
- down_weight: float32 [3072, 1024], P('fsdp'), may hold values from -0.15625 to 0.15625
Outputs:
- layer_output: float32 [4, 2048, 1024], P('fsdp', 'ctx')
- input_grad: float32 [4, 2048, 1024], P('fsdp', 'ctx')
- attn_gain_grad: float32 [1024], P('fsdp')
- query_weight_grad: float32 [1024, 2048], P('fsdp')
- key_weight_grad: float32 [1024, 1024], P('fsdp')
- value_weight_grad: float32 [1024, 1024], P('fsdp')
- query_gain_grad: float32 [128], P('fsdp')
- key_gain_grad: float32 [128], P('fsdp')
- out_weight_grad: float32 [2048, 1024], P('fsdp')
- mlp_gain_grad: float32 [1024], P('fsdp')
- gate_weight_grad: float32 [1024, 3072], P('fsdp')
- up_weight_grad: float32 [1024, 3072], P('fsdp')
- down_weight_grad: float32 [3072, 1024], P('fsdp')
The draws below stay inside these ranges and needn't reach their ends.
Inputs may be any that keep to these rules, and one draw needn't show every extreme that they name: `block_map`: row c is a pair (p, 15 - p) with p below 8; every block number appears exactly once. `positions`: along each sequence, taken in the order of the causal index, the first position is 0 and each next one exceeds the one before by 1 or 2; in one sequence every step is 2.
All inputs are finite; a program needn't handle non-finite values.
Results may differ from the reference program's by a relative error of at most 0.023.
Values may be sent and summed in bfloat16 or wider, within the bound.
A program may use at most 256 MiB of HBM per device.

```python
import math
import jax
import jax.numpy as jnp
from jax import lax

D = 1024
HQ = 16
HK = 8
HD = 128
FF = 3072
BLK = 128
PAIRS = 8
BLOCKS = 16
LEN = 2048
SEQS = 4


def pair_order(key):
    return jax.random.permutation(key, PAIRS).astype(jnp.int32)


def block_layout(order):
    return jnp.stack([order, BLOCKS - 1 - order], axis=1).astype(jnp.int32)


def draw_block_map(key, part):
    order = pair_order(key)
    return block_layout(order)


def draw_positions(key, part):
    order = pair_order(key)
    key = jax.random.fold_in(key, 23)
    strides = jax.random.randint(key, (SEQS, LEN), 1, 3).astype(jnp.int32)
    chosen = jax.random.randint(jax.random.fold_in(key, 5), (), 0, SEQS).astype(jnp.int32)
    rows = jnp.arange(SEQS, dtype=jnp.int32)[:, None]
    strides = jnp.where(rows == chosen, jnp.int32(2), strides).astype(jnp.int32)
    initial = jnp.cumsum(strides, axis=1).astype(jnp.int32) - strides
    flat_map = block_layout(order).reshape(-1)
    token_order = (flat_map[:, None] * BLK + jnp.arange(BLK, dtype=jnp.int32)[None, :]).reshape(-1)
    return jnp.take(initial, token_order, axis=1).astype(jnp.int32)


def block_scale(rng, dims, pieces, least, largest):
    loudness = 1.0
    for position, blocks in pieces:
        draws = jax.random.uniform(jax.random.fold_in(jax.random.fold_in(rng, 6), position), (blocks,), jnp.float32, least / len(pieces), largest / len(pieces))
        loudness = loudness * jnp.repeat(jnp.exp(draws), dims[position] // blocks).reshape((-1,) + (1,) * (len(dims) - 1 - position))
    return loudness


def bell_draw(rng, shape, spread, most, cuts=(), kind=jnp.bfloat16):
    array = jax.random.normal(rng, shape, jnp.float32) * spread
    if len(cuts) > 0:
        array = block_scale(rng, shape, cuts, -0.22, 0.18) * array
    return jnp.clip(array, min=-most, max=most).astype(kind)


def setup_inputs(seed: int = 0) -> dict:
    keys = jax.random.split(jax.random.key(seed), 16)
    tokens = bell_draw(keys[0], (SEQS, LEN, D), 1.0, 6.0, ((0, 4), (1, 8)))
    cotangent = bell_draw(keys[1], (SEQS, LEN, D), 1.0, 6.0, ((0, 4), (1, 8)))
    block_map = draw_block_map(jax.random.fold_in(keys[15], 71), 0)
    positions = draw_positions(jax.random.fold_in(keys[15], 71), 0)
    attn_gain = jnp.clip(1.0 + 0.18 * jax.random.normal(keys[4], (D,), jnp.float32), 0.1, 1.9)
    query_weight = bell_draw(keys[5], (D, HQ * HD), D ** -0.5, 0.1875, ((0, 4),), jnp.float32)
    key_weight = bell_draw(keys[6], (D, HK * HD), D ** -0.5, 0.1875, ((0, 4),), jnp.float32)
    value_weight = bell_draw(keys[7], (D, HK * HD), D ** -0.5, 0.1875, ((0, 4),), jnp.float32)
    query_gain = jnp.clip(1.0 + 1.0 * jax.random.uniform(keys[8], (HD,), jnp.float32) ** block_scale(keys[8], (HD,), ((0, 4),), -0.2, 0.2), 1.0, 2.0)
    key_gain = jnp.clip(1.0 + 1.0 * jax.random.uniform(keys[9], (HD,), jnp.float32) ** block_scale(keys[9], (HD,), ((0, 4),), -0.2, 0.2), 1.0, 2.0)
    out_weight = bell_draw(keys[10], (HQ * HD, D), (max(HQ * HD // 64, 1)) ** -0.5, 1.0, ((0, 4),), jnp.float32)
    mlp_gain = jnp.clip(1.0 + 0.18 * jax.random.normal(keys[11], (D,), jnp.float32), 0.1, 1.9)
    gate_weight = bell_draw(keys[12], (D, FF), D ** -0.5, 0.1875, ((0, 4),), jnp.float32)
    up_weight = bell_draw(keys[13], (D, FF), D ** -0.5, 0.1875, ((0, 4),), jnp.float32)
    down_weight = bell_draw(keys[14], (FF, D), (FF // 2) ** -0.5, 0.15625, ((0, 4),), jnp.float32)
    return dict(tokens=tokens, cotangent=cotangent, block_map=block_map, positions=positions, attn_gain=attn_gain, query_weight=query_weight, key_weight=key_weight, value_weight=value_weight, query_gain=query_gain, key_gain=key_gain, out_weight=out_weight, mlp_gain=mlp_gain, gate_weight=gate_weight, up_weight=up_weight, down_weight=down_weight)


epsilon = 1e-06
theta_base = 1000000.0
masked_value = -1e+30
highest = lax.Precision.HIGHEST

@jax.custom_vjp
def low(v):
    return lax.optimization_barrier(v.astype(jnp.bfloat16)).astype(jnp.float32)

@jax.custom_vjp
def low_back(v):
    return v

def low_keep(v):
    return (low(v), None)

def low_pass(kept, grad):
    return (grad,)

def back_keep(v):
    return (v, None)

def back_low(kept, grad):
    return (low(grad),)
low.defvjp(low_keep, low_pass)
low_back.defvjp(back_keep, back_low)

def rms_scale(values):
    return lax.rsqrt(lax.optimization_barrier(jnp.mean(values * values, axis=-1, keepdims=True)) + epsilon)

def rope_tables(positions, head_dim):
    frequency = jnp.exp(jnp.arange(0, head_dim, 2).astype(jnp.float32) * (-math.log(theta_base) / head_dim))
    angles = positions.astype(jnp.float32)[..., None] * frequency
    angles = jnp.concatenate([angles, angles], axis=-1)
    return (jnp.cos(angles), jnp.sin(angles))

def rotate(values, cosine, sine_table):
    half_width = values.shape[-1] // 2
    turned = jnp.concatenate([-values[..., half_width:], values[..., :half_width]], axis=-1)
    return values * cosine + turned * sine_table

def attend_plain(grouped, key_rows, value_rows, allowed):
    scores = jnp.einsum('qkgd,skd->kgqs', grouped, key_rows, precision=highest) * HD ** (-0.5)
    scores = jnp.where(allowed, low_back(scores), masked_value)
    row_max = lax.optimization_barrier(jnp.max(scores, axis=-1, keepdims=True))
    exp_scores = jnp.exp(scores - row_max)
    prob_low = low(exp_scores / lax.optimization_barrier(jnp.sum(exp_scores, axis=-1, keepdims=True)))
    return jnp.einsum('kgqs,skd->qkgd', prob_low, value_rows, precision=highest)
attend_one = jax.checkpoint(attend_plain)

def layer(tokens, attn_gain, query_weight, key_weight, value_weight, query_gain, key_gain, out_weight, mlp_gain, gate_weight, up_weight, down_weight, allowed, cosine, sine_table):
    seq_total = tokens.shape[0]
    flat = tokens.reshape(-1, D)
    normed = low(flat * rms_scale(flat) * attn_gain)
    query_rows = low_back(jnp.dot(normed, low(query_weight), precision=highest)).reshape(-1, HQ, HD)
    key_rows = low_back(jnp.dot(normed, low(key_weight), precision=highest)).reshape(-1, HK, HD)
    value_rows = low(low_back(jnp.dot(normed, low(value_weight), precision=highest)))
    query_rows = low(rotate(query_rows * rms_scale(query_rows) * query_gain, cosine, sine_table))
    key_rows = low(rotate(key_rows * rms_scale(key_rows) * key_gain, cosine, sine_table))
    query_rows = query_rows.reshape(seq_total, LEN, HK, HQ // HK, HD)
    key_rows = key_rows.reshape(seq_total, LEN, HK, HD)
    value_rows = value_rows.reshape(seq_total, LEN, HK, HD)

    def attend(inputs):
        return attend_one(inputs[0], inputs[1], inputs[2], allowed)
    attended = lax.map(attend, (query_rows, key_rows, value_rows))
    attended = low(low_back(attended.reshape(-1, HQ * HD)))
    middle = flat + low_back(jnp.dot(attended, low(out_weight), precision=highest))
    normed_two = low(middle * rms_scale(middle) * mlp_gain)
    gate = low_back(jnp.dot(normed_two, low(gate_weight), precision=highest))
    upward = low_back(jnp.dot(normed_two, low(up_weight), precision=highest))
    hidden = low(jax.nn.silu(gate) * upward)
    result = middle + low_back(jnp.dot(hidden, low(down_weight), precision=highest))
    return result.reshape(tokens.shape)

def reference(tokens, cotangent, block_map, positions, attn_gain, query_weight, key_weight, value_weight, query_gain, key_gain, out_weight, mlp_gain, gate_weight, up_weight, down_weight):
    flat_map = block_map.reshape(-1).astype(jnp.int32)
    offsets = jnp.arange(BLK, dtype=jnp.int32)
    token_index = (flat_map[:, None] * BLK + offsets[None, :]).reshape(-1)
    allowed = token_index[:, None] >= token_index[None, :]
    cosine, sine_table = rope_tables(positions.reshape(-1), HD)
    cosine = cosine[:, None, :]
    sine_table = sine_table[:, None, :]

    def wrapped(tokens_in, attn_in, query_in, key_in, value_in, qgain_in, kgain_in, out_in, mlp_in, gate_in, up_in, down_in):
        return layer(tokens_in, attn_in, query_in, key_in, value_in, qgain_in, kgain_in, out_in, mlp_in, gate_in, up_in, down_in, allowed, cosine, sine_table)
    result, pullback = jax.vjp(wrapped, tokens.astype(jnp.float32), attn_gain, query_weight, key_weight, value_weight, query_gain, key_gain, out_weight, mlp_gain, gate_weight, up_weight, down_weight)
    grads = pullback(cotangent.astype(jnp.float32))
    return (result, grads[0], grads[1], grads[2], grads[3], grads[4], grads[5], grads[6], grads[7], grads[8], grads[9], grads[10], grads[11])
```

```python
import math

import jax
import jax.numpy as jnp
from jax import lax
from jax.experimental import pallas as pl
from jax.experimental.pallas import tpu as pltpu
from jax.sharding import PartitionSpec as P

D = 1024
HQ = 16
HK = 8
HD = 128
BLK = 128


epsilon = 1e-06
theta_base = 1000000.0
masked_value = -1e30


def rms_scale(values):
    return lax.rsqrt(jnp.mean(values * values, axis=-1, keepdims=True) + epsilon)


def norm_back(upstream, values, scale):
    return scale * upstream - values * (scale * scale * scale) * jnp.mean(
        upstream * values, axis=-1, keepdims=True
    )


def rope_tables(positions, head_dim):
    frequency = jnp.exp(
        jnp.arange(0, head_dim, 2).astype(jnp.float32) * (-math.log(theta_base) / head_dim)
    )
    angles = positions.astype(jnp.float32)[..., None] * frequency
    angles = jnp.concatenate([angles, angles], axis=-1)
    return (jnp.cos(angles), jnp.sin(angles))


def rotate(values, cosine, sine_table):
    half_width = values.shape[-1] // 2
    turned = jnp.concatenate([-values[..., half_width:], values[..., :half_width]], axis=-1)
    return values * cosine + turned * sine_table


def unrotate(grads, cosine, sine_table):
    half_width = grads.shape[-1] // 2
    moved = grads * sine_table
    back_turn = jnp.concatenate([moved[..., half_width:], -moved[..., :half_width]], axis=-1)
    return grads * cosine + back_turn


def score_block(grouped, keys_head, allowed, scale):
    scores = (
        jnp.einsum("qgd,sd->gqs", grouped, keys_head, preferred_element_type=jnp.float32) * scale
    )
    return jnp.where(allowed, scores, masked_value)


def body(
    tokens,
    cotangent,
    block_map,
    positions,
    attn_gain,
    query_weight,
    key_weight,
    value_weight,
    query_gain,
    key_gain,
    out_weight,
    mlp_gain,
    gate_weight,
    up_weight,
    down_weight,
):
    seq_count = tokens.shape[0]
    seq_rows = tokens.shape[1]
    total_rows = seq_count * seq_rows
    groups = HQ // HK
    scale = HD ** (-0.5)
    attn_full, query_full, key_full, mlp_full = (
        lax.all_gather(attn_gain, "fsdp", axis=0, tiled=True),
        lax.all_gather(query_gain, "fsdp", axis=0, tiled=True),
        lax.all_gather(key_gain, "fsdp", axis=0, tiled=True),
        lax.all_gather(mlp_gain, "fsdp", axis=0, tiled=True),
    )
    query_w, key_w, value_w, out_w = (
        lax.all_gather(query_weight.astype(jnp.bfloat16), "fsdp", axis=0, tiled=True),
        lax.all_gather(key_weight.astype(jnp.bfloat16), "fsdp", axis=0, tiled=True),
        lax.all_gather(value_weight.astype(jnp.bfloat16), "fsdp", axis=0, tiled=True),
        lax.all_gather(out_weight.astype(jnp.bfloat16), "fsdp", axis=0, tiled=True),
    )
    flat = tokens.astype(jnp.float32).reshape(total_rows, D)
    scale_one = rms_scale(flat)
    normed = (flat * scale_one * attn_full).astype(jnp.bfloat16)
    query_raw = jnp.dot(normed, query_w, preferred_element_type=jnp.float32).reshape(
        total_rows, HQ, HD
    )
    key_raw = jnp.dot(normed, key_w, preferred_element_type=jnp.float32).reshape(total_rows, HK, HD)
    value_low = jnp.dot(normed, value_w, preferred_element_type=jnp.float32).astype(jnp.bfloat16)
    cosine, sine_table = rope_tables(positions.reshape(total_rows), HD)
    cosine = cosine[:, None, :]
    sine_table = sine_table[:, None, :]
    query_scale = rms_scale(query_raw)
    query_unit = query_raw * query_scale
    query_low = rotate(query_unit * query_full, cosine, sine_table).astype(jnp.bfloat16)
    key_scale = rms_scale(key_raw)
    key_unit = key_raw * key_scale
    key_low = rotate(key_unit * key_full, cosine, sine_table).astype(jnp.bfloat16)
    flat_map = block_map.reshape(-1)
    offsets = jnp.arange(BLK, dtype=jnp.int32)
    key_index = (flat_map[:, None] * BLK + offsets[None, :]).reshape(-1)
    own_blocks = lax.dynamic_slice_in_dim(flat_map, lax.axis_index("ctx") * 2, 2)
    query_index = (own_blocks[:, None] * BLK + offsets[None, :]).reshape(-1)
    allowed = query_index[:, None] >= key_index[None, :]
    query_seq = query_low.reshape(seq_count, seq_rows, HK, groups, HD)
    key_seq = key_low.reshape(seq_count, seq_rows, HK * HD)
    value_seq = value_low.reshape(seq_count, seq_rows, HK * HD)

    def forward_head(inputs):
        grouped, keys_head, values_head = inputs
        scores = score_block(grouped, keys_head, allowed, scale)
        row_max = jnp.max(scores, axis=-1, keepdims=True)
        exp_scores = jnp.exp(scores - row_max)
        row_total = jnp.sum(exp_scores, axis=-1, keepdims=True)
        prob_low = (exp_scores / row_total).astype(jnp.bfloat16)
        mixed = jnp.einsum("gqs,sd->qgd", prob_low, values_head, preferred_element_type=jnp.float32)
        return (mixed, row_max + jnp.log(row_total))

    seq_item = 0
    keys_all = lax.all_gather(key_seq[seq_item], "ctx", axis=0, tiled=True)
    values_all = lax.all_gather(value_seq[seq_item], "ctx", axis=0, tiled=True)
    keys_head = jnp.transpose(keys_all.reshape(-1, HK, HD), (1, 0, 2))
    values_head = jnp.transpose(values_all.reshape(-1, HK, HD), (1, 0, 2))
    grouped_head = jnp.transpose(query_seq[seq_item], (1, 0, 2, 3))
    mixed, lse = lax.map(forward_head, (grouped_head, keys_head, values_head))
    mixed_parts = jnp.transpose(mixed, (1, 0, 2, 3)).reshape(seq_rows, HQ * HD)
    lse_parts = [lse]
    gathered = [(grouped_head, keys_head, values_head)]
    attended = mixed_parts.astype(jnp.bfloat16)
    middle = flat + jnp.dot(attended, out_w, preferred_element_type=jnp.float32)
    gate_w, up_w, down_w = (
        lax.all_gather(gate_weight.astype(jnp.bfloat16), "fsdp", axis=0, tiled=True),
        lax.all_gather(up_weight.astype(jnp.bfloat16), "fsdp", axis=0, tiled=True),
        lax.all_gather(down_weight.astype(jnp.bfloat16), "fsdp", axis=0, tiled=True),
    )
    scale_two = rms_scale(middle)
    normed_two = (middle * scale_two * mlp_full).astype(jnp.bfloat16)
    gate = jnp.dot(normed_two, gate_w, preferred_element_type=jnp.float32)
    upward = jnp.dot(normed_two, up_w, preferred_element_type=jnp.float32)
    sigmoid_gate = jax.nn.sigmoid(gate)
    silu_gate = gate * sigmoid_gate
    hidden = (silu_gate * upward).astype(jnp.bfloat16)
    result = middle + jnp.dot(hidden, down_w, preferred_element_type=jnp.float32)
    query_back, key_back, value_back, out_back = (
        lax.all_gather(query_weight.astype(jnp.bfloat16), "fsdp", axis=0, tiled=True),
        lax.all_gather(key_weight.astype(jnp.bfloat16), "fsdp", axis=0, tiled=True),
        lax.all_gather(value_weight.astype(jnp.bfloat16), "fsdp", axis=0, tiled=True),
        lax.all_gather(out_weight.astype(jnp.bfloat16), "fsdp", axis=0, tiled=True),
    )
    gate_back, up_back, down_back = (
        lax.all_gather(gate_weight.astype(jnp.bfloat16), "fsdp", axis=0, tiled=True),
        lax.all_gather(up_weight.astype(jnp.bfloat16), "fsdp", axis=0, tiled=True),
        lax.all_gather(down_weight.astype(jnp.bfloat16), "fsdp", axis=0, tiled=True),
    )
    grad_out = cotangent.astype(jnp.float32).reshape(total_rows, D)
    grad_branch = grad_out.astype(jnp.bfloat16)
    down_grad = jnp.einsum("nf,nd->fd", hidden, grad_branch, preferred_element_type=jnp.float32)
    grad_hidden = jnp.einsum(
        "nd,fd->nf", grad_branch, down_back, preferred_element_type=jnp.float32
    )
    grad_gate = (grad_hidden * upward * sigmoid_gate * (1.0 + gate * (1.0 - sigmoid_gate))).astype(
        jnp.bfloat16
    )
    grad_up = (grad_hidden * silu_gate).astype(jnp.bfloat16)
    gate_grad = jnp.einsum("nd,nf->df", normed_two, grad_gate, preferred_element_type=jnp.float32)
    up_grad = jnp.einsum("nd,nf->df", normed_two, grad_up, preferred_element_type=jnp.float32)
    grad_normed_two = jnp.einsum(
        "nf,df->nd", grad_gate, gate_back, preferred_element_type=jnp.float32
    ) + jnp.einsum("nf,df->nd", grad_up, up_back, preferred_element_type=jnp.float32)
    mlp_local = jnp.sum(grad_normed_two * middle * scale_two, axis=0)
    grad_middle = grad_out + norm_back(grad_normed_two * mlp_full, middle, scale_two)
    grad_attn_low = grad_middle.astype(jnp.bfloat16)
    out_grad = jnp.einsum("nq,nd->qd", attended, grad_attn_low, preferred_element_type=jnp.float32)
    grad_mixed = jnp.einsum(
        "nd,qd->nq", grad_attn_low, out_back, preferred_element_type=jnp.float32
    ).astype(jnp.bfloat16)
    grad_mixed_seq = grad_mixed.reshape(seq_count, seq_rows, HK, groups, HD)

    def backward_head(inputs):
        grouped, keys_head, values_head, grad_head, lse = inputs
        scores = score_block(grouped, keys_head, allowed, scale)
        prob_full = jnp.exp(scores - lse)
        grad_prob = jnp.einsum(
            "qgd,sd->gqs", grad_head, values_head, preferred_element_type=jnp.float32
        )
        delta_row = jnp.sum(prob_full * grad_prob, axis=-1, keepdims=True)
        grad_scores = (prob_full * (grad_prob - delta_row)).astype(jnp.bfloat16)
        grad_query_head = (
            jnp.einsum("gqs,sd->qgd", grad_scores, keys_head, preferred_element_type=jnp.float32)
            * scale
        )
        grad_key_head = (
            jnp.einsum("gqs,qgd->sd", grad_scores, grouped, preferred_element_type=jnp.float32)
            * scale
        )
        grad_value_head = jnp.einsum(
            "gqs,qgd->sd",
            prob_full.astype(jnp.bfloat16),
            grad_head,
            preferred_element_type=jnp.float32,
        )
        return (grad_query_head, grad_key_head, grad_value_head)

    seq_item = 0
    grouped_head, keys_head, values_head = gathered[seq_item]
    grad_head = jnp.transpose(grad_mixed_seq[seq_item], (1, 0, 2, 3))
    grad_query_head, grad_key_head, grad_value_head = lax.map(
        backward_head, (grouped_head, keys_head, values_head, grad_head, lse_parts[seq_item])
    )
    grad_query_parts = jnp.transpose(grad_query_head, (1, 0, 2, 3)).reshape(seq_rows, HQ, HD)
    grad_keys_all = jnp.transpose(grad_key_head, (1, 0, 2)).reshape(-1, HK * HD)
    grad_values_all = jnp.transpose(grad_value_head, (1, 0, 2)).reshape(-1, HK * HD)
    grad_key_own = lax.psum_scatter(
        grad_keys_all.astype(jnp.bfloat16), "ctx", scatter_dimension=0, tiled=True
    ).astype(jnp.float32)
    grad_value_own = lax.psum_scatter(
        grad_values_all.astype(jnp.bfloat16), "ctx", scatter_dimension=0, tiled=True
    )
    grad_key = grad_key_own.reshape(total_rows, HK, HD)
    grad_query_unit = unrotate(grad_query_parts, cosine, sine_table)
    qgain_local = jnp.sum(grad_query_unit * query_unit, axis=(0, 1))
    grad_query_low = (
        norm_back(grad_query_unit * query_full, query_raw, query_scale)
        .astype(jnp.bfloat16)
        .reshape(total_rows, HQ * HD)
    )
    grad_key_unit = unrotate(grad_key, cosine, sine_table)
    kgain_local = jnp.sum(grad_key_unit * key_unit, axis=(0, 1))
    grad_key_low = (
        norm_back(grad_key_unit * key_full, key_raw, key_scale)
        .astype(jnp.bfloat16)
        .reshape(total_rows, HK * HD)
    )
    query_grad = jnp.einsum("nd,nc->dc", normed, grad_query_low, preferred_element_type=jnp.float32)
    key_grad = jnp.einsum("nd,nc->dc", normed, grad_key_low, preferred_element_type=jnp.float32)
    value_grad = jnp.einsum("nd,nc->dc", normed, grad_value_own, preferred_element_type=jnp.float32)
    grad_normed = jnp.einsum(
        "nc,dc->nd", grad_query_low, query_back, preferred_element_type=jnp.float32
    )
    grad_normed = grad_normed + jnp.einsum(
        "nc,dc->nd", grad_key_low, key_back, preferred_element_type=jnp.float32
    )
    grad_normed = grad_normed + jnp.einsum(
        "nc,dc->nd", grad_value_own, value_back, preferred_element_type=jnp.float32
    )
    attn_local = jnp.sum(grad_normed * flat * scale_one, axis=0)
    input_grad = grad_middle + norm_back(grad_normed * attn_full, flat, scale_one)
    shares = (
        lax.psum_scatter(
            attn_local.astype(jnp.bfloat16), "fsdp", scatter_dimension=0, tiled=True
        ).astype(jnp.float32),
        lax.psum_scatter(
            query_grad.astype(jnp.bfloat16), "fsdp", scatter_dimension=0, tiled=True
        ).astype(jnp.float32),
        lax.psum_scatter(
            key_grad.astype(jnp.bfloat16), "fsdp", scatter_dimension=0, tiled=True
        ).astype(jnp.float32),
        lax.psum_scatter(
            value_grad.astype(jnp.bfloat16), "fsdp", scatter_dimension=0, tiled=True
        ).astype(jnp.float32),
        lax.psum_scatter(
            qgain_local.astype(jnp.bfloat16), "fsdp", scatter_dimension=0, tiled=True
        ).astype(jnp.float32),
        lax.psum_scatter(
            kgain_local.astype(jnp.bfloat16), "fsdp", scatter_dimension=0, tiled=True
        ).astype(jnp.float32),
        lax.psum_scatter(
            out_grad.astype(jnp.bfloat16), "fsdp", scatter_dimension=0, tiled=True
        ).astype(jnp.float32),
        lax.psum_scatter(
            mlp_local.astype(jnp.bfloat16), "fsdp", scatter_dimension=0, tiled=True
        ).astype(jnp.float32),
        lax.psum_scatter(
            gate_grad.astype(jnp.bfloat16), "fsdp", scatter_dimension=0, tiled=True
        ).astype(jnp.float32),
        lax.psum_scatter(
            up_grad.astype(jnp.bfloat16), "fsdp", scatter_dimension=0, tiled=True
        ).astype(jnp.float32),
        lax.psum_scatter(
            down_grad.astype(jnp.bfloat16), "fsdp", scatter_dimension=0, tiled=True
        ).astype(jnp.float32),
    )
    summed = (
        lax.psum(shares[0].astype(jnp.bfloat16), "ctx").astype(jnp.float32),
        lax.psum(shares[1].astype(jnp.bfloat16), "ctx").astype(jnp.float32),
        lax.psum(shares[2].astype(jnp.bfloat16), "ctx").astype(jnp.float32),
        lax.psum(shares[3].astype(jnp.bfloat16), "ctx").astype(jnp.float32),
        lax.psum(shares[4].astype(jnp.bfloat16), "ctx").astype(jnp.float32),
        lax.psum(shares[5].astype(jnp.bfloat16), "ctx").astype(jnp.float32),
        lax.psum(shares[6].astype(jnp.bfloat16), "ctx").astype(jnp.float32),
        lax.psum(shares[7].astype(jnp.bfloat16), "ctx").astype(jnp.float32),
        lax.psum(shares[8].astype(jnp.bfloat16), "ctx").astype(jnp.float32),
        lax.psum(shares[9].astype(jnp.bfloat16), "ctx").astype(jnp.float32),
        lax.psum(shares[10].astype(jnp.bfloat16), "ctx").astype(jnp.float32),
    )
    return (
        result.reshape(tokens.shape),
        input_grad.reshape(tokens.shape),
        summed[0],
        summed[1],
        summed[2],
        summed[3],
        summed[4],
        summed[5],
        summed[6],
        summed[7],
        summed[8],
        summed[9],
        summed[10],
    )


MESH = pl.DeviceIdType.MESH
TILE = 128


def coords():
    a = lax.axis_index("ctx")
    f = lax.axis_index("fsdp")
    return lax.div(a, 2), lax.rem(a, 2), lax.div(f, 2), lax.rem(f, 2)


def device(z, x, y, c):
    return (z * 2 + x, y * 2 + c)


def both(p, q):
    if p is None:
        return q
    if q is None:
        return p
    return jnp.logical_and(p, q)


def guarded(p, fn):
    if p is None:
        fn()
    else:
        pl.when(p)(fn)


class Edge:
    def __init__(self, src, dst, to, frm, send_if=None, recv_if=None, after=()):
        self.src, self.dst, self.to, self.frm = src, dst, to, frm
        self.send_if, self.recv_if, self.after = send_if, recv_if, after


def run_edges(edges, locals_, send_sems, recv_sems, local_sems):
    barrier = pltpu.get_barrier_semaphore()
    for e in edges:
        guarded(
            e.recv_if,
            lambda e=e: pl.semaphore_signal(barrier, inc=1, device_id=e.frm, device_id_type=MESH),
        )
    copies = []
    for i, (src, dst, cond) in enumerate(locals_):
        cp = pltpu.make_async_copy(src, dst, local_sems.at[i])
        guarded(cond, cp.start)
        copies.append((cp, cond))
    greeted = sum(1 if e.send_if is None else e.send_if.astype(jnp.int32) for e in edges)
    if any(e.send_if is None for e in edges):
        pl.semaphore_wait(barrier, greeted)
    else:
        pl.when(greeted > 0)(lambda: pl.semaphore_wait(barrier, greeted))
    remote = [
        pltpu.make_async_remote_copy(
            src_ref=e.src,
            dst_ref=e.dst,
            send_sem=send_sems.at[i],
            recv_sem=recv_sems.at[i],
            device_id=e.to,
            device_id_type=MESH,
        )
        for i, e in enumerate(edges)
    ]
    waited = set()
    for i, e in enumerate(edges):
        if not e.after:
            guarded(e.send_if, remote[i].start)
    for i, e in enumerate(edges):
        for j in e.after:
            if j not in waited:
                guarded(edges[j].recv_if, remote[j].wait_recv)
                waited.add(j)
        if e.after:
            guarded(e.send_if, remote[i].start)
    for i, e in enumerate(edges):
        if i not in waited:
            guarded(e.recv_if, remote[i].wait_recv)
        guarded(e.send_if, remote[i].wait_send)
    for cp, cond in copies:
        guarded(cond, cp.wait)


def comm_call(name, cid, build, n_edges, n_locals, ins, outs):
    def kernel(*refs):
        i_refs, o_refs = refs[: len(ins)], refs[len(ins) : len(ins) + len(outs)]
        send_sems, recv_sems, local_sems = refs[len(ins) + len(outs) :]
        edges, locals_ = build(i_refs, o_refs)
        assert len(edges) == n_edges and len(locals_) == n_locals
        run_edges(edges, locals_, send_sems, recv_sems, local_sems)

    return pl.pallas_call(
        kernel,
        name=name,
        out_shape=outs,
        in_specs=[pl.BlockSpec(memory_space=pl.ANY)] * len(ins),
        out_specs=[pl.BlockSpec(memory_space=pl.ANY)] * len(outs),
        scratch_shapes=[
            pltpu.SemaphoreType.DMA((n_edges,)),
            pltpu.SemaphoreType.DMA((n_edges,)),
            pltpu.SemaphoreType.DMA((max(n_locals, 1),)),
        ],
        compiler_params=pltpu.CompilerParams(collective_id=cid, has_side_effects=True),
    )(*ins)


def shape(dims, dtype):
    return jax.ShapeDtypeStruct(dims, dtype)


def seq_partner(z, x, y, c):
    return device(2 * c + y, x, lax.rem(z, 2), lax.div(z, 2))


def spread(tok, cot, pos, gains, wqkv, wgu, wo, wd):
    ins = (tok, cot, pos, gains, wqkv, wgu, wo, wd)
    bf = jnp.bfloat16
    outs = [
        shape(tok.shape, bf),
        shape(cot.shape, bf),
        shape((4,) + pos.shape, jnp.float32),
        shape((4,) + gains.shape, jnp.float32),
        shape(wqkv.shape, bf),
        shape(wgu.shape, bf),
        shape(wo.shape, bf),
        shape(wd.shape, bf),
    ]

    def build(i, o):
        z, x, y, c = coords()
        f = 2 * y + c
        t = 2 * y + x
        stays = z == 2 * c + y
        moves = jnp.logical_not(stays)
        mate = seq_partner(z, x, y, c)
        core = device(z, x, y, 1 - c)
        flip_y = device(z, x, 1 - y, c)
        edges, locals_ = [], []

        def slab(w, r):
            locals_.append((w.at[t], r.at[f], None))
            edges.append(Edge(w.at[2 * (1 - y) + x], r.at[f], flip_y, flip_y))
            k = len(edges) - 1
            got = r.at[2 * (1 - y) + c]
            edges.append(Edge(w.at[t], r.at[f], core, core))
            return (got, core, k)

        relay = [slab(i[4], o[4])]
        edges.append(Edge(i[0], o[0], mate, mate, moves, moves))
        locals_.append((i[0], o[0], stays))
        slot = 2 * lax.rem(z, 2) + x
        for dy in range(2):
            for dx in range(2):
                xt = x if dx == 0 else 1 - x
                yt = lax.rem(z, 2) if dy == 0 else 1 - lax.rem(z, 2)
                to = device(2 * c + y, xt, yt, lax.div(z, 2))
                xs = x if dx == 0 else 1 - x
                ys = lax.rem(z, 2)
                zs = 2 * c + (y if dy == 0 else 1 - y)
                frm = device(zs, xs, ys, lax.div(z, 2))
                if dx == 0 and dy == 0:
                    edges.append(Edge(i[2], o[2].at[slot], to, frm, moves, moves))
                    locals_.append((i[2], o[2].at[slot], stays))
                else:
                    edges.append(Edge(i[2], o[2].at[slot], to, frm))
        locals_.append((i[3], o[3].at[f], None))
        for to in (core, flip_y, device(z, x, 1 - y, 1 - c)):
            edges.append(Edge(i[3], o[3].at[f], to, to))
        relay.append(slab(i[5], o[5]))
        edges.append(Edge(i[1], o[1], mate, mate, moves, moves))
        locals_.append((i[1], o[1], stays))
        own = c == x
        for k in (6, 7):
            locals_.append((i[k], o[k], own))
            edges.append(Edge(i[k], o[k], core, core, own, jnp.logical_not(own)))
        for got, to, k in relay:
            edges.append(Edge(got, got, to, to, after=(k,)))
        return edges, locals_

    return comm_call("spread", 0, build, 17, 8, ins, outs)


def core_swap(name, cid, pairs, ins, outs):
    def build(i, o):
        z, x, y, c = coords()
        core = device(z, x, y, 1 - c)
        sends, keeps = pairs(c)
        edges = [Edge(i[a].at[s], o[b].at[d], core, core) for a, s, b, d in sends]
        locals_ = [(i[a].at[s], o[b].at[d], None) for a, s, b, d in keeps]
        return edges, locals_

    n = [len(v) for v in pairs(0)]
    return comm_call(name, cid, build, n[0], n[1], ins, outs)


def plane_gather(name, cid, blocks):
    n_in = len(blocks)
    half = blocks[0].shape[0] // 2

    def kernel(*refs):
        i_refs, o_refs = refs[:n_in], refs[n_in : 2 * n_in]
        send_sems, recv_sems, local_sems = refs[2 * n_in :]
        z, x, y, c = coords()
        me, sx, sy = 2 * y + x, 2 * y + 1 - x, 2 * (1 - y) + x
        to_x, to_y = device(z, 1 - x, y, c), device(z, x, 1 - y, c)
        lo, hi = pl.ds(0, half), pl.ds(half, half)
        barrier = pltpu.get_barrier_semaphore()
        for d in (to_x, to_y):
            pl.semaphore_signal(barrier, inc=1, device_id=d, device_id_type=MESH)
        keep = [
            pltpu.make_async_copy(a, b.at[me], local_sems.at[k])
            for k, (a, b) in enumerate(zip(i_refs, o_refs))
        ]
        for cp in keep:
            cp.start()
        pl.semaphore_wait(barrier, 2)

        def copy(k, j, src, dst, to):
            return pltpu.make_async_remote_copy(
                src_ref=src,
                dst_ref=dst,
                send_sem=send_sems.at[k, j],
                recv_sem=recv_sems.at[k, j],
                device_id=to,
                device_id_type=MESH,
            )

        all_copies = []
        for k, (a, b) in enumerate(zip(i_refs, o_refs)):
            cps = [
                copy(k, 0, a.at[lo], b.at[me, lo], to_x),
                copy(k, 1, a.at[hi], b.at[me, hi], to_y),
                copy(k, 2, a.at[hi], b.at[me, hi], to_x),
                copy(k, 3, a.at[lo], b.at[me, lo], to_y),
                copy(k, 4, b.at[sy, hi], b.at[sy, hi], to_x),
                copy(k, 5, b.at[sx, lo], b.at[sx, lo], to_y),
            ]
            for cp in cps[:4]:
                cp.start()
            all_copies.append(cps)
        for cps in all_copies:
            cps[1].wait_recv()
            cps[4].start()
            cps[0].wait_recv()
            cps[5].start()
        for cps in all_copies:
            for j in (2, 3, 4, 5):
                cps[j].wait_recv()
            for cp in cps:
                cp.wait_send()
        for cp in keep:
            cp.wait()

    return pl.pallas_call(
        kernel,
        name=name,
        out_shape=[shape((4,) + b.shape, b.dtype) for b in blocks],
        in_specs=[pl.BlockSpec(memory_space=pl.ANY)] * n_in,
        out_specs=[pl.BlockSpec(memory_space=pl.ANY)] * n_in,
        scratch_shapes=[
            pltpu.SemaphoreType.DMA((n_in, 6)),
            pltpu.SemaphoreType.DMA((n_in, 6)),
            pltpu.SemaphoreType.DMA((n_in,)),
        ],
        compiler_params=pltpu.CompilerParams(collective_id=cid, has_side_effects=True),
    )(*blocks)


def plane_scatter(name, cid, partials):
    n_in = len(partials)
    rows, cols = partials[0].shape[1:]
    half = rows // 2

    def kernel(*refs):
        i_refs, o_refs = refs[:n_in], refs[n_in : 2 * n_in]
        got, mid, send_sems, recv_sems = refs[2 * n_in :]
        z, x, y, c = coords()
        me, sx, sy, sd = 2 * y + x, 2 * y + 1 - x, 2 * (1 - y) + x, 2 * (1 - y) + 1 - x
        to_x, to_y = device(z, 1 - x, y, c), device(z, x, 1 - y, c)
        lo, hi = pl.ds(0, half), pl.ds(half, half)
        barrier = pltpu.get_barrier_semaphore()
        for d in (to_x, to_y):
            pl.semaphore_signal(barrier, inc=1, device_id=d, device_id_type=MESH)
        pl.semaphore_wait(barrier, 2)

        def copy(k, j, src, to):
            return pltpu.make_async_remote_copy(
                src_ref=src,
                dst_ref=got.at[k, j],
                send_sem=send_sems.at[k, j],
                recv_sem=recv_sems.at[k, j],
                device_id=to,
                device_id_type=MESH,
            )

        every = []
        for k, a in enumerate(i_refs):
            cps = [
                copy(k, 0, a.at[sd, lo], to_x),
                copy(k, 1, a.at[sd, hi], to_y),
                copy(k, 2, a.at[sx, lo], to_x),
                copy(k, 3, a.at[sy, hi], to_y),
                copy(k, 4, mid.at[k, 0], to_x),
                copy(k, 5, mid.at[k, 1], to_y),
            ]
            for cp in cps[:4]:
                cp.start()
            every.append(cps)
        f32, bf = jnp.float32, jnp.bfloat16
        for k, a in enumerate(i_refs):
            cps = every[k]
            cps[0].wait_recv()
            mid[k, 1] = (a[sy, lo].astype(f32) + got[k, 0].astype(f32)).astype(bf)
            cps[5].start()
            cps[1].wait_recv()
            mid[k, 0] = (a[sx, hi].astype(f32) + got[k, 1].astype(f32)).astype(bf)
            cps[4].start()
        for k, (a, b) in enumerate(zip(i_refs, o_refs)):
            cps = every[k]
            for j in (2, 3, 4, 5):
                cps[j].wait_recv()
            b[lo] = a[me, lo].astype(f32) + got[k, 2].astype(f32) + got[k, 5].astype(f32)
            b[hi] = a[me, hi].astype(f32) + got[k, 3].astype(f32) + got[k, 4].astype(f32)
            for cp in cps:
                cp.wait_send()

    vm = pl.BlockSpec(memory_space=pltpu.VMEM)
    return pl.pallas_call(
        kernel,
        name=name,
        out_shape=[shape((rows, cols), jnp.float32) for _ in partials],
        in_specs=[vm] * n_in,
        out_specs=[vm] * n_in,
        scratch_shapes=[
            pltpu.VMEM((n_in, 6, half, cols), jnp.bfloat16),
            pltpu.VMEM((n_in, 2, half, cols), jnp.bfloat16),
            pltpu.SemaphoreType.DMA((n_in, 6)),
            pltpu.SemaphoreType.DMA((n_in, 6)),
        ],
        compiler_params=pltpu.CompilerParams(
            collective_id=cid, has_side_effects=True, vmem_limit_bytes=40 * 2**20
        ),
    )(*partials)


QT = 256
NEG = -1e30


def dot_nt(a, b):
    return lax.dot_general(a, b, (((1,), (1,)), ((), ())), preferred_element_type=jnp.float32)


def dot_tn(a, b):
    return lax.dot_general(a, b, (((0,), (0,)), ((), ())), preferred_element_type=jnp.float32)


def dot_nn(a, b):
    return jnp.dot(a, b, preferred_element_type=jnp.float32)


LOG2E = math.log2(math.e)


def attend_forward(inverse, qkv):
    length = qkv.shape[0]
    tiles = length // QT
    blocks = QT // BLK
    factor = HD ** (-0.5) * LOG2E

    def kernel(inv, x_ref, o_ref, lse_ref, q_s, k_s, v_s):
        @pl.loop(0, tiles)
        def _(i):
            for h in range(blocks):
                s = inv[i * blocks + h]
                rows = pl.ds(pl.multiple_of(s * BLK, BLK), BLK)
                at = pl.multiple_of(i * QT, QT) + h * BLK
                q_s[i, pl.ds(h * BLK, BLK), :] = x_ref[rows, 0:HD]
                q_s[i, pl.ds(QT + h * BLK, BLK), :] = x_ref[rows, HD : 2 * HD]
                k_s[pl.ds(at, BLK), :] = x_ref[rows, 2 * HD : 3 * HD]
                v_s[pl.ds(at, BLK), 0:HD] = x_ref[rows, 3 * HD : 4 * HD]
        v_s[:, HD : 2 * HD] = jnp.ones((length, HD), jnp.bfloat16)
        rows_ = lax.broadcasted_iota(jnp.int32, (2 * QT, QT), 0)
        cols_ = lax.broadcasted_iota(jnp.int32, (2 * QT, QT), 1)
        allowed = jnp.where(rows_ >= QT, rows_ - QT, rows_) >= cols_

        @pl.loop(0, tiles)
        def _(i):
            q = q_s[i]

            def step(j, acc):
                at = pl.ds(pl.multiple_of(j * QT, QT), QT)
                p = jnp.exp2(dot_nt(q, k_s[at, :]) * factor).astype(jnp.bfloat16)
                return acc + dot_nn(p, v_s[at, :])

            acc = lax.fori_loop(0, i, step, jnp.zeros((2 * QT, 2 * HD), jnp.float32))
            at = pl.ds(pl.multiple_of(i * QT, QT), QT)
            scores = jnp.where(allowed, dot_nt(q, k_s[at, :]) * factor, NEG)
            acc = acc + dot_nn(jnp.exp2(scores).astype(jnp.bfloat16), v_s[at, :])
            total = acc[:, HD:]
            out = acc[:, :HD] / total
            lse_ref[i] = jnp.log2(jnp.transpose(total)[0:8, :])
            for h in range(blocks):
                s = inv[i * blocks + h]
                rows = pl.ds(pl.multiple_of(s * BLK, BLK), BLK)
                o_ref[rows, 0:HD] = out[h * BLK : (h + 1) * BLK].astype(jnp.bfloat16)
                o_ref[rows, HD : 2 * HD] = out[QT + h * BLK : QT + (h + 1) * BLK].astype(
                    jnp.bfloat16
                )

    vm = pl.BlockSpec(memory_space=pltpu.VMEM)
    return pl.pallas_call(
        kernel,
        name="attend_forward",
        out_shape=[
            shape((length, 2 * HD), jnp.bfloat16),
            shape((tiles, 8, 2 * QT), jnp.float32),
        ],
        in_specs=[pl.BlockSpec(memory_space=pltpu.SMEM), vm],
        out_specs=[vm, vm],
        scratch_shapes=[
            pltpu.VMEM((tiles, 2 * QT, HD), jnp.bfloat16),
            pltpu.VMEM((length, HD), jnp.bfloat16),
            pltpu.VMEM((length, 2 * HD), jnp.bfloat16),
        ],
        compiler_params=pltpu.CompilerParams(vmem_limit_bytes=40 * 2**20),
        cost_estimate=pl.CostEstimate(
            flops=2 * 2 * 2 * length * length * HD, bytes_accessed=4 * 2**20, transcendentals=0
        ),
    )(inverse, qkv)


def attend_backward(inverse, qkv, mixed, grad, lse):
    length = qkv.shape[0]
    tiles = length // QT
    blocks = QT // BLK
    scale = HD ** (-0.5)
    factor = scale * LOG2E

    def kernel(inv, x_ref, o_ref, g_ref, lse_ref, d_ref, q_s, g_s, k_s, v_s, delta_s, dq_s):
        @pl.loop(0, tiles)
        def _(i):
            for h in range(blocks):
                s = inv[i * blocks + h]
                rows = pl.ds(pl.multiple_of(s * BLK, BLK), BLK)
                at = pl.ds(pl.multiple_of(i * QT, QT) + h * BLK, BLK)
                for u in range(2):
                    to = pl.ds(u * QT + h * BLK, BLK)
                    lanes = slice(u * HD, (u + 1) * HD)
                    q_s[i, to, :] = x_ref[rows, lanes]
                    g_s[i, to, :] = g_ref[rows, lanes]
                    product = g_ref[rows, lanes].astype(jnp.float32) * o_ref[
                        rows, lanes
                    ].astype(jnp.float32)
                    delta_s[i, :, to] = jnp.broadcast_to(
                        jnp.sum(jnp.transpose(product), axis=0, keepdims=True), (8, BLK)
                    )
                k_s[at, :] = x_ref[rows, 2 * HD : 3 * HD]
                v_s[at, :] = x_ref[rows, 3 * HD : 4 * HD]
        dq_s[...] = jnp.zeros_like(dq_s)
        rows_ = lax.broadcasted_iota(jnp.int32, (QT, 2 * QT), 0)
        cols_ = lax.broadcasted_iota(jnp.int32, (QT, 2 * QT), 1)
        allowed = jnp.where(cols_ >= QT, cols_ - QT, cols_) >= rows_

        @pl.loop(0, tiles)
        def _(j):
            at = pl.ds(pl.multiple_of(j * QT, QT), QT)
            k, v = k_s[at, :], v_s[at, :]

            def pair(i, carry, diagonal):
                dk, dv = carry
                q, g = q_s[i], g_s[i]
                scores = dot_nt(k, q) * factor - lse_ref[i, 0:1, :]
                if diagonal:
                    scores = jnp.where(allowed, scores, NEG)
                p = jnp.exp2(scores)
                ds = (p * (dot_nt(v, g) - delta_s[i, 0:1, :])).astype(jnp.bfloat16)
                dq_s[i] += dot_tn(ds, k)
                return (dk + dot_nn(ds, q), dv + dot_nn(p.astype(jnp.bfloat16), g))

            zero = jnp.zeros((QT, HD), jnp.float32)
            carry = pair(j, (zero, zero), True)
            dk, dv = lax.fori_loop(j + 1, tiles, lambda i, cr: pair(i, cr, False), carry)
            for h in range(blocks):
                s = inv[j * blocks + h]
                rows = pl.ds(pl.multiple_of(s * BLK, BLK), BLK)
                part = slice(h * BLK, (h + 1) * BLK)
                d_ref[rows, 2 * HD : 3 * HD] = (dk[part] * scale).astype(jnp.bfloat16)
                d_ref[rows, 3 * HD : 4 * HD] = dv[part].astype(jnp.bfloat16)

        @pl.loop(0, tiles)
        def _(i):
            for h in range(blocks):
                s = inv[i * blocks + h]
                rows = pl.ds(pl.multiple_of(s * BLK, BLK), BLK)
                for u in range(2):
                    d_ref[rows, u * HD : (u + 1) * HD] = (
                        dq_s[i, pl.ds(u * QT + h * BLK, BLK), :] * scale
                    ).astype(jnp.bfloat16)

    vm = pl.BlockSpec(memory_space=pltpu.VMEM)
    return pl.pallas_call(
        kernel,
        name="attend_backward",
        out_shape=shape((length, 4 * HD), jnp.bfloat16),
        in_specs=[pl.BlockSpec(memory_space=pltpu.SMEM), vm, vm, vm, vm],
        out_specs=vm,
        scratch_shapes=[
            pltpu.VMEM((tiles, 2 * QT, HD), jnp.bfloat16),
            pltpu.VMEM((tiles, 2 * QT, HD), jnp.bfloat16),
            pltpu.VMEM((length, HD), jnp.bfloat16),
            pltpu.VMEM((length, HD), jnp.bfloat16),
            pltpu.VMEM((tiles, 8, 2 * QT), jnp.float32),
            pltpu.VMEM((tiles, 2 * QT, HD), jnp.float32),
        ],
        compiler_params=pltpu.CompilerParams(vmem_limit_bytes=40 * 2**20),
        cost_estimate=pl.CostEstimate(
            flops=5 * 2 * 2 * length * length * HD, bytes_accessed=8 * 2**20, transcendentals=0
        ),
    )(inverse, qkv, mixed, grad, lse)


def line_sum(name, cid, own, lag=4):
    tiles, rows, cols = own.shape
    depth = lax.axis_size("ctx") // 2
    root = depth // 2

    def kernel(a, mine, other, low, high, part, s_sem, r_sem):
        z, x, y, c = coords()
        flip_x = device(z, 1 - x, y, c)
        up, down = device(z + 1, x, y, c), device(z - 1, x, y, c)
        has_down, has_up = z > 0, z < depth - 1
        below, above, is_root = z < root, z > root, z == root
        barrier = pltpu.get_barrier_semaphore()

        def signal(to):
            pl.semaphore_signal(barrier, inc=1, device_id=to, device_id_type=MESH)

        signal(flip_x)
        pl.when(has_down)(lambda: signal(down))
        pl.when(has_up)(lambda: signal(up))
        pl.semaphore_wait(barrier, 1 + has_down.astype(jnp.int32) + has_up.astype(jnp.int32))

        def copy(kind, k, src, dst, to):
            return pltpu.make_async_remote_copy(
                src_ref=src,
                dst_ref=dst.at[k],
                send_sem=s_sem.at[kind, k],
                recv_sem=r_sem.at[kind, k],
                device_id=to,
                device_id_type=MESH,
            )

        def up_part(k):
            return copy(0, k, part.at[k], low, up)

        def down_part(k):
            return copy(1, k, part.at[k], high, down)

        def down_sum(k):
            return copy(2, k, mine.at[k], mine, down)

        def up_sum(k):
            return copy(3, k, mine.at[k], mine, up)

        def x_sum(k):
            return copy(4, k, mine.at[k], other, flip_x)

        f32, bf = jnp.float32, jnp.bfloat16

        def gather(k):
            @pl.when(below)
            def _():
                @pl.when(has_down)
                def _():
                    up_part(k).wait_recv()
                    part[k] = (a[k].astype(f32) + low[k].astype(f32)).astype(bf)

                @pl.when(jnp.logical_not(has_down))
                def _():
                    part[k] = a[k]

                up_part(k).start()

            @pl.when(above)
            def _():
                @pl.when(has_up)
                def _():
                    down_part(k).wait_recv()
                    part[k] = (a[k].astype(f32) + high[k].astype(f32)).astype(bf)

                @pl.when(jnp.logical_not(has_up))
                def _():
                    part[k] = a[k]

                down_part(k).start()

        def finish(k):
            @pl.when(is_root)
            def _():
                up_part(k).wait_recv()
                total = a[k].astype(f32) + low[k].astype(f32)
                if root < depth - 1:
                    down_part(k).wait_recv()
                    total = total + high[k].astype(f32)
                mine[k] = total.astype(bf)
                down_sum(k).start()
                if root < depth - 1:
                    up_sum(k).start()

            @pl.when(below)
            def _():
                down_sum(k).wait_recv()
                pl.when(has_down)(lambda: down_sum(k).start())

            @pl.when(above)
            def _():
                up_sum(k).wait_recv()
                pl.when(has_up)(lambda: up_sum(k).start())

            x_sum(k).start()

        is_end = jnp.logical_or(z == 0, z == depth - 1)
        behind = jnp.where(is_end, tiles, lag)

        @pl.loop(0, 2 * tiles)
        def _(k):
            pl.when(k < tiles)(lambda: gather(k))
            pl.when(jnp.logical_and(k >= behind, k < tiles + behind))(lambda: finish(k - behind))

        @pl.loop(0, tiles)
        def _(k):
            pl.when(below)(lambda: up_part(k).wait_send())
            pl.when(above)(lambda: down_part(k).wait_send())
            pl.when(jnp.logical_and(has_down, jnp.logical_not(above)))(
                lambda: down_sum(k).wait_send()
            )
            pl.when(jnp.logical_and(has_up, jnp.logical_not(below)))(
                lambda: up_sum(k).wait_send()
            )
            x_sum(k).wait()

    vm = pl.BlockSpec(memory_space=pltpu.VMEM)
    bf = jnp.bfloat16
    return pl.pallas_call(
        kernel,
        name=name,
        out_shape=[shape(own.shape, bf), shape(own.shape, bf)],
        in_specs=[vm],
        out_specs=[vm, vm],
        scratch_shapes=[
            pltpu.VMEM(own.shape, bf),
            pltpu.VMEM(own.shape, bf),
            pltpu.VMEM(own.shape, bf),
            pltpu.SemaphoreType.DMA((5, tiles)),
            pltpu.SemaphoreType.DMA((5, tiles)),
        ],
        compiler_params=pltpu.CompilerParams(
            collective_id=cid, has_side_effects=True, vmem_limit_bytes=56 * 2**20
        ),
    )(own)


def fast_body(
    tokens,
    cotangent,
    block_map,
    positions,
    attn_gain,
    query_weight,
    key_weight,
    value_weight,
    query_gain,
    key_gain,
    out_weight,
    mlp_gain,
    gate_weight,
    up_weight,
    down_weight,
):
    bf, f32 = jnp.bfloat16, jnp.float32
    z, x, y, c = coords()
    rows = tokens.shape[1]
    d_rows = query_weight.shape[0]
    ff = gate_weight.shape[1]
    unit = ff // 4
    wqkv = jnp.concatenate(
        [
            query_weight.astype(bf).reshape(d_rows, 8, 2 * HD),
            key_weight.astype(bf).reshape(d_rows, 8, HD),
            value_weight.astype(bf).reshape(d_rows, 8, HD),
        ],
        axis=-1,
    ).reshape(d_rows, 4, 8 * HD)
    wqkv = jnp.transpose(wqkv, (1, 0, 2))
    wgu = jnp.concatenate(
        [
            gate_weight.astype(bf).reshape(d_rows, 4, unit),
            up_weight.astype(bf).reshape(d_rows, 4, unit),
        ],
        axis=-1,
    )
    wgu = jnp.transpose(wgu, (1, 0, 2))
    gains = jnp.concatenate([attn_gain, mlp_gain, query_gain, key_gain])
    n_gain = gains.shape[0]
    gains = jnp.pad(gains, (0, 1024 - n_gain)).reshape(8, 128)
    pos = jnp.pad(positions.reshape(-1).astype(f32), (0, 1024 - rows)).reshape(8, 128)
    tok, cot, pos_all, gains_all, wqkv, wgu, wo, wd = spread(
        tokens.reshape(rows, D),
        cotangent.reshape(rows, D),
        pos,
        gains,
        wqkv,
        wgu,
        out_weight.astype(bf),
        down_weight.astype(bf),
    )
    wqkv = wqkv.reshape(D, 8 * HD)
    wgu = wgu.reshape(D, 2 * unit)
    flat_gains = gains_all.reshape(4, 1024)
    attn_full = flat_gains[:, :d_rows].reshape(-1)
    mlp_full = flat_gains[:, d_rows : 2 * d_rows].reshape(-1)
    hd = HD // 4
    query_full = flat_gains[:, 2 * d_rows : 2 * d_rows + hd].reshape(-1)
    key_full = flat_gains[:, 2 * d_rows + hd : 2 * d_rows + 2 * hd].reshape(-1)
    pos_rows = pos_all.reshape(4, 1024)[:, :rows].reshape(-1)

    flat = tok.astype(f32)
    scale_one = rms_scale(flat)
    n1_own = (flat * scale_one * attn_full).astype(bf)
    n1, dy = plane_gather("gather_n1", 1, [n1_own, cot])
    n1, dy = n1.reshape(-1, D), dy.reshape(-1, D)
    half = n1.shape[0]
    raw = jnp.dot(n1, wqkv, preferred_element_type=f32).reshape(half, 2, 4, HD)
    cosine, sine = rope_tables(pos_rows, HD)
    cosine, sine = cosine[:, None, None, :], sine[:, None, None, :]
    qk_raw = raw[:, :, :3]
    qk_scale = rms_scale(qk_raw)
    qk_unit = qk_raw * qk_scale
    qk_gain = jnp.stack([query_full, query_full, key_full])
    qk = rotate(qk_unit * qk_gain, cosine, sine).astype(bf)
    qkv = jnp.concatenate([qk, raw[:, :, 3:].astype(bf)], axis=2).reshape(half, 2, 4 * HD)
    qkv = jnp.transpose(qkv, (1, 0, 2))

    (qkv_core,) = core_swap(
        "swap_qkv",
        2,
        lambda c: (
            [(0, 1 - c, 0, c)],
            [(0, c, 0, c)],
        ),
        (qkv,),
        [shape((2, half, 4 * HD), bf)],
    )
    qkv_core = qkv_core.reshape(2 * half, 4 * HD)
    inverse = jnp.argsort(block_map.reshape(-1)).astype(jnp.int32)
    mixed, lse = attend_forward(inverse, qkv_core)
    mixed2 = mixed.reshape(2, half, 2 * HD)

    (attended,) = core_swap(
        "swap_mixed",
        3,
        lambda c: ([(0, 1 - c, 0, c)], [(0, c, 0, c)]),
        (mixed2,),
        [shape((2, half, 2 * HD), bf)],
    )
    attended = jnp.concatenate([attended[0], attended[1]], axis=-1)
    part = jnp.dot(attended, wo, preferred_element_type=f32).astype(bf).reshape(4, rows, D)
    (delta,) = plane_scatter("scatter_out", 4, [part])
    middle = flat + delta
    scale_two = rms_scale(middle)
    n2_own = (middle * scale_two * mlp_full).astype(bf)
    (n2,) = plane_gather("gather_n2", 5, [n2_own])
    n2 = n2.reshape(-1, D)
    gate_up = jnp.dot(n2, wgu, preferred_element_type=f32)
    gate, upward = gate_up[:, :unit], gate_up[:, unit:]
    sigmoid_gate = jax.nn.sigmoid(gate)
    silu_gate = gate * sigmoid_gate
    hidden = (silu_gate * upward).astype(bf)
    result_part = jnp.dot(hidden, wd, preferred_element_type=f32).astype(bf).reshape(4, rows, D)
    grad_hidden = lax.dot_general(
        dy, wd, (((1,), (1,)), ((), ())), preferred_element_type=f32
    )
    grad_gate = (grad_hidden * upward * sigmoid_gate * (1.0 + gate * (1.0 - sigmoid_gate))).astype(
        bf
    )
    grad_up = (grad_hidden * silu_gate).astype(bf)
    grad_gu = jnp.concatenate([grad_gate, grad_up], axis=-1)
    dn2_part = (
        lax.dot_general(grad_gu, wgu, (((1,), (1,)), ((), ())), preferred_element_type=f32)
        .astype(bf)
        .reshape(4, rows, D)
    )
    grad_normed_two, result_add = plane_scatter("scatter_mlp", 6, [dn2_part, result_part])
    result = middle + result_add
    grad_out = cot.astype(f32)
    mlp_local = jnp.sum(grad_normed_two * middle * scale_two, axis=0)
    grad_middle = grad_out + norm_back(grad_normed_two * mlp_full, middle, scale_two)
    (dmb,) = plane_gather("gather_dmiddle", 7, [grad_middle.astype(bf)])
    dmb = dmb.reshape(-1, D)
    grad_mixed = lax.dot_general(
        dmb, wo, (((1,), (1,)), ((), ())), preferred_element_type=f32
    ).astype(bf)
    (grad_core,) = core_swap(
        "swap_grad_mixed",
        8,
        lambda c: ([(0, 1 - c, 0, c)], [(0, c, 0, c)]),
        (jnp.stack([grad_mixed[:, : 2 * HD], grad_mixed[:, 2 * HD :]]),),
        [shape((2, half, 2 * HD), bf)],
    )
    grad_core = grad_core.reshape(2 * half, 2 * HD)
    dqkv_core = attend_backward(inverse, qkv_core, mixed, grad_core, lse)
    (dqkv,) = core_swap(
        "swap_dqkv",
        9,
        lambda c: ([(0, 1 - c, 0, c)], [(0, c, 0, c)]),
        (dqkv_core.reshape(2, half, 4 * HD),),
        [shape((2, half, 4 * HD), bf)],
    )
    dqkv = jnp.stack([dqkv[0], dqkv[1]], axis=1).reshape(half, 2, 4, HD)
    grad_unit = unrotate(dqkv[:, :, :3].astype(f32), cosine, sine)
    gain_local = jnp.sum(grad_unit * qk_unit, axis=(0, 1))
    grad_qk = norm_back(grad_unit * qk_gain, qk_raw, qk_scale).astype(bf)
    dqkv = jnp.concatenate([grad_qk, dqkv[:, :, 3:]], axis=2).reshape(half, 8 * HD)
    dn1_part = (
        lax.dot_general(dqkv, wqkv, (((1,), (1,)), ((), ())), preferred_element_type=f32)
        .astype(bf)
        .reshape(4, rows, D)
    )
    (grad_normed,) = plane_scatter("scatter_dn1", 10, [dn1_part])
    attn_local = jnp.sum(grad_normed * flat * scale_one, axis=0)
    input_grad = grad_middle + norm_back(grad_normed * attn_full, flat, scale_one)

    def back(i, o):
        z, x, y, c = coords()
        stays = z == 2 * c + y
        moves = jnp.logical_not(stays)
        mate = seq_partner(z, x, y, c)
        edges = [Edge(i[k], o[k], mate, mate, moves, moves) for k in range(2)]
        return edges, [(i[k], o[k], stays) for k in range(2)]

    result, input_grad = comm_call(
        "outputs_back",
        11,
        back,
        2,
        2,
        (result.astype(bf), input_grad.astype(bf)),
        [shape((rows, D), bf)] * 2,
    )

    n_q = gain_local[0] + gain_local[1]
    gain_sums = lax.psum(
        jnp.concatenate([attn_local, mlp_local, n_q, gain_local[2]]), ("ctx", "fsdp")
    )
    f = 2 * y + c

    def own_gain(at, size):
        return lax.dynamic_slice_in_dim(gain_sums, at + f * (size // 4), size // 4)

    dqkv_w = lax.dot_general(
        n1, dqkv, (((0,), (0,)), ((), ())), preferred_element_type=f32
    ).astype(bf)
    dgu_w = lax.dot_general(
        n2, grad_gu, (((0,), (0,)), ((), ())), preferred_element_type=f32
    ).astype(bf)
    do_w = lax.dot_general(
        attended, dmb, (((0,), (0,)), ((), ())), preferred_element_type=f32
    ).astype(bf)
    dd_w = lax.dot_general(hidden, dy, (((0,), (0,)), ((), ())), preferred_element_type=f32).astype(
        bf
    )
    dqkv_w = dqkv_w.reshape(4, d_rows, 8 * HD)
    dgu_w = dgu_w.reshape(4, d_rows, 2 * unit)
    do_w = do_w.reshape(2, -1, D)
    dd_w = dd_w.reshape(2, -1, D)
    ins = (dqkv_w, dgu_w, do_w, dd_w)
    got = core_swap(
        "swap_weight_grads",
        12,
        lambda c: (
            [(k, 2 * yy + (1 - c), k, yy) for k in range(2) for yy in range(2)]
            + [(k, 1 - c, k, slice(None)) for k in (2, 3)],
            [],
        ),
        ins,
        [
            shape((2,) + dqkv_w.shape[1:], bf),
            shape((2,) + dgu_w.shape[1:], bf),
            shape(do_w.shape[1:], bf),
            shape(dd_w.shape[1:], bf),
        ],
    )

    def own_half(w, axis_pairs):
        if axis_pairs:
            w = w.reshape((2, 2) + w.shape[1:])
            return lax.dynamic_index_in_dim(w, c, 1, keepdims=False)
        return lax.dynamic_index_in_dim(w, c, 0, keepdims=False)

    sums = [
        (own_half(w, k < 2).astype(f32) + r.astype(f32)).astype(bf)
        for k, (w, r) in enumerate(zip(ins, got))
    ]
    def y_swap(i, o):
        z, x, y, c = coords()
        flip = device(z, x, 1 - y, c)
        edges = [Edge(i[k].at[1 - y], o[k].at[y], flip, flip) for k in range(2)]
        locals_ = [(i[k].at[y], o[k].at[y], None) for k in range(2)]
        return edges, locals_

    sq, sg = comm_call(
        "swap_rows",
        13,
        y_swap,
        2,
        2,
        (sums[0], sums[1]),
        [shape(sums[0].shape, bf), shape(sums[1].shape, bf)],
    )
    cols = 512

    def to_tiles(w):
        w = w.reshape((-1, TILE, w.shape[-1] // cols, cols))
        return jnp.transpose(w, (0, 2, 1, 3)).reshape(-1, TILE, cols)

    pieces = [to_tiles(w) for w in (sq, sg, sums[2], sums[3])]
    mine, other = line_sum("line_sum", 14, jnp.concatenate(pieces))
    counts = [p.shape[0] for p in pieces]
    starts = [sum(counts[:k]) for k in range(len(counts))]

    def from_tiles(tiles_, like):
        n_rows, n_cols = like
        w = tiles_.reshape(n_rows // TILE, n_cols // cols, TILE, cols)
        return jnp.transpose(w, (0, 2, 1, 3)).reshape(n_rows, n_cols)

    def part_of(tiles_, k):
        return tiles_[starts[k] : starts[k] + counts[k]]

    od_first = starts[2]
    od_count = counts[2] + counts[3]
    (od_got,) = core_swap(
        "swap_od",
        15,
        lambda c: ([(0, 1 - c, 0, slice(None))], []),
        (
            jnp.where(
                x == 0,
                jnp.stack([mine[od_first:], other[od_first:]]),
                jnp.stack([other[od_first:], mine[od_first:]]),
            ),
        ),
        [shape((od_count, TILE, cols), bf)],
    )
    od_own = jnp.where(c == x, mine[od_first:], other[od_first:])
    od = jnp.where(c == 0, jnp.stack([od_own, od_got]), jnp.stack([od_got, od_own]))
    grad_o = jnp.concatenate(
        [from_tiles(od[k, : counts[2]], do_w.shape[1:]) for k in range(2)]
    ).astype(f32)
    grad_d = jnp.concatenate(
        [from_tiles(od[k, counts[2] :], dd_w.shape[1:]) for k in range(2)]
    ).astype(f32)

    def quarters(k, n_cols):
        m = from_tiles(part_of(mine, k), (2 * d_rows, n_cols)).reshape(2, d_rows, n_cols)
        o = from_tiles(part_of(other, k), (2 * d_rows, n_cols)).reshape(2, d_rows, n_cols)
        first = jnp.where(x == 0, m, o)
        second = jnp.where(x == 0, o, m)
        q = jnp.stack([first, second], axis=1).reshape(4, d_rows, n_cols)
        return jnp.transpose(q, (1, 0, 2)).astype(f32)

    gq = quarters(0, 8 * HD).reshape(d_rows, 8, 4 * HD)
    gg = quarters(1, 2 * unit)
    return (
        result.astype(f32).reshape(tokens.shape),
        input_grad.astype(f32).reshape(tokens.shape),
        own_gain(0, D),
        gq[:, :, : 2 * HD].reshape(d_rows, -1),
        gq[:, :, 2 * HD : 3 * HD].reshape(d_rows, -1),
        gq[:, :, 3 * HD :].reshape(d_rows, -1),
        own_gain(2 * D, HD),
        own_gain(2 * D + HD, HD),
        grad_o,
        own_gain(D, D),
        gg[:, :, :unit].reshape(d_rows, -1),
        gg[:, :, unit:].reshape(d_rows, -1),
        grad_d,
    )


def solution(mesh):
    placed = (
        P("fsdp", "ctx", None),
        P("fsdp", "ctx", None),
        P(),
        P("fsdp", "ctx"),
        P("fsdp"),
        P("fsdp", None),
        P("fsdp", None),
        P("fsdp", None),
        P("fsdp"),
        P("fsdp"),
        P("fsdp", None),
        P("fsdp"),
        P("fsdp", None),
        P("fsdp", None),
        P("fsdp", None),
    )
    fits = mesh.shape["fsdp"] == 4 and mesh.shape["ctx"] == 8
    return jax.shard_map(
        fast_body if fits else body,
        mesh=mesh,
        in_specs=placed,
        out_specs=(
            P("fsdp", "ctx", None),
            P("fsdp", "ctx", None),
            P("fsdp"),
            P("fsdp", None),
            P("fsdp", None),
            P("fsdp", None),
            P("fsdp"),
            P("fsdp"),
            P("fsdp", None),
            P("fsdp"),
            P("fsdp", None),
            P("fsdp", None),
            P("fsdp", None),
        ),
        check_vma=False,
    )
```

```python
import math

import jax
import jax.numpy as jnp
from jax import lax
from jax.experimental import pallas as pl
from jax.experimental.pallas import tpu as pltpu
from jax.sharding import PartitionSpec as P

D = 1024
HQ = 16
HK = 8
HD = 128
BLK = 128


epsilon = 1e-06
theta_base = 1000000.0
masked_value = -1e30


def rms_scale(values):
    return lax.rsqrt(jnp.mean(values * values, axis=-1, keepdims=True) + epsilon)


def norm_back(upstream, values, scale):
    return scale * upstream - values * (scale * scale * scale) * jnp.mean(
        upstream * values, axis=-1, keepdims=True
    )


def rope_tables(positions, head_dim):
    frequency = jnp.exp(
        jnp.arange(0, head_dim, 2).astype(jnp.float32) * (-math.log(theta_base) / head_dim)
    )
    angles = positions.astype(jnp.float32)[..., None] * frequency
    angles = jnp.concatenate([angles, angles], axis=-1)
    return (jnp.cos(angles), jnp.sin(angles))


def rotate(values, cosine, sine_table):
    half_width = values.shape[-1] // 2
    turned = jnp.concatenate([-values[..., half_width:], values[..., :half_width]], axis=-1)
    return values * cosine + turned * sine_table


def unrotate(grads, cosine, sine_table):
    half_width = grads.shape[-1] // 2
    moved = grads * sine_table
    back_turn = jnp.concatenate([moved[..., half_width:], -moved[..., :half_width]], axis=-1)
    return grads * cosine + back_turn


def score_block(grouped, keys_head, allowed, scale):
    scores = (
        jnp.einsum("qgd,sd->gqs", grouped, keys_head, preferred_element_type=jnp.float32) * scale
    )
    return jnp.where(allowed, scores, masked_value)


def body(
    tokens,
    cotangent,
    block_map,
    positions,
    attn_gain,
    query_weight,
    key_weight,
    value_weight,
    query_gain,
    key_gain,
    out_weight,
    mlp_gain,
    gate_weight,
    up_weight,
    down_weight,
):
    seq_count = tokens.shape[0]
    seq_rows = tokens.shape[1]
    total_rows = seq_count * seq_rows
    groups = HQ // HK
    scale = HD ** (-0.5)
    attn_full, query_full, key_full, mlp_full = (
        lax.all_gather(attn_gain, "fsdp", axis=0, tiled=True),
        lax.all_gather(query_gain, "fsdp", axis=0, tiled=True),
        lax.all_gather(key_gain, "fsdp", axis=0, tiled=True),
        lax.all_gather(mlp_gain, "fsdp", axis=0, tiled=True),
    )
    query_w, key_w, value_w, out_w = (
        lax.all_gather(query_weight.astype(jnp.bfloat16), "fsdp", axis=0, tiled=True),
        lax.all_gather(key_weight.astype(jnp.bfloat16), "fsdp", axis=0, tiled=True),
        lax.all_gather(value_weight.astype(jnp.bfloat16), "fsdp", axis=0, tiled=True),
        lax.all_gather(out_weight.astype(jnp.bfloat16), "fsdp", axis=0, tiled=True),
    )
    flat = tokens.astype(jnp.float32).reshape(total_rows, D)
    scale_one = rms_scale(flat)
    normed = (flat * scale_one * attn_full).astype(jnp.bfloat16)
    query_raw = jnp.dot(normed, query_w, preferred_element_type=jnp.float32).reshape(
        total_rows, HQ, HD
    )
    key_raw = jnp.dot(normed, key_w, preferred_element_type=jnp.float32).reshape(total_rows, HK, HD)
    value_low = jnp.dot(normed, value_w, preferred_element_type=jnp.float32).astype(jnp.bfloat16)
    cosine, sine_table = rope_tables(positions.reshape(total_rows), HD)
    cosine = cosine[:, None, :]
    sine_table = sine_table[:, None, :]
    query_scale = rms_scale(query_raw)
    query_unit = query_raw * query_scale
    query_low = rotate(query_unit * query_full, cosine, sine_table).astype(jnp.bfloat16)
    key_scale = rms_scale(key_raw)
    key_unit = key_raw * key_scale
    key_low = rotate(key_unit * key_full, cosine, sine_table).astype(jnp.bfloat16)
    flat_map = block_map.reshape(-1)
    offsets = jnp.arange(BLK, dtype=jnp.int32)
    key_index = (flat_map[:, None] * BLK + offsets[None, :]).reshape(-1)
    own_blocks = lax.dynamic_slice_in_dim(flat_map, lax.axis_index("ctx") * 2, 2)
    query_index = (own_blocks[:, None] * BLK + offsets[None, :]).reshape(-1)
    allowed = query_index[:, None] >= key_index[None, :]
    query_seq = query_low.reshape(seq_count, seq_rows, HK, groups, HD)
    key_seq = key_low.reshape(seq_count, seq_rows, HK * HD)
    value_seq = value_low.reshape(seq_count, seq_rows, HK * HD)

    def forward_head(inputs):
        grouped, keys_head, values_head = inputs
        scores = score_block(grouped, keys_head, allowed, scale)
        row_max = jnp.max(scores, axis=-1, keepdims=True)
        exp_scores = jnp.exp(scores - row_max)
        row_total = jnp.sum(exp_scores, axis=-1, keepdims=True)
        prob_low = (exp_scores / row_total).astype(jnp.bfloat16)
        mixed = jnp.einsum("gqs,sd->qgd", prob_low, values_head, preferred_element_type=jnp.float32)
        return (mixed, row_max + jnp.log(row_total))

    seq_item = 0
    keys_all = lax.all_gather(key_seq[seq_item], "ctx", axis=0, tiled=True)
    values_all = lax.all_gather(value_seq[seq_item], "ctx", axis=0, tiled=True)
    keys_head = jnp.transpose(keys_all.reshape(-1, HK, HD), (1, 0, 2))
    values_head = jnp.transpose(values_all.reshape(-1, HK, HD), (1, 0, 2))
    grouped_head = jnp.transpose(query_seq[seq_item], (1, 0, 2, 3))
    mixed, lse = lax.map(forward_head, (grouped_head, keys_head, values_head))
    mixed_parts = jnp.transpose(mixed, (1, 0, 2, 3)).reshape(seq_rows, HQ * HD)
    lse_parts = [lse]
    gathered = [(grouped_head, keys_head, values_head)]
    attended = mixed_parts.astype(jnp.bfloat16)
    middle = flat + jnp.dot(attended, out_w, preferred_element_type=jnp.float32)
    gate_w, up_w, down_w = (
        lax.all_gather(gate_weight.astype(jnp.bfloat16), "fsdp", axis=0, tiled=True),
        lax.all_gather(up_weight.astype(jnp.bfloat16), "fsdp", axis=0, tiled=True),
        lax.all_gather(down_weight.astype(jnp.bfloat16), "fsdp", axis=0, tiled=True),
    )
    scale_two = rms_scale(middle)
    normed_two = (middle * scale_two * mlp_full).astype(jnp.bfloat16)
    gate = jnp.dot(normed_two, gate_w, preferred_element_type=jnp.float32)
    upward = jnp.dot(normed_two, up_w, preferred_element_type=jnp.float32)
    sigmoid_gate = jax.nn.sigmoid(gate)
    silu_gate = gate * sigmoid_gate
    hidden = (silu_gate * upward).astype(jnp.bfloat16)
    result = middle + jnp.dot(hidden, down_w, preferred_element_type=jnp.float32)
    query_back, key_back, value_back, out_back = (
        lax.all_gather(query_weight.astype(jnp.bfloat16), "fsdp", axis=0, tiled=True),
        lax.all_gather(key_weight.astype(jnp.bfloat16), "fsdp", axis=0, tiled=True),
        lax.all_gather(value_weight.astype(jnp.bfloat16), "fsdp", axis=0, tiled=True),
        lax.all_gather(out_weight.astype(jnp.bfloat16), "fsdp", axis=0, tiled=True),
    )
    gate_back, up_back, down_back = (
        lax.all_gather(gate_weight.astype(jnp.bfloat16), "fsdp", axis=0, tiled=True),
        lax.all_gather(up_weight.astype(jnp.bfloat16), "fsdp", axis=0, tiled=True),
        lax.all_gather(down_weight.astype(jnp.bfloat16), "fsdp", axis=0, tiled=True),
    )
    grad_out = cotangent.astype(jnp.float32).reshape(total_rows, D)
    grad_branch = grad_out.astype(jnp.bfloat16)
    down_grad = jnp.einsum("nf,nd->fd", hidden, grad_branch, preferred_element_type=jnp.float32)
    grad_hidden = jnp.einsum(
        "nd,fd->nf", grad_branch, down_back, preferred_element_type=jnp.float32
    )
    grad_gate = (grad_hidden * upward * sigmoid_gate * (1.0 + gate * (1.0 - sigmoid_gate))).astype(
        jnp.bfloat16
    )
    grad_up = (grad_hidden * silu_gate).astype(jnp.bfloat16)
    gate_grad = jnp.einsum("nd,nf->df", normed_two, grad_gate, preferred_element_type=jnp.float32)
    up_grad = jnp.einsum("nd,nf->df", normed_two, grad_up, preferred_element_type=jnp.float32)
    grad_normed_two = jnp.einsum(
        "nf,df->nd", grad_gate, gate_back, preferred_element_type=jnp.float32
    ) + jnp.einsum("nf,df->nd", grad_up, up_back, preferred_element_type=jnp.float32)
    mlp_local = jnp.sum(grad_normed_two * middle * scale_two, axis=0)
    grad_middle = grad_out + norm_back(grad_normed_two * mlp_full, middle, scale_two)
    grad_attn_low = grad_middle.astype(jnp.bfloat16)
    out_grad = jnp.einsum("nq,nd->qd", attended, grad_attn_low, preferred_element_type=jnp.float32)
    grad_mixed = jnp.einsum(
        "nd,qd->nq", grad_attn_low, out_back, preferred_element_type=jnp.float32
    ).astype(jnp.bfloat16)
    grad_mixed_seq = grad_mixed.reshape(seq_count, seq_rows, HK, groups, HD)

    def backward_head(inputs):
        grouped, keys_head, values_head, grad_head, lse = inputs
        scores = score_block(grouped, keys_head, allowed, scale)
        prob_full = jnp.exp(scores - lse)
        grad_prob = jnp.einsum(
            "qgd,sd->gqs", grad_head, values_head, preferred_element_type=jnp.float32
        )
        delta_row = jnp.sum(prob_full * grad_prob, axis=-1, keepdims=True)
        grad_scores = (prob_full * (grad_prob - delta_row)).astype(jnp.bfloat16)
        grad_query_head = (
            jnp.einsum("gqs,sd->qgd", grad_scores, keys_head, preferred_element_type=jnp.float32)
            * scale
        )
        grad_key_head = (
            jnp.einsum("gqs,qgd->sd", grad_scores, grouped, preferred_element_type=jnp.float32)
            * scale
        )
        grad_value_head = jnp.einsum(
            "gqs,qgd->sd",
            prob_full.astype(jnp.bfloat16),
            grad_head,
            preferred_element_type=jnp.float32,
        )
        return (grad_query_head, grad_key_head, grad_value_head)

    seq_item = 0
    grouped_head, keys_head, values_head = gathered[seq_item]
    grad_head = jnp.transpose(grad_mixed_seq[seq_item], (1, 0, 2, 3))
    grad_query_head, grad_key_head, grad_value_head = lax.map(
        backward_head, (grouped_head, keys_head, values_head, grad_head, lse_parts[seq_item])
    )
    grad_query_parts = jnp.transpose(grad_query_head, (1, 0, 2, 3)).reshape(seq_rows, HQ, HD)
    grad_keys_all = jnp.transpose(grad_key_head, (1, 0, 2)).reshape(-1, HK * HD)
    grad_values_all = jnp.transpose(grad_value_head, (1, 0, 2)).reshape(-1, HK * HD)
    grad_key_own = lax.psum_scatter(
        grad_keys_all.astype(jnp.bfloat16), "ctx", scatter_dimension=0, tiled=True
    ).astype(jnp.float32)
    grad_value_own = lax.psum_scatter(
        grad_values_all.astype(jnp.bfloat16), "ctx", scatter_dimension=0, tiled=True
    )
    grad_key = grad_key_own.reshape(total_rows, HK, HD)
    grad_query_unit = unrotate(grad_query_parts, cosine, sine_table)
    qgain_local = jnp.sum(grad_query_unit * query_unit, axis=(0, 1))
    grad_query_low = (
        norm_back(grad_query_unit * query_full, query_raw, query_scale)
        .astype(jnp.bfloat16)
        .reshape(total_rows, HQ * HD)
    )
    grad_key_unit = unrotate(grad_key, cosine, sine_table)
    kgain_local = jnp.sum(grad_key_unit * key_unit, axis=(0, 1))
    grad_key_low = (
        norm_back(grad_key_unit * key_full, key_raw, key_scale)
        .astype(jnp.bfloat16)
        .reshape(total_rows, HK * HD)
    )
    query_grad = jnp.einsum("nd,nc->dc", normed, grad_query_low, preferred_element_type=jnp.float32)
    key_grad = jnp.einsum("nd,nc->dc", normed, grad_key_low, preferred_element_type=jnp.float32)
    value_grad = jnp.einsum("nd,nc->dc", normed, grad_value_own, preferred_element_type=jnp.float32)
    grad_normed = jnp.einsum(
        "nc,dc->nd", grad_query_low, query_back, preferred_element_type=jnp.float32
    )
    grad_normed = grad_normed + jnp.einsum(
        "nc,dc->nd", grad_key_low, key_back, preferred_element_type=jnp.float32
    )
    grad_normed = grad_normed + jnp.einsum(
        "nc,dc->nd", grad_value_own, value_back, preferred_element_type=jnp.float32
    )
    attn_local = jnp.sum(grad_normed * flat * scale_one, axis=0)
    input_grad = grad_middle + norm_back(grad_normed * attn_full, flat, scale_one)
    shares = (
        lax.psum_scatter(
            attn_local.astype(jnp.bfloat16), "fsdp", scatter_dimension=0, tiled=True
        ).astype(jnp.float32),
        lax.psum_scatter(
            query_grad.astype(jnp.bfloat16), "fsdp", scatter_dimension=0, tiled=True
        ).astype(jnp.float32),
        lax.psum_scatter(
            key_grad.astype(jnp.bfloat16), "fsdp", scatter_dimension=0, tiled=True
        ).astype(jnp.float32),
        lax.psum_scatter(
            value_grad.astype(jnp.bfloat16), "fsdp", scatter_dimension=0, tiled=True
        ).astype(jnp.float32),
        lax.psum_scatter(
            qgain_local.astype(jnp.bfloat16), "fsdp", scatter_dimension=0, tiled=True
        ).astype(jnp.float32),
        lax.psum_scatter(
            kgain_local.astype(jnp.bfloat16), "fsdp", scatter_dimension=0, tiled=True
        ).astype(jnp.float32),
        lax.psum_scatter(
            out_grad.astype(jnp.bfloat16), "fsdp", scatter_dimension=0, tiled=True
        ).astype(jnp.float32),
        lax.psum_scatter(
            mlp_local.astype(jnp.bfloat16), "fsdp", scatter_dimension=0, tiled=True
        ).astype(jnp.float32),
        lax.psum_scatter(
            gate_grad.astype(jnp.bfloat16), "fsdp", scatter_dimension=0, tiled=True
        ).astype(jnp.float32),
        lax.psum_scatter(
            up_grad.astype(jnp.bfloat16), "fsdp", scatter_dimension=0, tiled=True
        ).astype(jnp.float32),
        lax.psum_scatter(
            down_grad.astype(jnp.bfloat16), "fsdp", scatter_dimension=0, tiled=True
        ).astype(jnp.float32),
    )
    summed = (
        lax.psum(shares[0].astype(jnp.bfloat16), "ctx").astype(jnp.float32),
        lax.psum(shares[1].astype(jnp.bfloat16), "ctx").astype(jnp.float32),
        lax.psum(shares[2].astype(jnp.bfloat16), "ctx").astype(jnp.float32),
        lax.psum(shares[3].astype(jnp.bfloat16), "ctx").astype(jnp.float32),
        lax.psum(shares[4].astype(jnp.bfloat16), "ctx").astype(jnp.float32),
        lax.psum(shares[5].astype(jnp.bfloat16), "ctx").astype(jnp.float32),
        lax.psum(shares[6].astype(jnp.bfloat16), "ctx").astype(jnp.float32),
        lax.psum(shares[7].astype(jnp.bfloat16), "ctx").astype(jnp.float32),
        lax.psum(shares[8].astype(jnp.bfloat16), "ctx").astype(jnp.float32),
        lax.psum(shares[9].astype(jnp.bfloat16), "ctx").astype(jnp.float32),
        lax.psum(shares[10].astype(jnp.bfloat16), "ctx").astype(jnp.float32),
    )
    return (
        result.reshape(tokens.shape),
        input_grad.reshape(tokens.shape),
        summed[0],
        summed[1],
        summed[2],
        summed[3],
        summed[4],
        summed[5],
        summed[6],
        summed[7],
        summed[8],
        summed[9],
        summed[10],
    )


MESH = pl.DeviceIdType.MESH
BF = jnp.bfloat16
F32 = jnp.float32
LOG2E = math.log2(math.e)
QT = 256
NEG = -1e30


def shape(dims, dtype):
    return jax.ShapeDtypeStruct(dims, dtype)


def dot_nn(a, b):
    return jnp.dot(a, b, preferred_element_type=F32)


def dot_nt(a, b):
    return lax.dot_general(a, b, (((1,), (1,)), ((), ())), preferred_element_type=F32)


def dot_tn(a, b):
    return lax.dot_general(a, b, (((0,), (0,)), ((), ())), preferred_element_type=F32)


def device(z, x, y, c):
    return (z * 2 + x, y * 2 + c)


def coords():
    a = lax.axis_index("ctx")
    f = lax.axis_index("fsdp")
    return lax.div(a, 2), lax.rem(a, 2), lax.div(f, 2), lax.rem(f, 2)


class Net:
    def __init__(self, send_sems, recv_sems):
        self.z, self.x, self.y, self.c = z, x, y, c = coords()
        self.depth = lax.axis_size("ctx") // 2
        self.to_x = device(z, 1 - x, y, c)
        self.to_y = device(z, x, 1 - y, c)
        self.to_core = device(z, x, y, 1 - c)
        self.to_x_other = device(z, 1 - x, y, 1 - c)
        self.up = device(z + 1, x, y, c)
        self.down = device(z - 1, x, y, c)
        self.has_up = z < self.depth - 1
        self.has_down = z > 0
        self.send_sems, self.recv_sems = send_sems, recv_sems
        self.used = 0
        self.me = 2 * y + x
        self.sx = 2 * y + 1 - x
        self.sy = 2 * (1 - y) + x
        self.sd = 2 * (1 - y) + 1 - x

    def greet(self, line=True, owners=False, mate=None):
        barrier = pltpu.get_barrier_semaphore()

        def signal(to):
            pl.semaphore_signal(barrier, inc=1, device_id=to, device_id_type=MESH)

        for to in (self.to_x, self.to_y, self.to_core):
            signal(to)
        count = 3
        if owners:
            signal(self.to_x_other)
            count = count + 1
        if mate is not None:
            pl.when(mate[0])(lambda: signal(mate[1]))
            count = count + mate[0].astype(jnp.int32)
        if line:
            pl.when(self.has_up)(lambda: signal(self.up))
            pl.when(self.has_down)(lambda: signal(self.down))
            count = count + self.has_up.astype(jnp.int32) + self.has_down.astype(jnp.int32)
        pl.semaphore_wait(barrier, count)

    def take(self, count=1):
        first = self.used
        self.used += count
        assert self.used <= self.send_sems.shape[0], self.used
        return first

    def copy(self, sem, src, dst, to):
        return pltpu.make_async_remote_copy(
            src_ref=src,
            dst_ref=dst,
            send_sem=self.send_sems.at[sem],
            recv_sem=self.recv_sems.at[sem],
            device_id=to,
            device_id_type=MESH,
        )

    def new(self, src, dst, to):
        return self.copy(self.take(), src, dst, to)


def rms(values):
    return lax.rsqrt(jnp.mean(values * values, axis=-1, keepdims=True) + epsilon)


class PlaneGather:
    def __init__(self, net, src, out):
        half = out.shape[1] // 2
        lo, hi = pl.ds(0, half), pl.ds(half, half)
        me, sx, sy = net.me, net.sx, net.sy
        self.x_lo = net.new(src.at[lo], out.at[me, lo], net.to_x)
        self.y_hi = net.new(src.at[hi], out.at[me, hi], net.to_y)
        self.x_hi = net.new(src.at[hi], out.at[me, hi], net.to_x)
        self.y_lo = net.new(src.at[lo], out.at[me, lo], net.to_y)
        self.fx = net.new(out.at[sy, hi], out.at[sy, hi], net.to_x)
        self.fy = net.new(out.at[sx, lo], out.at[sx, lo], net.to_y)

    def start(self):
        for cp in (self.x_lo, self.y_hi, self.x_hi, self.y_lo):
            cp.start()

    def forward(self):
        self.y_hi.wait_recv()
        self.fx.start()
        self.x_lo.wait_recv()
        self.fy.start()

    def wait_sides(self):
        self.x_hi.wait_recv()
        self.y_lo.wait_recv()

    def wait_diagonal(self):
        self.fx.wait_recv()
        self.fy.wait_recv()

    def drain(self):
        for cp in (self.x_lo, self.y_hi, self.x_hi, self.y_lo, self.fx, self.fy):
            cp.wait_send()


class PlaneSum:
    def __init__(self, net, part, got, mid):
        half = part.shape[1] // 2
        self.half = half
        self.lo, self.hi = lo, hi = pl.ds(0, half), pl.ds(half, half)
        self.net, self.part, self.got, self.mid = net, part, got, mid
        me, sx, sy, sd = net.me, net.sx, net.sy, net.sd
        self.c0 = net.new(part.at[sd, lo], got.at[0], net.to_x)
        self.c1 = net.new(part.at[sd, hi], got.at[1], net.to_y)
        self.c2 = net.new(part.at[sx, lo], got.at[2], net.to_x)
        self.c3 = net.new(part.at[sy, hi], got.at[3], net.to_y)
        self.c4 = net.new(mid.at[0], got.at[4], net.to_x)
        self.c5 = net.new(mid.at[1], got.at[5], net.to_y)

    def start_diagonal(self):
        self.c0.start()
        self.c1.start()

    def start_sides(self):
        self.c2.start()
        self.c3.start()

    def forward(self):
        net = self.net
        self.c0.wait_recv()
        self.mid[1] = (
            self.part[net.sy, self.lo].astype(F32) + self.got[0].astype(F32)
        ).astype(BF)
        self.c5.start()
        self.c1.wait_recv()
        self.mid[0] = (
            self.part[net.sx, self.hi].astype(F32) + self.got[1].astype(F32)
        ).astype(BF)
        self.c4.start()

    def finish(self, use):
        me = self.net.me
        for rows, a, b, first, second in (
            (self.lo, self.c2, self.c5, 2, 5),
            (self.hi, self.c3, self.c4, 3, 4),
        ):
            a.wait_recv()
            b.wait_recv()
            use(
                rows,
                self.part[me, rows].astype(F32)
                + self.got[first].astype(F32)
                + self.got[second].astype(F32),
            )

    def drain(self):
        for cp in (self.c0, self.c1, self.c2, self.c3, self.c4, self.c5):
            cp.wait_send()


class Route:
    def __init__(self, net, src, line, out, parts=2):
        self.net, self.src, self.line, self.out = net, src, line, out
        self.SUB = parts
        self.rows = src.shape[0] // self.SUB
        depth = net.depth
        self.l_sem = net.take(depth * self.SUB)
        self.c_sem = net.take(2 * self.SUB)
        self.y_sem = net.take(2 * self.SUB)
        self.x_sem = net.take(2 * self.SUB)
        self.place = 2 * net.c + net.y
        self.entry = net.z == self.place
        self.row0 = net.y == lax.rem(net.z, 2)

    def part(self, s):
        return pl.ds(s * self.rows, self.rows)

    def hop(self, k, s, own, to):
        src = self.src.at[self.part(s)] if own else self.line.at[k, self.part(s)]
        return self.net.copy(self.l_sem + k * self.SUB + s, src, self.line.at[k, self.part(s)], to)

    def chip(self, k, s):
        j = lax.rem(k, 2)
        return self.net.copy(
            self.c_sem + j * self.SUB + s,
            self.line.at[k, self.part(s)],
            self.out.at[2 * j + self.net.x, self.part(s)],
            self.net.to_core,
        )

    def over_y(self, j, s):
        at = self.out.at[2 * j + self.net.x, self.part(s)]
        return self.net.copy(self.y_sem + j * self.SUB + s, at, at, self.net.to_y)

    def over_x(self, j, s):
        at = self.out.at[2 * j + self.net.x, self.part(s)]
        return self.net.copy(self.x_sem + j * self.SUB + s, at, at, self.net.to_x)

    def from_x(self, j, s):
        at = self.out.at[2 * j + 1 - self.net.x, self.part(s)]
        return self.net.copy(self.x_sem + j * self.SUB + s, at, at, self.net.to_x)

    def start(self):
        net = self.net
        for s in range(self.SUB):
            pl.when(net.z < self.place)(lambda: self.hop(net.z, s, True, net.up).start())
            pl.when(net.z > self.place)(lambda: self.hop(net.z, s, True, net.down).start())

    def relay(self):
        net = self.net
        for d in range(1, net.depth):
            for s in range(self.SUB):

                @pl.when(jnp.logical_and(net.z < self.place, net.z >= d))
                def _():
                    self.hop(net.z - d, s, False, net.up).wait_recv()
                    self.hop(net.z - d, s, False, net.up).start()

                @pl.when(jnp.logical_and(net.z > self.place, net.z < net.depth - d))
                def _():
                    self.hop(net.z + d, s, False, net.down).wait_recv()
                    self.hop(net.z + d, s, False, net.down).start()

    def enter(self):
        net = self.net
        for d in range(net.depth):
            for s in range(self.SUB):
                for k in range(net.depth):
                    near = jnp.logical_or(self.place - k == d, k - self.place == d)
                    here = jnp.logical_and(self.entry, near)

                    @pl.when(here)
                    def _():
                        if d > 0:
                            self.hop(k, s, False, net.up).wait_recv()
                        else:
                            self.line[k, self.part(s)] = self.src[self.part(s)]

                    @pl.when(jnp.logical_and(here, net.c == k // 2))
                    def _():
                        self.out[2 * (k % 2) + net.x, self.part(s)] = self.line[k, self.part(s)]
                        self.over_x(k % 2, s).start()
                        self.over_y(k % 2, s).start()

                    @pl.when(jnp.logical_and(here, net.c != k // 2))
                    def _():
                        self.chip(k, s).start()

    def spread(self):
        net = self.net
        beside = jnp.logical_and(self.row0, jnp.logical_not(self.entry))

        def one(j, s):
            @pl.when(beside)
            def _():
                self.chip(j, s).wait_recv()
                self.over_x(j, s).start()
                self.over_y(j, s).start()

            @pl.when(jnp.logical_not(self.row0))
            def _():
                self.over_y(j, s).wait_recv()
                self.over_x(j, s).start()

        @pl.loop(0, 2)
        def _(n):
            j = jnp.where(net.z <= 2 * net.c, n, 1 - n)
            for s in range(self.SUB):
                one(j, s)

    def wait(self, j):
        for s in range(self.SUB):
            self.from_x(j, s).wait_recv()

    def drain(self):
        net = self.net
        for s in range(self.SUB):
            pl.when(net.z < self.place)(lambda: self.hop(net.z, s, True, net.up).wait_send())
            pl.when(net.z > self.place)(lambda: self.hop(net.z, s, True, net.down).wait_send())
            for d in range(1, net.depth):

                @pl.when(jnp.logical_and(net.z < self.place, net.z >= d))
                def _():
                    self.hop(net.z - d, s, False, net.up).wait_send()

                @pl.when(jnp.logical_and(net.z > self.place, net.z < net.depth - d))
                def _():
                    self.hop(net.z + d, s, False, net.down).wait_send()

            for k in range(net.depth):

                @pl.when(jnp.logical_and(self.entry, net.c != k // 2))
                def _():
                    self.chip(k, s).wait_send()

            for j in range(2):
                self.over_x(j, s).wait_send()
                pl.when(self.row0)(lambda: self.over_y(j, s).wait_send())


class LineSum:
    def __init__(self, net, tiles, src, mine, low, high, part, deliver):
        self.net, self.tiles, self.src, self.mine = net, tiles, src, mine
        self.low, self.high, self.part, self.deliver = low, high, part, deliver
        self.sems = net.take(4 * tiles)
        self.root = net.depth // 2
        self.below = net.z < self.root
        self.above = net.z > self.root
        self.middle = net.z == self.root
        self.two_sided = self.root < net.depth - 1

    def hop(self, kind, k):
        net = self.net
        src, dst, to = (
            (self.part.at[k], self.low.at[k], net.up),
            (self.part.at[k], self.high.at[k], net.down),
            (self.mine(k), self.mine(k), net.down),
            (self.mine(k), self.mine(k), net.up),
        )[kind]
        return net.copy(self.sems + kind * self.tiles + k, src, dst, to)

    def gather(self, k):
        net = self.net

        def send(kind, slots, has_before):
            @pl.when(has_before)
            def _():
                self.hop(kind, k).wait_recv()
                total = self.src(k)[...].astype(F32) + slots[k].astype(F32)
                self.part[k] = total.astype(self.part.dtype)

            @pl.when(jnp.logical_not(has_before))
            def _():
                self.part[k] = self.src(k)[...]

            self.hop(kind, k).start()

        pl.when(self.below)(lambda: send(0, self.low, net.has_down))
        pl.when(self.above)(lambda: send(1, self.high, net.has_up))

    def finish(self, k):
        net = self.net

        @pl.when(self.middle)
        def _():
            self.hop(0, k).wait_recv()
            total = self.src(k)[...].astype(F32) + self.low[k].astype(F32)
            if self.two_sided:
                self.hop(1, k).wait_recv()
                total = total + self.high[k].astype(F32)
            self.mine(k)[...] = total.astype(self.part.dtype)
            self.hop(2, k).start()
            if self.two_sided:
                self.hop(3, k).start()

        @pl.when(self.below)
        def _():
            self.hop(2, k).wait_recv()
            pl.when(net.has_down)(lambda: self.hop(2, k).start())

        @pl.when(self.above)
        def _():
            self.hop(3, k).wait_recv()
            pl.when(net.has_up)(lambda: self.hop(3, k).start())

        self.deliver(k)

    def drain(self, k):
        net = self.net
        pl.when(self.below)(lambda: self.hop(0, k).wait_send())
        pl.when(self.above)(lambda: self.hop(1, k).wait_send())
        sends_down = jnp.logical_and(net.has_down, jnp.logical_not(self.above))
        sends_up = jnp.logical_and(net.has_up, jnp.logical_not(self.below))
        pl.when(sends_down)(lambda: self.hop(2, k).wait_send())
        pl.when(sends_up)(lambda: self.hop(3, k).wait_send())


def any_spec():
    return pl.BlockSpec(memory_space=pl.ANY)


def vmem_spec():
    return pl.BlockSpec(memory_space=pltpu.VMEM)


def params(cid, mib=60):
    return pltpu.CompilerParams(
        collective_id=cid, has_side_effects=True, vmem_limit_bytes=mib * 2**20
    )


def enter(tok, pos, gains, frequency, wq, wk, wv):
    rows = tok.shape[0]
    d_rows = wq.shape[0]
    half = 4 * rows
    n_sems = 48

    def kernel(
        tok_ref,
        pos_ref,
        gain_ref,
        freq_ref,
        wq_ref,
        wk_ref,
        wv_ref,
        x_own,
        n1,
        raw_ref,
        table,
        core,
        wall,
        gains_ref,
        wq_s,
        wk_s,
        wv_s,
        wloc,
        line,
        toks,
        pos_line,
        poss,
        heads,
        gslots,
        ssem,
        rsem,
        lsem,
    ):
        net = Net(ssem, rsem)
        y, c = net.y, net.c
        f = 2 * y + c
        fy = 2 * (1 - y) + c
        loads = [
            pltpu.make_async_copy(a, b, lsem.at[k])
            for k, (a, b) in enumerate(((wq_ref, wq_s), (wk_ref, wk_s), (wv_ref, wv_s)))
        ]
        for cp in loads:
            cp.start()
        net.greet()
        pos_route = Route(net, pos_ref, pos_line, poss, 1)
        route = Route(net, tok_ref, line, toks)
        pos_route.start()
        route.start()
        g_core = net.new(gain_ref, gslots.at[f], net.to_core)
        g_y = net.new(gain_ref, gslots.at[f], net.to_y)
        g_relay = net.new(gslots.at[fy], gslots.at[fy], net.to_core)
        g_core.start()
        g_y.start()
        gslots[f] = gain_ref[...]
        for cp in loads:
            cp.wait()
        for t in range(4):
            at = t * 4 * HD
            wloc[t, :, 0 : 4 * HD] = wq_s[:, at : at + 4 * HD].astype(BF)
            at = t * 2 * HD
            wloc[t, :, 4 * HD : 6 * HD] = wk_s[:, at : at + 2 * HD].astype(BF)
            wloc[t, :, 6 * HD : 8 * HD] = wv_s[:, at : at + 2 * HD].astype(BF)
        w_y = net.new(wloc.at[net.sy], wall.at[f], net.to_y)
        w_core = net.new(wloc.at[net.me], wall.at[f], net.to_core)
        w_relay = net.new(wall.at[fy], wall.at[fy], net.to_core)
        w_y.start()
        w_core.start()
        wall[f] = wloc[net.me]
        pos_route.relay()
        route.relay()
        pos_route.enter()
        route.enter()
        pos_route.spread()
        route.spread()
        g_y.wait_recv()
        g_relay.start()
        w_y.wait_recv()
        w_relay.start()
        g_core.wait_recv()
        g_relay.wait_recv()
        w_core.wait_recv()
        w_relay.wait_recv()
        full = gslots[0] + gslots[1] + gslots[2] + gslots[3]
        gains_ref[...] = full
        attn_gain, q_gain, k_gain = full[0:1, :], full[2:3, 0:HD], full[3:4, 0:HD]
        for j in range(2):
            pos_route.wait(j)
            route.wait(j)
        x_own[...] = toks[net.me]
        swaps = net.take(4)

        def swap(k):
            at = pl.ds(pl.multiple_of(k * rows, rows), rows)
            return net.copy(swaps + k, heads.at[1 - c, at], core.at[c, at], net.to_core)

        @pl.loop(0, 4)
        def _(k):
            at = pl.ds(pl.multiple_of(k * rows, rows), rows)
            flat = toks[k].astype(F32)
            normed = (flat * rms(flat) * attn_gain).astype(BF)
            n1[at, :] = normed
            raw = dot_nn(normed[:, 0:d_rows], wall[0])
            for g in range(1, 4):
                raw = raw + dot_nn(normed[:, g * d_rows : (g + 1) * d_rows], wall[g])
            raw_ref[at, :] = raw[:, 0 : 6 * HD]
            place = jnp.transpose(poss[k])
            angles = jnp.concatenate(
                [place[:, h : h + 1] * freq_ref[0:1, 0 : HD // 2] for h in range(rows // 128)],
                axis=0,
            )
            cosine, sine = jnp.cos(angles), jnp.sin(angles)
            table[at, :] = jnp.concatenate([cosine, sine], axis=-1)
            cosine = jnp.concatenate([cosine, cosine], axis=-1)
            sine = jnp.concatenate([-sine, sine], axis=-1)
            for h in range(6):
                u = raw[:, h * HD : (h + 1) * HD]
                unit = u * rms(u) * (q_gain if h < 4 else k_gain)
                turned = unit * cosine + pltpu.roll(unit, HD // 2, 1) * sine
                g, lane = (h // 2, (h % 2) * HD) if h < 4 else (h - 4, 2 * HD)
                heads[g, at, lane : lane + HD] = turned.astype(BF)
            for g in range(2):
                v = raw[:, (6 + g) * HD : (7 + g) * HD]
                heads[g, at, 3 * HD : 4 * HD] = v.astype(BF)
            swap(k).start()
            core[c, at] = heads[c, at]

        for k in range(4):
            swap(k).wait()
        for cp in (g_core, g_y, g_relay, w_core, w_y, w_relay):
            cp.wait_send()
        pos_route.drain()
        route.drain()

    vm = vmem_spec()
    return pl.pallas_call(
        kernel,
        name="enter",
        out_shape=[
            shape((rows, D), BF),
            shape((half, D), BF),
            shape((half, 6 * HD), F32),
            shape((half, HD), F32),
            shape((2, half, 4 * HD), BF),
            shape((4, d_rows, 8 * HD), BF),
            shape((8, D), F32),
        ],
        in_specs=[vm] * 4 + [any_spec()] * 3,
        out_specs=[vm] * 7,
        scratch_shapes=[
            pltpu.VMEM(wq.shape, F32),
            pltpu.VMEM(wk.shape, F32),
            pltpu.VMEM(wv.shape, F32),
            pltpu.VMEM((4, d_rows, 8 * HD), BF),
            pltpu.VMEM((4, rows, D), BF),
            pltpu.VMEM((4, rows, D), BF),
            pltpu.VMEM((4, 8, 128), F32),
            pltpu.VMEM((4, 8, 128), F32),
            pltpu.VMEM((2, half, 4 * HD), BF),
            pltpu.VMEM((4, 8, D), F32),
            pltpu.SemaphoreType.DMA((n_sems,)),
            pltpu.SemaphoreType.DMA((n_sems,)),
            pltpu.SemaphoreType.DMA((3,)),
        ],
        compiler_params=params(0),
        cost_estimate=pl.CostEstimate(
            flops=2 * half * D * 8 * HD, bytes_accessed=16 * 2**20, transcendentals=0
        ),
    )(tok, pos, gains, frequency, wq, wk, wv)


def attend(block_map, inverse, core, cot, wg, wu, wo, wd):
    half = core.shape[1]
    length = 2 * half
    tiles = length // QT
    blocks = QT // BLK
    n_blocks = length // BLK
    factor = HD ** (-0.5) * LOG2E
    rows = cot.shape[0]
    d_rows = wg.shape[0]
    unit = wg.shape[1] // 4
    n_sems = 48

    def kernel(
        bm,
        inv,
        x_ref,
        cot_ref,
        wg_ref,
        wu_ref,
        wo_ref,
        wd_ref,
        att,
        mixed,
        lse_ref,
        cots,
        cot_own,
        wgu,
        wo_out,
        wd_out,
        q_s,
        k_s,
        v_s,
        o_s,
        wg_s,
        wu_s,
        wo_s,
        wd_s,
        wloc,
        line,
        ssem,
        rsem,
        lsem,
    ):
        net = Net(ssem, rsem)
        x, y, c = net.x, net.y, net.c
        f = 2 * y + c
        fy = 2 * (1 - y) + c
        loads = [
            pltpu.make_async_copy(a, b, lsem.at[k])
            for k, (a, b) in enumerate(
                ((wg_ref, wg_s), (wu_ref, wu_s), (wo_ref, wo_s), (wd_ref, wd_s))
            )
        ]
        for cp in loads:
            cp.start()
        net.greet()
        route = Route(net, cot_ref, line, cots)
        route.start()
        w_y = net.new(wloc.at[net.sy], wgu.at[f], net.to_y)
        w_core = net.new(wloc.at[net.me], wgu.at[f], net.to_core)
        w_relay = net.new(wgu.at[fy], wgu.at[fy], net.to_core)
        o_core = net.new(wo_out, wo_out, net.to_core)
        d_core = net.new(wd_out, wd_out, net.to_core)
        own = c == x

        @pl.loop(0, tiles)
        def _(i):
            for h in range(blocks):
                block = x_ref[inv[i * blocks + h]]
                at = pl.multiple_of(i * QT, QT) + h * BLK
                q_s[i, pl.ds(h * BLK, BLK), :] = block[:, 0:HD]
                q_s[i, pl.ds(QT + h * BLK, BLK), :] = block[:, HD : 2 * HD]
                k_s[pl.ds(at, BLK), :] = block[:, 2 * HD : 3 * HD]
                v_s[pl.ds(at, BLK), 0:HD] = block[:, 3 * HD : 4 * HD]

        v_s[:, HD : 2 * HD] = jnp.ones((length, HD), BF)
        for cp in loads:
            cp.wait()
        for t in range(4):
            wloc[t, :, 0:unit] = wg_s[:, t * unit : (t + 1) * unit].astype(BF)
            wloc[t, :, unit : 2 * unit] = wu_s[:, t * unit : (t + 1) * unit].astype(BF)
        w_y.start()
        w_core.start()
        wgu[f] = wloc[net.me]

        @pl.when(own)
        def _():
            wo_out[...] = wo_s[...].astype(BF)
            wd_out[...] = wd_s[...].astype(BF)
            o_core.start()
            d_core.start()

        q_row = lax.broadcasted_iota(jnp.int32, (2 * QT, QT), 0)
        k_row = lax.broadcasted_iota(jnp.int32, (2 * QT, QT), 1)
        allowed = jnp.where(q_row >= QT, q_row - QT, q_row) >= k_row

        def tile(i):
            q = q_s[i]

            def step(j, acc):
                at = pl.ds(pl.multiple_of(j * QT, QT), QT)
                p = jnp.exp2(dot_nt(q, k_s[at, :]) * factor).astype(BF)
                return acc + dot_nn(p, v_s[at, :])

            acc = lax.fori_loop(0, i, step, jnp.zeros((2 * QT, 2 * HD), F32))
            at = pl.ds(pl.multiple_of(i * QT, QT), QT)
            scores = jnp.where(allowed, dot_nt(q, k_s[at, :]) * factor, NEG)
            acc = acc + dot_nn(jnp.exp2(scores).astype(BF), v_s[at, :])
            total = acc[:, HD:]
            out = acc[:, :HD] / total
            lse_ref[i] = jnp.log2(jnp.transpose(total)[0:8, :])
            for h in range(blocks):
                for u in range(2):
                    o_s[i * blocks + h, :, u * HD : (u + 1) * HD] = out[
                        u * QT + h * BLK : u * QT + (h + 1) * BLK
                    ].astype(BF)

        @pl.loop(0, tiles)
        def _(i):
            tile(i)

            @pl.when(i == tiles // 2)
            def _():
                route.relay()

            @pl.when(i == tiles - 2)
            def _():
                route.enter()

        route.spread()
        w_y.wait_recv()
        w_relay.start()
        swap = net.take(1)

        @pl.loop(0, n_blocks)
        def _(s):
            mixed[pl.ds(pl.multiple_of(s * BLK, BLK), BLK), :] = o_s[bm[s]]

        away = mixed.at[pl.ds(pl.multiple_of((1 - c) * half, half), half)]
        o_swap = net.copy(swap, away, att.at[c], net.to_core)
        o_swap.start()
        att[c] = mixed[pl.ds(pl.multiple_of(c * half, half), half), :]
        pl.when(jnp.logical_not(own))(lambda: o_core.wait_recv())
        pl.when(jnp.logical_not(own))(lambda: d_core.wait_recv())
        w_core.wait_recv()
        w_relay.wait_recv()
        for j in range(2):
            route.wait(j)
        cot_own[...] = cots[net.me]
        o_swap.wait()
        pl.when(own)(lambda: o_core.wait_send())
        pl.when(own)(lambda: d_core.wait_send())
        for cp in (w_y, w_core, w_relay):
            cp.wait_send()
        route.drain()

    vm = vmem_spec()
    smem = pl.BlockSpec(memory_space=pltpu.SMEM)
    return pl.pallas_call(
        kernel,
        name="attend",
        out_shape=[
            shape((2, half, 2 * HD), BF),
            shape((length, 2 * HD), BF),
            shape((tiles, 8, 2 * QT), F32),
            shape((4, rows, D), BF),
            shape((rows, D), BF),
            shape((4, d_rows, 2 * unit), BF),
            shape(wo.shape, BF),
            shape(wd.shape, BF),
        ],
        in_specs=[smem, smem, vm, vm] + [any_spec()] * 4,
        out_specs=[vm] * 8,
        scratch_shapes=[
            pltpu.VMEM((tiles, 2 * QT, HD), BF),
            pltpu.VMEM((length, HD), BF),
            pltpu.VMEM((length, 2 * HD), BF),
            pltpu.VMEM((n_blocks, BLK, 2 * HD), BF),
            pltpu.VMEM(wg.shape, F32),
            pltpu.VMEM(wu.shape, F32),
            pltpu.VMEM(wo.shape, F32),
            pltpu.VMEM(wd.shape, F32),
            pltpu.VMEM((4, d_rows, 2 * unit), BF),
            pltpu.VMEM((4, rows, D), BF),
            pltpu.SemaphoreType.DMA((n_sems,)),
            pltpu.SemaphoreType.DMA((n_sems,)),
            pltpu.SemaphoreType.DMA((4,)),
        ],
        compiler_params=params(1),
        cost_estimate=pl.CostEstimate(
            flops=2 * 2 * 2 * length * length * HD, bytes_accessed=16 * 2**20, transcendentals=0
        ),
    )(block_map, inverse, core.reshape(n_blocks, BLK, 4 * HD), cot, wg, wu, wo, wd)


def feed_forward(att, x_own, wo, wgu, wd, cots, cot_own, gains):
    half = att.shape[1]
    rows = half // 4
    unit = wd.shape[0]
    d_rows = wgu.shape[1]
    n_sems = 48

    def kernel(
        att_ref,
        x_ref,
        wo_ref,
        wgu_ref,
        wd_ref,
        dy_ref,
        cot_ref,
        gain_ref,
        core,
        middle,
        dmiddle,
        result_part,
        sum_gu,
        sum_od,
        mlp_gain_part,
        part,
        got,
        mid,
        n2,
        hid,
        dgu,
        got2,
        mid2,
        dmb,
        gm,
        w_gu,
        got_gu,
        w_d,
        got_d,
        w_o,
        got_o,
        ssem,
        rsem,
    ):
        net = Net(ssem, rsem)
        c, me, sx, sy, sd = net.c, net.me, net.sx, net.sy, net.sd
        mlp_gain = gain_ref[1:2, :]
        net.greet(False)
        out_sum = PlaneSum(net, part, got, mid)

        def chunk(k):
            return pl.ds(pl.multiple_of(k * rows, rows), rows)

        def project(k):
            part[k] = (
                dot_nn(att_ref[0, chunk(k)], wo_ref[0 : 2 * HD, :])
                + dot_nn(att_ref[1, chunk(k)], wo_ref[2 * HD : 4 * HD, :])
            ).astype(BF)

        project(sd)
        out_sum.start_diagonal()
        project(sx)
        project(sy)
        out_sum.start_sides()
        project(me)
        out_sum.forward()

        def add_residual(at, total):
            value = x_ref[at].astype(F32) + total
            middle[at] = value
            n2[me, at] = (value * rms(value) * mlp_gain).astype(BF)

        out_sum.finish(add_residual)
        gather = PlaneGather(net, n2.at[me], n2)
        gather.start()

        def forward_back(k):
            rows_k = n2[k]
            gate_up = dot_nn(rows_k[:, 0:d_rows], wgu_ref[0])
            for g in range(1, 4):
                gate_up = gate_up + dot_nn(rows_k[:, g * d_rows : (g + 1) * d_rows], wgu_ref[g])
            gate, upward = gate_up[:, 0:unit], gate_up[:, unit : 2 * unit]
            sigmoid = 1.0 / (1.0 + jnp.exp(-gate))
            silu = gate * sigmoid
            hid[k] = (silu * upward).astype(BF)
            dh = dot_nt(dy_ref[k], wd_ref[...])
            dgu[k, :, 0:unit] = (
                dh * upward * sigmoid * (1.0 + gate * (1.0 - sigmoid))
            ).astype(BF)
            dgu[k, :, unit : 2 * unit] = (dh * silu).astype(BF)
            grads = dgu[k]
            for g in range(4):
                part[k, :, g * d_rows : (g + 1) * d_rows] = dot_nt(grads, wgu_ref[g]).astype(BF)

        out_sum.drain()
        forward_back(me)
        gather.forward()
        gather.wait_sides()
        back_sum = PlaneSum(net, part, got2, mid2)

        @pl.loop(0, 2)
        def _(n):
            forward_back(jnp.where(n == 0, sx, sy))

        back_sum.start_sides()
        gather.wait_diagonal()
        forward_back(sd)
        back_sum.start_diagonal()

        @pl.loop(0, 4)
        def _(k):
            result_part[k] = dot_nn(hid[k], wd_ref[...]).astype(BF)

        back_sum.forward()
        gu_sem = net.take(2)
        d_sem = net.take(1)
        o_sem = net.take(1)

        def gu_copy(n):
            return net.copy(gu_sem + n, w_gu.at[n], got_gu.at[n], net.to_core)

        d_copy = net.copy(d_sem, w_d, got_d, net.to_core)
        o_copy = net.copy(o_sem, w_o, got_o, net.to_core)
        all_dgu = dgu.shape[2]

        def slab(n, core_of):
            f = 2 * n + core_of
            at = pl.ds(pl.multiple_of(f * d_rows, d_rows), d_rows)
            return dot_tn(n2[:, :, at].reshape(half, d_rows), dgu[...].reshape(half, all_dgu))

        @pl.loop(0, 2)
        def _(n):
            w_gu[n] = slab(n, 1 - c).astype(BF)
            gu_copy(n).start()

        unit_half = unit // 2

        def down(core_of):
            at = pl.ds(pl.multiple_of(core_of * unit_half, unit_half), unit_half)
            return dot_tn(hid[:, :, at].reshape(half, unit_half), dy_ref[...].reshape(half, D))

        w_d[...] = down(1 - c).astype(BF)
        d_copy.start()

        def back_through_norm(at, dn2):
            value = middle[at]
            scale = rms(value)
            w2 = dn2 * mlp_gain
            grad = cot_ref[at].astype(F32) + norm_back(w2, value, scale)
            dmiddle[at] = grad
            dmb[me, at] = grad.astype(BF)
            first = back_sum.half // 8
            folded = jnp.sum((dn2 * value * scale).reshape(first, 8, D), axis=0)
            mlp_gain_part[...] += folded

        mlp_gain_part[...] = jnp.zeros_like(mlp_gain_part)
        back_sum.finish(back_through_norm)
        gather2 = PlaneGather(net, dmb.at[me], dmb)
        gather2.start()
        swap_sem = net.take(4)

        def swap(k):
            return net.copy(
                swap_sem + k, gm.at[1 - c, chunk(k)], core.at[c, chunk(k)], net.to_core
            )

        def grad_mixed(k):
            value = dot_nt(dmb[k], wo_ref[...]).astype(BF)
            gm[0, chunk(k)] = value[:, 0 : 2 * HD]
            gm[1, chunk(k)] = value[:, 2 * HD : 4 * HD]
            swap(k).start()
            core[c, chunk(k)] = gm[c, chunk(k)]

        grad_mixed(me)

        @pl.loop(0, 2)
        def _(n):
            value = slab(n, c)
            gu_copy(n).wait_recv()
            sum_gu[n] = (value + got_gu[n].astype(F32)).astype(BF)

        gather2.forward()
        value = down(c)
        d_copy.wait_recv()
        sum_od[0:unit_half] = (value + got_d[...].astype(F32)).astype(BF)
        gather2.wait_sides()

        @pl.loop(0, 2)
        def _(n):
            grad_mixed(jnp.where(n == 0, sx, sy))

        gather2.wait_diagonal()
        grad_mixed(sd)

        def out_grad(g):
            return dot_tn(att_ref[g], dmb[...].reshape(half, D))

        w_o[...] = out_grad(1 - c).astype(BF)
        o_copy.start()
        value = out_grad(c)
        o_copy.wait_recv()
        sum_od[unit_half : unit_half + 2 * HD] = (value + got_o[...].astype(F32)).astype(BF)
        for k in range(4):
            swap(k).wait()
        for n in range(2):
            gu_copy(n).wait_send()
        d_copy.wait_send()
        o_copy.wait_send()
        gather.drain()
        gather2.drain()
        back_sum.drain()

    vm = vmem_spec()
    half_rows = rows // 2
    return pl.pallas_call(
        kernel,
        name="feed_forward",
        out_shape=[
            shape((2, half, 2 * HD), BF),
            shape((rows, D), F32),
            shape((rows, D), F32),
            shape((4, rows, D), BF),
            shape((2, d_rows, 2 * unit), BF),
            shape((unit // 2 + 2 * HD, D), BF),
            shape((8, D), F32),
        ],
        in_specs=[vm] * 8,
        out_specs=[vm] * 7,
        scratch_shapes=[
            pltpu.VMEM((4, rows, D), BF),
            pltpu.VMEM((6, half_rows, D), BF),
            pltpu.VMEM((2, half_rows, D), BF),
            pltpu.VMEM((4, rows, D), BF),
            pltpu.VMEM((4, rows, unit), BF),
            pltpu.VMEM((4, rows, 2 * unit), BF),
            pltpu.VMEM((6, half_rows, D), BF),
            pltpu.VMEM((2, half_rows, D), BF),
            pltpu.VMEM((4, rows, D), BF),
            pltpu.VMEM((2, half, 2 * HD), BF),
            pltpu.VMEM((2, d_rows, 2 * unit), BF),
            pltpu.VMEM((2, d_rows, 2 * unit), BF),
            pltpu.VMEM((unit // 2, D), BF),
            pltpu.VMEM((unit // 2, D), BF),
            pltpu.VMEM((2 * HD, D), BF),
            pltpu.VMEM((2 * HD, D), BF),
            pltpu.SemaphoreType.DMA((n_sems,)),
            pltpu.SemaphoreType.DMA((n_sems,)),
        ],
        compiler_params=params(2, 62),
        cost_estimate=pl.CostEstimate(
            flops=24 * half * D * unit, bytes_accessed=32 * 2**20, transcendentals=0
        ),
    )(att, x_own, wo, wgu, wd, cots, cot_own, gains)


TILE = 64


def attend_back(block_map, inverse, core, mixed, grad, lse, sum_od, sum_gu, result_part, middle):
    half = core.shape[1]
    length = 2 * half
    tiles = length // QT
    blocks = QT // BLK
    n_blocks = length // BLK
    scale = HD ** (-0.5)
    factor = scale * LOG2E
    rows = middle.shape[0]
    od_tiles = sum_od.shape[0] // TILE
    pairs = tiles * (tiles + 1) // 2
    every = 3
    n_sems = 4 * od_tiles + 3 * od_tiles + 16

    def kernel(
        bm,
        inv,
        x_ref,
        o_ref,
        g_ref,
        lse_ref,
        od_ref,
        gu_ref,
        rp_ref,
        mid_ref,
        dq,
        result,
        od_final,
        gu_rows,
        q_s,
        g_s,
        k_s,
        v_s,
        delta_s,
        dq_s,
        d_s,
        d_c,
        got,
        mid,
        low,
        high,
        part,
        od_sum,
        ssem,
        rsem,
    ):
        net = Net(ssem, rsem)
        x, y, c = net.x, net.y, net.c
        net.greet(True, True)
        total = PlaneSum(net, rp_ref, got, mid)
        gu_y = net.new(gu_ref.at[1 - y], gu_rows.at[1], net.to_y)
        swap = net.new(
            d_s.at[pl.ds(pl.multiple_of((1 - c) * half, half), half)], dq.at[c], net.to_core
        )
        x_sem = net.take(2 * od_tiles)
        chip_sem = net.take(od_tiles)
        owner = device(net.z, 1 - x, y, x)
        owns = c == x

        def cross(k, h):
            return net.copy(
                x_sem + h * od_tiles + k, od_sum.at[k], od_final.at[h, k], owner
            )

        def chip(k, h):
            return net.copy(chip_sem + k, od_sum.at[k], od_final.at[h, k], net.to_core)

        def deliver(k):
            cross(k, c).start()

            @pl.when(owns)
            def _():
                od_final[c, k] = od_sum[k]

            pl.when(jnp.logical_not(owns))(lambda: chip(k, c).start())

        line = LineSum(
            net,
            od_tiles,
            lambda k: od_ref.at[pl.ds(pl.multiple_of(k * TILE, TILE), TILE)],
            lambda k: od_sum.at[k],
            low,
            high,
            part,
            deliver,
        )
        total.start_diagonal()
        total.start_sides()
        gu_y.start()
        gu_rows[0] = gu_ref[y]
        at_end = jnp.logical_or(net.z == 0, net.z == net.depth - 1)
        lag = jnp.where(line.middle, 1, jnp.where(at_end, 6, 4))

        @pl.when(at_end)
        def _():
            @pl.loop(0, od_tiles)
            def _(k):
                line.gather(k)

        @pl.loop(0, tiles)
        def _(i):
            for h in range(blocks):
                s = inv[i * blocks + h]
                block, out, grad_ = x_ref[s], o_ref[s], g_ref[s]
                at = pl.ds(pl.multiple_of(i * QT, QT) + h * BLK, BLK)
                for u in range(2):
                    to = pl.ds(u * QT + h * BLK, BLK)
                    lanes = slice(u * HD, (u + 1) * HD)
                    q_s[i, to, :] = block[:, lanes]
                    g_s[i, to, :] = grad_[:, lanes]
                    product = grad_[:, lanes].astype(F32) * out[:, lanes].astype(F32)
                    delta_s[i, :, to] = jnp.broadcast_to(
                        jnp.sum(jnp.transpose(product), axis=0, keepdims=True), (8, BLK)
                    )
                k_s[at, :] = block[:, 2 * HD : 3 * HD]
                v_s[at, :] = block[:, 3 * HD : 4 * HD]

        dq_s[...] = jnp.zeros_like(dq_s)
        k_row = lax.broadcasted_iota(jnp.int32, (QT, 2 * QT), 0)
        q_row = lax.broadcasted_iota(jnp.int32, (QT, 2 * QT), 1)
        allowed = jnp.where(q_row >= QT, q_row - QT, q_row) >= k_row

        def pump(n):
            k = lax.div(n, every)
            due = lax.rem(n, every) == 0

            @pl.when(jnp.logical_and(due, jnp.logical_and(k < od_tiles, jnp.logical_not(at_end))))
            def _():
                line.gather(k)

            @pl.when(jnp.logical_and(due, jnp.logical_and(k >= lag, k - lag < od_tiles)))
            def _():
                line.finish(k - lag)

            pl.when(n == 10)(total.forward)

        @pl.loop(0, tiles)
        def _(j):
            at = pl.ds(pl.multiple_of(j * QT, QT), QT)
            k, v = k_s[at, :], v_s[at, :]
            first = j * tiles - lax.div(j * (j - 1), 2)

            def pair(i, carry, diagonal):
                pump(first + i - j)
                dk, dv = carry
                q, g = q_s[i], g_s[i]
                scores = dot_nt(k, q) * factor - lse_ref[i, 0:1, :]
                if diagonal:
                    scores = jnp.where(allowed, scores, NEG)
                p = jnp.exp2(scores)
                ds = (p * (dot_nt(v, g) - delta_s[i, 0:1, :])).astype(BF)
                dq_s[i] += dot_tn(ds, k)
                return (dk + dot_nn(ds, q), dv + dot_nn(p.astype(BF), g))

            zero = jnp.zeros((QT, HD), F32)
            carry = pair(j, (zero, zero), True)
            dk, dv = lax.fori_loop(j + 1, tiles, lambda i, cr: pair(i, cr, False), carry)
            for h in range(blocks):
                part_ = slice(h * BLK, (h + 1) * BLK)
                b = j * blocks + h
                d_c[b, :, 2 * HD : 3 * HD] = (dk[part_] * scale).astype(BF)
                d_c[b, :, 3 * HD : 4 * HD] = dv[part_].astype(BF)

        @pl.loop(0, tiles)
        def _(i):
            for h in range(blocks):
                for u in range(2):
                    at = pl.ds(u * QT + h * BLK, BLK)
                    d_c[i * blocks + h, :, u * HD : (u + 1) * HD] = (
                        dq_s[i, at, :] * scale
                    ).astype(BF)

        @pl.loop(0, n_blocks)
        def _(s):
            d_s[pl.ds(pl.multiple_of(s * BLK, BLK), BLK), :] = d_c[bm[s]]

        swap.start()
        dq[c] = d_s[pl.ds(pl.multiple_of(c * half, half), half), :]

        def add(at, value):
            result[at] = (mid_ref[at] + value).astype(BF)

        total.finish(add)
        done_tiles = -(-pairs // every) - lag

        @pl.loop(0, od_tiles)
        def _(k):
            pl.when(k >= done_tiles)(lambda: line.finish(k))

        @pl.loop(0, od_tiles)
        def _(k):
            @pl.when(owns)
            def _():
                chip(k, 1 - c).wait_recv()

            @pl.when(jnp.logical_not(owns))
            def _():
                for h in range(2):
                    cross(k, h).wait_recv()
                chip(k, c).wait_send()

            cross(k, c).wait_send()
            line.drain(k)

        gu_y.wait()
        swap.wait()
        total.drain()

    vm = vmem_spec()
    smem = pl.BlockSpec(memory_space=pltpu.SMEM)
    half_rows = rows // 2
    slots = pltpu.VMEM((od_tiles, TILE, D), BF)
    return pl.pallas_call(
        kernel,
        name="attend_back",
        out_shape=[
            shape((2, half, 4 * HD), BF),
            shape((rows, D), BF),
            shape((2, od_tiles, TILE, D), BF),
            shape(sum_gu.shape, BF),
        ],
        in_specs=[smem, smem] + [vm] * 8,
        out_specs=[vm] * 4,
        scratch_shapes=[
            pltpu.VMEM((tiles, 2 * QT, HD), BF),
            pltpu.VMEM((tiles, 2 * QT, HD), BF),
            pltpu.VMEM((length, HD), BF),
            pltpu.VMEM((length, HD), BF),
            pltpu.VMEM((tiles, 8, 2 * QT), F32),
            pltpu.VMEM((tiles, 2 * QT, HD), F32),
            pltpu.VMEM((length, 4 * HD), BF),
            pltpu.VMEM((n_blocks, BLK, 4 * HD), BF),
            pltpu.VMEM((6, half_rows, D), BF),
            pltpu.VMEM((2, half_rows, D), BF),
            slots,
            slots,
            slots,
            slots,
            pltpu.SemaphoreType.DMA((n_sems,)),
            pltpu.SemaphoreType.DMA((n_sems,)),
        ],
        compiler_params=params(3),
        cost_estimate=pl.CostEstimate(
            flops=5 * 2 * 2 * length * length * HD, bytes_accessed=16 * 2**20, transcendentals=0
        ),
    )(
        block_map,
        inverse,
        core.reshape(n_blocks, BLK, 4 * HD),
        mixed.reshape(n_blocks, BLK, 2 * HD),
        grad.reshape(n_blocks, BLK, 2 * HD),
        lse,
        sum_od,
        sum_gu,
        result_part,
        middle,
    )


def leave(dq, raw, table, n1, wall, x_own, dmiddle, gains, result, gu_rows, mlp_gain_part):
    half = n1.shape[0]
    rows = half // 4
    d_rows = wall.shape[1]
    gu_cols = gu_rows.shape[2]
    unit = gu_cols // 2
    per = d_rows // TILE
    tiles = 2 * per
    n_sems = 2 * 5 * tiles + 40

    def kernel(
        dq_ref,
        raw_ref,
        table_ref,
        n1_ref,
        wall_ref,
        x_ref,
        dmid_ref,
        gain_ref,
        res_ref,
        gu_ref,
        mlp_ref,
        result_out,
        input_out,
        out_q,
        out_k,
        out_v,
        out_g,
        out_u,
        gain_out,
        dcat,
        part,
        got,
        mid,
        grad_in,
        w_out,
        w_got,
        w_sum,
        w_rows,
        gu_low,
        gu_high,
        gu_part,
        gu_mine,
        gu_other,
        w_low,
        w_high,
        w_part,
        w_mine,
        w_other,
        g_sum,
        g_got,
        g_low,
        g_high,
        g_part,
        g_mine,
        acc,
        ssem,
        rsem,
    ):
        net = Net(ssem, rsem)
        z, x, y, c = net.z, net.x, net.y, net.c
        stays = z == 2 * c + y
        moves = jnp.logical_not(stays)
        mate = device(2 * c + y, x, lax.rem(z, 2), lax.div(z, 2))
        net.greet(True, False, (moves, mate))
        res_copy = net.new(res_ref, result_out, mate)
        in_copy = net.new(grad_in, input_out, mate)

        def send_home(cp, src, dst):
            pl.when(moves)(cp.start)

            @pl.when(stays)
            def _():
                dst[...] = src[...]

        def row_tile(ref):
            def at(k):
                return ref.at[lax.div(k, per), pl.ds(pl.multiple_of(lax.rem(k, per) * TILE, TILE), TILE)]

            return at

        gx_sem = net.take(tiles)
        wx_sem = net.take(tiles)

        def gu_cross(k):
            return net.copy(gx_sem + k, gu_mine.at[k], gu_other.at[k], net.to_x)

        def w_cross(k):
            return net.copy(wx_sem + k, w_mine.at[k], w_other.at[k], net.to_x)

        gu_line = LineSum(
            net,
            tiles,
            row_tile(gu_ref),
            lambda k: gu_mine.at[k],
            gu_low,
            gu_high,
            gu_part,
            lambda k: gu_cross(k).start(),
        )
        w_line = LineSum(
            net,
            tiles,
            row_tile(w_rows),
            lambda k: w_mine.at[k],
            w_low,
            w_high,
            w_part,
            lambda k: w_cross(k).start(),
        )
        g_line = LineSum(
            net,
            1,
            lambda k: g_sum.at[0],
            lambda k: g_mine.at[0],
            g_low,
            g_high,
            g_part,
            lambda k: None,
        )
        at_end = jnp.logical_or(z == 0, z == net.depth - 1)

        @pl.when(at_end)
        def _():
            @pl.loop(0, tiles)
            def _(k):
                gu_line.gather(k)

        def gu_gather(k):
            pl.when(jnp.logical_not(at_end))(lambda: gu_line.gather(k))

        send_home(res_copy, res_ref, result_out)
        total = PlaneSum(net, part, got, mid)
        attn_gain, q_gain, k_gain = gain_ref[0:1, :], gain_ref[2:3, 0:HD], gain_ref[3:4, 0:HD]
        acc[...] = jnp.zeros_like(acc)

        def fold(v):
            return jnp.sum(v.reshape(v.shape[0] // 8, 8, v.shape[1]), axis=0)

        def chunk(k):
            at = pl.ds(pl.multiple_of(k * rows, rows), rows)
            half_w = HD // 2
            cosine, sine = table_ref[at, 0:half_w], table_ref[at, half_w:HD]
            cosine = jnp.concatenate([cosine, cosine], axis=-1)
            sine = jnp.concatenate([-sine, sine], axis=-1)
            for h in range(6):
                g, lane = (h // 2, (h % 2) * HD) if h < 4 else (h - 4, 2 * HD)
                gain = q_gain if h < 4 else k_gain
                grad = dq_ref[g, at, lane : lane + HD].astype(F32)
                du = grad * cosine - pltpu.roll(grad, half_w, 1) * sine
                u = raw_ref[at, h * HD : (h + 1) * HD]
                scale = rms(u)
                lanes = slice(0, HD) if h < 4 else slice(HD, 2 * HD)
                acc[2, :, lanes] += fold(du * u * scale)
                dcat[at, h * HD : (h + 1) * HD] = norm_back(du * gain, u, scale).astype(BF)
            for g in range(2):
                dcat[at, (6 + g) * HD : (7 + g) * HD] = dq_ref[g, at, 3 * HD : 4 * HD]
            d = dcat[at, :]
            for g in range(4):
                part[k, :, g * d_rows : (g + 1) * d_rows] = dot_nt(d, wall_ref[g]).astype(BF)

        chunk(net.sd)
        total.start_diagonal()
        gu_gather(0)

        @pl.loop(0, 2)
        def _(n):
            chunk(jnp.where(n == 0, net.sx, net.sy))

        total.start_sides()
        gu_gather(1)
        chunk(net.me)
        pl.when(gu_line.middle)(lambda: gu_line.finish(0))
        gu_gather(2)
        total.forward()

        def slab(n, core_of):
            f = 2 * n + core_of
            at = pl.ds(pl.multiple_of(f * d_rows, d_rows), d_rows)
            return dot_tn(n1_ref[:, at], dcat[...])

        w_sem = net.take(2)

        def w_copy(n):
            return net.copy(w_sem + n, w_out.at[n], w_got.at[n], net.to_core)

        @pl.loop(0, 2)
        def _(n):
            w_out[n] = slab(n, 1 - c).astype(BF)
            w_copy(n).start()

        pl.when(gu_line.middle)(lambda: gu_line.finish(1))
        gu_gather(3)

        w_y = net.new(w_sum, w_rows.at[1], net.to_y)
        value = slab(1 - y, c)
        w_copy(1 - y).wait_recv()
        w_sum[...] = (value + w_got[1 - y].astype(F32)).astype(BF)
        w_y.start()
        value = slab(y, c)
        w_copy(y).wait_recv()
        w_rows[0] = (value + w_got[y].astype(F32)).astype(BF)
        pl.when(gu_line.middle)(lambda: gu_line.finish(2))
        gu_gather(4)

        def back_through_norm(at, dn1):
            value = x_ref[at].astype(F32)
            scale = rms(value)
            acc[0] += fold(dn1 * value * scale)
            grad_in[at] = (dmid_ref[at] + norm_back(dn1 * attn_gain, value, scale)).astype(BF)

        total.finish(back_through_norm)
        send_home(in_copy, grad_in, input_out)
        acc[1] = mlp_ref[...]
        for row in range(3):
            g_sum[0, row : row + 1, :] = jnp.sum(acc[row], axis=0, keepdims=True)
        g_sum[0, 3:8, :] = jnp.zeros((5, D), F32)
        g_swaps = []
        for n, to in enumerate((net.to_core, net.to_y, net.to_x)):
            cp = net.new(g_sum.at[0], g_got.at[n], to)
            cp.start()
            pl.when(gu_line.middle)(lambda: gu_line.finish(3 + n))
            gu_gather(5 + n) if 5 + n < tiles else None
            cp.wait()
            g_sum[0] = g_sum[0] + g_got[n]
        g_line.gather(0)

        @pl.when(at_end)
        def _():
            @pl.loop(0, per)
            def _(k):
                w_line.gather(k)

            w_y.wait_recv()

            @pl.loop(per, tiles)
            def _(k):
                w_line.gather(k)

            @pl.loop(0, tiles)
            def _(k):
                gu_line.finish(k)

            g_line.finish(0)

            @pl.loop(0, tiles)
            def _(k):
                w_line.finish(k)

        @pl.when(line_between(net, gu_line, at_end))
        def _():
            @pl.loop(0, tiles)
            def _(k):
                gu_line.finish(k)
                pl.when(k == per)(w_y.wait_recv)
                w_line.gather(k)

            g_line.finish(0)

            @pl.loop(0, tiles)
            def _(k):
                w_line.finish(k)

        @pl.when(gu_line.middle)
        def _():
            @pl.loop(6, tiles)
            def _(k):
                gu_line.finish(k)

            g_line.finish(0)

            @pl.loop(0, tiles)
            def _(k):
                pl.when(k == per)(w_y.wait_recv)
                w_line.finish(k)

        gain_out[...] = g_mine[0]

        def place(mine, copies, outs, widths):
            @pl.loop(0, tiles)
            def _(k):
                copies(k).wait_recv()
                row_half = jnp.where(k < per, y, 1 - y)
                at = pl.ds(pl.multiple_of(lax.rem(k, per) * TILE, TILE), TILE)
                for slots, x_of in ((mine[0], x), (mine[1], 1 - x)):
                    quarter = 2 * row_half + x_of
                    first = 0
                    for out, width in zip(outs, widths):
                        lanes = pl.ds(pl.multiple_of(quarter * width, width), width)
                        out[at, lanes] = slots[k, :, first : first + width]
                        first += width

        place((gu_mine, gu_other), gu_cross, (out_g, out_u), (unit, unit))
        place((w_mine, w_other), w_cross, (out_q, out_k, out_v), (4 * HD, 2 * HD, 2 * HD))

        @pl.loop(0, tiles)
        def _(k):
            gu_line.drain(k)
            w_line.drain(k)
            gu_cross(k).wait_send()
            w_cross(k).wait_send()

        g_line.drain(0)
        for n in range(2):
            w_copy(n).wait_send()
        w_y.wait_send()
        total.drain()
        pl.when(moves)(lambda: res_copy.wait())
        pl.when(moves)(lambda: in_copy.wait())

    def line_between(net, line, at_end):
        return jnp.logical_not(jnp.logical_or(line.middle, at_end))

    vm = vmem_spec()
    half_rows = rows // 2
    gu_slots = pltpu.VMEM((tiles, TILE, gu_cols), BF)
    w_slots = pltpu.VMEM((tiles, TILE, 8 * HD), BF)
    g_slot = pltpu.VMEM((1, 8, D), F32)
    return pl.pallas_call(
        kernel,
        name="leave",
        out_shape=[
            shape((rows, D), BF),
            shape((rows, D), BF),
            shape((d_rows, 16 * HD), BF),
            shape((d_rows, 8 * HD), BF),
            shape((d_rows, 8 * HD), BF),
            shape((d_rows, 4 * unit), BF),
            shape((d_rows, 4 * unit), BF),
            shape((8, D), F32),
        ],
        in_specs=[vm] * 11,
        out_specs=[vm] * 8,
        scratch_shapes=[
            pltpu.VMEM((half, 8 * HD), BF),
            pltpu.VMEM((4, rows, D), BF),
            pltpu.VMEM((6, half_rows, D), BF),
            pltpu.VMEM((2, half_rows, D), BF),
            pltpu.VMEM((rows, D), BF),
            pltpu.VMEM((2, d_rows, 8 * HD), BF),
            pltpu.VMEM((2, d_rows, 8 * HD), BF),
            pltpu.VMEM((d_rows, 8 * HD), BF),
            pltpu.VMEM((2, d_rows, 8 * HD), BF),
        ]
        + [gu_slots] * 5
        + [w_slots] * 5
        + [g_slot, pltpu.VMEM((3, 8, D), F32)]
        + [g_slot] * 4
        + [
            pltpu.VMEM((3, 8, D), F32),
            pltpu.SemaphoreType.DMA((n_sems,)),
            pltpu.SemaphoreType.DMA((n_sems,)),
        ],
        compiler_params=params(4, 62),
        cost_estimate=pl.CostEstimate(
            flops=4 * half * D * 8 * HD, bytes_accessed=32 * 2**20, transcendentals=0
        ),
    )(dq, raw, table, n1, wall, x_own, dmiddle, gains, result, gu_rows, mlp_gain_part)


def plane_body(
    tokens,
    cotangent,
    block_map,
    positions,
    attn_gain,
    query_weight,
    key_weight,
    value_weight,
    query_gain,
    key_gain,
    out_weight,
    mlp_gain,
    gate_weight,
    up_weight,
    down_weight,
):
    z, x, y, c = coords()
    f = 2 * y + c
    rows = tokens.shape[1]
    parts = lax.axis_size("fsdp")

    def spread_out(gain):
        n = gain.shape[0]
        full = jnp.concatenate([gain] * parts)
        kept = jnp.where(jnp.arange(n * parts) // n == f, full, 0.0)
        return jnp.pad(kept, (0, D - n * parts))

    gains = jnp.stack(
        [spread_out(g) for g in (attn_gain, mlp_gain, query_gain, key_gain)]
        + [jnp.zeros((D,), F32)] * 4
    )
    pos = jnp.pad(positions.reshape(rows // 128, 128).astype(F32), ((0, 8 - rows // 128), (0, 0)))
    frequency = jnp.exp(
        jnp.arange(0, HD, 2).astype(F32) * (-math.log(theta_base) / HD)
    )
    frequency = jnp.broadcast_to(jnp.pad(frequency, (0, HD // 2))[None], (8, HD))
    flat_map = block_map.reshape(-1)
    n_blocks = flat_map.shape[0]
    order = jnp.arange(n_blocks, dtype=jnp.int32)
    inverse = jnp.sum(
        jnp.where(flat_map[None, :] == order[:, None], order[None, :], 0), axis=1
    ).astype(jnp.int32)
    x_own, n1, raw, table, core, wall, gains = enter(
        tokens.reshape(rows, D),
        pos,
        gains,
        frequency,
        query_weight,
        key_weight,
        value_weight,
    )
    att, mixed, lse, cots, cot_own, wgu, wo, wd = attend(
        flat_map,
        inverse,
        core,
        cotangent.reshape(rows, D),
        gate_weight,
        up_weight,
        out_weight,
        down_weight,
    )
    grad, middle, dmiddle, result_part, sum_gu, sum_od, mlp_gain_part = feed_forward(
        att, x_own, wo, wgu, wd, cots, cot_own, gains
    )
    dq, result, od, gu_rows = attend_back(
        flat_map, inverse, core, mixed, grad, lse, sum_od, sum_gu, result_part, middle
    )
    result, input_grad, grad_q, grad_k, grad_v, grad_g, grad_u, gain_sums = leave(
        dq, raw, table, n1, wall, x_own, dmiddle, gains, result, gu_rows, mlp_gain_part
    )
    od = od.reshape(2, -1, D)
    down_half = down_weight.shape[0] // 2

    def own_gain(values, size):
        return lax.dynamic_slice_in_dim(values, f * (size // parts), size // parts)

    return (
        result.astype(F32).reshape(tokens.shape),
        input_grad.astype(F32).reshape(tokens.shape),
        own_gain(gain_sums[0], D),
        grad_q.astype(F32),
        grad_k.astype(F32),
        grad_v.astype(F32),
        own_gain(gain_sums[2, :HD], HD),
        own_gain(gain_sums[2, HD : 2 * HD], HD),
        od[:, down_half:].reshape(out_weight.shape).astype(F32),
        own_gain(gain_sums[1], D),
        grad_g.astype(F32),
        grad_u.astype(F32),
        od[:, :down_half].reshape(down_weight.shape).astype(F32),
    )


def solution(mesh):
    placed = (
        P("fsdp", "ctx", None),
        P("fsdp", "ctx", None),
        P(),
        P("fsdp", "ctx"),
        P("fsdp"),
        P("fsdp", None),
        P("fsdp", None),
        P("fsdp", None),
        P("fsdp"),
        P("fsdp"),
        P("fsdp", None),
        P("fsdp"),
        P("fsdp", None),
        P("fsdp", None),
        P("fsdp", None),
    )
    fits = mesh.shape["fsdp"] == 4 and mesh.shape["ctx"] == 8
    return jax.shard_map(
        plane_body if fits else body,
        mesh=mesh,
        in_specs=placed,
        out_specs=(
            P("fsdp", "ctx", None),
            P("fsdp", "ctx", None),
            P("fsdp"),
            P("fsdp", None),
            P("fsdp", None),
            P("fsdp", None),
            P("fsdp"),
            P("fsdp"),
            P("fsdp", None),
            P("fsdp"),
            P("fsdp", None),
            P("fsdp", None),
            P("fsdp", None),
        ),
        check_vma=False,
    )
```

```python
import math

import jax
import jax.numpy as jnp
from jax import lax
from jax.experimental import pallas as pl
from jax.experimental.pallas import tpu as pltpu
from jax.sharding import PartitionSpec as P

D = 1024
HQ = 16
HK = 8
HD = 128
BLK = 128


epsilon = 1e-06
theta_base = 1000000.0
masked_value = -1e30


def rms_scale(values):
    return lax.rsqrt(jnp.mean(values * values, axis=-1, keepdims=True) + epsilon)


def norm_back(upstream, values, scale):
    return scale * upstream - values * (scale * scale * scale) * jnp.mean(
        upstream * values, axis=-1, keepdims=True
    )


def rope_tables(positions, head_dim):
    frequency = jnp.exp(
        jnp.arange(0, head_dim, 2).astype(jnp.float32) * (-math.log(theta_base) / head_dim)
    )
    angles = positions.astype(jnp.float32)[..., None] * frequency
    angles = jnp.concatenate([angles, angles], axis=-1)
    return (jnp.cos(angles), jnp.sin(angles))


def rotate(values, cosine, sine_table):
    half_width = values.shape[-1] // 2
    turned = jnp.concatenate([-values[..., half_width:], values[..., :half_width]], axis=-1)
    return values * cosine + turned * sine_table


def unrotate(grads, cosine, sine_table):
    half_width = grads.shape[-1] // 2
    moved = grads * sine_table
    back_turn = jnp.concatenate([moved[..., half_width:], -moved[..., :half_width]], axis=-1)
    return grads * cosine + back_turn


def score_block(grouped, keys_head, allowed, scale):
    scores = (
        jnp.einsum("qgd,sd->gqs", grouped, keys_head, preferred_element_type=jnp.float32) * scale
    )
    return jnp.where(allowed, scores, masked_value)


def body(
    tokens,
    cotangent,
    block_map,
    positions,
    attn_gain,
    query_weight,
    key_weight,
    value_weight,
    query_gain,
    key_gain,
    out_weight,
    mlp_gain,
    gate_weight,
    up_weight,
    down_weight,
):
    seq_count = tokens.shape[0]
    seq_rows = tokens.shape[1]
    total_rows = seq_count * seq_rows
    groups = HQ // HK
    scale = HD ** (-0.5)
    attn_full, query_full, key_full, mlp_full = (
        lax.all_gather(attn_gain, "fsdp", axis=0, tiled=True),
        lax.all_gather(query_gain, "fsdp", axis=0, tiled=True),
        lax.all_gather(key_gain, "fsdp", axis=0, tiled=True),
        lax.all_gather(mlp_gain, "fsdp", axis=0, tiled=True),
    )
    query_w, key_w, value_w, out_w = (
        lax.all_gather(query_weight.astype(jnp.bfloat16), "fsdp", axis=0, tiled=True),
        lax.all_gather(key_weight.astype(jnp.bfloat16), "fsdp", axis=0, tiled=True),
        lax.all_gather(value_weight.astype(jnp.bfloat16), "fsdp", axis=0, tiled=True),
        lax.all_gather(out_weight.astype(jnp.bfloat16), "fsdp", axis=0, tiled=True),
    )
    flat = tokens.astype(jnp.float32).reshape(total_rows, D)
    scale_one = rms_scale(flat)
    normed = (flat * scale_one * attn_full).astype(jnp.bfloat16)
    query_raw = jnp.dot(normed, query_w, preferred_element_type=jnp.float32).reshape(
        total_rows, HQ, HD
    )
    key_raw = jnp.dot(normed, key_w, preferred_element_type=jnp.float32).reshape(total_rows, HK, HD)
    value_low = jnp.dot(normed, value_w, preferred_element_type=jnp.float32).astype(jnp.bfloat16)
    cosine, sine_table = rope_tables(positions.reshape(total_rows), HD)
    cosine = cosine[:, None, :]
    sine_table = sine_table[:, None, :]
    query_scale = rms_scale(query_raw)
    query_unit = query_raw * query_scale
    query_low = rotate(query_unit * query_full, cosine, sine_table).astype(jnp.bfloat16)
    key_scale = rms_scale(key_raw)
    key_unit = key_raw * key_scale
    key_low = rotate(key_unit * key_full, cosine, sine_table).astype(jnp.bfloat16)
    flat_map = block_map.reshape(-1)
    offsets = jnp.arange(BLK, dtype=jnp.int32)
    key_index = (flat_map[:, None] * BLK + offsets[None, :]).reshape(-1)
    own_blocks = lax.dynamic_slice_in_dim(flat_map, lax.axis_index("ctx") * 2, 2)
    query_index = (own_blocks[:, None] * BLK + offsets[None, :]).reshape(-1)
    allowed = query_index[:, None] >= key_index[None, :]
    query_seq = query_low.reshape(seq_count, seq_rows, HK, groups, HD)
    key_seq = key_low.reshape(seq_count, seq_rows, HK * HD)
    value_seq = value_low.reshape(seq_count, seq_rows, HK * HD)

    def forward_head(inputs):
        grouped, keys_head, values_head = inputs
        scores = score_block(grouped, keys_head, allowed, scale)
        row_max = jnp.max(scores, axis=-1, keepdims=True)
        exp_scores = jnp.exp(scores - row_max)
        row_total = jnp.sum(exp_scores, axis=-1, keepdims=True)
        prob_low = (exp_scores / row_total).astype(jnp.bfloat16)
        mixed = jnp.einsum("gqs,sd->qgd", prob_low, values_head, preferred_element_type=jnp.float32)
        return (mixed, row_max + jnp.log(row_total))

    seq_item = 0
    keys_all = lax.all_gather(key_seq[seq_item], "ctx", axis=0, tiled=True)
    values_all = lax.all_gather(value_seq[seq_item], "ctx", axis=0, tiled=True)
    keys_head = jnp.transpose(keys_all.reshape(-1, HK, HD), (1, 0, 2))
    values_head = jnp.transpose(values_all.reshape(-1, HK, HD), (1, 0, 2))
    grouped_head = jnp.transpose(query_seq[seq_item], (1, 0, 2, 3))
    mixed, lse = lax.map(forward_head, (grouped_head, keys_head, values_head))
    mixed_parts = jnp.transpose(mixed, (1, 0, 2, 3)).reshape(seq_rows, HQ * HD)
    lse_parts = [lse]
    gathered = [(grouped_head, keys_head, values_head)]
    attended = mixed_parts.astype(jnp.bfloat16)
    middle = flat + jnp.dot(attended, out_w, preferred_element_type=jnp.float32)
    gate_w, up_w, down_w = (
        lax.all_gather(gate_weight.astype(jnp.bfloat16), "fsdp", axis=0, tiled=True),
        lax.all_gather(up_weight.astype(jnp.bfloat16), "fsdp", axis=0, tiled=True),
        lax.all_gather(down_weight.astype(jnp.bfloat16), "fsdp", axis=0, tiled=True),
    )
    scale_two = rms_scale(middle)
    normed_two = (middle * scale_two * mlp_full).astype(jnp.bfloat16)
    gate = jnp.dot(normed_two, gate_w, preferred_element_type=jnp.float32)
    upward = jnp.dot(normed_two, up_w, preferred_element_type=jnp.float32)
    sigmoid_gate = jax.nn.sigmoid(gate)
    silu_gate = gate * sigmoid_gate
    hidden = (silu_gate * upward).astype(jnp.bfloat16)
    result = middle + jnp.dot(hidden, down_w, preferred_element_type=jnp.float32)
    query_back, key_back, value_back, out_back = (
        lax.all_gather(query_weight.astype(jnp.bfloat16), "fsdp", axis=0, tiled=True),
        lax.all_gather(key_weight.astype(jnp.bfloat16), "fsdp", axis=0, tiled=True),
        lax.all_gather(value_weight.astype(jnp.bfloat16), "fsdp", axis=0, tiled=True),
        lax.all_gather(out_weight.astype(jnp.bfloat16), "fsdp", axis=0, tiled=True),
    )
    gate_back, up_back, down_back = (
        lax.all_gather(gate_weight.astype(jnp.bfloat16), "fsdp", axis=0, tiled=True),
        lax.all_gather(up_weight.astype(jnp.bfloat16), "fsdp", axis=0, tiled=True),
        lax.all_gather(down_weight.astype(jnp.bfloat16), "fsdp", axis=0, tiled=True),
    )
    grad_out = cotangent.astype(jnp.float32).reshape(total_rows, D)
    grad_branch = grad_out.astype(jnp.bfloat16)
    down_grad = jnp.einsum("nf,nd->fd", hidden, grad_branch, preferred_element_type=jnp.float32)
    grad_hidden = jnp.einsum(
        "nd,fd->nf", grad_branch, down_back, preferred_element_type=jnp.float32
    )
    grad_gate = (grad_hidden * upward * sigmoid_gate * (1.0 + gate * (1.0 - sigmoid_gate))).astype(
        jnp.bfloat16
    )
    grad_up = (grad_hidden * silu_gate).astype(jnp.bfloat16)
    gate_grad = jnp.einsum("nd,nf->df", normed_two, grad_gate, preferred_element_type=jnp.float32)
    up_grad = jnp.einsum("nd,nf->df", normed_two, grad_up, preferred_element_type=jnp.float32)
    grad_normed_two = jnp.einsum(
        "nf,df->nd", grad_gate, gate_back, preferred_element_type=jnp.float32
    ) + jnp.einsum("nf,df->nd", grad_up, up_back, preferred_element_type=jnp.float32)
    mlp_local = jnp.sum(grad_normed_two * middle * scale_two, axis=0)
    grad_middle = grad_out + norm_back(grad_normed_two * mlp_full, middle, scale_two)
    grad_attn_low = grad_middle.astype(jnp.bfloat16)
    out_grad = jnp.einsum("nq,nd->qd", attended, grad_attn_low, preferred_element_type=jnp.float32)
    grad_mixed = jnp.einsum(
        "nd,qd->nq", grad_attn_low, out_back, preferred_element_type=jnp.float32
    ).astype(jnp.bfloat16)
    grad_mixed_seq = grad_mixed.reshape(seq_count, seq_rows, HK, groups, HD)

    def backward_head(inputs):
        grouped, keys_head, values_head, grad_head, lse = inputs
        scores = score_block(grouped, keys_head, allowed, scale)
        prob_full = jnp.exp(scores - lse)
        grad_prob = jnp.einsum(
            "qgd,sd->gqs", grad_head, values_head, preferred_element_type=jnp.float32
        )
        delta_row = jnp.sum(prob_full * grad_prob, axis=-1, keepdims=True)
        grad_scores = (prob_full * (grad_prob - delta_row)).astype(jnp.bfloat16)
        grad_query_head = (
            jnp.einsum("gqs,sd->qgd", grad_scores, keys_head, preferred_element_type=jnp.float32)
            * scale
        )
        grad_key_head = (
            jnp.einsum("gqs,qgd->sd", grad_scores, grouped, preferred_element_type=jnp.float32)
            * scale
        )
        grad_value_head = jnp.einsum(
            "gqs,qgd->sd",
            prob_full.astype(jnp.bfloat16),
            grad_head,
            preferred_element_type=jnp.float32,
        )
        return (grad_query_head, grad_key_head, grad_value_head)

    seq_item = 0
    grouped_head, keys_head, values_head = gathered[seq_item]
    grad_head = jnp.transpose(grad_mixed_seq[seq_item], (1, 0, 2, 3))
    grad_query_head, grad_key_head, grad_value_head = lax.map(
        backward_head, (grouped_head, keys_head, values_head, grad_head, lse_parts[seq_item])
    )
    grad_query_parts = jnp.transpose(grad_query_head, (1, 0, 2, 3)).reshape(seq_rows, HQ, HD)
    grad_keys_all = jnp.transpose(grad_key_head, (1, 0, 2)).reshape(-1, HK * HD)
    grad_values_all = jnp.transpose(grad_value_head, (1, 0, 2)).reshape(-1, HK * HD)
    grad_key_own = lax.psum_scatter(
        grad_keys_all.astype(jnp.bfloat16), "ctx", scatter_dimension=0, tiled=True
    ).astype(jnp.float32)
    grad_value_own = lax.psum_scatter(
        grad_values_all.astype(jnp.bfloat16), "ctx", scatter_dimension=0, tiled=True
    )
    grad_key = grad_key_own.reshape(total_rows, HK, HD)
    grad_query_unit = unrotate(grad_query_parts, cosine, sine_table)
    qgain_local = jnp.sum(grad_query_unit * query_unit, axis=(0, 1))
    grad_query_low = (
        norm_back(grad_query_unit * query_full, query_raw, query_scale)
        .astype(jnp.bfloat16)
        .reshape(total_rows, HQ * HD)
    )
    grad_key_unit = unrotate(grad_key, cosine, sine_table)
    kgain_local = jnp.sum(grad_key_unit * key_unit, axis=(0, 1))
    grad_key_low = (
        norm_back(grad_key_unit * key_full, key_raw, key_scale)
        .astype(jnp.bfloat16)
        .reshape(total_rows, HK * HD)
    )
    query_grad = jnp.einsum("nd,nc->dc", normed, grad_query_low, preferred_element_type=jnp.float32)
    key_grad = jnp.einsum("nd,nc->dc", normed, grad_key_low, preferred_element_type=jnp.float32)
    value_grad = jnp.einsum("nd,nc->dc", normed, grad_value_own, preferred_element_type=jnp.float32)
    grad_normed = jnp.einsum(
        "nc,dc->nd", grad_query_low, query_back, preferred_element_type=jnp.float32
    )
    grad_normed = grad_normed + jnp.einsum(
        "nc,dc->nd", grad_key_low, key_back, preferred_element_type=jnp.float32
    )
    grad_normed = grad_normed + jnp.einsum(
        "nc,dc->nd", grad_value_own, value_back, preferred_element_type=jnp.float32
    )
    attn_local = jnp.sum(grad_normed * flat * scale_one, axis=0)
    input_grad = grad_middle + norm_back(grad_normed * attn_full, flat, scale_one)
    shares = (
        lax.psum_scatter(
            attn_local.astype(jnp.bfloat16), "fsdp", scatter_dimension=0, tiled=True
        ).astype(jnp.float32),
        lax.psum_scatter(
            query_grad.astype(jnp.bfloat16), "fsdp", scatter_dimension=0, tiled=True
        ).astype(jnp.float32),
        lax.psum_scatter(
            key_grad.astype(jnp.bfloat16), "fsdp", scatter_dimension=0, tiled=True
        ).astype(jnp.float32),
        lax.psum_scatter(
            value_grad.astype(jnp.bfloat16), "fsdp", scatter_dimension=0, tiled=True
        ).astype(jnp.float32),
        lax.psum_scatter(
            qgain_local.astype(jnp.bfloat16), "fsdp", scatter_dimension=0, tiled=True
        ).astype(jnp.float32),
        lax.psum_scatter(
            kgain_local.astype(jnp.bfloat16), "fsdp", scatter_dimension=0, tiled=True
        ).astype(jnp.float32),
        lax.psum_scatter(
            out_grad.astype(jnp.bfloat16), "fsdp", scatter_dimension=0, tiled=True
        ).astype(jnp.float32),
        lax.psum_scatter(
            mlp_local.astype(jnp.bfloat16), "fsdp", scatter_dimension=0, tiled=True
        ).astype(jnp.float32),
        lax.psum_scatter(
            gate_grad.astype(jnp.bfloat16), "fsdp", scatter_dimension=0, tiled=True
        ).astype(jnp.float32),
        lax.psum_scatter(
            up_grad.astype(jnp.bfloat16), "fsdp", scatter_dimension=0, tiled=True
        ).astype(jnp.float32),
        lax.psum_scatter(
            down_grad.astype(jnp.bfloat16), "fsdp", scatter_dimension=0, tiled=True
        ).astype(jnp.float32),
    )
    summed = (
        lax.psum(shares[0].astype(jnp.bfloat16), "ctx").astype(jnp.float32),
        lax.psum(shares[1].astype(jnp.bfloat16), "ctx").astype(jnp.float32),
        lax.psum(shares[2].astype(jnp.bfloat16), "ctx").astype(jnp.float32),
        lax.psum(shares[3].astype(jnp.bfloat16), "ctx").astype(jnp.float32),
        lax.psum(shares[4].astype(jnp.bfloat16), "ctx").astype(jnp.float32),
        lax.psum(shares[5].astype(jnp.bfloat16), "ctx").astype(jnp.float32),
        lax.psum(shares[6].astype(jnp.bfloat16), "ctx").astype(jnp.float32),
        lax.psum(shares[7].astype(jnp.bfloat16), "ctx").astype(jnp.float32),
        lax.psum(shares[8].astype(jnp.bfloat16), "ctx").astype(jnp.float32),
        lax.psum(shares[9].astype(jnp.bfloat16), "ctx").astype(jnp.float32),
        lax.psum(shares[10].astype(jnp.bfloat16), "ctx").astype(jnp.float32),
    )
    return (
        result.reshape(tokens.shape),
        input_grad.reshape(tokens.shape),
        summed[0],
        summed[1],
        summed[2],
        summed[3],
        summed[4],
        summed[5],
        summed[6],
        summed[7],
        summed[8],
        summed[9],
        summed[10],
    )


MESH = pl.DeviceIdType.MESH
BF = jnp.bfloat16
F32 = jnp.float32
LOG2E = math.log2(math.e)
QT = 256
NEG = -1e30
SMALL = 32


def shape(dims, dtype):
    return jax.ShapeDtypeStruct(dims, dtype)


def dot_nn(a, b):
    return jnp.dot(a, b, preferred_element_type=F32)


def dot_nt(a, b):
    return lax.dot_general(a, b, (((1,), (1,)), ((), ())), preferred_element_type=F32)


def dot_tn(a, b):
    return lax.dot_general(a, b, (((0,), (0,)), ((), ())), preferred_element_type=F32)


def device(z, x, y, c):
    return (z * 2 + x, y * 2 + c)


def coords():
    a = lax.axis_index("ctx")
    f = lax.axis_index("fsdp")
    return lax.div(a, 2), lax.rem(a, 2), lax.div(f, 2), lax.rem(f, 2)


class Net:
    def __init__(self, send_sems, recv_sems):
        self.z, self.x, self.y, self.c = z, x, y, c = coords()
        self.depth = lax.axis_size("ctx") // 2
        self.to_x = device(z, 1 - x, y, c)
        self.to_y = device(z, x, 1 - y, c)
        self.to_core = device(z, x, y, 1 - c)
        self.to_x_other = device(z, 1 - x, y, 1 - c)
        self.to_y_other = device(z, x, 1 - y, 1 - c)
        self.up = device(z + 1, x, y, c)
        self.down = device(z - 1, x, y, c)
        self.has_up = z < self.depth - 1
        self.has_down = z > 0
        self.send_sems, self.recv_sems = send_sems, recv_sems
        self.used = 0
        self.me = 2 * y + x
        self.sx = 2 * y + 1 - x
        self.sy = 2 * (1 - y) + x
        self.sd = 2 * (1 - y) + 1 - x

    def greet(self, line=True, owners=False, homes=False):
        barrier = pltpu.get_barrier_semaphore()

        def signal(to):
            pl.semaphore_signal(barrier, inc=1, device_id=to, device_id_type=MESH)

        for to in (self.to_x, self.to_y, self.to_core):
            signal(to)
        count = 3
        if owners:
            signal(self.to_x_other)
            count = count + 1
        if homes:
            signal(self.to_y_other)
            count = count + 1
        if line:
            pl.when(self.has_up)(lambda: signal(self.up))
            pl.when(self.has_down)(lambda: signal(self.down))
            count = count + self.has_up.astype(jnp.int32) + self.has_down.astype(jnp.int32)
        pl.semaphore_wait(barrier, count)

    def take(self, count=1):
        first = self.used
        self.used += count
        assert self.used <= self.send_sems.shape[0], self.used
        return first

    def copy(self, sem, src, dst, to):
        return pltpu.make_async_remote_copy(
            src_ref=src,
            dst_ref=dst,
            send_sem=self.send_sems.at[sem],
            recv_sem=self.recv_sems.at[sem],
            device_id=to,
            device_id_type=MESH,
        )

    def new(self, src, dst, to):
        return self.copy(self.take(), src, dst, to)


def rms(values):
    return lax.rsqrt(jnp.mean(values * values, axis=-1, keepdims=True) + epsilon)


class PlaneGather:
    def __init__(self, net, src, out):
        half = out.shape[1] // 2
        lo, hi = pl.ds(0, half), pl.ds(half, half)
        me, sx, sy = net.me, net.sx, net.sy
        self.x_lo = net.new(src.at[lo], out.at[me, lo], net.to_x)
        self.y_hi = net.new(src.at[hi], out.at[me, hi], net.to_y)
        self.x_hi = net.new(src.at[hi], out.at[me, hi], net.to_x)
        self.y_lo = net.new(src.at[lo], out.at[me, lo], net.to_y)
        self.fx = net.new(out.at[sy, hi], out.at[sy, hi], net.to_x)
        self.fy = net.new(out.at[sx, lo], out.at[sx, lo], net.to_y)

    def start(self):
        for cp in (self.x_lo, self.y_hi, self.x_hi, self.y_lo):
            cp.start()

    def forward(self):
        self.y_hi.wait_recv()
        self.fx.start()
        self.x_lo.wait_recv()
        self.fy.start()

    def wait_sides(self):
        self.x_hi.wait_recv()
        self.y_lo.wait_recv()

    def wait_diagonal(self):
        self.fx.wait_recv()
        self.fy.wait_recv()

    def drain(self):
        for cp in (self.x_lo, self.y_hi, self.x_hi, self.y_lo, self.fx, self.fy):
            cp.wait_send()


class PlaneSum:
    def __init__(self, net, part, got, mid, split=None):
        rows = part.shape[1]
        split = rows // 2 if split is None else split
        self.net, self.part, self.got, self.mid = net, part, got, mid
        me, sx, sy, sd = net.me, net.sx, net.sy, net.sd
        self.ways = []
        for first, size, near, far, s_near, s_far in (
            (0, split, net.to_x, net.to_y, sx, sy),
            (split, rows - split, net.to_y, net.to_x, sy, sx),
        ):
            if size:
                at = pl.ds(first, size)
                self.ways.append(
                    (
                        at,
                        s_far,
                        net.new(part.at[sd, at], got.at[0, at], near),
                        net.new(part.at[s_near, at], got.at[1, at], near),
                        net.new(mid.at[at], got.at[2, at], far),
                    )
                )

    def start_diagonal(self):
        for _, _, diagonal, _, _ in self.ways:
            diagonal.start()

    def start_sides(self):
        for _, _, _, side, _ in self.ways:
            side.start()

    def forward(self):
        for at, s_far, diagonal, _, relay in self.ways:
            diagonal.wait_recv()
            self.mid[at] = (self.part[s_far, at].astype(F32) + self.got[0, at].astype(F32)).astype(
                BF
            )
            relay.start()

    def finish(self, use):
        for at, _, _, side, relay in self.ways:
            side.wait_recv()
            relay.wait_recv()
            use(
                at,
                self.part[self.net.me, at].astype(F32)
                + self.got[1, at].astype(F32)
                + self.got[2, at].astype(F32),
            )

    def drain(self):
        for _, _, diagonal, side, relay in self.ways:
            diagonal.wait_send()
            side.wait_send()
            relay.wait_send()


class Route:
    def __init__(self, net, src, line, out, parts=2, first=0, mirrored=False):
        self.net, self.src, self.line, self.out = net, src, line, out
        self.SUB = parts
        self.rows = src.shape[0] // self.SUB
        self.first = first
        depth = net.depth
        self.l_sem = net.take(depth * self.SUB)
        self.c_sem = net.take(2 * self.SUB)
        self.y_sem = net.take(2 * self.SUB)
        self.x_sem = net.take(2 * self.SUB)
        row = 1 - net.y if mirrored else net.y
        self.place = 2 * net.c + row
        self.entry = net.z == self.place
        self.row0 = row == lax.rem(net.z, 2)

    def to(self, s):
        return pl.ds(self.first + s * self.rows, self.rows)

    def part(self, s):
        return pl.ds(s * self.rows, self.rows)

    def hop(self, k, s, own, to):
        src = self.src.at[self.part(s)] if own else self.line.at[k, self.part(s)]
        return self.net.copy(self.l_sem + k * self.SUB + s, src, self.line.at[k, self.part(s)], to)

    def chip(self, k, s):
        j = lax.rem(k, 2)
        return self.net.copy(
            self.c_sem + j * self.SUB + s,
            self.line.at[k, self.part(s)],
            self.out.at[2 * j + self.net.x, self.to(s)],
            self.net.to_core,
        )

    def over_y(self, j, s):
        at = self.out.at[2 * j + self.net.x, self.to(s)]
        return self.net.copy(self.y_sem + j * self.SUB + s, at, at, self.net.to_y)

    def over_x(self, j, s):
        at = self.out.at[2 * j + self.net.x, self.to(s)]
        return self.net.copy(self.x_sem + j * self.SUB + s, at, at, self.net.to_x)

    def from_x(self, j, s):
        at = self.out.at[2 * j + 1 - self.net.x, self.to(s)]
        return self.net.copy(self.x_sem + j * self.SUB + s, at, at, self.net.to_x)

    def start(self):
        net = self.net
        for s in range(self.SUB):
            pl.when(net.z < self.place)(lambda: self.hop(net.z, s, True, net.up).start())
            pl.when(net.z > self.place)(lambda: self.hop(net.z, s, True, net.down).start())

    def relay(self, distances=None):
        net = self.net
        for d in range(1, net.depth) if distances is None else distances:
            for s in range(self.SUB):

                @pl.when(jnp.logical_and(net.z < self.place, net.z >= d))
                def _():
                    self.hop(net.z - d, s, False, net.up).wait_recv()
                    self.hop(net.z - d, s, False, net.up).start()

                @pl.when(jnp.logical_and(net.z > self.place, net.z < net.depth - d))
                def _():
                    self.hop(net.z + d, s, False, net.down).wait_recv()
                    self.hop(net.z + d, s, False, net.down).start()

    def enter(self, distances=None):
        net = self.net
        for d in range(net.depth) if distances is None else distances:
            for s in range(self.SUB):
                for k in range(net.depth):
                    near = jnp.logical_or(self.place - k == d, k - self.place == d)
                    here = jnp.logical_and(self.entry, near)

                    @pl.when(here)
                    def _():
                        if d > 0:
                            self.hop(k, s, False, net.up).wait_recv()
                        else:
                            self.line[k, self.part(s)] = self.src[self.part(s)]

                    @pl.when(jnp.logical_and(here, net.c == k // 2))
                    def _():
                        self.out[2 * (k % 2) + net.x, self.to(s)] = self.line[k, self.part(s)]
                        self.over_x(k % 2, s).start()
                        self.over_y(k % 2, s).start()

                    @pl.when(jnp.logical_and(here, net.c != k // 2))
                    def _():
                        self.chip(k, s).start()

    def spread(self, which=None):
        net = self.net
        beside = jnp.logical_and(self.row0, jnp.logical_not(self.entry))

        def one(j, s):
            @pl.when(beside)
            def _():
                self.chip(j, s).wait_recv()
                self.over_x(j, s).start()
                self.over_y(j, s).start()

            @pl.when(jnp.logical_not(self.row0))
            def _():
                self.over_y(j, s).wait_recv()
                self.over_x(j, s).start()

        @pl.loop(*((0, 2) if which is None else (which, which + 1)))
        def _(n):
            j = jnp.where(net.z <= 2 * net.c, n, 1 - n)
            for s in range(self.SUB):
                one(j, s)

    def wait(self, j):
        for s in range(self.SUB):
            self.from_x(j, s).wait_recv()

    def drain(self):
        net = self.net
        for s in range(self.SUB):
            pl.when(net.z < self.place)(lambda: self.hop(net.z, s, True, net.up).wait_send())
            pl.when(net.z > self.place)(lambda: self.hop(net.z, s, True, net.down).wait_send())
            for d in range(1, net.depth):

                @pl.when(jnp.logical_and(net.z < self.place, net.z >= d))
                def _():
                    self.hop(net.z - d, s, False, net.up).wait_send()

                @pl.when(jnp.logical_and(net.z > self.place, net.z < net.depth - d))
                def _():
                    self.hop(net.z + d, s, False, net.down).wait_send()

            for k in range(net.depth):

                @pl.when(jnp.logical_and(self.entry, net.c != k // 2))
                def _():
                    self.chip(k, s).wait_send()

            for j in range(2):
                self.over_x(j, s).wait_send()
                pl.when(self.row0)(lambda: self.over_y(j, s).wait_send())


class HomeRoute:
    def __init__(self, net, src, hub, out):
        self.net, self.src, self.hub, self.out = net, src, hub, out
        self.rows = src.shape[0] // 2
        self.chunk = 2 * net.c + net.y
        self.stays = net.z == self.chunk
        self.e_sem = net.take(net.depth * 2)
        self.l_sem = net.take(net.depth * 2)
        self.y_sem = net.take()
        self.core0 = net.c == lax.div(net.z, 2)

    def part(self, s):
        return pl.ds(s * self.rows, self.rows)

    def place(self, s):
        return 2 * self.net.c + (1 - self.net.y if s else self.net.y)

    def entry(self, s):
        return self.net.z == self.place(s)

    def to_entry(self, k, s, to):
        src = self.src.at[self.part(s)]
        return self.net.copy(self.e_sem + 2 * k + s, src, self.hub.at[k, self.part(s)], to)

    def hop(self, k, s, to):
        at = self.hub.at[k, self.part(s)]
        return self.net.copy(self.l_sem + 2 * k + s, at, at, to)

    def swap(self):
        at = self.part(1)
        return self.net.copy(
            self.y_sem, self.hub.at[self.net.z, at], self.out.at[at], self.net.to_y
        )

    def sends(self, s):
        net = self.net
        row = lax.rem(net.z, 2)
        here = net.y == (1 - row if s else row)
        away = jnp.logical_not
        if s:
            go = away(self.stays)
            ways = (
                (jnp.logical_and(here, away(self.core0)), net.to_core),
                (jnp.logical_and(away(here), self.core0), net.to_y),
                (jnp.logical_and(away(here), away(self.core0)), net.to_y_other),
            )
            return [(jnp.logical_and(go, cond), to) for cond, to in ways]
        return [
            (jnp.logical_and(here, away(self.core0)), net.to_core),
            (jnp.logical_and(away(here), self.core0), net.to_y),
            (jnp.logical_and(away(here), away(self.core0)), net.to_y_other),
        ]

    def start(self):
        for s in range(2):
            for cond, to in self.sends(s):
                pl.when(cond)(lambda to=to: self.to_entry(self.chunk, s, to).start())

        @pl.when(self.stays)
        def _():
            self.out[...] = self.src[...]

    def away(self, s, distances=None):
        net = self.net
        for d in range(net.depth - 1, 0, -1) if distances is None else distances:
            for sign, to in ((-1, net.down), (1, net.up)) if d else ():
                k = net.z + sign * d
                yield k, (k >= 0 if sign < 0 else k < net.depth), to

    def enter(self, distances=None):
        net = self.net
        for s in range(2):
            for k, there, to in self.away(s, distances):

                @pl.when(jnp.logical_and(self.entry(s), there))
                def _():
                    if s:

                        @pl.when(k == self.chunk)
                        def _():
                            self.hub[k, self.part(s)] = self.src[self.part(s)]

                        @pl.when(k != self.chunk)
                        def _():
                            self.to_entry(k, s, net.to_core).wait_recv()
                    else:
                        self.to_entry(k, s, net.to_core).wait_recv()
                    self.hop(k, s, to).start()

    def relay(self, distances=None):
        net = self.net
        for s in range(2):
            place = self.place(s)
            for k, there, to in self.away(s, distances):
                side = net.z < place if to is net.down else net.z > place

                @pl.when(jnp.logical_and(side, there))
                def _():
                    self.hop(k, s, to).wait_recv()
                    self.hop(k, s, to).start()

            if distances is not None and 0 not in distances:
                continue

            @pl.when(jnp.logical_not(self.entry(s)))
            def _():
                self.hop(net.z, s, net.up).wait_recv()
                if s:
                    self.swap().start()
                else:
                    self.out[self.part(0)] = self.hub[net.z, self.part(0)]

    def drain(self):
        net = self.net
        for s in range(2):
            place = self.place(s)
            for k, there, to in self.away(s):
                side = net.z <= place if to is net.down else net.z >= place
                pl.when(jnp.logical_and(side, there))(
                    lambda k=k, to=to: self.hop(k, s, to).wait_send()
                )
            for cond, to in self.sends(s):
                pl.when(cond)(lambda to=to: self.to_entry(self.chunk, s, to).wait_send())
        pl.when(jnp.logical_not(self.entry(1)))(lambda: self.swap().wait_send())
        pl.when(jnp.logical_not(self.stays))(lambda: self.swap().wait_recv())


class LineSum:
    def __init__(self, net, tiles, src, mine, slots, deliver):
        self.net, self.tiles, self.src, self.mine = net, tiles, src, mine
        self.slots, self.deliver = slots, deliver
        self.sems = net.take(4 * tiles)
        self.root = net.depth // 2
        self.below = net.z < self.root
        self.above = net.z > self.root
        self.middle = net.z == self.root
        self.two_sided = self.root < net.depth - 1
        self.at_end = jnp.logical_or(net.z == 0, net.z == net.depth - 1)
        self.between = jnp.logical_not(jnp.logical_or(self.middle, self.at_end))

    def hop(self, kind, k):
        net, slots = self.net, self.slots
        src, dst, to = (
            (slots.at[1, k], slots.at[0, k], net.up),
            (slots.at[0, k], slots.at[1, k], net.down),
            (self.mine(k), self.mine(k), net.down),
            (self.mine(k), self.mine(k), net.up),
        )[kind]
        return net.copy(self.sems + kind * self.tiles + k, src, dst, to)

    def gather(self, k):
        net, slots = self.net, self.slots

        def send(kind, has_before):
            @pl.when(has_before)
            def _():
                self.hop(kind, k).wait_recv()
                total = self.src(k)[...].astype(F32) + slots[kind, k].astype(F32)
                slots[1 - kind, k] = total.astype(slots.dtype)

            @pl.when(jnp.logical_not(has_before))
            def _():
                slots[1 - kind, k] = self.src(k)[...]

            self.hop(kind, k).start()

        pl.when(self.below)(lambda: send(0, net.has_down))
        pl.when(self.above)(lambda: send(1, net.has_up))

    def finish(self, k):
        net, slots = self.net, self.slots

        @pl.when(self.middle)
        def _():
            self.hop(0, k).wait_recv()
            total = self.src(k)[...].astype(F32) + slots[0, k].astype(F32)
            if self.two_sided:
                self.hop(1, k).wait_recv()
                total = total + slots[1, k].astype(F32)
            self.mine(k)[...] = total.astype(slots.dtype)
            self.hop(2, k).start()
            if self.two_sided:
                self.hop(3, k).start()

        @pl.when(self.below)
        def _():
            self.hop(2, k).wait_recv()
            pl.when(net.has_down)(lambda: self.hop(2, k).start())

        @pl.when(self.above)
        def _():
            self.hop(3, k).wait_recv()
            pl.when(net.has_up)(lambda: self.hop(3, k).start())

        self.deliver(k)

    def drain(self, k):
        net = self.net
        pl.when(self.below)(lambda: self.hop(0, k).wait_send())
        pl.when(self.above)(lambda: self.hop(1, k).wait_send())
        sends_down = jnp.logical_and(net.has_down, jnp.logical_not(self.above))
        sends_up = jnp.logical_and(net.has_up, jnp.logical_not(self.below))
        pl.when(sends_down)(lambda: self.hop(2, k).wait_send())
        pl.when(sends_up)(lambda: self.hop(3, k).wait_send())


def within(k, first, last):
    return jnp.logical_and(k >= first, k < last)


class Pump:
    def __init__(self, lines, lags=(1, 3, 5, 7), placed=None):
        self.lines = lines
        self.total = sum(line.tiles for line in lines)
        self.gather_lag, self.middle_lag, self.between_lag, self.end_lag = lags
        self.placed = placed

    def each(self, s, run):
        if isinstance(s, int):
            for line in self.lines:
                if 0 <= s < line.tiles:
                    run(line, s)
                s -= line.tiles
            return
        first = 0
        for line in self.lines:
            pl.when(within(s, first, first + line.tiles))(
                lambda line=line, first=first: run(line, s - first)
            )
            first += line.tiles

    def step(self, p, before=None):
        line = self.lines[0]

        @pl.when(line.between)
        def _():
            if before is not None:
                before(p - self.gather_lag)
            self.each(p - self.gather_lag, lambda ln, k: ln.gather(k))
            self.each(p - self.between_lag, lambda ln, k: ln.finish(k))

        @pl.when(line.middle)
        def _():
            if before is not None:
                before(p - self.middle_lag)
            self.each(p - self.middle_lag, lambda ln, k: ln.finish(k))

        @pl.when(line.at_end)
        def _():
            self.each(p - self.end_lag, lambda ln, k: ln.finish(k))

    def steps(self):
        return self.total + max(self.gather_lag, self.middle_lag, self.between_lag, self.end_lag)


def any_spec():
    return pl.BlockSpec(memory_space=pl.ANY)


def vmem_spec():
    return pl.BlockSpec(memory_space=pltpu.VMEM)


def params(cid, mib=60):
    return pltpu.CompilerParams(
        collective_id=cid, has_side_effects=True, vmem_limit_bytes=mib * 2**20
    )


def enter(tok, pos, gains, wq, wk, wv):
    rows = tok.shape[0]
    d_rows = wq.shape[0]
    half = 4 * rows
    n_sems = 72

    def kernel(
        tok_ref,
        pos_in,
        attn_ref,
        mlp_ref,
        query_ref,
        key_ref,
        wq_ref,
        wk_ref,
        wv_ref,
        x_own,
        n1,
        raw_ref,
        table,
        core,
        wall,
        gains_ref,
        wq_s,
        wk_s,
        wv_s,
        wloc,
        handed,
        line,
        toks,
        pos_ref,
        gain_ref,
        pos_line,
        poss,
        heads,
        gslots,
        ssem,
        rsem,
        lsem,
    ):
        net = Net(ssem, rsem)
        y, c = net.y, net.c
        f = 2 * y + c
        fy = 2 * (1 - y) + c
        loads = [
            pltpu.make_async_copy(a, b, lsem.at[k])
            for k, (a, b) in enumerate(((wq_ref, wq_s), (wk_ref, wk_s), (wv_ref, wv_s)))
        ]
        for cp in loads:
            cp.start()
        for h in range(rows // 128):
            pos_ref[h : h + 1, :] = pos_in[0:1, h * 128 : (h + 1) * 128].astype(F32)
        gain_ref[...] = jnp.zeros_like(gain_ref)
        at = pl.ds(pl.multiple_of(f * d_rows, d_rows), d_rows)
        gain_ref[0:1, at] = attn_ref[...]
        gain_ref[1:2, at] = mlp_ref[...]
        for row, ref in ((2, query_ref), (3, key_ref)):
            n = ref.shape[1]
            wide = jnp.concatenate([ref[...], jnp.zeros((1, HD - n), F32)], axis=-1)
            wide = pltpu.roll(jnp.broadcast_to(wide, (8, HD)), f * n, 1)
            gain_ref[row : row + 1, 0:HD] = wide[0:1]
        net.greet()
        pos_route = Route(net, pos_ref, pos_line, poss, 1)
        n = rows // 2
        hand = net.new(tok_ref.at[pl.ds(n, n)], handed, net.to_y)
        route = Route(net, tok_ref.at[pl.ds(0, n)], line.at[:, pl.ds(0, n)], toks, 2)
        route2 = Route(net, handed, line.at[:, pl.ds(n, n)], toks, 2, n, True)
        hand.start()
        pos_route.start()
        route.start()
        g_core = net.new(gain_ref, gslots.at[f], net.to_core)
        g_y = net.new(gain_ref, gslots.at[f], net.to_y)
        g_relay = net.new(gslots.at[fy], gslots.at[fy], net.to_core)
        g_core.start()
        g_y.start()
        gslots[f] = gain_ref[...]
        for cp in loads:
            cp.wait()
        for t in range(4):
            at = t * 4 * HD
            wloc[t, :, 0 : 4 * HD] = wq_s[:, at : at + 4 * HD].astype(BF)
            at = t * 2 * HD
            wloc[t, :, 4 * HD : 6 * HD] = wk_s[:, at : at + 2 * HD].astype(BF)
            wloc[t, :, 6 * HD : 8 * HD] = wv_s[:, at : at + 2 * HD].astype(BF)
        w_y = net.new(wloc.at[net.sy], wall.at[f], net.to_y)
        w_core = net.new(wloc.at[net.me], wall.at[f], net.to_core)
        w_relay = net.new(wall.at[fy], wall.at[fy], net.to_core)
        w_y.start()
        w_core.start()
        wall[f] = wloc[net.me]
        hand.wait_recv()
        route2.start()
        pos_route.relay()
        pos_route.enter()
        route.enter([0, 1])
        route2.enter([0])
        route.relay()
        route2.relay()
        route2.enter([1])
        for d in (2, 3):
            route.enter([d])
            route2.enter([d])
        pos_route.spread()
        for j in range(2):
            route.spread(j)
            route2.spread(j)
        g_y.wait_recv()
        g_relay.start()
        w_y.wait_recv()
        w_relay.start()
        g_core.wait_recv()
        g_relay.wait_recv()
        w_core.wait_recv()
        w_relay.wait_recv()
        index = lax.broadcasted_iota(jnp.int32, (8, HD // 2), 1).astype(F32)
        frequency = jnp.exp(index * (-2.0 * math.log(theta_base) / HD))[0:1]
        full = gslots[0] + gslots[1] + gslots[2] + gslots[3]
        gains_ref[...] = full
        attn_gain, q_gain, k_gain = full[0:1, :], full[2:3, 0:HD], full[3:4, 0:HD]
        for j in range(2):
            pos_route.wait(j)
            route.wait(j)
            route2.wait(j)
        x_own[...] = toks[net.me]
        swaps = net.take(4)

        def swap(k):
            at = pl.ds(pl.multiple_of(k * rows, rows), rows)
            return net.copy(swaps + k, heads.at[1 - c, at], core.at[c, at], net.to_core)

        @pl.loop(0, 4)
        def _(k):
            at = pl.ds(pl.multiple_of(k * rows, rows), rows)
            flat = toks[k].astype(F32)
            normed = (flat * rms(flat) * attn_gain).astype(BF)
            n1[at, :] = normed
            raw = dot_nn(normed[:, 0:d_rows], wall[0])
            for g in range(1, 4):
                raw = raw + dot_nn(normed[:, g * d_rows : (g + 1) * d_rows], wall[g])
            raw_ref[at, :] = raw[:, 0 : 6 * HD]
            place = jnp.transpose(poss[k])
            angles = jnp.concatenate(
                [place[:, h : h + 1] * frequency for h in range(rows // 128)],
                axis=0,
            )
            cosine, sine = jnp.cos(angles), jnp.sin(angles)
            table[at, :] = jnp.concatenate([cosine, sine], axis=-1)
            cosine = jnp.concatenate([cosine, cosine], axis=-1)
            sine = jnp.concatenate([-sine, sine], axis=-1)
            for h in range(6):
                u = raw[:, h * HD : (h + 1) * HD]
                unit = u * rms(u) * (q_gain if h < 4 else k_gain)
                turned = unit * cosine + pltpu.roll(unit, HD // 2, 1) * sine
                g, lane = (h // 2, (h % 2) * HD) if h < 4 else (h - 4, 2 * HD)
                heads[g, at, lane : lane + HD] = turned.astype(BF)
            for g in range(2):
                v = raw[:, (6 + g) * HD : (7 + g) * HD]
                heads[g, at, 3 * HD : 4 * HD] = v.astype(BF)
            swap(k).start()
            core[c, at] = heads[c, at]

        for k in range(4):
            swap(k).wait()
        for cp in (g_core, g_y, g_relay, w_core, w_y, w_relay):
            cp.wait_send()
        hand.wait_send()
        pos_route.drain()
        route.drain()
        route2.drain()

    vm = vmem_spec()
    return pl.pallas_call(
        kernel,
        name="enter",
        out_shape=[
            shape((rows, D), BF),
            shape((half, D), BF),
            shape((half, 6 * HD), F32),
            shape((half, HD), F32),
            shape((2, half, 4 * HD), BF),
            shape((4, d_rows, 8 * HD), BF),
            shape((8, D), F32),
        ],
        in_specs=[vm] * 6 + [any_spec()] * 3,
        out_specs=[vm] * 7,
        scratch_shapes=[
            pltpu.VMEM(wq.shape, F32),
            pltpu.VMEM(wk.shape, F32),
            pltpu.VMEM(wv.shape, F32),
            pltpu.VMEM((4, d_rows, 8 * HD), BF),
            pltpu.VMEM((rows // 2, D), BF),
            pltpu.VMEM((4, rows, D), BF),
            pltpu.VMEM((4, rows, D), BF),
            pltpu.VMEM((8, 128), F32),
            pltpu.VMEM((8, D), F32),
            pltpu.VMEM((4, 8, 128), F32),
            pltpu.VMEM((4, 8, 128), F32),
            pltpu.VMEM((2, half, 4 * HD), BF),
            pltpu.VMEM((4, 8, D), F32),
            pltpu.SemaphoreType.DMA((n_sems,)),
            pltpu.SemaphoreType.DMA((n_sems,)),
            pltpu.SemaphoreType.DMA((3,)),
        ],
        compiler_params=params(0),
        cost_estimate=pl.CostEstimate(
            flops=2 * half * D * 8 * HD, bytes_accessed=16 * 2**20, transcendentals=0
        ),
    )(tok, pos, *gains, wq, wk, wv)


def attend(block_map, inverse, core, cot, wg, wu, wo, wd):
    half = core.shape[1]
    length = 2 * half
    tiles = length // QT
    blocks = QT // BLK
    n_blocks = length // BLK
    factor = HD ** (-0.5) * LOG2E
    rows = cot.shape[0]
    d_rows = wg.shape[0]
    unit = wg.shape[1] // 4
    n_sems = 72

    def kernel(
        bm,
        inv,
        x_ref,
        cot_ref,
        wg_ref,
        wu_ref,
        wo_ref,
        wd_ref,
        att,
        mixed,
        lse_ref,
        cots,
        cot_own,
        wgu,
        wo_out,
        wd_out,
        q_s,
        k_s,
        v_s,
        o_s,
        wg_s,
        wu_s,
        wo_s,
        wd_s,
        wloc,
        handed,
        line,
        ssem,
        rsem,
        lsem,
    ):
        net = Net(ssem, rsem)
        x, y, c = net.x, net.y, net.c
        f = 2 * y + c
        fy = 2 * (1 - y) + c
        loads = [
            pltpu.make_async_copy(a, b, lsem.at[k])
            for k, (a, b) in enumerate(
                ((wg_ref, wg_s), (wu_ref, wu_s), (wo_ref, wo_s), (wd_ref, wd_s))
            )
        ]
        for cp in loads:
            cp.start()
        net.greet()
        n = rows // 2
        hand = net.new(cot_ref.at[pl.ds(n, n)], handed, net.to_y)
        route = Route(net, cot_ref.at[pl.ds(0, n)], line.at[:, pl.ds(0, n)], cots, 2)
        route2 = Route(net, handed, line.at[:, pl.ds(n, n)], cots, 2, n, True)
        hand.start()
        route.start()
        w_y = net.new(wloc.at[net.sy], wgu.at[f], net.to_y)
        w_core = net.new(wloc.at[net.me], wgu.at[f], net.to_core)
        w_relay = net.new(wgu.at[fy], wgu.at[fy], net.to_core)
        o_core = net.new(wo_out, wo_out, net.to_core)
        d_core = net.new(wd_out, wd_out, net.to_core)
        own = c == x

        @pl.loop(0, tiles)
        def _(i):
            for h in range(blocks):
                block = x_ref[inv[i * blocks + h]]
                at = pl.multiple_of(i * QT, QT) + h * BLK
                q_s[i, pl.ds(h * BLK, BLK), :] = block[:, 0:HD]
                q_s[i, pl.ds(QT + h * BLK, BLK), :] = block[:, HD : 2 * HD]
                k_s[pl.ds(at, BLK), :] = block[:, 2 * HD : 3 * HD]
                v_s[pl.ds(at, BLK), 0:HD] = block[:, 3 * HD : 4 * HD]

        v_s[:, HD : 2 * HD] = jnp.ones((length, HD), BF)
        for cp in loads:
            cp.wait()
        for t in range(4):
            wloc[t, :, 0:unit] = wg_s[:, t * unit : (t + 1) * unit].astype(BF)
            wloc[t, :, unit : 2 * unit] = wu_s[:, t * unit : (t + 1) * unit].astype(BF)
        w_y.start()
        w_core.start()
        wgu[f] = wloc[net.me]

        @pl.when(own)
        def _():
            wo_out[...] = wo_s[...].astype(BF)
            wd_out[...] = wd_s[...].astype(BF)
            o_core.start()
            d_core.start()

        q_row = lax.broadcasted_iota(jnp.int32, (2 * QT, QT), 0)
        k_row = lax.broadcasted_iota(jnp.int32, (2 * QT, QT), 1)
        allowed = jnp.where(q_row >= QT, q_row - QT, q_row) >= k_row

        def tile(i):
            q = q_s[i]
            acc = None
            for j in range(i + 1):
                at = slice(j * QT, (j + 1) * QT)
                scores = dot_nt(q, k_s[at, :]) * factor
                if j == i:
                    scores = jnp.where(allowed, scores, NEG)
                add = dot_nn(jnp.exp2(scores).astype(BF), v_s[at, :])
                acc = add if acc is None else acc + add
            total = acc[:, HD:]
            out = acc[:, :HD] / total
            lse_ref[i] = jnp.log2(jnp.transpose(total)[0:8, :])
            for h in range(blocks):
                for u in range(2):
                    o_s[i * blocks + h, :, u * HD : (u + 1) * HD] = out[
                        u * QT + h * BLK : u * QT + (h + 1) * BLK
                    ].astype(BF)

        def both(step, *args):
            getattr(route, step)(*args)
            getattr(route2, step)(*args)

        hand.wait_recv()
        route2.start()
        for i in range(tiles):
            tile(i)
            if i == 2:
                both("enter", [0])
            if i == 3:
                both("relay", [1])
                both("enter", [1])
            if i == 4:
                both("spread", 0)
            if i == 5:
                both("relay", [2])
                both("enter", [2])
            if i == 6:
                both("relay", [3])

        both("enter", [3])
        both("spread", 1)
        w_y.wait_recv()
        w_relay.start()
        swap = net.take(1)

        @pl.loop(0, n_blocks)
        def _(s):
            mixed[pl.ds(pl.multiple_of(s * BLK, BLK), BLK), :] = o_s[bm[s]]

        away = mixed.at[pl.ds(pl.multiple_of((1 - c) * half, half), half)]
        o_swap = net.copy(swap, away, att.at[c], net.to_core)
        o_swap.start()
        att[c] = mixed[pl.ds(pl.multiple_of(c * half, half), half), :]
        pl.when(jnp.logical_not(own))(lambda: o_core.wait_recv())
        pl.when(jnp.logical_not(own))(lambda: d_core.wait_recv())
        w_core.wait_recv()
        w_relay.wait_recv()
        for j in range(2):
            both("wait", j)
        cot_own[...] = cots[net.me]
        o_swap.wait()
        pl.when(own)(lambda: o_core.wait_send())
        pl.when(own)(lambda: d_core.wait_send())
        for cp in (w_y, w_core, w_relay):
            cp.wait_send()
        hand.wait_send()
        both("drain")

    vm = vmem_spec()
    smem = pl.BlockSpec(memory_space=pltpu.SMEM)
    return pl.pallas_call(
        kernel,
        name="attend",
        out_shape=[
            shape((2, half, 2 * HD), BF),
            shape((length, 2 * HD), BF),
            shape((tiles, 8, 2 * QT), F32),
            shape((4, rows, D), BF),
            shape((rows, D), BF),
            shape((4, d_rows, 2 * unit), BF),
            shape(wo.shape, BF),
            shape(wd.shape, BF),
        ],
        in_specs=[smem, smem, vm, vm] + [any_spec()] * 4,
        out_specs=[vm] * 8,
        scratch_shapes=[
            pltpu.VMEM((tiles, 2 * QT, HD), BF),
            pltpu.VMEM((length, HD), BF),
            pltpu.VMEM((length, 2 * HD), BF),
            pltpu.VMEM((n_blocks, BLK, 2 * HD), BF),
            pltpu.VMEM(wg.shape, F32),
            pltpu.VMEM(wu.shape, F32),
            pltpu.VMEM(wo.shape, F32),
            pltpu.VMEM(wd.shape, F32),
            pltpu.VMEM((4, d_rows, 2 * unit), BF),
            pltpu.VMEM((rows // 2, D), BF),
            pltpu.VMEM((4, rows, D), BF),
            pltpu.SemaphoreType.DMA((n_sems,)),
            pltpu.SemaphoreType.DMA((n_sems,)),
            pltpu.SemaphoreType.DMA((4,)),
        ],
        compiler_params=params(1),
        cost_estimate=pl.CostEstimate(
            flops=2 * 2 * 2 * length * length * HD, bytes_accessed=16 * 2**20, transcendentals=0
        ),
    )(block_map, inverse, core.reshape(n_blocks, BLK, 4 * HD), cot, wg, wu, wo, wd)


def feed_forward(att, x_own, wo, wgu, wd, cots, cot_own, gains):
    half = att.shape[1]
    rows = half // 4
    unit = wd.shape[0]
    d_rows = wgu.shape[1]
    d_tiles = unit // 2 // SMALL
    n_sems = 48 + 4 * d_tiles

    def kernel(
        att_ref,
        x_ref,
        wo_ref,
        wgu_ref,
        wd_ref,
        dy_ref,
        cot_ref,
        gain_ref,
        core,
        middle,
        dmiddle,
        result_part,
        sum_gu,
        sum_o,
        total_d,
        mlp_gain_part,
        part,
        got,
        mid,
        n2,
        hid,
        dgu,
        got2,
        mid2,
        dmb,
        gm,
        w_gu,
        got_gu,
        w_d,
        got_d,
        w_o,
        got_o,
        sum_d,
        d_slots,
        ssem,
        rsem,
    ):
        net = Net(ssem, rsem)
        c, me, sx, sy, sd = net.c, net.me, net.sx, net.sy, net.sd
        mlp_gain = gain_ref[1:2, :]
        net.greet()
        out_sum = PlaneSum(net, part, got, mid)

        def chunk(k):
            return pl.ds(pl.multiple_of(k * rows, rows), rows)

        def project(k):
            part[k] = (
                dot_nn(att_ref[0, chunk(k)], wo_ref[0 : 2 * HD, :])
                + dot_nn(att_ref[1, chunk(k)], wo_ref[2 * HD : 4 * HD, :])
            ).astype(BF)

        project(sd)
        out_sum.start_diagonal()
        project(sx)
        project(sy)
        out_sum.start_sides()
        project(me)
        out_sum.forward()

        def add_residual(at, total):
            value = x_ref[at].astype(F32) + total
            middle[at] = value
            n2[me, at] = (value * rms(value) * mlp_gain).astype(BF)

        out_sum.finish(add_residual)
        gather = PlaneGather(net, n2.at[me], n2)
        gather.start()

        def forward_back(k):
            rows_k = n2[k]
            gate_up = dot_nn(rows_k[:, 0:d_rows], wgu_ref[0])
            for g in range(1, 4):
                gate_up = gate_up + dot_nn(rows_k[:, g * d_rows : (g + 1) * d_rows], wgu_ref[g])
            gate, upward = gate_up[:, 0:unit], gate_up[:, unit : 2 * unit]
            sigmoid = 1.0 / (1.0 + jnp.exp(-gate))
            silu = gate * sigmoid
            hid[k] = (silu * upward).astype(BF)
            dh = dot_nt(dy_ref[k], wd_ref[...])
            dgu[k, :, 0:unit] = (
                dh * upward * sigmoid * (1.0 + gate * (1.0 - sigmoid))
            ).astype(BF)
            dgu[k, :, unit : 2 * unit] = (dh * silu).astype(BF)
            grads = dgu[k]
            for g in range(4):
                part[k, :, g * d_rows : (g + 1) * d_rows] = dot_nt(grads, wgu_ref[g]).astype(BF)

        out_sum.drain()
        forward_back(me)
        gather.forward()
        gather.wait_sides()
        back_sum = PlaneSum(net, part, got2, mid2)

        @pl.loop(0, 2)
        def _(n):
            forward_back(jnp.where(n == 0, sx, sy))

        back_sum.start_sides()
        gather.wait_diagonal()
        forward_back(sd)
        back_sum.start_diagonal()

        gu_sem = net.take(2)
        d_sem = net.take(1)
        o_sem = net.take(1)

        def gu_copy(n):
            return net.copy(gu_sem + n, w_gu.at[n], got_gu.at[n], net.to_core)

        d_copy = net.copy(d_sem, w_d, got_d, net.to_core)
        o_copy = net.copy(o_sem, w_o, got_o, net.to_core)
        all_dgu = dgu.shape[2]
        unit_half = unit // 2

        def down(core_of):
            at = pl.ds(pl.multiple_of(core_of * unit_half, unit_half), unit_half)
            return dot_tn(hid[:, :, at].reshape(half, unit_half), dy_ref[...].reshape(half, D))

        line = LineSum(
            net,
            d_tiles,
            lambda k: sum_d.at[pl.ds(pl.multiple_of(k * SMALL, SMALL), SMALL)],
            lambda k: total_d.at[pl.ds(pl.multiple_of(k * SMALL, SMALL), SMALL)],
            d_slots,
            lambda k: None,
        )
        pump = Pump([line], (0, 2, 5, 7))

        w_d[...] = down(1 - c).astype(BF)
        d_copy.start()
        value = down(c)
        d_copy.wait_recv()
        sum_d[...] = (value + got_d[...].astype(F32)).astype(BF)

        @pl.when(line.at_end)
        def _():
            @pl.loop(0, d_tiles)
            def _(k):
                line.gather(k)

        @pl.loop(0, 4)
        def _(k):
            result_part[k] = dot_nn(hid[k], wd_ref[...]).astype(BF)

        back_sum.forward()
        pump.step(0)

        def slab(n, core_of):
            f = 2 * n + core_of
            at = pl.ds(pl.multiple_of(f * d_rows, d_rows), d_rows)
            return dot_tn(n2[:, :, at].reshape(half, d_rows), dgu[...].reshape(half, all_dgu))

        for n in range(2):
            w_gu[n] = slab(n, 1 - c).astype(BF)
            gu_copy(n).start()
            pump.step(1 + n)

        def back_through_norm(at, dn2):
            value = middle[at]
            scale = rms(value)
            w2 = dn2 * mlp_gain
            grad = cot_ref[at].astype(F32) + norm_back(w2, value, scale)
            dmiddle[at] = grad
            dmb[me, at] = grad.astype(BF)
            first = dn2.shape[0] // 8
            folded = jnp.sum((dn2 * value * scale).reshape(first, 8, D), axis=0)
            mlp_gain_part[...] += folded

        mlp_gain_part[...] = jnp.zeros_like(mlp_gain_part)
        back_sum.finish(back_through_norm)
        gather2 = PlaneGather(net, dmb.at[me], dmb)
        gather2.start()
        swap_sem = net.take(4)

        def swap(k):
            return net.copy(
                swap_sem + k, gm.at[1 - c, chunk(k)], core.at[c, chunk(k)], net.to_core
            )

        def grad_mixed(k):
            value = dot_nt(dmb[k], wo_ref[...]).astype(BF)
            gm[0, chunk(k)] = value[:, 0 : 2 * HD]
            gm[1, chunk(k)] = value[:, 2 * HD : 4 * HD]
            swap(k).start()
            core[c, chunk(k)] = gm[c, chunk(k)]

        pump.step(3)
        pump.step(4)
        grad_mixed(me)
        pump.step(5)
        for n in range(2):
            value = slab(n, c)
            gu_copy(n).wait_recv()
            sum_gu[n] = (value + got_gu[n].astype(F32)).astype(BF)
            pump.step(6 + n)

        gather2.forward()
        for n in range(8, 11):
            pump.step(n)
        gather2.wait_sides()

        @pl.loop(0, 2)
        def _(n):
            grad_mixed(jnp.where(n == 0, sx, sy))

        for n in range(11, 14):
            pump.step(n)
        gather2.wait_diagonal()
        grad_mixed(sd)

        def out_grad(g):
            return dot_tn(att_ref[g], dmb[...].reshape(half, D))

        w_o[...] = out_grad(1 - c).astype(BF)
        o_copy.start()
        value = out_grad(c)
        o_copy.wait_recv()
        sum_o[...] = (value + got_o[...].astype(F32)).astype(BF)
        @pl.loop(14, pump.steps())
        def _(p):
            pump.step(p)

        @pl.loop(0, d_tiles)
        def _(k):
            line.drain(k)

        for k in range(4):
            swap(k).wait()
        for n in range(2):
            gu_copy(n).wait_send()
        d_copy.wait_send()
        o_copy.wait_send()
        gather.drain()
        gather2.drain()
        back_sum.drain()

    vm = vmem_spec()
    return pl.pallas_call(
        kernel,
        name="feed_forward",
        out_shape=[
            shape((2, half, 2 * HD), BF),
            shape((rows, D), F32),
            shape((rows, D), F32),
            shape((4, rows, D), BF),
            shape((2, d_rows, 2 * unit), BF),
            shape((2 * HD, D), BF),
            shape((unit // 2, D), BF),
            shape((8, D), F32),
        ],
        in_specs=[vm] * 8,
        out_specs=[vm] * 8,
        scratch_shapes=[
            pltpu.VMEM((4, rows, D), BF),
            pltpu.VMEM((3, rows, D), BF),
            pltpu.VMEM((rows, D), BF),
            pltpu.VMEM((4, rows, D), BF),
            pltpu.VMEM((4, rows, unit), BF),
            pltpu.VMEM((4, rows, 2 * unit), BF),
            pltpu.VMEM((3, rows, D), BF),
            pltpu.VMEM((rows, D), BF),
            pltpu.VMEM((4, rows, D), BF),
            pltpu.VMEM((2, half, 2 * HD), BF),
            pltpu.VMEM((2, d_rows, 2 * unit), BF),
            pltpu.VMEM((2, d_rows, 2 * unit), BF),
            pltpu.VMEM((unit // 2, D), BF),
            pltpu.VMEM((unit // 2, D), BF),
            pltpu.VMEM((2 * HD, D), BF),
            pltpu.VMEM((2 * HD, D), BF),
            pltpu.VMEM((unit // 2, D), BF),
            pltpu.VMEM((2, d_tiles, SMALL, D), BF),
            pltpu.SemaphoreType.DMA((n_sems,)),
            pltpu.SemaphoreType.DMA((n_sems,)),
        ],
        compiler_params=params(2, 62),
        cost_estimate=pl.CostEstimate(
            flops=24 * half * D * unit, bytes_accessed=32 * 2**20, transcendentals=0
        ),
    )(att, x_own, wo, wgu, wd, cots, cot_own, gains)


def finish_back(
    block_map,
    inverse,
    core,
    mixed,
    grad,
    lse,
    sum_o,
    total_d,
    sum_gu,
    result_part,
    middle,
    raw,
    table,
    n1,
    wall,
    x_own,
    dmiddle,
    gains,
    mlp_gain_part,
):
    half = core.shape[1]
    length = 2 * half
    blocks = QT // BLK
    n_blocks = length // BLK
    wide = 2 * QT
    tiles = length // wide
    scale = HD ** (-0.5)
    factor = scale * LOG2E
    rows = middle.shape[0]
    d_rows = wall.shape[1]
    gu_cols = sum_gu.shape[2]
    unit = gu_cols // 2
    o_tiles = sum_o.shape[0] // SMALL
    per = d_rows // SMALL
    w_tiles = 2 * per
    n_sems = 7 * o_tiles + 10 * w_tiles + 90

    def kernel(
        bm,
        inv,
        core_hbm,
        mixed_hbm,
        grad_hbm,
        lse_ref,
        o_part,
        d_ref,
        gu_ref,
        rp_hbm,
        mid_hbm,
        raw_hbm,
        table_hbm,
        n1_hbm,
        wall_hbm,
        x_hbm,
        dmid_hbm,
        gain_ref,
        mlp_ref,
        result,
        input_out,
        o_final,
        d_final,
        out_q,
        out_k,
        out_v,
        out_g,
        out_u,
        gain_out,
        dq,
        d_s,
        result_part_s,
        part,
        res,
        hub,
        got,
        mid,
        grad_in,
        hub2,
        got2,
        mid2,
        o_slots,
        o_sum,
        gu_rows,
        gu_slots,
        gu_mine,
        gu_other,
        w_out,
        w_got,
        w_sum,
        w_rows,
        w_slots,
        w_mine,
        w_other,
        g_sum,
        g_got,
        g_slots,
        g_mine,
        acc,
        ssem,
        rsem,
        lsem,
    ):
        net = Net(ssem, rsem)
        z, x, y, c = net.z, net.x, net.y, net.c
        load_part = pltpu.make_async_copy(rp_hbm, result_part_s, lsem.at[0])
        load_part.start()
        net.greet(True, True, True)
        total = PlaneSum(net, result_part_s, got, mid, rows // 4)
        total2 = PlaneSum(net, part, got2, mid2, rows // 4)
        gu_y = net.new(gu_ref.at[1 - y], gu_rows.at[1], net.to_y)
        home = HomeRoute(net, res, hub, result)
        home2 = HomeRoute(net, grad_in, hub2, input_out)
        swap = net.new(
            d_s.at[pl.ds(pl.multiple_of((1 - c) * half, half), half)], dq.at[c], net.to_core
        )
        x_sem = net.take(2 * o_tiles)
        chip_sem = net.take(o_tiles)
        owner = device(z, 1 - x, y, x)
        owns = c == x

        def cross(k, h):
            return net.copy(x_sem + h * o_tiles + k, o_sum.at[k], o_final.at[h, k], owner)

        def chip(k, h):
            return net.copy(chip_sem + k, o_sum.at[k], o_final.at[h, k], net.to_core)

        def deliver(k):
            cross(k, c).start()

            @pl.when(owns)
            def _():
                o_final[c, k] = o_sum[k]

            pl.when(jnp.logical_not(owns))(lambda: chip(k, c).start())

        d_x = [net.new(d_ref, d_final.at[h], owner) for h in range(2)]
        d_chip = net.new(d_ref, d_final.at[c], net.to_core)
        gx_sem = net.take(w_tiles)
        wx_sem = net.take(w_tiles)

        def gu_cross(k):
            return net.copy(gx_sem + k, gu_mine.at[k], gu_other.at[k], net.to_x)

        def w_cross(k):
            return net.copy(wx_sem + k, w_mine.at[k], w_other.at[k], net.to_x)

        def row_tile(ref):
            def at(k):
                first = pl.multiple_of(lax.rem(k, per) * SMALL, SMALL)
                return ref.at[lax.div(k, per), pl.ds(first, SMALL)]

            return at

        o_line = LineSum(
            net,
            o_tiles,
            lambda k: o_part.at[pl.ds(pl.multiple_of(k * SMALL, SMALL), SMALL)],
            lambda k: o_sum.at[k],
            o_slots,
            deliver,
        )
        gu_line = LineSum(
            net,
            w_tiles,
            row_tile(gu_rows),
            lambda k: gu_mine.at[k],
            gu_slots,
            lambda k: gu_cross(k).start(),
        )
        w_line = LineSum(
            net,
            w_tiles,
            row_tile(w_rows),
            lambda k: w_mine.at[k],
            w_slots,
            lambda k: w_cross(k).start(),
        )
        g_line = LineSum(
            net, 1, lambda k: g_sum.at[0], lambda k: g_mine.at[0], g_slots, lambda k: None
        )
        pump = Pump([o_line, gu_line, w_line], (1, 3, 5, 7))
        gu_first, w_first = o_tiles, o_tiles + w_tiles

        def rows_come(s):
            if isinstance(s, int):
                if s == gu_first + per:
                    gu_y.wait_recv()
                if s == w_first + per:
                    w_y.wait_recv()
            else:
                pl.when(s == gu_first + per)(gu_y.wait_recv)
                pl.when(s == w_first + per)(w_y.wait_recv)

        w_y = net.new(w_sum, w_rows.at[1], net.to_y)
        state = [0]

        def pump_on(count=1):
            for _ in range(count):
                pump.step(state[0], rows_come)
                state[0] += 1

        def ends(line, first, last):
            @pl.when(line.at_end)
            def _():
                @pl.loop(first, last)
                def _(k):
                    line.gather(k)

        gu_y.start()
        ends(o_line, 0, o_tiles)
        load_part.wait()
        total.start_diagonal()
        total.start_sides()
        gu_rows[0] = gu_ref[y]
        ends(gu_line, 0, per)
        for h in range(2):
            pl.when(c == h)(d_x[h].start)
        pl.when(jnp.logical_not(owns))(d_chip.start)

        d_keep = pltpu.make_async_copy(d_ref, d_final.at[c], lsem.at[11])
        pl.when(owns)(d_keep.start)
        def attention(x_s, o_s, g_in, q_s, g_s, k_s, v_s, delta_s):
            loads = [
                pltpu.make_async_copy(a, b, lsem.at[1 + n])
                for n, (a, b) in enumerate(((core_hbm, x_s), (mixed_hbm, o_s), (grad_hbm, g_in)))
            ]
            for cp in loads:
                cp.start()
            for cp in loads:
                cp.wait()
            for i in range(2 * tiles):
                for h in range(blocks):
                    s = inv[i * blocks + h]
                    block, out, grad_ = x_s[s], o_s[s], g_in[s]
                    at = slice((i * blocks + h) * BLK, (i * blocks + h + 1) * BLK)
                    for u in range(2):
                        first = (i % 2) * 2 * QT + u * QT + h * BLK
                        to = slice(first, first + BLK)
                        lanes = slice(u * HD, (u + 1) * HD)
                        q_s[i // 2, to, :] = block[:, lanes]
                        g_s[i // 2, to, :] = grad_[:, lanes]
                        product = grad_[:, lanes].astype(F32) * out[:, lanes].astype(F32)
                        delta_s[i // 2, :, to] = jnp.broadcast_to(
                            jnp.sum(jnp.transpose(product), axis=0, keepdims=True), (8, BLK)
                        )
                    k_s[at, :] = block[:, 2 * HD : 3 * HD]
                    v_s[at, :] = block[:, 3 * HD : 4 * HD]
                if i % 3 == 1:
                    pump_on()

            k_row = lax.broadcasted_iota(jnp.int32, (wide, 2 * wide), 0)
            q_row = lax.broadcasted_iota(jnp.int32, (wide, 2 * wide), 1)
            q_row = lax.shift_right_logical(q_row, 9) * QT + lax.bitwise_and(q_row, QT - 1)
            allowed = q_row >= k_row
            dq_t = [None] * tiles
            for j in range(tiles):
                at = slice(j * wide, (j + 1) * wide)
                k, v = k_s[at, :], v_s[at, :]
                k_t = jnp.transpose(k)
                dk = dv = None
                for i in range(j, tiles):
                    q, g = q_s[i], g_s[i]
                    shift = jnp.concatenate(
                        [lse_ref[2 * i, 0:1, :], lse_ref[2 * i + 1, 0:1, :]], 1
                    )
                    scores = dot_nt(k, q) * factor - shift
                    if i == j:
                        scores = jnp.where(allowed, scores, NEG)
                    p = jnp.exp2(scores)
                    ds = (p * (dot_nt(v, g) - delta_s[i, 0:1, :])).astype(BF)
                    add = dot_nn(k_t, ds)
                    dq_t[i] = add if dq_t[i] is None else dq_t[i] + add
                    add_k, add_v = dot_nn(ds, q), dot_nn(p.astype(BF), g)
                    dk = add_k if dk is None else dk + add_k
                    dv = add_v if dv is None else dv + add_v
                    pump_on()
                for h in range(wide // BLK):
                    part_ = slice(h * BLK, (h + 1) * BLK)
                    b = j * (wide // BLK) + h
                    x_s[b, :, 2 * HD : 3 * HD] = (dk[part_] * scale).astype(BF)
                    x_s[b, :, 3 * HD : 4 * HD] = dv[part_].astype(BF)
                dq_j = jnp.transpose(dq_t[j]) * scale
                for e in range(2):
                    for u in range(2):
                        for h in range(blocks):
                            first = e * 2 * QT + u * QT + h * BLK
                            x_s[(2 * j + e) * blocks + h, :, u * HD : (u + 1) * HD] = dq_j[
                                first : first + BLK
                            ].astype(BF)

            @pl.loop(0, n_blocks)
            def _(s):
                d_s[pl.ds(pl.multiple_of(s * BLK, BLK), BLK), :] = x_s[bm[s]]

        pl.run_scoped(
            attention,
            pltpu.VMEM((n_blocks, BLK, 4 * HD), BF),
            pltpu.VMEM((n_blocks, BLK, 2 * HD), BF),
            pltpu.VMEM((n_blocks, BLK, 2 * HD), BF),
            pltpu.VMEM((tiles, 2 * wide, HD), BF),
            pltpu.VMEM((tiles, 2 * wide, HD), BF),
            pltpu.VMEM((length, HD), BF),
            pltpu.VMEM((length, HD), BF),
            pltpu.VMEM((tiles, 8, 2 * wide), F32),
        )
        swap.start()
        dq[c] = d_s[pl.ds(pl.multiple_of(c * half, half), half), :]

        @pl.when(gu_line.at_end)
        def _():
            gu_y.wait_recv()

        ends(gu_line, per, w_tiles)
        pump_on()

        def norms(raw_ref, table_ref, n1_ref, wall_ref, x_ref, dmid_ref, mid_ref, dcat):
            loads = [
                pltpu.make_async_copy(a, b, lsem.at[4 + n])
                for n, (a, b) in enumerate(
                    (
                        (raw_hbm, raw_ref),
                        (table_hbm, table_ref),
                        (n1_hbm, n1_ref),
                        (wall_hbm, wall_ref),
                        (x_hbm, x_ref),
                        (dmid_hbm, dmid_ref),
                        (mid_hbm, mid_ref),
                    )
                )
            ]
            for cp in loads:
                cp.start()
            swap.wait_recv()
            for cp in loads:
                cp.wait()
            attn_gain, q_gain, k_gain = gain_ref[0:1, :], gain_ref[2:3, 0:HD], gain_ref[3:4, 0:HD]
            acc[...] = jnp.zeros_like(acc)

            def fold(v):
                return jnp.sum(v.reshape(v.shape[0] // 8, 8, v.shape[1]), axis=0)

            def chunk(k):
                at = pl.ds(pl.multiple_of(k * rows, rows), rows)
                half_w = HD // 2
                cosine, sine = table_ref[at, 0:half_w], table_ref[at, half_w:HD]
                cosine = jnp.concatenate([cosine, cosine], axis=-1)
                sine = jnp.concatenate([-sine, sine], axis=-1)
                for h in range(6):
                    g, lane = (h // 2, (h % 2) * HD) if h < 4 else (h - 4, 2 * HD)
                    gain = q_gain if h < 4 else k_gain
                    grad_ = dq[g, at, lane : lane + HD].astype(F32)
                    du = grad_ * cosine - pltpu.roll(grad_, half_w, 1) * sine
                    u = raw_ref[at, h * HD : (h + 1) * HD]
                    size = rms(u)
                    lanes = slice(0, HD) if h < 4 else slice(HD, 2 * HD)
                    acc[2, :, lanes] += fold(du * u * size)
                    dcat[at, h * HD : (h + 1) * HD] = norm_back(du * gain, u, size).astype(BF)
                for g in range(2):
                    dcat[at, (6 + g) * HD : (7 + g) * HD] = dq[g, at, 3 * HD : 4 * HD]

            def project(k):
                d = dcat[pl.ds(pl.multiple_of(k * rows, rows), rows), :]
                for g in range(4):
                    part[k, :, g * d_rows : (g + 1) * d_rows] = dot_nt(d, wall_ref[g]).astype(BF)

            def add(at, value):
                res[at] = (mid_ref[at] + value).astype(BF)

            chunk(net.sd)
            pump_on()
            project(net.sd)
            total2.start_diagonal()
            pump_on()
            total.forward()
            for k in (net.sx, net.sy):
                chunk(k)
                pump_on()
                project(k)
                pump_on()
            total2.start_sides()
            chunk(net.me)
            pump_on()
            project(net.me)
            total2.forward()
            pump_on()

            def slab(n, core_of):
                f = 2 * n + core_of
                at = pl.ds(pl.multiple_of(f * d_rows, d_rows), d_rows)
                return dot_tn(n1_ref[:, at], dcat[...])

            w_sem = net.take(2)

            def w_copy(n):
                return net.copy(w_sem + n, w_out.at[n], w_got.at[n], net.to_core)

            for n in range(2):
                w_out[n] = slab(n, 1 - c).astype(BF)
                w_copy(n).start()
                pump_on()
            total.finish(add)
            home.start()
            value = slab(1 - y, c)
            w_copy(1 - y).wait_recv()
            w_sum[...] = (value + w_got[1 - y].astype(F32)).astype(BF)
            w_y.start()
            pump_on()
            value = slab(y, c)
            w_copy(y).wait_recv()
            w_rows[0] = (value + w_got[y].astype(F32)).astype(BF)
            ends(w_line, 0, per)
            pump_on()

            def back_through_norm(at, dn1):
                value = x_ref[at].astype(F32)
                size = rms(value)
                acc[0] += fold(dn1 * value * size)
                grad_in[at] = (dmid_ref[at] + norm_back(dn1 * attn_gain, value, size)).astype(BF)

            total2.finish(back_through_norm)
            for n in range(2):
                w_copy(n).wait_send()

        pl.run_scoped(
            norms,
            pltpu.VMEM(raw.shape, F32),
            pltpu.VMEM(table.shape, F32),
            pltpu.VMEM(n1.shape, BF),
            pltpu.VMEM(wall.shape, BF),
            pltpu.VMEM((rows, D), BF),
            pltpu.VMEM((rows, D), F32),
            pltpu.VMEM((rows, D), F32),
            pltpu.VMEM((half, 8 * HD), BF),
        )
        home2.start()
        pump_on()

        def place(k, slots, copies, outs, widths):
            copies(k).wait_recv()
            row_half = jnp.where(k < per, y, 1 - y)
            at = pl.ds(pl.multiple_of(lax.rem(k, per) * SMALL, SMALL), SMALL)
            for tile, x_of in zip(slots, (x, 1 - x)):
                quarter = 2 * row_half + x_of
                first = 0
                for out, width in zip(outs, widths):
                    lanes = pl.ds(pl.multiple_of(quarter * width, width), width)
                    out[at, lanes] = tile[k, :, first : first + width]
                    first += width

        def place_gu(k):
            place(k, (gu_mine, gu_other), gu_cross, (out_g, out_u), (unit, unit))

        def place_w(k):
            place(k, (w_mine, w_other), w_cross, (out_q, out_k, out_v), (4 * HD, 2 * HD, 2 * HD))

        acc[1] = mlp_ref[...]
        for row in range(3):
            g_sum[0, row : row + 1, :] = jnp.sum(acc[row], axis=0, keepdims=True)
        g_sum[0, 3:8, :] = jnp.zeros((5, D), F32)
        for n, to in enumerate((net.to_core, net.to_y, net.to_x)):
            cp = net.new(g_sum.at[0], g_got.at[n], to)
            cp.start()
            pump_on()
            cp.wait()
            g_sum[0] = g_sum[0] + g_got[n]
        g_line.gather(0)

        @pl.when(w_line.at_end)
        def _():
            w_y.wait_recv()

        ends(w_line, per, w_tiles)
        home.enter()
        pump_on()
        home2.enter()
        pump_on()
        so_far = state[0]
        place_lag = 14

        @pl.loop(0, so_far - place_lag - gu_first)
        def _(k):
            place_gu(k)

        @pl.loop(so_far, pump.steps())
        def _(p):
            pump.step(p, rows_come)
            for n, distance in enumerate((3, 2, 1, 0)):

                @pl.when(p == so_far + 1 + 2 * n)
                def _():
                    home.relay([distance])
                    home2.relay([distance])

            q = p - place_lag
            pl.when(within(q, gu_first, w_first))(lambda: place_gu(q - gu_first))
            pl.when(within(q, w_first, w_first + w_tiles))(lambda: place_w(q - w_first))

        g_line.finish(0)
        gain_out[...] = g_mine[0]

        @pl.loop(pump.steps() - place_lag - w_first, w_tiles)
        def _(k):
            place_w(k)

        @pl.loop(0, o_tiles)
        def _(k):
            @pl.when(owns)
            def _():
                chip(k, 1 - c).wait_recv()

            @pl.when(jnp.logical_not(owns))
            def _():
                for h in range(2):
                    cross(k, h).wait_recv()
                chip(k, c).wait_send()

            cross(k, c).wait_send()
            o_line.drain(k)

        @pl.when(owns)
        def _():
            d_chip.wait_recv()
            d_keep.wait()

        @pl.when(jnp.logical_not(owns))
        def _():
            for h in range(2):
                d_x[h].wait_recv()
            d_chip.wait_send()

        for h in range(2):
            pl.when(c == h)(d_x[h].wait_send)

        @pl.loop(0, w_tiles)
        def _(k):
            gu_line.drain(k)
            w_line.drain(k)
            gu_cross(k).wait_send()
            w_cross(k).wait_send()

        g_line.drain(0)
        gu_y.wait_send()
        w_y.wait_send()
        swap.wait_send()
        total.drain()
        total2.drain()
        home.drain()
        home2.drain()

    vm = vmem_spec()
    hbm = any_spec()
    smem = pl.BlockSpec(memory_space=pltpu.SMEM)
    chunk_ = pltpu.VMEM((rows, D), BF)
    four = pltpu.VMEM((4, rows, D), BF)
    three = pltpu.VMEM((3, rows, D), BF)
    gu_tiles = pltpu.VMEM((w_tiles, SMALL, gu_cols), BF)
    gu_pairs = pltpu.VMEM((2, w_tiles, SMALL, gu_cols), BF)
    qkv_tiles = pltpu.VMEM((w_tiles, SMALL, 8 * HD), BF)
    qkv_pairs = pltpu.VMEM((2, w_tiles, SMALL, 8 * HD), BF)
    g_tile = pltpu.VMEM((1, 8, D), F32)
    slabs = pltpu.VMEM((2, d_rows, 8 * HD), BF)
    return pl.pallas_call(
        kernel,
        name="finish_back",
        out_shape=[
            shape((rows, D), BF),
            shape((rows, D), BF),
            shape((2, o_tiles, SMALL, D), BF),
            shape((2,) + total_d.shape, BF),
            shape((d_rows, 16 * HD), BF),
            shape((d_rows, 8 * HD), BF),
            shape((d_rows, 8 * HD), BF),
            shape((d_rows, 4 * unit), BF),
            shape((d_rows, 4 * unit), BF),
            shape((8, D), F32),
        ],
        in_specs=[smem, smem] + [hbm] * 3 + [vm] * 4 + [hbm] * 8 + [vm] * 2,
        out_specs=[vm] * 3 + [hbm] + [vm] * 6,
        scratch_shapes=[
            pltpu.VMEM((2, half, 4 * HD), BF),
            pltpu.VMEM((length, 4 * HD), BF),
            four,
            four,
            chunk_,
            four,
            three,
            chunk_,
            chunk_,
            four,
            three,
            chunk_,
            pltpu.VMEM((2, o_tiles, SMALL, D), BF),
            pltpu.VMEM((o_tiles, SMALL, D), BF),
            pltpu.VMEM(sum_gu.shape, BF),
            gu_pairs,
            gu_tiles,
            gu_tiles,
            slabs,
            slabs,
            pltpu.VMEM((d_rows, 8 * HD), BF),
            slabs,
            qkv_pairs,
            qkv_tiles,
            qkv_tiles,
            g_tile,
            pltpu.VMEM((3, 8, D), F32),
            pltpu.VMEM((2, 1, 8, D), F32),
            g_tile,
            pltpu.VMEM((3, 8, D), F32),
            pltpu.SemaphoreType.DMA((n_sems,)),
            pltpu.SemaphoreType.DMA((n_sems,)),
            pltpu.SemaphoreType.DMA((12,)),
        ],
        compiler_params=params(3, 63),
        cost_estimate=pl.CostEstimate(
            flops=5 * 2 * 2 * length * length * HD, bytes_accessed=32 * 2**20, transcendentals=0
        ),
    )(
        block_map,
        inverse,
        core.reshape(n_blocks, BLK, 4 * HD),
        mixed.reshape(n_blocks, BLK, 2 * HD),
        grad.reshape(n_blocks, BLK, 2 * HD),
        lse,
        sum_o,
        total_d,
        sum_gu,
        result_part,
        middle,
        raw,
        table,
        n1,
        wall,
        x_own,
        dmiddle,
        gains,
        mlp_gain_part,
    )


def widen(arrays, gain_sums, parts, steps=8):
    n = len(arrays)
    d_part, h_part = D // parts, HD // parts

    def kernel(*refs):
        for a, b in zip(refs[:n], refs[n + 1 : 2 * n + 1]):
            b[...] = a[...].astype(F32)
        sums = refs[n]
        attn, mlp, query, key = refs[2 * n + 1 :]

        @pl.when(pl.program_id(0) == 0)
        def _():
            f = lax.axis_index("fsdp")
            at = pl.ds(pl.multiple_of(f * d_part, d_part), d_part)
            attn[...] = sums[0:1, at]
            mlp[...] = sums[1:2, at]
            for out, first in ((query, 0), (key, HD)):
                turned = pltpu.roll(sums[0:8, first : first + HD], HD - f * h_part, 1)
                out[...] = turned[2:3, 0:h_part]

    def spec(a):
        return pl.BlockSpec((a.shape[0] // steps, a.shape[1]), lambda i: (i, 0))

    def whole(dims):
        return pl.BlockSpec(dims, lambda i: (0, 0))

    small = [(1, d_part), (1, d_part), (1, h_part), (1, h_part)]
    return pl.pallas_call(
        kernel,
        name="widen",
        grid=(steps,),
        out_shape=[shape(a.shape, F32) for a in arrays] + [shape(s, F32) for s in small],
        in_specs=[spec(a) for a in arrays] + [whole(gain_sums.shape)],
        out_specs=[spec(a) for a in arrays] + [whole(s) for s in small],
        compiler_params=pltpu.CompilerParams(vmem_limit_bytes=62 * 2**20),
    )(*arrays, gain_sums)


def plane_body(
    tokens,
    cotangent,
    block_map,
    positions,
    attn_gain,
    query_weight,
    key_weight,
    value_weight,
    query_gain,
    key_gain,
    out_weight,
    mlp_gain,
    gate_weight,
    up_weight,
    down_weight,
):
    rows = tokens.shape[1]
    parts = lax.axis_size("fsdp")
    flat_map = block_map.reshape(-1)
    n_blocks = flat_map.shape[0]
    order = jnp.arange(n_blocks, dtype=jnp.int32)
    inverse = jnp.sum(
        jnp.where(flat_map[None, :] == order[:, None], order[None, :], 0), axis=1
    ).astype(jnp.int32)
    x_own, n1, raw, table, core, wall, gains = enter(
        tokens.reshape(rows, D),
        positions,
        [g.reshape(1, -1) for g in (attn_gain, mlp_gain, query_gain, key_gain)],
        query_weight,
        key_weight,
        value_weight,
    )
    att, mixed, lse, cots, cot_own, wgu, wo, wd = attend(
        flat_map,
        inverse,
        core,
        cotangent.reshape(rows, D),
        gate_weight,
        up_weight,
        out_weight,
        down_weight,
    )
    grad, middle, dmiddle, result_part, sum_gu, sum_o, total_d, mlp_gain_part = feed_forward(
        att, x_own, wo, wgu, wd, cots, cot_own, gains
    )
    (
        result,
        input_grad,
        grad_o,
        grad_d,
        grad_q,
        grad_k,
        grad_v,
        grad_g,
        grad_u,
        gain_sums,
    ) = finish_back(
        flat_map,
        inverse,
        core,
        mixed,
        grad,
        lse,
        sum_o,
        total_d,
        sum_gu,
        result_part,
        middle,
        raw,
        table,
        n1,
        wall,
        x_own,
        dmiddle,
        gains,
        mlp_gain_part,
    )

    (
        result,
        input_grad,
        grad_q,
        grad_k,
        grad_v,
        grad_o,
        grad_g,
        grad_u,
        grad_d,
        *gain_grads,
    ) = widen(
        [
            result,
            input_grad,
            grad_q,
            grad_k,
            grad_v,
            grad_o.reshape(out_weight.shape),
            grad_g,
            grad_u,
            grad_d.reshape(down_weight.shape),
        ],
        gain_sums,
        parts,
    )
    attn_grad, mlp_grad, query_grad, key_grad = [g.reshape(-1) for g in gain_grads]
    return (
        result.reshape(tokens.shape),
        input_grad.reshape(tokens.shape),
        attn_grad,
        grad_q,
        grad_k,
        grad_v,
        query_grad,
        key_grad,
        grad_o,
        mlp_grad,
        grad_g,
        grad_u,
        grad_d,
    )


def solution(mesh):
    placed = (
        P("fsdp", "ctx", None),
        P("fsdp", "ctx", None),
        P(),
        P("fsdp", "ctx"),
        P("fsdp"),
        P("fsdp", None),
        P("fsdp", None),
        P("fsdp", None),
        P("fsdp"),
        P("fsdp"),
        P("fsdp", None),
        P("fsdp"),
        P("fsdp", None),
        P("fsdp", None),
        P("fsdp", None),
    )
    fits = mesh.shape["fsdp"] == 4 and mesh.shape["ctx"] == 8
    return jax.shard_map(
        plane_body if fits else body,
        mesh=mesh,
        in_specs=placed,
        out_specs=(
            P("fsdp", "ctx", None),
            P("fsdp", "ctx", None),
            P("fsdp"),
            P("fsdp", None),
            P("fsdp", None),
            P("fsdp", None),
            P("fsdp"),
            P("fsdp"),
            P("fsdp", None),
            P("fsdp"),
            P("fsdp", None),
            P("fsdp", None),
            P("fsdp", None),
        ),
        check_vma=False,
    )
```

```python
import math

import jax
import jax.numpy as jnp
from jax import lax
from jax.experimental import pallas as pl
from jax.experimental.pallas import tpu as pltpu
from jax.sharding import PartitionSpec as P

D = 1024
HQ = 16
HK = 8
HD = 128
BLK = 128


epsilon = 1e-06
theta_base = 1000000.0
masked_value = -1e30


def rms_scale(values):
    return lax.rsqrt(jnp.mean(values * values, axis=-1, keepdims=True) + epsilon)


def norm_back(upstream, values, scale):
    return scale * upstream - values * (scale * scale * scale) * jnp.mean(
        upstream * values, axis=-1, keepdims=True
    )


def rope_tables(positions, head_dim):
    frequency = jnp.exp(
        jnp.arange(0, head_dim, 2).astype(jnp.float32) * (-math.log(theta_base) / head_dim)
    )
    angles = positions.astype(jnp.float32)[..., None] * frequency
    angles = jnp.concatenate([angles, angles], axis=-1)
    return (jnp.cos(angles), jnp.sin(angles))


def rotate(values, cosine, sine_table):
    half_width = values.shape[-1] // 2
    turned = jnp.concatenate([-values[..., half_width:], values[..., :half_width]], axis=-1)
    return values * cosine + turned * sine_table


def unrotate(grads, cosine, sine_table):
    half_width = grads.shape[-1] // 2
    moved = grads * sine_table
    back_turn = jnp.concatenate([moved[..., half_width:], -moved[..., :half_width]], axis=-1)
    return grads * cosine + back_turn


def score_block(grouped, keys_head, allowed, scale):
    scores = (
        jnp.einsum("qgd,sd->gqs", grouped, keys_head, preferred_element_type=jnp.float32) * scale
    )
    return jnp.where(allowed, scores, masked_value)


def body(
    tokens,
    cotangent,
    block_map,
    positions,
    attn_gain,
    query_weight,
    key_weight,
    value_weight,
    query_gain,
    key_gain,
    out_weight,
    mlp_gain,
    gate_weight,
    up_weight,
    down_weight,
):
    seq_count = tokens.shape[0]
    seq_rows = tokens.shape[1]
    total_rows = seq_count * seq_rows
    groups = HQ // HK
    scale = HD ** (-0.5)
    attn_full, query_full, key_full, mlp_full = (
        lax.all_gather(attn_gain, "fsdp", axis=0, tiled=True),
        lax.all_gather(query_gain, "fsdp", axis=0, tiled=True),
        lax.all_gather(key_gain, "fsdp", axis=0, tiled=True),
        lax.all_gather(mlp_gain, "fsdp", axis=0, tiled=True),
    )
    query_w, key_w, value_w, out_w = (
        lax.all_gather(query_weight.astype(jnp.bfloat16), "fsdp", axis=0, tiled=True),
        lax.all_gather(key_weight.astype(jnp.bfloat16), "fsdp", axis=0, tiled=True),
        lax.all_gather(value_weight.astype(jnp.bfloat16), "fsdp", axis=0, tiled=True),
        lax.all_gather(out_weight.astype(jnp.bfloat16), "fsdp", axis=0, tiled=True),
    )
    flat = tokens.astype(jnp.float32).reshape(total_rows, D)
    scale_one = rms_scale(flat)
    normed = (flat * scale_one * attn_full).astype(jnp.bfloat16)
    query_raw = jnp.dot(normed, query_w, preferred_element_type=jnp.float32).reshape(
        total_rows, HQ, HD
    )
    key_raw = jnp.dot(normed, key_w, preferred_element_type=jnp.float32).reshape(total_rows, HK, HD)
    value_low = jnp.dot(normed, value_w, preferred_element_type=jnp.float32).astype(jnp.bfloat16)
    cosine, sine_table = rope_tables(positions.reshape(total_rows), HD)
    cosine = cosine[:, None, :]
    sine_table = sine_table[:, None, :]
    query_scale = rms_scale(query_raw)
    query_unit = query_raw * query_scale
    query_low = rotate(query_unit * query_full, cosine, sine_table).astype(jnp.bfloat16)
    key_scale = rms_scale(key_raw)
    key_unit = key_raw * key_scale
    key_low = rotate(key_unit * key_full, cosine, sine_table).astype(jnp.bfloat16)
    flat_map = block_map.reshape(-1)
    offsets = jnp.arange(BLK, dtype=jnp.int32)
    key_index = (flat_map[:, None] * BLK + offsets[None, :]).reshape(-1)
    own_blocks = lax.dynamic_slice_in_dim(flat_map, lax.axis_index("ctx") * 2, 2)
    query_index = (own_blocks[:, None] * BLK + offsets[None, :]).reshape(-1)
    allowed = query_index[:, None] >= key_index[None, :]
    query_seq = query_low.reshape(seq_count, seq_rows, HK, groups, HD)
    key_seq = key_low.reshape(seq_count, seq_rows, HK * HD)
    value_seq = value_low.reshape(seq_count, seq_rows, HK * HD)

    def forward_head(inputs):
        grouped, keys_head, values_head = inputs
        scores = score_block(grouped, keys_head, allowed, scale)
        row_max = jnp.max(scores, axis=-1, keepdims=True)
        exp_scores = jnp.exp(scores - row_max)
        row_total = jnp.sum(exp_scores, axis=-1, keepdims=True)
        prob_low = (exp_scores / row_total).astype(jnp.bfloat16)
        mixed = jnp.einsum("gqs,sd->qgd", prob_low, values_head, preferred_element_type=jnp.float32)
        return (mixed, row_max + jnp.log(row_total))

    seq_item = 0
    keys_all = lax.all_gather(key_seq[seq_item], "ctx", axis=0, tiled=True)
    values_all = lax.all_gather(value_seq[seq_item], "ctx", axis=0, tiled=True)
    keys_head = jnp.transpose(keys_all.reshape(-1, HK, HD), (1, 0, 2))
    values_head = jnp.transpose(values_all.reshape(-1, HK, HD), (1, 0, 2))
    grouped_head = jnp.transpose(query_seq[seq_item], (1, 0, 2, 3))
    mixed, lse = lax.map(forward_head, (grouped_head, keys_head, values_head))
    mixed_parts = jnp.transpose(mixed, (1, 0, 2, 3)).reshape(seq_rows, HQ * HD)
    lse_parts = [lse]
    gathered = [(grouped_head, keys_head, values_head)]
    attended = mixed_parts.astype(jnp.bfloat16)
    middle = flat + jnp.dot(attended, out_w, preferred_element_type=jnp.float32)
    gate_w, up_w, down_w = (
        lax.all_gather(gate_weight.astype(jnp.bfloat16), "fsdp", axis=0, tiled=True),
        lax.all_gather(up_weight.astype(jnp.bfloat16), "fsdp", axis=0, tiled=True),
        lax.all_gather(down_weight.astype(jnp.bfloat16), "fsdp", axis=0, tiled=True),
    )
    scale_two = rms_scale(middle)
    normed_two = (middle * scale_two * mlp_full).astype(jnp.bfloat16)
    gate = jnp.dot(normed_two, gate_w, preferred_element_type=jnp.float32)
    upward = jnp.dot(normed_two, up_w, preferred_element_type=jnp.float32)
    sigmoid_gate = jax.nn.sigmoid(gate)
    silu_gate = gate * sigmoid_gate
    hidden = (silu_gate * upward).astype(jnp.bfloat16)
    result = middle + jnp.dot(hidden, down_w, preferred_element_type=jnp.float32)
    query_back, key_back, value_back, out_back = (
        lax.all_gather(query_weight.astype(jnp.bfloat16), "fsdp", axis=0, tiled=True),
        lax.all_gather(key_weight.astype(jnp.bfloat16), "fsdp", axis=0, tiled=True),
        lax.all_gather(value_weight.astype(jnp.bfloat16), "fsdp", axis=0, tiled=True),
        lax.all_gather(out_weight.astype(jnp.bfloat16), "fsdp", axis=0, tiled=True),
    )
    gate_back, up_back, down_back = (
        lax.all_gather(gate_weight.astype(jnp.bfloat16), "fsdp", axis=0, tiled=True),
        lax.all_gather(up_weight.astype(jnp.bfloat16), "fsdp", axis=0, tiled=True),
        lax.all_gather(down_weight.astype(jnp.bfloat16), "fsdp", axis=0, tiled=True),
    )
    grad_out = cotangent.astype(jnp.float32).reshape(total_rows, D)
    grad_branch = grad_out.astype(jnp.bfloat16)
    down_grad = jnp.einsum("nf,nd->fd", hidden, grad_branch, preferred_element_type=jnp.float32)
    grad_hidden = jnp.einsum(
        "nd,fd->nf", grad_branch, down_back, preferred_element_type=jnp.float32
    )
    grad_gate = (grad_hidden * upward * sigmoid_gate * (1.0 + gate * (1.0 - sigmoid_gate))).astype(
        jnp.bfloat16
    )
    grad_up = (grad_hidden * silu_gate).astype(jnp.bfloat16)
    gate_grad = jnp.einsum("nd,nf->df", normed_two, grad_gate, preferred_element_type=jnp.float32)
    up_grad = jnp.einsum("nd,nf->df", normed_two, grad_up, preferred_element_type=jnp.float32)
    grad_normed_two = jnp.einsum(
        "nf,df->nd", grad_gate, gate_back, preferred_element_type=jnp.float32
    ) + jnp.einsum("nf,df->nd", grad_up, up_back, preferred_element_type=jnp.float32)
    mlp_local = jnp.sum(grad_normed_two * middle * scale_two, axis=0)
    grad_middle = grad_out + norm_back(grad_normed_two * mlp_full, middle, scale_two)
    grad_attn_low = grad_middle.astype(jnp.bfloat16)
    out_grad = jnp.einsum("nq,nd->qd", attended, grad_attn_low, preferred_element_type=jnp.float32)
    grad_mixed = jnp.einsum(
        "nd,qd->nq", grad_attn_low, out_back, preferred_element_type=jnp.float32
    ).astype(jnp.bfloat16)
    grad_mixed_seq = grad_mixed.reshape(seq_count, seq_rows, HK, groups, HD)

    def backward_head(inputs):
        grouped, keys_head, values_head, grad_head, lse = inputs
        scores = score_block(grouped, keys_head, allowed, scale)
        prob_full = jnp.exp(scores - lse)
        grad_prob = jnp.einsum(
            "qgd,sd->gqs", grad_head, values_head, preferred_element_type=jnp.float32
        )
        delta_row = jnp.sum(prob_full * grad_prob, axis=-1, keepdims=True)
        grad_scores = (prob_full * (grad_prob - delta_row)).astype(jnp.bfloat16)
        grad_query_head = (
            jnp.einsum("gqs,sd->qgd", grad_scores, keys_head, preferred_element_type=jnp.float32)
            * scale
        )
        grad_key_head = (
            jnp.einsum("gqs,qgd->sd", grad_scores, grouped, preferred_element_type=jnp.float32)
            * scale
        )
        grad_value_head = jnp.einsum(
            "gqs,qgd->sd",
            prob_full.astype(jnp.bfloat16),
            grad_head,
            preferred_element_type=jnp.float32,
        )
        return (grad_query_head, grad_key_head, grad_value_head)

    seq_item = 0
    grouped_head, keys_head, values_head = gathered[seq_item]
    grad_head = jnp.transpose(grad_mixed_seq[seq_item], (1, 0, 2, 3))
    grad_query_head, grad_key_head, grad_value_head = lax.map(
        backward_head, (grouped_head, keys_head, values_head, grad_head, lse_parts[seq_item])
    )
    grad_query_parts = jnp.transpose(grad_query_head, (1, 0, 2, 3)).reshape(seq_rows, HQ, HD)
    grad_keys_all = jnp.transpose(grad_key_head, (1, 0, 2)).reshape(-1, HK * HD)
    grad_values_all = jnp.transpose(grad_value_head, (1, 0, 2)).reshape(-1, HK * HD)
    grad_key_own = lax.psum_scatter(
        grad_keys_all.astype(jnp.bfloat16), "ctx", scatter_dimension=0, tiled=True
    ).astype(jnp.float32)
    grad_value_own = lax.psum_scatter(
        grad_values_all.astype(jnp.bfloat16), "ctx", scatter_dimension=0, tiled=True
    )
    grad_key = grad_key_own.reshape(total_rows, HK, HD)
    grad_query_unit = unrotate(grad_query_parts, cosine, sine_table)
    qgain_local = jnp.sum(grad_query_unit * query_unit, axis=(0, 1))
    grad_query_low = (
        norm_back(grad_query_unit * query_full, query_raw, query_scale)
        .astype(jnp.bfloat16)
        .reshape(total_rows, HQ * HD)
    )
    grad_key_unit = unrotate(grad_key, cosine, sine_table)
    kgain_local = jnp.sum(grad_key_unit * key_unit, axis=(0, 1))
    grad_key_low = (
        norm_back(grad_key_unit * key_full, key_raw, key_scale)
        .astype(jnp.bfloat16)
        .reshape(total_rows, HK * HD)
    )
    query_grad = jnp.einsum("nd,nc->dc", normed, grad_query_low, preferred_element_type=jnp.float32)
    key_grad = jnp.einsum("nd,nc->dc", normed, grad_key_low, preferred_element_type=jnp.float32)
    value_grad = jnp.einsum("nd,nc->dc", normed, grad_value_own, preferred_element_type=jnp.float32)
    grad_normed = jnp.einsum(
        "nc,dc->nd", grad_query_low, query_back, preferred_element_type=jnp.float32
    )
    grad_normed = grad_normed + jnp.einsum(
        "nc,dc->nd", grad_key_low, key_back, preferred_element_type=jnp.float32
    )
    grad_normed = grad_normed + jnp.einsum(
        "nc,dc->nd", grad_value_own, value_back, preferred_element_type=jnp.float32
    )
    attn_local = jnp.sum(grad_normed * flat * scale_one, axis=0)
    input_grad = grad_middle + norm_back(grad_normed * attn_full, flat, scale_one)
    shares = (
        lax.psum_scatter(
            attn_local.astype(jnp.bfloat16), "fsdp", scatter_dimension=0, tiled=True
        ).astype(jnp.float32),
        lax.psum_scatter(
            query_grad.astype(jnp.bfloat16), "fsdp", scatter_dimension=0, tiled=True
        ).astype(jnp.float32),
        lax.psum_scatter(
            key_grad.astype(jnp.bfloat16), "fsdp", scatter_dimension=0, tiled=True
        ).astype(jnp.float32),
        lax.psum_scatter(
            value_grad.astype(jnp.bfloat16), "fsdp", scatter_dimension=0, tiled=True
        ).astype(jnp.float32),
        lax.psum_scatter(
            qgain_local.astype(jnp.bfloat16), "fsdp", scatter_dimension=0, tiled=True
        ).astype(jnp.float32),
        lax.psum_scatter(
            kgain_local.astype(jnp.bfloat16), "fsdp", scatter_dimension=0, tiled=True
        ).astype(jnp.float32),
        lax.psum_scatter(
            out_grad.astype(jnp.bfloat16), "fsdp", scatter_dimension=0, tiled=True
        ).astype(jnp.float32),
        lax.psum_scatter(
            mlp_local.astype(jnp.bfloat16), "fsdp", scatter_dimension=0, tiled=True
        ).astype(jnp.float32),
        lax.psum_scatter(
            gate_grad.astype(jnp.bfloat16), "fsdp", scatter_dimension=0, tiled=True
        ).astype(jnp.float32),
        lax.psum_scatter(
            up_grad.astype(jnp.bfloat16), "fsdp", scatter_dimension=0, tiled=True
        ).astype(jnp.float32),
        lax.psum_scatter(
            down_grad.astype(jnp.bfloat16), "fsdp", scatter_dimension=0, tiled=True
        ).astype(jnp.float32),
    )
    summed = (
        lax.psum(shares[0].astype(jnp.bfloat16), "ctx").astype(jnp.float32),
        lax.psum(shares[1].astype(jnp.bfloat16), "ctx").astype(jnp.float32),
        lax.psum(shares[2].astype(jnp.bfloat16), "ctx").astype(jnp.float32),
        lax.psum(shares[3].astype(jnp.bfloat16), "ctx").astype(jnp.float32),
        lax.psum(shares[4].astype(jnp.bfloat16), "ctx").astype(jnp.float32),
        lax.psum(shares[5].astype(jnp.bfloat16), "ctx").astype(jnp.float32),
        lax.psum(shares[6].astype(jnp.bfloat16), "ctx").astype(jnp.float32),
        lax.psum(shares[7].astype(jnp.bfloat16), "ctx").astype(jnp.float32),
        lax.psum(shares[8].astype(jnp.bfloat16), "ctx").astype(jnp.float32),
        lax.psum(shares[9].astype(jnp.bfloat16), "ctx").astype(jnp.float32),
        lax.psum(shares[10].astype(jnp.bfloat16), "ctx").astype(jnp.float32),
    )
    return (
        result.reshape(tokens.shape),
        input_grad.reshape(tokens.shape),
        summed[0],
        summed[1],
        summed[2],
        summed[3],
        summed[4],
        summed[5],
        summed[6],
        summed[7],
        summed[8],
        summed[9],
        summed[10],
    )


MESH = pl.DeviceIdType.MESH
BF = jnp.bfloat16
F32 = jnp.float32
LOG2E = math.log2(math.e)
QT = 256
NEG = -1e30
SMALL = 32


def shape(dims, dtype):
    return jax.ShapeDtypeStruct(dims, dtype)


def dot_nn(a, b):
    return jnp.dot(a, b, preferred_element_type=F32)


def dot_nt(a, b):
    return lax.dot_general(a, b, (((1,), (1,)), ((), ())), preferred_element_type=F32)


def dot_tn(a, b):
    return lax.dot_general(a, b, (((0,), (0,)), ((), ())), preferred_element_type=F32)


def device(z, x, y, c):
    return (z * 2 + x, y * 2 + c)


def coords():
    a = lax.axis_index("ctx")
    f = lax.axis_index("fsdp")
    return lax.div(a, 2), lax.rem(a, 2), lax.div(f, 2), lax.rem(f, 2)


class Net:
    def __init__(self, send_sems, recv_sems):
        self.z, self.x, self.y, self.c = z, x, y, c = coords()
        self.depth = lax.axis_size("ctx") // 2
        self.to_x = device(z, 1 - x, y, c)
        self.to_y = device(z, x, 1 - y, c)
        self.to_core = device(z, x, y, 1 - c)
        self.to_x_other = device(z, 1 - x, y, 1 - c)
        self.to_y_other = device(z, x, 1 - y, 1 - c)
        self.up = device(z + 1, x, y, c)
        self.down = device(z - 1, x, y, c)
        self.mate = device(2 * c + y, x, lax.rem(z, 2), lax.div(z, 2))
        self.moves = z != 2 * c + y
        self.mate_chunk = 2 * lax.rem(z, 2) + x
        self.has_up = z < self.depth - 1
        self.has_down = z > 0
        self.send_sems, self.recv_sems = send_sems, recv_sems
        self.used = 0
        self.me = 2 * y + x
        self.sx = 2 * y + 1 - x
        self.sy = 2 * (1 - y) + x
        self.sd = 2 * (1 - y) + 1 - x

    def greet(self, line=True, owners=False, homes=False, mate=False):
        barrier = pltpu.get_barrier_semaphore()

        def signal(to):
            pl.semaphore_signal(barrier, inc=1, device_id=to, device_id_type=MESH)

        for to in (self.to_x, self.to_y, self.to_core):
            signal(to)
        count = 3
        if owners:
            signal(self.to_x_other)
            count = count + 1
        if mate:
            pl.when(self.moves)(lambda: signal(self.mate))
            count = count + self.moves.astype(jnp.int32)
        if homes:
            signal(self.to_y_other)
            count = count + 1
        if line:
            pl.when(self.has_up)(lambda: signal(self.up))
            pl.when(self.has_down)(lambda: signal(self.down))
            count = count + self.has_up.astype(jnp.int32) + self.has_down.astype(jnp.int32)
        pl.semaphore_wait(barrier, count)

    def take(self, count=1):
        first = self.used
        self.used += count
        assert self.used <= self.send_sems.shape[0], self.used
        return first

    def copy(self, sem, src, dst, to):
        return pltpu.make_async_remote_copy(
            src_ref=src,
            dst_ref=dst,
            send_sem=self.send_sems.at[sem],
            recv_sem=self.recv_sems.at[sem],
            device_id=to,
            device_id_type=MESH,
        )

    def new(self, src, dst, to):
        return self.copy(self.take(), src, dst, to)


def rms(values):
    return lax.rsqrt(jnp.mean(values * values, axis=-1, keepdims=True) + epsilon)


class PlaneGather:
    def __init__(self, net, src, out, split=None):
        rows = out.shape[1]
        split = rows // 2 if split is None else split
        self.net = net
        me, sx, sy = net.me, net.sx, net.sy
        self.sides, self.relays = [], []
        for first, size, near, far, s_near in (
            (split, rows - split, net.to_y, net.to_x, sy),
            (0, split, net.to_x, net.to_y, sx),
        ):
            if size:
                at = pl.ds(first, size)
                one = net.new(src.at[at], out.at[me, at], near)
                self.sides.append(one)
                self.relays.append((one, net.new(out.at[s_near, at], out.at[s_near, at], far)))
        self.rest = []
        for first, size, far in ((split, rows - split, net.to_x), (0, split, net.to_y)):
            if size:
                at = pl.ds(first, size)
                self.rest.append(net.new(src.at[at], out.at[me, at], far))

    def start(self):
        for cp in self.sides + self.rest:
            cp.start()

    def forward(self):
        for one, relay in self.relays:
            one.wait_recv()
            relay.start()

    def wait_sides(self):
        for cp in self.rest:
            cp.wait_recv()

    def wait_diagonal(self):
        for _, relay in self.relays:
            relay.wait_recv()

    def drain(self):
        for cp in self.sides + self.rest:
            cp.wait_send()
        for _, relay in self.relays:
            relay.wait_send()


class PlaneSum:
    def __init__(self, net, part, got, mid, split=None):
        rows = part.shape[1]
        split = rows // 2 if split is None else split
        self.net, self.part, self.got, self.mid = net, part, got, mid
        me, sx, sy, sd = net.me, net.sx, net.sy, net.sd
        self.ways = []
        for first, size, near, far, s_near, s_far in (
            (0, split, net.to_x, net.to_y, sx, sy),
            (split, rows - split, net.to_y, net.to_x, sy, sx),
        ):
            if size:
                at = pl.ds(first, size)
                self.ways.append(
                    (
                        at,
                        s_far,
                        net.new(part.at[sd, at], got.at[0, at], near),
                        net.new(part.at[s_near, at], got.at[1, at], near),
                        net.new(mid.at[at], got.at[2, at], far),
                    )
                )

    def start_diagonal(self):
        for _, _, diagonal, _, _ in self.ways:
            diagonal.start()

    def start_sides(self):
        for _, _, _, side, _ in self.ways:
            side.start()

    def forward(self):
        for at, s_far, diagonal, _, relay in self.ways:
            diagonal.wait_recv()
            self.mid[at] = (self.part[s_far, at].astype(F32) + self.got[0, at].astype(F32)).astype(
                BF
            )
            relay.start()

    def finish(self, use):
        for at, _, _, side, relay in self.ways:
            side.wait_recv()
            relay.wait_recv()
            use(
                at,
                self.part[self.net.me, at].astype(F32)
                + self.got[1, at].astype(F32)
                + self.got[2, at].astype(F32),
            )

    def drain(self):
        for _, _, diagonal, side, relay in self.ways:
            diagonal.wait_send()
            side.wait_send()
            relay.wait_send()


class Fetch:
    def __init__(self, net, src, out):
        self.net, self.src = net, src
        whole = len(out.shape) == len(src.shape)
        self.out = out if whole else out.at[net.me]
        self.cp = net.new(src, out if whole else out.at[net.mate_chunk], net.mate)

    def start(self):
        pl.when(self.net.moves)(self.cp.start)

        @pl.when(jnp.logical_not(self.net.moves))
        def _():
            self.out[...] = self.src[...]

    def wait(self):
        pl.when(self.net.moves)(self.cp.wait_recv)

    def drain(self):
        pl.when(self.net.moves)(self.cp.wait_send)


class HomeRoute:
    def __init__(self, net, src, hub, out):
        self.net, self.src, self.hub, self.out = net, src, hub, out
        self.rows = src.shape[0] // 2
        self.chunk = 2 * net.c + net.y
        self.stays = net.z == self.chunk
        self.e_sem = net.take(net.depth * 2)
        self.l_sem = net.take(net.depth * 2)
        self.y_sem = net.take()
        self.core0 = net.c == lax.div(net.z, 2)

    def part(self, s):
        return pl.ds(s * self.rows, self.rows)

    def place(self, s):
        return 2 * self.net.c + (1 - self.net.y if s else self.net.y)

    def entry(self, s):
        return self.net.z == self.place(s)

    def to_entry(self, k, s, to):
        src = self.src.at[self.part(s)]
        return self.net.copy(self.e_sem + 2 * k + s, src, self.hub.at[k, self.part(s)], to)

    def hop(self, k, s, to):
        at = self.hub.at[k, self.part(s)]
        return self.net.copy(self.l_sem + 2 * k + s, at, at, to)

    def swap(self):
        at = self.part(1)
        return self.net.copy(
            self.y_sem, self.hub.at[self.net.z, at], self.out.at[at], self.net.to_y
        )

    def sends(self, s):
        net = self.net
        row = lax.rem(net.z, 2)
        here = net.y == (1 - row if s else row)
        away = jnp.logical_not
        if s:
            go = away(self.stays)
            ways = (
                (jnp.logical_and(here, away(self.core0)), net.to_core),
                (jnp.logical_and(away(here), self.core0), net.to_y),
                (jnp.logical_and(away(here), away(self.core0)), net.to_y_other),
            )
            return [(jnp.logical_and(go, cond), to) for cond, to in ways]
        return [
            (jnp.logical_and(here, away(self.core0)), net.to_core),
            (jnp.logical_and(away(here), self.core0), net.to_y),
            (jnp.logical_and(away(here), away(self.core0)), net.to_y_other),
        ]

    def start(self):
        for s in range(2):
            for cond, to in self.sends(s):
                pl.when(cond)(lambda to=to: self.to_entry(self.chunk, s, to).start())

        @pl.when(self.stays)
        def _():
            self.out[...] = self.src[...]

    def away(self, s, distances=None):
        net = self.net
        for d in range(net.depth - 1, 0, -1) if distances is None else distances:
            for sign, to in ((-1, net.down), (1, net.up)) if d else ():
                k = net.z + sign * d
                yield k, (k >= 0 if sign < 0 else k < net.depth), to

    def enter(self, distances=None):
        net = self.net
        for s in range(2):
            for k, there, to in self.away(s, distances):

                @pl.when(jnp.logical_and(self.entry(s), there))
                def _():
                    if s:

                        @pl.when(k == self.chunk)
                        def _():
                            self.hub[k, self.part(s)] = self.src[self.part(s)]

                        @pl.when(k != self.chunk)
                        def _():
                            self.to_entry(k, s, net.to_core).wait_recv()
                    else:
                        self.to_entry(k, s, net.to_core).wait_recv()
                    self.hop(k, s, to).start()

    def relay(self, distances=None):
        net = self.net
        for s in range(2):
            place = self.place(s)
            for k, there, to in self.away(s, distances):
                side = net.z < place if to is net.down else net.z > place

                @pl.when(jnp.logical_and(side, there))
                def _():
                    self.hop(k, s, to).wait_recv()
                    self.hop(k, s, to).start()

            if distances is not None and 0 not in distances:
                continue

            @pl.when(jnp.logical_not(self.entry(s)))
            def _():
                self.hop(net.z, s, net.up).wait_recv()
                if s:
                    self.swap().start()
                else:
                    self.out[self.part(0)] = self.hub[net.z, self.part(0)]

    def drain(self):
        net = self.net
        for s in range(2):
            place = self.place(s)
            for k, there, to in self.away(s):
                side = net.z <= place if to is net.down else net.z >= place
                pl.when(jnp.logical_and(side, there))(
                    lambda k=k, to=to: self.hop(k, s, to).wait_send()
                )
            for cond, to in self.sends(s):
                pl.when(cond)(lambda to=to: self.to_entry(self.chunk, s, to).wait_send())
        pl.when(jnp.logical_not(self.entry(1)))(lambda: self.swap().wait_send())
        pl.when(jnp.logical_not(self.stays))(lambda: self.swap().wait_recv())


class LineSum:
    def __init__(self, net, tiles, src, mine, slots, deliver):
        self.net, self.tiles, self.src, self.mine = net, tiles, src, mine
        self.slots, self.deliver = slots, deliver
        self.sems = net.take(4 * tiles)
        self.root = net.depth // 2
        self.below = net.z < self.root
        self.above = net.z > self.root
        self.middle = net.z == self.root
        self.two_sided = self.root < net.depth - 1
        self.at_end = jnp.logical_or(net.z == 0, net.z == net.depth - 1)
        self.between = jnp.logical_not(jnp.logical_or(self.middle, self.at_end))

    def hop(self, kind, k):
        net, slots = self.net, self.slots
        src, dst, to = (
            (slots.at[1, k], slots.at[0, k], net.up),
            (slots.at[0, k], slots.at[1, k], net.down),
            (self.mine(k), self.mine(k), net.down),
            (self.mine(k), self.mine(k), net.up),
        )[kind]
        return net.copy(self.sems + kind * self.tiles + k, src, dst, to)

    def gather(self, k):
        net, slots = self.net, self.slots

        def send(kind, has_before):
            @pl.when(has_before)
            def _():
                self.hop(kind, k).wait_recv()
                total = self.src(k)[...].astype(F32) + slots[kind, k].astype(F32)
                slots[1 - kind, k] = total.astype(slots.dtype)

            @pl.when(jnp.logical_not(has_before))
            def _():
                slots[1 - kind, k] = self.src(k)[...]

            self.hop(kind, k).start()

        pl.when(self.below)(lambda: send(0, net.has_down))
        pl.when(self.above)(lambda: send(1, net.has_up))

    def finish(self, k):
        net, slots = self.net, self.slots

        @pl.when(self.middle)
        def _():
            self.hop(0, k).wait_recv()
            total = self.src(k)[...].astype(F32) + slots[0, k].astype(F32)
            if self.two_sided:
                self.hop(1, k).wait_recv()
                total = total + slots[1, k].astype(F32)
            self.mine(k)[...] = total.astype(slots.dtype)
            self.hop(2, k).start()
            if self.two_sided:
                self.hop(3, k).start()

        @pl.when(self.below)
        def _():
            self.hop(2, k).wait_recv()
            pl.when(net.has_down)(lambda: self.hop(2, k).start())

        @pl.when(self.above)
        def _():
            self.hop(3, k).wait_recv()
            pl.when(net.has_up)(lambda: self.hop(3, k).start())

        self.deliver(k)

    def drain(self, k):
        net = self.net
        pl.when(self.below)(lambda: self.hop(0, k).wait_send())
        pl.when(self.above)(lambda: self.hop(1, k).wait_send())
        sends_down = jnp.logical_and(net.has_down, jnp.logical_not(self.above))
        sends_up = jnp.logical_and(net.has_up, jnp.logical_not(self.below))
        pl.when(sends_down)(lambda: self.hop(2, k).wait_send())
        pl.when(sends_up)(lambda: self.hop(3, k).wait_send())


def within(k, first, last):
    return jnp.logical_and(k >= first, k < last)


class Pump:
    def __init__(self, lines, lags=(1, 3, 5, 7), placed=None):
        self.lines = lines
        self.total = sum(line.tiles for line in lines)
        self.gather_lag, self.middle_lag, self.between_lag, self.end_lag = lags
        self.placed = placed

    def each(self, s, run):
        if isinstance(s, int):
            for line in self.lines:
                if 0 <= s < line.tiles:
                    run(line, s)
                s -= line.tiles
            return
        first = 0
        for line in self.lines:
            pl.when(within(s, first, first + line.tiles))(
                lambda line=line, first=first: run(line, s - first)
            )
            first += line.tiles

    def step(self, p, before=None):
        line = self.lines[0]

        @pl.when(line.between)
        def _():
            if before is not None:
                before(p - self.gather_lag)
            self.each(p - self.gather_lag, lambda ln, k: ln.gather(k))
            self.each(p - self.between_lag, lambda ln, k: ln.finish(k))

        @pl.when(line.middle)
        def _():
            if before is not None:
                before(p - self.middle_lag)
            self.each(p - self.middle_lag, lambda ln, k: ln.finish(k))

        @pl.when(line.at_end)
        def _():
            self.each(p - self.end_lag, lambda ln, k: ln.finish(k))

    def steps(self):
        return self.total + max(self.gather_lag, self.middle_lag, self.between_lag, self.end_lag)


def any_spec():
    return pl.BlockSpec(memory_space=pl.ANY)


def vmem_spec():
    return pl.BlockSpec(memory_space=pltpu.VMEM)


def params(cid, mib=60):
    return pltpu.CompilerParams(
        collective_id=cid, has_side_effects=True, vmem_limit_bytes=mib * 2**20
    )


def enter(tok, cot, pos, gains, wq, wk, wv, wg, wu):
    rows = tok.shape[0]
    d_rows = wq.shape[0]
    half = 4 * rows
    unit = wg.shape[1] // 4
    n_sems = 48

    def kernel(
        tok_ref,
        cot_ref,
        pos_in,
        attn_ref,
        mlp_ref,
        query_ref,
        key_ref,
        wq_ref,
        wk_ref,
        wv_ref,
        wg_ref,
        wu_ref,
        x_own,
        n1,
        raw_ref,
        table,
        core,
        wall,
        gains_ref,
        cot_own,
        wgu,
        wq_s,
        wk_s,
        wv_s,
        wg_s,
        wu_s,
        wloc,
        wloc2,
        toks,
        pos_ref,
        gain_ref,
        poss,
        heads,
        gslots,
        ssem,
        rsem,
        lsem,
    ):
        net = Net(ssem, rsem)
        y, c = net.y, net.c
        f = 2 * y + c
        fy = 2 * (1 - y) + c
        loads = [
            pltpu.make_async_copy(a, b, lsem.at[k])
            for k, (a, b) in enumerate(
                ((wq_ref, wq_s), (wk_ref, wk_s), (wv_ref, wv_s), (wg_ref, wg_s), (wu_ref, wu_s))
            )
        ]
        for cp in loads:
            cp.start()
        for h in range(rows // 128):
            pos_ref[8 * h : 8 * h + 1, :] = pos_in[0:1, h * 128 : (h + 1) * 128].astype(F32)
        gain_ref[...] = jnp.zeros_like(gain_ref)
        at = pl.ds(pl.multiple_of(f * d_rows, d_rows), d_rows)
        gain_ref[0:1, at] = attn_ref[...]
        gain_ref[1:2, at] = mlp_ref[...]
        for row, ref in ((2, query_ref), (3, key_ref)):
            n = ref.shape[1]
            wide = jnp.concatenate([ref[...], jnp.zeros((1, HD - n), F32)], axis=-1)
            wide = pltpu.roll(jnp.broadcast_to(wide, (8, HD)), f * n, 1)
            gain_ref[row : row + 1, 0:HD] = wide[0:1]
        net.greet(False, mate=True)
        fetch, pos_fetch = Fetch(net, tok_ref, toks), Fetch(net, pos_ref, poss)
        cot_fetch = Fetch(net, cot_ref, cot_own)
        fetch.start()
        pos_fetch.start()
        g_core = net.new(gain_ref, gslots.at[f], net.to_core)
        g_y = net.new(gain_ref, gslots.at[f], net.to_y)
        g_relay = net.new(gslots.at[fy], gslots.at[fy], net.to_core)
        g_core.start()
        g_y.start()
        gslots[f] = gain_ref[...]
        for cp in loads[:3]:
            cp.wait()
        for t in range(4):
            at = t * 4 * HD
            wloc[t, :, 0 : 4 * HD] = wq_s[:, at : at + 4 * HD].astype(BF)
            at = t * 2 * HD
            wloc[t, :, 4 * HD : 6 * HD] = wk_s[:, at : at + 2 * HD].astype(BF)
            wloc[t, :, 6 * HD : 8 * HD] = wv_s[:, at : at + 2 * HD].astype(BF)
        w_y = net.new(wloc.at[net.sy], wall.at[f], net.to_y)
        w_core = net.new(wloc.at[net.me], wall.at[f], net.to_core)
        w_relay = net.new(wall.at[fy], wall.at[fy], net.to_core)
        w_y.start()
        w_core.start()
        wall[f] = wloc[net.me]
        pos_fetch.wait()
        pos_gather = PlaneGather(net, poss.at[net.me], poss)
        pos_gather.start()
        fetch.wait()
        gather = PlaneGather(net, toks.at[net.me], toks, rows // 4)
        gather.start()
        cot_fetch.start()
        pos_gather.forward()
        for cp in loads[3:]:
            cp.wait()
        for t in range(4):
            at = t * unit
            wloc2[t, :, 0:unit] = wg_s[:, at : at + unit].astype(BF)
            wloc2[t, :, unit : 2 * unit] = wu_s[:, at : at + unit].astype(BF)
        gu_y = net.new(wloc2.at[net.sy], wgu.at[f], net.to_y)
        gu_core = net.new(wloc2.at[net.me], wgu.at[f], net.to_core)
        gu_relay = net.new(wgu.at[fy], wgu.at[fy], net.to_core)
        gu_y.start()
        gu_core.start()
        wgu[f] = wloc2[net.me]
        gather.forward()
        g_y.wait_recv()
        g_relay.start()
        w_y.wait_recv()
        w_relay.start()
        g_core.wait_recv()
        g_relay.wait_recv()
        w_core.wait_recv()
        w_relay.wait_recv()
        index = lax.broadcasted_iota(jnp.int32, (8, HD // 2), 1).astype(F32)
        frequency = jnp.exp(index * (-2.0 * math.log(theta_base) / HD))[0:1]
        full = gslots[0] + gslots[1] + gslots[2] + gslots[3]
        gains_ref[...] = full
        attn_gain, q_gain, k_gain = full[0:1, :], full[2:3, 0:HD], full[3:4, 0:HD]
        pos_gather.wait_sides()
        pos_gather.wait_diagonal()
        x_own[...] = toks[net.me]
        swaps = net.take(4)

        def swap(k):
            at = pl.ds(pl.multiple_of(k * rows, rows), rows)
            return net.copy(swaps + k, heads.at[1 - c, at], core.at[c, at], net.to_core)

        @pl.loop(0, 4)
        def _(n):
            pl.when(n == 1)(gather.wait_sides)
            pl.when(n == 3)(gather.wait_diagonal)
            k = jnp.where(
                n == 0, net.me, jnp.where(n == 1, net.sx, jnp.where(n == 2, net.sy, net.sd))
            )
            at = pl.ds(pl.multiple_of(k * rows, rows), rows)
            flat = toks[k].astype(F32)
            normed = (flat * rms(flat) * attn_gain).astype(BF)
            n1[at, :] = normed
            raw = dot_nn(normed[:, 0:d_rows], wall[0])
            for g in range(1, 4):
                raw = raw + dot_nn(normed[:, g * d_rows : (g + 1) * d_rows], wall[g])
            raw_ref[at, :] = raw[:, 0 : 6 * HD]
            place = jnp.transpose(poss[k])
            angles = jnp.concatenate(
                [place[:, 8 * h : 8 * h + 1] * frequency for h in range(rows // 128)],
                axis=0,
            )
            cosine, sine = jnp.cos(angles), jnp.sin(angles)
            table[at, :] = jnp.concatenate([cosine, sine], axis=-1)
            cosine = jnp.concatenate([cosine, cosine], axis=-1)
            sine = jnp.concatenate([-sine, sine], axis=-1)
            for h in range(6):
                u = raw[:, h * HD : (h + 1) * HD]
                unit = u * rms(u) * (q_gain if h < 4 else k_gain)
                turned = unit * cosine + pltpu.roll(unit, HD // 2, 1) * sine
                g, lane = (h // 2, (h % 2) * HD) if h < 4 else (h - 4, 2 * HD)
                heads[g, at, lane : lane + HD] = turned.astype(BF)
            for g in range(2):
                v = raw[:, (6 + g) * HD : (7 + g) * HD]
                heads[g, at, 3 * HD : 4 * HD] = v.astype(BF)
            swap(k).start()
            core[c, at] = heads[c, at]

        gu_y.wait_recv()
        gu_relay.start()
        for k in range(4):
            swap(k).wait()
        cot_fetch.wait()
        gu_core.wait_recv()
        gu_relay.wait_recv()
        for cp in (g_core, g_y, g_relay, w_core, w_y, w_relay, gu_core, gu_y, gu_relay):
            cp.wait_send()
        for item in (fetch, pos_fetch, cot_fetch, gather, pos_gather):
            item.drain()

    vm = vmem_spec()
    return pl.pallas_call(
        kernel,
        name="enter",
        out_shape=[
            shape((rows, D), BF),
            shape((half, D), BF),
            shape((half, 6 * HD), F32),
            shape((half, HD), F32),
            shape((2, half, 4 * HD), BF),
            shape((4, d_rows, 8 * HD), BF),
            shape((8, D), F32),
            shape((rows, D), BF),
            shape((4, d_rows, 2 * unit), BF),
        ],
        in_specs=[vm] * 7 + [any_spec()] * 5,
        out_specs=[vm] * 9,
        scratch_shapes=[
            pltpu.VMEM(wq.shape, F32),
            pltpu.VMEM(wk.shape, F32),
            pltpu.VMEM(wv.shape, F32),
            pltpu.VMEM(wg.shape, F32),
            pltpu.VMEM(wu.shape, F32),
            pltpu.VMEM((4, d_rows, 8 * HD), BF),
            pltpu.VMEM((4, d_rows, 2 * unit), BF),
            pltpu.VMEM((4, rows, D), BF),
            pltpu.VMEM((16, 128), F32),
            pltpu.VMEM((8, D), F32),
            pltpu.VMEM((4, 16, 128), F32),
            pltpu.VMEM((2, half, 4 * HD), BF),
            pltpu.VMEM((4, 8, D), F32),
            pltpu.SemaphoreType.DMA((n_sems,)),
            pltpu.SemaphoreType.DMA((n_sems,)),
            pltpu.SemaphoreType.DMA((5,)),
        ],
        compiler_params=params(0),
        cost_estimate=pl.CostEstimate(
            flops=2 * half * D * 8 * HD, bytes_accessed=16 * 2**20, transcendentals=0
        ),
    )(tok, cot, pos, *gains, wq, wk, wv, wg, wu)


def attend(block_map, inverse, core, cot, wo, wd):
    half = core.shape[1]
    length = 2 * half
    tiles = length // QT
    blocks = QT // BLK
    n_blocks = length // BLK
    factor = HD ** (-0.5) * LOG2E
    n_sems = 16
    rows = cot.shape[0]

    def kernel(
        bm,
        inv,
        x_ref,
        cot_ref,
        wo_ref,
        wd_ref,
        att,
        mixed,
        lse_ref,
        cots,
        wo_out,
        wd_out,
        q_s,
        k_s,
        v_s,
        o_s,
        wo_s,
        wd_s,
        ssem,
        rsem,
        lsem,
    ):
        net = Net(ssem, rsem)
        x, c = net.x, net.c
        loads = [
            pltpu.make_async_copy(a, b, lsem.at[k])
            for k, (a, b) in enumerate(((wo_ref, wo_s), (wd_ref, wd_s)))
        ]
        for cp in loads:
            cp.start()
        net.greet(False)
        gather = PlaneGather(net, cot_ref, cots)
        gather.start()
        o_core = net.new(wo_out, wo_out, net.to_core)
        d_core = net.new(wd_out, wd_out, net.to_core)
        own = c == x

        @pl.loop(0, tiles)
        def _(i):
            for h in range(blocks):
                block = x_ref[inv[i * blocks + h]]
                at = pl.multiple_of(i * QT, QT) + h * BLK
                q_s[i, pl.ds(h * BLK, BLK), :] = block[:, 0:HD]
                q_s[i, pl.ds(QT + h * BLK, BLK), :] = block[:, HD : 2 * HD]
                k_s[pl.ds(at, BLK), :] = block[:, 2 * HD : 3 * HD]
                v_s[pl.ds(at, BLK), 0:HD] = block[:, 3 * HD : 4 * HD]

        v_s[:, HD : 2 * HD] = jnp.ones((length, HD), BF)
        for cp in loads:
            cp.wait()

        @pl.when(own)
        def _():
            wo_out[...] = wo_s[...].astype(BF)
            wd_out[...] = wd_s[...].astype(BF)
            o_core.start()
            d_core.start()

        q_row = lax.broadcasted_iota(jnp.int32, (2 * QT, QT), 0)
        k_row = lax.broadcasted_iota(jnp.int32, (2 * QT, QT), 1)
        allowed = jnp.where(q_row >= QT, q_row - QT, q_row) >= k_row

        def tile(i):
            q = q_s[i]
            acc = None
            for j in range(i + 1):
                at = slice(j * QT, (j + 1) * QT)
                scores = dot_nt(q, k_s[at, :]) * factor
                if j == i:
                    scores = jnp.where(allowed, scores, NEG)
                add = dot_nn(jnp.exp2(scores).astype(BF), v_s[at, :])
                acc = add if acc is None else acc + add
            total = acc[:, HD:]
            out = acc[:, :HD] / total
            lse_ref[i] = jnp.log2(jnp.transpose(total)[0:8, :])
            for h in range(blocks):
                for u in range(2):
                    o_s[i * blocks + h, :, u * HD : (u + 1) * HD] = out[
                        u * QT + h * BLK : u * QT + (h + 1) * BLK
                    ].astype(BF)

        for i in range(tiles):
            tile(i)
            if i == tiles - 2:
                gather.forward()

        cots[net.me] = cot_ref[...]
        swap = net.take(1)

        @pl.loop(0, n_blocks)
        def _(s):
            mixed[pl.ds(pl.multiple_of(s * BLK, BLK), BLK), :] = o_s[bm[s]]

        away = mixed.at[pl.ds(pl.multiple_of((1 - c) * half, half), half)]
        o_swap = net.copy(swap, away, att.at[c], net.to_core)
        o_swap.start()
        att[c] = mixed[pl.ds(pl.multiple_of(c * half, half), half), :]
        pl.when(jnp.logical_not(own))(lambda: o_core.wait_recv())
        pl.when(jnp.logical_not(own))(lambda: d_core.wait_recv())
        gather.wait_sides()
        gather.wait_diagonal()
        o_swap.wait()
        gather.drain()
        pl.when(own)(lambda: o_core.wait_send())
        pl.when(own)(lambda: d_core.wait_send())

    vm = vmem_spec()
    smem = pl.BlockSpec(memory_space=pltpu.SMEM)
    return pl.pallas_call(
        kernel,
        name="attend",
        out_shape=[
            shape((2, half, 2 * HD), BF),
            shape((length, 2 * HD), BF),
            shape((tiles, 8, 2 * QT), F32),
            shape((4, rows, D), BF),
            shape(wo.shape, BF),
            shape(wd.shape, BF),
        ],
        in_specs=[smem, smem, vm, vm] + [any_spec()] * 2,
        out_specs=[vm] * 6,
        scratch_shapes=[
            pltpu.VMEM((tiles, 2 * QT, HD), BF),
            pltpu.VMEM((length, HD), BF),
            pltpu.VMEM((length, 2 * HD), BF),
            pltpu.VMEM((n_blocks, BLK, 2 * HD), BF),
            pltpu.VMEM(wo.shape, F32),
            pltpu.VMEM(wd.shape, F32),
            pltpu.SemaphoreType.DMA((n_sems,)),
            pltpu.SemaphoreType.DMA((n_sems,)),
            pltpu.SemaphoreType.DMA((2,)),
        ],
        compiler_params=params(1),
        cost_estimate=pl.CostEstimate(
            flops=2 * 2 * 2 * length * length * HD, bytes_accessed=16 * 2**20, transcendentals=0
        ),
    )(block_map, inverse, core.reshape(n_blocks, BLK, 4 * HD), cot, wo, wd)


def feed_forward(att, x_own, wo, wgu, wd, cots, cot_own, gains):
    half = att.shape[1]
    rows = half // 4
    unit = wd.shape[0]
    d_rows = wgu.shape[1]
    d_tiles = unit // 2 // SMALL
    n_sems = 48 + 4 * d_tiles

    def kernel(
        att_ref,
        x_ref,
        wo_ref,
        wgu_ref,
        wd_ref,
        dy_ref,
        cot_ref,
        gain_ref,
        core,
        middle,
        dmiddle,
        result_part,
        sum_gu,
        sum_o,
        total_d,
        mlp_gain_part,
        part,
        got,
        mid,
        n2,
        hid,
        dgu,
        got2,
        mid2,
        dmb,
        gm,
        w_gu,
        got_gu,
        w_d,
        got_d,
        w_o,
        got_o,
        sum_d,
        d_slots,
        ssem,
        rsem,
    ):
        net = Net(ssem, rsem)
        c, me, sx, sy, sd = net.c, net.me, net.sx, net.sy, net.sd
        mlp_gain = gain_ref[1:2, :]
        net.greet()
        out_sum = PlaneSum(net, part, got, mid)

        def chunk(k):
            return pl.ds(pl.multiple_of(k * rows, rows), rows)

        def project(k):
            part[k] = (
                dot_nn(att_ref[0, chunk(k)], wo_ref[0 : 2 * HD, :])
                + dot_nn(att_ref[1, chunk(k)], wo_ref[2 * HD : 4 * HD, :])
            ).astype(BF)

        project(sd)
        out_sum.start_diagonal()
        project(sx)
        project(sy)
        out_sum.start_sides()
        project(me)
        out_sum.forward()

        def add_residual(at, total):
            value = x_ref[at].astype(F32) + total
            middle[at] = value
            n2[me, at] = (value * rms(value) * mlp_gain).astype(BF)

        out_sum.finish(add_residual)
        gather = PlaneGather(net, n2.at[me], n2)
        gather.start()

        def forward_back(k):
            rows_k = n2[k]
            gate_up = dot_nn(rows_k[:, 0:d_rows], wgu_ref[0])
            for g in range(1, 4):
                gate_up = gate_up + dot_nn(rows_k[:, g * d_rows : (g + 1) * d_rows], wgu_ref[g])
            gate, upward = gate_up[:, 0:unit], gate_up[:, unit : 2 * unit]
            sigmoid = 1.0 / (1.0 + jnp.exp(-gate))
            silu = gate * sigmoid
            hid[k] = (silu * upward).astype(BF)
            dh = dot_nt(dy_ref[k], wd_ref[...])
            dgu[k, :, 0:unit] = (
                dh * upward * sigmoid * (1.0 + gate * (1.0 - sigmoid))
            ).astype(BF)
            dgu[k, :, unit : 2 * unit] = (dh * silu).astype(BF)
            grads = dgu[k]
            for g in range(4):
                part[k, :, g * d_rows : (g + 1) * d_rows] = dot_nt(grads, wgu_ref[g]).astype(BF)

        out_sum.drain()
        forward_back(me)
        gather.forward()
        gather.wait_sides()
        back_sum = PlaneSum(net, part, got2, mid2)

        @pl.loop(0, 2)
        def _(n):
            forward_back(jnp.where(n == 0, sx, sy))

        back_sum.start_sides()
        gather.wait_diagonal()
        forward_back(sd)
        back_sum.start_diagonal()

        gu_sem = net.take(2)
        d_sem = net.take(1)
        o_sem = net.take(1)

        def gu_copy(n):
            return net.copy(gu_sem + n, w_gu.at[n], got_gu.at[n], net.to_core)

        d_copy = net.copy(d_sem, w_d, got_d, net.to_core)
        o_copy = net.copy(o_sem, w_o, got_o, net.to_core)
        all_dgu = dgu.shape[2]
        unit_half = unit // 2

        def down(core_of):
            at = pl.ds(pl.multiple_of(core_of * unit_half, unit_half), unit_half)
            return dot_tn(hid[:, :, at].reshape(half, unit_half), dy_ref[...].reshape(half, D))

        line = LineSum(
            net,
            d_tiles,
            lambda k: sum_d.at[pl.ds(pl.multiple_of(k * SMALL, SMALL), SMALL)],
            lambda k: total_d.at[pl.ds(pl.multiple_of(k * SMALL, SMALL), SMALL)],
            d_slots,
            lambda k: None,
        )
        pump = Pump([line], (0, 2, 5, 7))

        w_d[...] = down(1 - c).astype(BF)
        d_copy.start()
        value = down(c)
        d_copy.wait_recv()
        sum_d[...] = (value + got_d[...].astype(F32)).astype(BF)

        @pl.when(line.at_end)
        def _():
            @pl.loop(0, d_tiles)
            def _(k):
                line.gather(k)

        @pl.loop(0, 4)
        def _(k):
            result_part[k] = dot_nn(hid[k], wd_ref[...]).astype(BF)

        back_sum.forward()
        pump.step(0)

        def slab(n, core_of):
            f = 2 * n + core_of
            at = pl.ds(pl.multiple_of(f * d_rows, d_rows), d_rows)
            return dot_tn(n2[:, :, at].reshape(half, d_rows), dgu[...].reshape(half, all_dgu))

        for n in range(2):
            w_gu[n] = slab(n, 1 - c).astype(BF)
            gu_copy(n).start()
            pump.step(1 + n)

        def back_through_norm(at, dn2):
            value = middle[at]
            scale = rms(value)
            w2 = dn2 * mlp_gain
            grad = cot_ref[at].astype(F32) + norm_back(w2, value, scale)
            dmiddle[at] = grad
            dmb[me, at] = grad.astype(BF)
            first = dn2.shape[0] // 8
            folded = jnp.sum((dn2 * value * scale).reshape(first, 8, D), axis=0)
            mlp_gain_part[...] += folded

        mlp_gain_part[...] = jnp.zeros_like(mlp_gain_part)
        back_sum.finish(back_through_norm)
        gather2 = PlaneGather(net, dmb.at[me], dmb)
        gather2.start()
        swap_sem = net.take(4)

        def swap(k):
            return net.copy(
                swap_sem + k, gm.at[1 - c, chunk(k)], core.at[c, chunk(k)], net.to_core
            )

        def grad_mixed(k):
            value = dot_nt(dmb[k], wo_ref[...]).astype(BF)
            gm[0, chunk(k)] = value[:, 0 : 2 * HD]
            gm[1, chunk(k)] = value[:, 2 * HD : 4 * HD]
            swap(k).start()
            core[c, chunk(k)] = gm[c, chunk(k)]

        pump.step(3)
        pump.step(4)
        grad_mixed(me)
        pump.step(5)
        for n in range(2):
            value = slab(n, c)
            gu_copy(n).wait_recv()
            sum_gu[n] = (value + got_gu[n].astype(F32)).astype(BF)
            pump.step(6 + n)

        gather2.forward()
        for n in range(8, 11):
            pump.step(n)
        gather2.wait_sides()

        @pl.loop(0, 2)
        def _(n):
            grad_mixed(jnp.where(n == 0, sx, sy))

        for n in range(11, 14):
            pump.step(n)
        gather2.wait_diagonal()
        grad_mixed(sd)

        def out_grad(g):
            return dot_tn(att_ref[g], dmb[...].reshape(half, D))

        w_o[...] = out_grad(1 - c).astype(BF)
        o_copy.start()
        value = out_grad(c)
        o_copy.wait_recv()
        sum_o[...] = (value + got_o[...].astype(F32)).astype(BF)
        @pl.loop(14, pump.steps())
        def _(p):
            pump.step(p)

        @pl.loop(0, d_tiles)
        def _(k):
            line.drain(k)

        for k in range(4):
            swap(k).wait()
        for n in range(2):
            gu_copy(n).wait_send()
        d_copy.wait_send()
        o_copy.wait_send()
        gather.drain()
        gather2.drain()
        back_sum.drain()

    vm = vmem_spec()
    return pl.pallas_call(
        kernel,
        name="feed_forward",
        out_shape=[
            shape((2, half, 2 * HD), BF),
            shape((rows, D), F32),
            shape((rows, D), F32),
            shape((4, rows, D), BF),
            shape((2, d_rows, 2 * unit), BF),
            shape((2 * HD, D), BF),
            shape((unit // 2, D), BF),
            shape((8, D), F32),
        ],
        in_specs=[vm] * 8,
        out_specs=[vm] * 8,
        scratch_shapes=[
            pltpu.VMEM((4, rows, D), BF),
            pltpu.VMEM((3, rows, D), BF),
            pltpu.VMEM((rows, D), BF),
            pltpu.VMEM((4, rows, D), BF),
            pltpu.VMEM((4, rows, unit), BF),
            pltpu.VMEM((4, rows, 2 * unit), BF),
            pltpu.VMEM((3, rows, D), BF),
            pltpu.VMEM((rows, D), BF),
            pltpu.VMEM((4, rows, D), BF),
            pltpu.VMEM((2, half, 2 * HD), BF),
            pltpu.VMEM((2, d_rows, 2 * unit), BF),
            pltpu.VMEM((2, d_rows, 2 * unit), BF),
            pltpu.VMEM((unit // 2, D), BF),
            pltpu.VMEM((unit // 2, D), BF),
            pltpu.VMEM((2 * HD, D), BF),
            pltpu.VMEM((2 * HD, D), BF),
            pltpu.VMEM((unit // 2, D), BF),
            pltpu.VMEM((2, d_tiles, SMALL, D), BF),
            pltpu.SemaphoreType.DMA((n_sems,)),
            pltpu.SemaphoreType.DMA((n_sems,)),
        ],
        compiler_params=params(2, 62),
        cost_estimate=pl.CostEstimate(
            flops=24 * half * D * unit, bytes_accessed=32 * 2**20, transcendentals=0
        ),
    )(att, x_own, wo, wgu, wd, cots, cot_own, gains)


def finish_back(
    block_map,
    inverse,
    core,
    mixed,
    grad,
    lse,
    sum_o,
    total_d,
    sum_gu,
    result_part,
    middle,
    raw,
    table,
    n1,
    wall,
    x_own,
    dmiddle,
    gains,
    mlp_gain_part,
):
    half = core.shape[1]
    length = 2 * half
    blocks = QT // BLK
    n_blocks = length // BLK
    wide = 2 * QT
    tiles = length // wide
    scale = HD ** (-0.5)
    factor = scale * LOG2E
    rows = middle.shape[0]
    d_rows = wall.shape[1]
    gu_cols = sum_gu.shape[2]
    unit = gu_cols // 2
    o_tiles = sum_o.shape[0] // SMALL
    per = d_rows // SMALL
    w_tiles = 2 * per
    n_sems = 7 * o_tiles + 10 * w_tiles + 90

    def kernel(
        bm,
        inv,
        core_hbm,
        mixed_hbm,
        grad_hbm,
        lse_ref,
        o_part,
        d_ref,
        gu_ref,
        rp_hbm,
        mid_hbm,
        raw_hbm,
        table_hbm,
        n1_hbm,
        wall_hbm,
        x_hbm,
        dmid_hbm,
        gain_ref,
        mlp_ref,
        result,
        input_out,
        o_final,
        d_final,
        out_q,
        out_k,
        out_v,
        out_g,
        out_u,
        gain_out,
        dq,
        d_s,
        result_part_s,
        part,
        res,
        hub,
        got,
        mid,
        grad_in,
        hub2,
        got2,
        mid2,
        o_slots,
        o_sum,
        gu_rows,
        gu_slots,
        gu_mine,
        gu_other,
        w_out,
        w_got,
        w_sum,
        w_rows,
        w_slots,
        w_mine,
        w_other,
        g_sum,
        g_got,
        g_slots,
        g_mine,
        acc,
        ssem,
        rsem,
        lsem,
    ):
        net = Net(ssem, rsem)
        z, x, y, c = net.z, net.x, net.y, net.c
        load_part = pltpu.make_async_copy(rp_hbm, result_part_s, lsem.at[0])
        load_part.start()
        net.greet(True, True, True)
        total = PlaneSum(net, result_part_s, got, mid, rows // 4)
        total2 = PlaneSum(net, part, got2, mid2, rows // 4)
        gu_y = net.new(gu_ref.at[1 - y], gu_rows.at[1], net.to_y)
        home = HomeRoute(net, res, hub, result)
        home2 = HomeRoute(net, grad_in, hub2, input_out)
        swap = net.new(
            d_s.at[pl.ds(pl.multiple_of((1 - c) * half, half), half)], dq.at[c], net.to_core
        )
        x_sem = net.take(2 * o_tiles)
        chip_sem = net.take(o_tiles)
        owner = device(z, 1 - x, y, x)
        owns = c == x

        def cross(k, h):
            return net.copy(x_sem + h * o_tiles + k, o_sum.at[k], o_final.at[h, k], owner)

        def chip(k, h):
            return net.copy(chip_sem + k, o_sum.at[k], o_final.at[h, k], net.to_core)

        def deliver(k):
            cross(k, c).start()

            @pl.when(owns)
            def _():
                o_final[c, k] = o_sum[k]

            pl.when(jnp.logical_not(owns))(lambda: chip(k, c).start())

        d_x = [net.new(d_ref, d_final.at[h], owner) for h in range(2)]
        d_chip = net.new(d_ref, d_final.at[c], net.to_core)
        gx_sem = net.take(w_tiles)
        wx_sem = net.take(w_tiles)

        def gu_cross(k):
            return net.copy(gx_sem + k, gu_mine.at[k], gu_other.at[k], net.to_x)

        def w_cross(k):
            return net.copy(wx_sem + k, w_mine.at[k], w_other.at[k], net.to_x)

        def row_tile(ref):
            def at(k):
                first = pl.multiple_of(lax.rem(k, per) * SMALL, SMALL)
                return ref.at[lax.div(k, per), pl.ds(first, SMALL)]

            return at

        o_line = LineSum(
            net,
            o_tiles,
            lambda k: o_part.at[pl.ds(pl.multiple_of(k * SMALL, SMALL), SMALL)],
            lambda k: o_sum.at[k],
            o_slots,
            deliver,
        )
        gu_line = LineSum(
            net,
            w_tiles,
            row_tile(gu_rows),
            lambda k: gu_mine.at[k],
            gu_slots,
            lambda k: gu_cross(k).start(),
        )
        w_line = LineSum(
            net,
            w_tiles,
            row_tile(w_rows),
            lambda k: w_mine.at[k],
            w_slots,
            lambda k: w_cross(k).start(),
        )
        g_line = LineSum(
            net, 1, lambda k: g_sum.at[0], lambda k: g_mine.at[0], g_slots, lambda k: None
        )
        pump = Pump([o_line, gu_line, w_line], (1, 3, 5, 7))
        gu_first, w_first = o_tiles, o_tiles + w_tiles

        def rows_come(s):
            if isinstance(s, int):
                if s == gu_first + per:
                    gu_y.wait_recv()
                if s == w_first + per:
                    w_y.wait_recv()
            else:
                pl.when(s == gu_first + per)(gu_y.wait_recv)
                pl.when(s == w_first + per)(w_y.wait_recv)

        w_y = net.new(w_sum, w_rows.at[1], net.to_y)
        state = [0]

        def pump_on(count=1):
            for _ in range(count):
                pump.step(state[0], rows_come)
                state[0] += 1

        def ends(line, first, last):
            @pl.when(line.at_end)
            def _():
                @pl.loop(first, last)
                def _(k):
                    line.gather(k)

        gu_y.start()
        ends(o_line, 0, o_tiles)
        load_part.wait()
        total.start_diagonal()
        total.start_sides()
        gu_rows[0] = gu_ref[y]
        ends(gu_line, 0, per)
        for h in range(2):
            pl.when(c == h)(d_x[h].start)
        pl.when(jnp.logical_not(owns))(d_chip.start)

        d_keep = pltpu.make_async_copy(d_ref, d_final.at[c], lsem.at[11])
        pl.when(owns)(d_keep.start)
        def attention(x_s, o_s, g_in, q_s, g_s, k_s, v_s, delta_s):
            loads = [
                pltpu.make_async_copy(a, b, lsem.at[1 + n])
                for n, (a, b) in enumerate(((core_hbm, x_s), (mixed_hbm, o_s), (grad_hbm, g_in)))
            ]
            for cp in loads:
                cp.start()
            for cp in loads:
                cp.wait()
            for i in range(2 * tiles):
                for h in range(blocks):
                    s = inv[i * blocks + h]
                    block, out, grad_ = x_s[s], o_s[s], g_in[s]
                    at = slice((i * blocks + h) * BLK, (i * blocks + h + 1) * BLK)
                    for u in range(2):
                        first = (i % 2) * 2 * QT + u * QT + h * BLK
                        to = slice(first, first + BLK)
                        lanes = slice(u * HD, (u + 1) * HD)
                        q_s[i // 2, to, :] = block[:, lanes]
                        g_s[i // 2, to, :] = grad_[:, lanes]
                        product = grad_[:, lanes].astype(F32) * out[:, lanes].astype(F32)
                        delta_s[i // 2, :, to] = jnp.broadcast_to(
                            jnp.sum(jnp.transpose(product), axis=0, keepdims=True), (8, BLK)
                        )
                    k_s[at, :] = block[:, 2 * HD : 3 * HD]
                    v_s[at, :] = block[:, 3 * HD : 4 * HD]
                if i % 3 == 1:
                    pump_on()

            k_row = lax.broadcasted_iota(jnp.int32, (wide, 2 * wide), 0)
            q_row = lax.broadcasted_iota(jnp.int32, (wide, 2 * wide), 1)
            q_row = lax.shift_right_logical(q_row, 9) * QT + lax.bitwise_and(q_row, QT - 1)
            allowed = q_row >= k_row
            dq_t = [None] * tiles
            for j in range(tiles):
                at = slice(j * wide, (j + 1) * wide)
                k, v = k_s[at, :], v_s[at, :]
                k_t = jnp.transpose(k)
                dk = dv = None
                for i in range(j, tiles):
                    q, g = q_s[i], g_s[i]
                    shift = jnp.concatenate(
                        [lse_ref[2 * i, 0:1, :], lse_ref[2 * i + 1, 0:1, :]], 1
                    )
                    scores = dot_nt(k, q) * factor - shift
                    if i == j:
                        scores = jnp.where(allowed, scores, NEG)
                    p = jnp.exp2(scores)
                    ds = (p * (dot_nt(v, g) - delta_s[i, 0:1, :])).astype(BF)
                    add = dot_nn(k_t, ds)
                    dq_t[i] = add if dq_t[i] is None else dq_t[i] + add
                    add_k, add_v = dot_nn(ds, q), dot_nn(p.astype(BF), g)
                    dk = add_k if dk is None else dk + add_k
                    dv = add_v if dv is None else dv + add_v
                    pump_on()
                for h in range(wide // BLK):
                    part_ = slice(h * BLK, (h + 1) * BLK)
                    b = j * (wide // BLK) + h
                    x_s[b, :, 2 * HD : 3 * HD] = (dk[part_] * scale).astype(BF)
                    x_s[b, :, 3 * HD : 4 * HD] = dv[part_].astype(BF)
                dq_j = jnp.transpose(dq_t[j]) * scale
                for e in range(2):
                    for u in range(2):
                        for h in range(blocks):
                            first = e * 2 * QT + u * QT + h * BLK
                            x_s[(2 * j + e) * blocks + h, :, u * HD : (u + 1) * HD] = dq_j[
                                first : first + BLK
                            ].astype(BF)

            @pl.loop(0, n_blocks)
            def _(s):
                d_s[pl.ds(pl.multiple_of(s * BLK, BLK), BLK), :] = x_s[bm[s]]

        pl.run_scoped(
            attention,
            pltpu.VMEM((n_blocks, BLK, 4 * HD), BF),
            pltpu.VMEM((n_blocks, BLK, 2 * HD), BF),
            pltpu.VMEM((n_blocks, BLK, 2 * HD), BF),
            pltpu.VMEM((tiles, 2 * wide, HD), BF),
            pltpu.VMEM((tiles, 2 * wide, HD), BF),
            pltpu.VMEM((length, HD), BF),
            pltpu.VMEM((length, HD), BF),
            pltpu.VMEM((tiles, 8, 2 * wide), F32),
        )
        swap.start()
        dq[c] = d_s[pl.ds(pl.multiple_of(c * half, half), half), :]

        @pl.when(gu_line.at_end)
        def _():
            gu_y.wait_recv()

        ends(gu_line, per, w_tiles)
        pump_on()

        def norms(raw_ref, table_ref, n1_ref, wall_ref, x_ref, dmid_ref, mid_ref, dcat):
            loads = [
                pltpu.make_async_copy(a, b, lsem.at[4 + n])
                for n, (a, b) in enumerate(
                    (
                        (raw_hbm, raw_ref),
                        (table_hbm, table_ref),
                        (n1_hbm, n1_ref),
                        (wall_hbm, wall_ref),
                        (x_hbm, x_ref),
                        (dmid_hbm, dmid_ref),
                        (mid_hbm, mid_ref),
                    )
                )
            ]
            for cp in loads:
                cp.start()
            swap.wait_recv()
            for cp in loads:
                cp.wait()
            attn_gain, q_gain, k_gain = gain_ref[0:1, :], gain_ref[2:3, 0:HD], gain_ref[3:4, 0:HD]
            acc[...] = jnp.zeros_like(acc)

            def fold(v):
                return jnp.sum(v.reshape(v.shape[0] // 8, 8, v.shape[1]), axis=0)

            def chunk(k):
                at = pl.ds(pl.multiple_of(k * rows, rows), rows)
                half_w = HD // 2
                cosine, sine = table_ref[at, 0:half_w], table_ref[at, half_w:HD]
                cosine = jnp.concatenate([cosine, cosine], axis=-1)
                sine = jnp.concatenate([-sine, sine], axis=-1)
                for h in range(6):
                    g, lane = (h // 2, (h % 2) * HD) if h < 4 else (h - 4, 2 * HD)
                    gain = q_gain if h < 4 else k_gain
                    grad_ = dq[g, at, lane : lane + HD].astype(F32)
                    du = grad_ * cosine - pltpu.roll(grad_, half_w, 1) * sine
                    u = raw_ref[at, h * HD : (h + 1) * HD]
                    size = rms(u)
                    lanes = slice(0, HD) if h < 4 else slice(HD, 2 * HD)
                    acc[2, :, lanes] += fold(du * u * size)
                    dcat[at, h * HD : (h + 1) * HD] = norm_back(du * gain, u, size).astype(BF)
                for g in range(2):
                    dcat[at, (6 + g) * HD : (7 + g) * HD] = dq[g, at, 3 * HD : 4 * HD]

            def project(k):
                d = dcat[pl.ds(pl.multiple_of(k * rows, rows), rows), :]
                for g in range(4):
                    part[k, :, g * d_rows : (g + 1) * d_rows] = dot_nt(d, wall_ref[g]).astype(BF)

            def add(at, value):
                res[at] = (mid_ref[at] + value).astype(BF)

            chunk(net.sd)
            pump_on()
            project(net.sd)
            total2.start_diagonal()
            pump_on()
            total.forward()
            for k in (net.sx, net.sy):
                chunk(k)
                pump_on()
                project(k)
                pump_on()
            total2.start_sides()
            chunk(net.me)
            pump_on()
            project(net.me)
            total2.forward()
            pump_on()

            def slab(n, core_of):
                f = 2 * n + core_of
                at = pl.ds(pl.multiple_of(f * d_rows, d_rows), d_rows)
                return dot_tn(n1_ref[:, at], dcat[...])

            w_sem = net.take(2)

            def w_copy(n):
                return net.copy(w_sem + n, w_out.at[n], w_got.at[n], net.to_core)

            for n in range(2):
                w_out[n] = slab(n, 1 - c).astype(BF)
                w_copy(n).start()
                pump_on()
            total.finish(add)
            home.start()
            value = slab(1 - y, c)
            w_copy(1 - y).wait_recv()
            w_sum[...] = (value + w_got[1 - y].astype(F32)).astype(BF)
            w_y.start()
            pump_on()
            value = slab(y, c)
            w_copy(y).wait_recv()
            w_rows[0] = (value + w_got[y].astype(F32)).astype(BF)
            ends(w_line, 0, per)
            pump_on()

            def back_through_norm(at, dn1):
                value = x_ref[at].astype(F32)
                size = rms(value)
                acc[0] += fold(dn1 * value * size)
                grad_in[at] = (dmid_ref[at] + norm_back(dn1 * attn_gain, value, size)).astype(BF)

            total2.finish(back_through_norm)
            for n in range(2):
                w_copy(n).wait_send()

        pl.run_scoped(
            norms,
            pltpu.VMEM(raw.shape, F32),
            pltpu.VMEM(table.shape, F32),
            pltpu.VMEM(n1.shape, BF),
            pltpu.VMEM(wall.shape, BF),
            pltpu.VMEM((rows, D), BF),
            pltpu.VMEM((rows, D), F32),
            pltpu.VMEM((rows, D), F32),
            pltpu.VMEM((half, 8 * HD), BF),
        )
        home2.start()
        pump_on()

        def place(k, slots, copies, outs, widths):
            copies(k).wait_recv()
            row_half = jnp.where(k < per, y, 1 - y)
            at = pl.ds(pl.multiple_of(lax.rem(k, per) * SMALL, SMALL), SMALL)
            for tile, x_of in zip(slots, (x, 1 - x)):
                quarter = 2 * row_half + x_of
                first = 0
                for out, width in zip(outs, widths):
                    lanes = pl.ds(pl.multiple_of(quarter * width, width), width)
                    out[at, lanes] = tile[k, :, first : first + width]
                    first += width

        def place_gu(k):
            place(k, (gu_mine, gu_other), gu_cross, (out_g, out_u), (unit, unit))

        def place_w(k):
            place(k, (w_mine, w_other), w_cross, (out_q, out_k, out_v), (4 * HD, 2 * HD, 2 * HD))

        acc[1] = mlp_ref[...]
        for row in range(3):
            g_sum[0, row : row + 1, :] = jnp.sum(acc[row], axis=0, keepdims=True)
        g_sum[0, 3:8, :] = jnp.zeros((5, D), F32)
        for n, to in enumerate((net.to_core, net.to_y, net.to_x)):
            cp = net.new(g_sum.at[0], g_got.at[n], to)
            cp.start()
            pump_on()
            cp.wait()
            g_sum[0] = g_sum[0] + g_got[n]
        g_line.gather(0)

        @pl.when(w_line.at_end)
        def _():
            w_y.wait_recv()

        ends(w_line, per, w_tiles)
        home.enter()
        pump_on()
        home2.enter()
        pump_on()
        so_far = state[0]
        place_lag = 14

        @pl.loop(0, so_far - place_lag - gu_first)
        def _(k):
            place_gu(k)

        @pl.loop(so_far, pump.steps())
        def _(p):
            pump.step(p, rows_come)
            for n, distance in enumerate((3, 2, 1, 0)):

                @pl.when(p == so_far + 1 + 2 * n)
                def _():
                    home.relay([distance])
                    home2.relay([distance])

            q = p - place_lag
            pl.when(within(q, gu_first, w_first))(lambda: place_gu(q - gu_first))
            pl.when(within(q, w_first, w_first + w_tiles))(lambda: place_w(q - w_first))

        g_line.finish(0)
        gain_out[...] = g_mine[0]

        @pl.loop(pump.steps() - place_lag - w_first, w_tiles)
        def _(k):
            place_w(k)

        @pl.loop(0, o_tiles)
        def _(k):
            @pl.when(owns)
            def _():
                chip(k, 1 - c).wait_recv()

            @pl.when(jnp.logical_not(owns))
            def _():
                for h in range(2):
                    cross(k, h).wait_recv()
                chip(k, c).wait_send()

            cross(k, c).wait_send()
            o_line.drain(k)

        @pl.when(owns)
        def _():
            d_chip.wait_recv()
            d_keep.wait()

        @pl.when(jnp.logical_not(owns))
        def _():
            for h in range(2):
                d_x[h].wait_recv()
            d_chip.wait_send()

        for h in range(2):
            pl.when(c == h)(d_x[h].wait_send)

        @pl.loop(0, w_tiles)
        def _(k):
            gu_line.drain(k)
            w_line.drain(k)
            gu_cross(k).wait_send()
            w_cross(k).wait_send()

        g_line.drain(0)
        gu_y.wait_send()
        w_y.wait_send()
        swap.wait_send()
        total.drain()
        total2.drain()
        home.drain()
        home2.drain()

    vm = vmem_spec()
    hbm = any_spec()
    smem = pl.BlockSpec(memory_space=pltpu.SMEM)
    chunk_ = pltpu.VMEM((rows, D), BF)
    four = pltpu.VMEM((4, rows, D), BF)
    three = pltpu.VMEM((3, rows, D), BF)
    gu_tiles = pltpu.VMEM((w_tiles, SMALL, gu_cols), BF)
    gu_pairs = pltpu.VMEM((2, w_tiles, SMALL, gu_cols), BF)
    qkv_tiles = pltpu.VMEM((w_tiles, SMALL, 8 * HD), BF)
    qkv_pairs = pltpu.VMEM((2, w_tiles, SMALL, 8 * HD), BF)
    g_tile = pltpu.VMEM((1, 8, D), F32)
    slabs = pltpu.VMEM((2, d_rows, 8 * HD), BF)
    return pl.pallas_call(
        kernel,
        name="finish_back",
        out_shape=[
            shape((rows, D), BF),
            shape((rows, D), BF),
            shape((2, o_tiles, SMALL, D), BF),
            shape((2,) + total_d.shape, BF),
            shape((d_rows, 16 * HD), BF),
            shape((d_rows, 8 * HD), BF),
            shape((d_rows, 8 * HD), BF),
            shape((d_rows, 4 * unit), BF),
            shape((d_rows, 4 * unit), BF),
            shape((8, D), F32),
        ],
        in_specs=[smem, smem] + [hbm] * 3 + [vm] * 4 + [hbm] * 8 + [vm] * 2,
        out_specs=[vm] * 3 + [hbm] + [vm] * 6,
        scratch_shapes=[
            pltpu.VMEM((2, half, 4 * HD), BF),
            pltpu.VMEM((length, 4 * HD), BF),
            four,
            four,
            chunk_,
            four,
            three,
            chunk_,
            chunk_,
            four,
            three,
            chunk_,
            pltpu.VMEM((2, o_tiles, SMALL, D), BF),
            pltpu.VMEM((o_tiles, SMALL, D), BF),
            pltpu.VMEM(sum_gu.shape, BF),
            gu_pairs,
            gu_tiles,
            gu_tiles,
            slabs,
            slabs,
            pltpu.VMEM((d_rows, 8 * HD), BF),
            slabs,
            qkv_pairs,
            qkv_tiles,
            qkv_tiles,
            g_tile,
            pltpu.VMEM((3, 8, D), F32),
            pltpu.VMEM((2, 1, 8, D), F32),
            g_tile,
            pltpu.VMEM((3, 8, D), F32),
            pltpu.SemaphoreType.DMA((n_sems,)),
            pltpu.SemaphoreType.DMA((n_sems,)),
            pltpu.SemaphoreType.DMA((12,)),
        ],
        compiler_params=params(3, 63),
        cost_estimate=pl.CostEstimate(
            flops=5 * 2 * 2 * length * length * HD, bytes_accessed=32 * 2**20, transcendentals=0
        ),
    )(
        block_map,
        inverse,
        core.reshape(n_blocks, BLK, 4 * HD),
        mixed.reshape(n_blocks, BLK, 2 * HD),
        grad.reshape(n_blocks, BLK, 2 * HD),
        lse,
        sum_o,
        total_d,
        sum_gu,
        result_part,
        middle,
        raw,
        table,
        n1,
        wall,
        x_own,
        dmiddle,
        gains,
        mlp_gain_part,
    )


def widen(arrays, gain_sums, parts, steps=8):
    n = len(arrays)
    d_part, h_part = D // parts, HD // parts

    def kernel(*refs):
        for a, b in zip(refs[:n], refs[n + 1 : 2 * n + 1]):
            b[...] = a[...].astype(F32)
        sums = refs[n]
        attn, mlp, query, key = refs[2 * n + 1 :]

        @pl.when(pl.program_id(0) == 0)
        def _():
            f = lax.axis_index("fsdp")
            at = pl.ds(pl.multiple_of(f * d_part, d_part), d_part)
            attn[...] = sums[0:1, at]
            mlp[...] = sums[1:2, at]
            for out, first in ((query, 0), (key, HD)):
                turned = pltpu.roll(sums[0:8, first : first + HD], HD - f * h_part, 1)
                out[...] = turned[2:3, 0:h_part]

    def spec(a):
        return pl.BlockSpec((a.shape[0] // steps, a.shape[1]), lambda i: (i, 0))

    def whole(dims):
        return pl.BlockSpec(dims, lambda i: (0, 0))

    small = [(1, d_part), (1, d_part), (1, h_part), (1, h_part)]
    return pl.pallas_call(
        kernel,
        name="widen",
        grid=(steps,),
        out_shape=[shape(a.shape, F32) for a in arrays] + [shape(s, F32) for s in small],
        in_specs=[spec(a) for a in arrays] + [whole(gain_sums.shape)],
        out_specs=[spec(a) for a in arrays] + [whole(s) for s in small],
        compiler_params=pltpu.CompilerParams(vmem_limit_bytes=62 * 2**20),
    )(*arrays, gain_sums)


def plane_body(
    tokens,
    cotangent,
    block_map,
    positions,
    attn_gain,
    query_weight,
    key_weight,
    value_weight,
    query_gain,
    key_gain,
    out_weight,
    mlp_gain,
    gate_weight,
    up_weight,
    down_weight,
):
    rows = tokens.shape[1]
    parts = lax.axis_size("fsdp")
    flat_map = block_map.reshape(-1)
    n_blocks = flat_map.shape[0]
    order = jnp.arange(n_blocks, dtype=jnp.int32)
    inverse = jnp.sum(
        jnp.where(flat_map[None, :] == order[:, None], order[None, :], 0), axis=1
    ).astype(jnp.int32)
    x_own, n1, raw, table, core, wall, gains, cot_own, wgu = enter(
        tokens.reshape(rows, D),
        cotangent.reshape(rows, D),
        positions,
        [g.reshape(1, -1) for g in (attn_gain, mlp_gain, query_gain, key_gain)],
        query_weight,
        key_weight,
        value_weight,
        gate_weight,
        up_weight,
    )
    att, mixed, lse, cots, wo, wd = attend(
        flat_map, inverse, core, cot_own, out_weight, down_weight
    )
    grad, middle, dmiddle, result_part, sum_gu, sum_o, total_d, mlp_gain_part = feed_forward(
        att, x_own, wo, wgu, wd, cots, cot_own, gains
    )
    (
        result,
        input_grad,
        grad_o,
        grad_d,
        grad_q,
        grad_k,
        grad_v,
        grad_g,
        grad_u,
        gain_sums,
    ) = finish_back(
        flat_map,
        inverse,
        core,
        mixed,
        grad,
        lse,
        sum_o,
        total_d,
        sum_gu,
        result_part,
        middle,
        raw,
        table,
        n1,
        wall,
        x_own,
        dmiddle,
        gains,
        mlp_gain_part,
    )

    (
        result,
        input_grad,
        grad_q,
        grad_k,
        grad_v,
        grad_o,
        grad_g,
        grad_u,
        grad_d,
        *gain_grads,
    ) = widen(
        [
            result,
            input_grad,
            grad_q,
            grad_k,
            grad_v,
            grad_o.reshape(out_weight.shape),
            grad_g,
            grad_u,
            grad_d.reshape(down_weight.shape),
        ],
        gain_sums,
        parts,
    )
    attn_grad, mlp_grad, query_grad, key_grad = [g.reshape(-1) for g in gain_grads]
    return (
        result.reshape(tokens.shape),
        input_grad.reshape(tokens.shape),
        attn_grad,
        grad_q,
        grad_k,
        grad_v,
        query_grad,
        key_grad,
        grad_o,
        mlp_grad,
        grad_g,
        grad_u,
        grad_d,
    )


def solution(mesh):
    placed = (
        P("fsdp", "ctx", None),
        P("fsdp", "ctx", None),
        P(),
        P("fsdp", "ctx"),
        P("fsdp"),
        P("fsdp", None),
        P("fsdp", None),
        P("fsdp", None),
        P("fsdp"),
        P("fsdp"),
        P("fsdp", None),
        P("fsdp"),
        P("fsdp", None),
        P("fsdp", None),
        P("fsdp", None),
    )
    fits = mesh.shape["fsdp"] == 4 and mesh.shape["ctx"] == 8
    return jax.shard_map(
        plane_body if fits else body,
        mesh=mesh,
        in_specs=placed,
        out_specs=(
            P("fsdp", "ctx", None),
            P("fsdp", "ctx", None),
            P("fsdp"),
            P("fsdp", None),
            P("fsdp", None),
            P("fsdp", None),
            P("fsdp"),
            P("fsdp"),
            P("fsdp", None),
            P("fsdp"),
            P("fsdp", None),
            P("fsdp", None),
            P("fsdp", None),
        ),
        check_vma=False,
    )
```

```python
import math

import jax
import jax.numpy as jnp
from jax import lax
from jax.experimental import pallas as pl
from jax.experimental.pallas import tpu as pltpu
from jax.sharding import PartitionSpec as P

D = 1024
HQ = 16
HK = 8
HD = 128
BLK = 128


epsilon = 1e-06
theta_base = 1000000.0
masked_value = -1e30


def rms_scale(values):
    return lax.rsqrt(jnp.mean(values * values, axis=-1, keepdims=True) + epsilon)


def norm_back(upstream, values, scale):
    return scale * upstream - values * (scale * scale * scale) * jnp.mean(
        upstream * values, axis=-1, keepdims=True
    )


def rope_tables(positions, head_dim):
    frequency = jnp.exp(
        jnp.arange(0, head_dim, 2).astype(jnp.float32) * (-math.log(theta_base) / head_dim)
    )
    angles = positions.astype(jnp.float32)[..., None] * frequency
    angles = jnp.concatenate([angles, angles], axis=-1)
    return (jnp.cos(angles), jnp.sin(angles))


def rotate(values, cosine, sine_table):
    half_width = values.shape[-1] // 2
    turned = jnp.concatenate([-values[..., half_width:], values[..., :half_width]], axis=-1)
    return values * cosine + turned * sine_table


def unrotate(grads, cosine, sine_table):
    half_width = grads.shape[-1] // 2
    moved = grads * sine_table
    back_turn = jnp.concatenate([moved[..., half_width:], -moved[..., :half_width]], axis=-1)
    return grads * cosine + back_turn


def score_block(grouped, keys_head, allowed, scale):
    scores = (
        jnp.einsum("qgd,sd->gqs", grouped, keys_head, preferred_element_type=jnp.float32) * scale
    )
    return jnp.where(allowed, scores, masked_value)


def body(
    tokens,
    cotangent,
    block_map,
    positions,
    attn_gain,
    query_weight,
    key_weight,
    value_weight,
    query_gain,
    key_gain,
    out_weight,
    mlp_gain,
    gate_weight,
    up_weight,
    down_weight,
):
    seq_count = tokens.shape[0]
    seq_rows = tokens.shape[1]
    total_rows = seq_count * seq_rows
    groups = HQ // HK
    scale = HD ** (-0.5)
    attn_full, query_full, key_full, mlp_full = (
        lax.all_gather(attn_gain, "fsdp", axis=0, tiled=True),
        lax.all_gather(query_gain, "fsdp", axis=0, tiled=True),
        lax.all_gather(key_gain, "fsdp", axis=0, tiled=True),
        lax.all_gather(mlp_gain, "fsdp", axis=0, tiled=True),
    )
    query_w, key_w, value_w, out_w = (
        lax.all_gather(query_weight.astype(jnp.bfloat16), "fsdp", axis=0, tiled=True),
        lax.all_gather(key_weight.astype(jnp.bfloat16), "fsdp", axis=0, tiled=True),
        lax.all_gather(value_weight.astype(jnp.bfloat16), "fsdp", axis=0, tiled=True),
        lax.all_gather(out_weight.astype(jnp.bfloat16), "fsdp", axis=0, tiled=True),
    )
    flat = tokens.astype(jnp.float32).reshape(total_rows, D)
    scale_one = rms_scale(flat)
    normed = (flat * scale_one * attn_full).astype(jnp.bfloat16)
    query_raw = jnp.dot(normed, query_w, preferred_element_type=jnp.float32).reshape(
        total_rows, HQ, HD
    )
    key_raw = jnp.dot(normed, key_w, preferred_element_type=jnp.float32).reshape(total_rows, HK, HD)
    value_low = jnp.dot(normed, value_w, preferred_element_type=jnp.float32).astype(jnp.bfloat16)
    cosine, sine_table = rope_tables(positions.reshape(total_rows), HD)
    cosine = cosine[:, None, :]
    sine_table = sine_table[:, None, :]
    query_scale = rms_scale(query_raw)
    query_unit = query_raw * query_scale
    query_low = rotate(query_unit * query_full, cosine, sine_table).astype(jnp.bfloat16)
    key_scale = rms_scale(key_raw)
    key_unit = key_raw * key_scale
    key_low = rotate(key_unit * key_full, cosine, sine_table).astype(jnp.bfloat16)
    flat_map = block_map.reshape(-1)
    offsets = jnp.arange(BLK, dtype=jnp.int32)
    key_index = (flat_map[:, None] * BLK + offsets[None, :]).reshape(-1)
    own_blocks = lax.dynamic_slice_in_dim(flat_map, lax.axis_index("ctx") * 2, 2)
    query_index = (own_blocks[:, None] * BLK + offsets[None, :]).reshape(-1)
    allowed = query_index[:, None] >= key_index[None, :]
    query_seq = query_low.reshape(seq_count, seq_rows, HK, groups, HD)
    key_seq = key_low.reshape(seq_count, seq_rows, HK * HD)
    value_seq = value_low.reshape(seq_count, seq_rows, HK * HD)

    def forward_head(inputs):
        grouped, keys_head, values_head = inputs
        scores = score_block(grouped, keys_head, allowed, scale)
        row_max = jnp.max(scores, axis=-1, keepdims=True)
        exp_scores = jnp.exp(scores - row_max)
        row_total = jnp.sum(exp_scores, axis=-1, keepdims=True)
        prob_low = (exp_scores / row_total).astype(jnp.bfloat16)
        mixed = jnp.einsum("gqs,sd->qgd", prob_low, values_head, preferred_element_type=jnp.float32)
        return (mixed, row_max + jnp.log(row_total))

    seq_item = 0
    keys_all = lax.all_gather(key_seq[seq_item], "ctx", axis=0, tiled=True)
    values_all = lax.all_gather(value_seq[seq_item], "ctx", axis=0, tiled=True)
    keys_head = jnp.transpose(keys_all.reshape(-1, HK, HD), (1, 0, 2))
    values_head = jnp.transpose(values_all.reshape(-1, HK, HD), (1, 0, 2))
    grouped_head = jnp.transpose(query_seq[seq_item], (1, 0, 2, 3))
    mixed, lse = lax.map(forward_head, (grouped_head, keys_head, values_head))
    mixed_parts = jnp.transpose(mixed, (1, 0, 2, 3)).reshape(seq_rows, HQ * HD)
    lse_parts = [lse]
    gathered = [(grouped_head, keys_head, values_head)]
    attended = mixed_parts.astype(jnp.bfloat16)
    middle = flat + jnp.dot(attended, out_w, preferred_element_type=jnp.float32)
    gate_w, up_w, down_w = (
        lax.all_gather(gate_weight.astype(jnp.bfloat16), "fsdp", axis=0, tiled=True),
        lax.all_gather(up_weight.astype(jnp.bfloat16), "fsdp", axis=0, tiled=True),
        lax.all_gather(down_weight.astype(jnp.bfloat16), "fsdp", axis=0, tiled=True),
    )
    scale_two = rms_scale(middle)
    normed_two = (middle * scale_two * mlp_full).astype(jnp.bfloat16)
    gate = jnp.dot(normed_two, gate_w, preferred_element_type=jnp.float32)
    upward = jnp.dot(normed_two, up_w, preferred_element_type=jnp.float32)
    sigmoid_gate = jax.nn.sigmoid(gate)
    silu_gate = gate * sigmoid_gate
    hidden = (silu_gate * upward).astype(jnp.bfloat16)
    result = middle + jnp.dot(hidden, down_w, preferred_element_type=jnp.float32)
    query_back, key_back, value_back, out_back = (
        lax.all_gather(query_weight.astype(jnp.bfloat16), "fsdp", axis=0, tiled=True),
        lax.all_gather(key_weight.astype(jnp.bfloat16), "fsdp", axis=0, tiled=True),
        lax.all_gather(value_weight.astype(jnp.bfloat16), "fsdp", axis=0, tiled=True),
        lax.all_gather(out_weight.astype(jnp.bfloat16), "fsdp", axis=0, tiled=True),
    )
    gate_back, up_back, down_back = (
        lax.all_gather(gate_weight.astype(jnp.bfloat16), "fsdp", axis=0, tiled=True),
        lax.all_gather(up_weight.astype(jnp.bfloat16), "fsdp", axis=0, tiled=True),
        lax.all_gather(down_weight.astype(jnp.bfloat16), "fsdp", axis=0, tiled=True),
    )
    grad_out = cotangent.astype(jnp.float32).reshape(total_rows, D)
    grad_branch = grad_out.astype(jnp.bfloat16)
    down_grad = jnp.einsum("nf,nd->fd", hidden, grad_branch, preferred_element_type=jnp.float32)
    grad_hidden = jnp.einsum(
        "nd,fd->nf", grad_branch, down_back, preferred_element_type=jnp.float32
    )
    grad_gate = (grad_hidden * upward * sigmoid_gate * (1.0 + gate * (1.0 - sigmoid_gate))).astype(
        jnp.bfloat16
    )
    grad_up = (grad_hidden * silu_gate).astype(jnp.bfloat16)
    gate_grad = jnp.einsum("nd,nf->df", normed_two, grad_gate, preferred_element_type=jnp.float32)
    up_grad = jnp.einsum("nd,nf->df", normed_two, grad_up, preferred_element_type=jnp.float32)
    grad_normed_two = jnp.einsum(
        "nf,df->nd", grad_gate, gate_back, preferred_element_type=jnp.float32
    ) + jnp.einsum("nf,df->nd", grad_up, up_back, preferred_element_type=jnp.float32)
    mlp_local = jnp.sum(grad_normed_two * middle * scale_two, axis=0)
    grad_middle = grad_out + norm_back(grad_normed_two * mlp_full, middle, scale_two)
    grad_attn_low = grad_middle.astype(jnp.bfloat16)
    out_grad = jnp.einsum("nq,nd->qd", attended, grad_attn_low, preferred_element_type=jnp.float32)
    grad_mixed = jnp.einsum(
        "nd,qd->nq", grad_attn_low, out_back, preferred_element_type=jnp.float32
    ).astype(jnp.bfloat16)
    grad_mixed_seq = grad_mixed.reshape(seq_count, seq_rows, HK, groups, HD)

    def backward_head(inputs):
        grouped, keys_head, values_head, grad_head, lse = inputs
        scores = score_block(grouped, keys_head, allowed, scale)
        prob_full = jnp.exp(scores - lse)
        grad_prob = jnp.einsum(
            "qgd,sd->gqs", grad_head, values_head, preferred_element_type=jnp.float32
        )
        delta_row = jnp.sum(prob_full * grad_prob, axis=-1, keepdims=True)
        grad_scores = (prob_full * (grad_prob - delta_row)).astype(jnp.bfloat16)
        grad_query_head = (
            jnp.einsum("gqs,sd->qgd", grad_scores, keys_head, preferred_element_type=jnp.float32)
            * scale
        )
        grad_key_head = (
            jnp.einsum("gqs,qgd->sd", grad_scores, grouped, preferred_element_type=jnp.float32)
            * scale
        )
        grad_value_head = jnp.einsum(
            "gqs,qgd->sd",
            prob_full.astype(jnp.bfloat16),
            grad_head,
            preferred_element_type=jnp.float32,
        )
        return (grad_query_head, grad_key_head, grad_value_head)

    seq_item = 0
    grouped_head, keys_head, values_head = gathered[seq_item]
    grad_head = jnp.transpose(grad_mixed_seq[seq_item], (1, 0, 2, 3))
    grad_query_head, grad_key_head, grad_value_head = lax.map(
        backward_head, (grouped_head, keys_head, values_head, grad_head, lse_parts[seq_item])
    )
    grad_query_parts = jnp.transpose(grad_query_head, (1, 0, 2, 3)).reshape(seq_rows, HQ, HD)
    grad_keys_all = jnp.transpose(grad_key_head, (1, 0, 2)).reshape(-1, HK * HD)
    grad_values_all = jnp.transpose(grad_value_head, (1, 0, 2)).reshape(-1, HK * HD)
    grad_key_own = lax.psum_scatter(
        grad_keys_all.astype(jnp.bfloat16), "ctx", scatter_dimension=0, tiled=True
    ).astype(jnp.float32)
    grad_value_own = lax.psum_scatter(
        grad_values_all.astype(jnp.bfloat16), "ctx", scatter_dimension=0, tiled=True
    )
    grad_key = grad_key_own.reshape(total_rows, HK, HD)
    grad_query_unit = unrotate(grad_query_parts, cosine, sine_table)
    qgain_local = jnp.sum(grad_query_unit * query_unit, axis=(0, 1))
    grad_query_low = (
        norm_back(grad_query_unit * query_full, query_raw, query_scale)
        .astype(jnp.bfloat16)
        .reshape(total_rows, HQ * HD)
    )
    grad_key_unit = unrotate(grad_key, cosine, sine_table)
    kgain_local = jnp.sum(grad_key_unit * key_unit, axis=(0, 1))
    grad_key_low = (
        norm_back(grad_key_unit * key_full, key_raw, key_scale)
        .astype(jnp.bfloat16)
        .reshape(total_rows, HK * HD)
    )
    query_grad = jnp.einsum("nd,nc->dc", normed, grad_query_low, preferred_element_type=jnp.float32)
    key_grad = jnp.einsum("nd,nc->dc", normed, grad_key_low, preferred_element_type=jnp.float32)
    value_grad = jnp.einsum("nd,nc->dc", normed, grad_value_own, preferred_element_type=jnp.float32)
    grad_normed = jnp.einsum(
        "nc,dc->nd", grad_query_low, query_back, preferred_element_type=jnp.float32
    )
    grad_normed = grad_normed + jnp.einsum(
        "nc,dc->nd", grad_key_low, key_back, preferred_element_type=jnp.float32
    )
    grad_normed = grad_normed + jnp.einsum(
        "nc,dc->nd", grad_value_own, value_back, preferred_element_type=jnp.float32
    )
    attn_local = jnp.sum(grad_normed * flat * scale_one, axis=0)
    input_grad = grad_middle + norm_back(grad_normed * attn_full, flat, scale_one)
    shares = (
        lax.psum_scatter(
            attn_local.astype(jnp.bfloat16), "fsdp", scatter_dimension=0, tiled=True
        ).astype(jnp.float32),
        lax.psum_scatter(
            query_grad.astype(jnp.bfloat16), "fsdp", scatter_dimension=0, tiled=True
        ).astype(jnp.float32),
        lax.psum_scatter(
            key_grad.astype(jnp.bfloat16), "fsdp", scatter_dimension=0, tiled=True
        ).astype(jnp.float32),
        lax.psum_scatter(
            value_grad.astype(jnp.bfloat16), "fsdp", scatter_dimension=0, tiled=True
        ).astype(jnp.float32),
        lax.psum_scatter(
            qgain_local.astype(jnp.bfloat16), "fsdp", scatter_dimension=0, tiled=True
        ).astype(jnp.float32),
        lax.psum_scatter(
            kgain_local.astype(jnp.bfloat16), "fsdp", scatter_dimension=0, tiled=True
        ).astype(jnp.float32),
        lax.psum_scatter(
            out_grad.astype(jnp.bfloat16), "fsdp", scatter_dimension=0, tiled=True
        ).astype(jnp.float32),
        lax.psum_scatter(
            mlp_local.astype(jnp.bfloat16), "fsdp", scatter_dimension=0, tiled=True
        ).astype(jnp.float32),
        lax.psum_scatter(
            gate_grad.astype(jnp.bfloat16), "fsdp", scatter_dimension=0, tiled=True
        ).astype(jnp.float32),
        lax.psum_scatter(
            up_grad.astype(jnp.bfloat16), "fsdp", scatter_dimension=0, tiled=True
        ).astype(jnp.float32),
        lax.psum_scatter(
            down_grad.astype(jnp.bfloat16), "fsdp", scatter_dimension=0, tiled=True
        ).astype(jnp.float32),
    )
    summed = (
        lax.psum(shares[0].astype(jnp.bfloat16), "ctx").astype(jnp.float32),
        lax.psum(shares[1].astype(jnp.bfloat16), "ctx").astype(jnp.float32),
        lax.psum(shares[2].astype(jnp.bfloat16), "ctx").astype(jnp.float32),
        lax.psum(shares[3].astype(jnp.bfloat16), "ctx").astype(jnp.float32),
        lax.psum(shares[4].astype(jnp.bfloat16), "ctx").astype(jnp.float32),
        lax.psum(shares[5].astype(jnp.bfloat16), "ctx").astype(jnp.float32),
        lax.psum(shares[6].astype(jnp.bfloat16), "ctx").astype(jnp.float32),
        lax.psum(shares[7].astype(jnp.bfloat16), "ctx").astype(jnp.float32),
        lax.psum(shares[8].astype(jnp.bfloat16), "ctx").astype(jnp.float32),
        lax.psum(shares[9].astype(jnp.bfloat16), "ctx").astype(jnp.float32),
        lax.psum(shares[10].astype(jnp.bfloat16), "ctx").astype(jnp.float32),
    )
    return (
        result.reshape(tokens.shape),
        input_grad.reshape(tokens.shape),
        summed[0],
        summed[1],
        summed[2],
        summed[3],
        summed[4],
        summed[5],
        summed[6],
        summed[7],
        summed[8],
        summed[9],
        summed[10],
    )


MESH = pl.DeviceIdType.MESH
BF = jnp.bfloat16
F32 = jnp.float32
LOG2E = math.log2(math.e)
QT = 256
NEG = -1e30
SMALL = 32


def shape(dims, dtype):
    return jax.ShapeDtypeStruct(dims, dtype)


def dot_nn(a, b):
    return jnp.dot(a, b, preferred_element_type=F32)


def dot_nt(a, b):
    return lax.dot_general(a, b, (((1,), (1,)), ((), ())), preferred_element_type=F32)


def dot_tn(a, b):
    return lax.dot_general(a, b, (((0,), (0,)), ((), ())), preferred_element_type=F32)


def device(z, x, y, c):
    return (z * 2 + x, y * 2 + c)


def coords():
    a = lax.axis_index("ctx")
    f = lax.axis_index("fsdp")
    return lax.div(a, 2), lax.rem(a, 2), lax.div(f, 2), lax.rem(f, 2)


class Net:
    def __init__(self, send_sems, recv_sems):
        self.z, self.x, self.y, self.c = z, x, y, c = coords()
        self.depth = lax.axis_size("ctx") // 2
        self.to_x = device(z, 1 - x, y, c)
        self.to_y = device(z, x, 1 - y, c)
        self.to_core = device(z, x, y, 1 - c)
        self.to_x_other = device(z, 1 - x, y, 1 - c)
        self.up = device(z + 1, x, y, c)
        self.down = device(z - 1, x, y, c)
        self.mate = device(2 * c + y, x, lax.rem(z, 2), lax.div(z, 2))
        self.moves = z != 2 * c + y
        self.mate_chunk = 2 * lax.rem(z, 2) + x
        self.has_up = z < self.depth - 1
        self.has_down = z > 0
        self.send_sems, self.recv_sems = send_sems, recv_sems
        self.used = 0
        self.me = 2 * y + x
        self.sx = 2 * y + 1 - x
        self.sy = 2 * (1 - y) + x
        self.sd = 2 * (1 - y) + 1 - x

    def greet(self, line=True, owners=False, mate=False):
        barrier = pltpu.get_barrier_semaphore()

        def signal(to):
            pl.semaphore_signal(barrier, inc=1, device_id=to, device_id_type=MESH)

        for to in (self.to_x, self.to_y, self.to_core):
            signal(to)
        count = 3
        if owners:
            signal(self.to_x_other)
            count = count + 1
        if mate:
            pl.when(self.moves)(lambda: signal(self.mate))
            count = count + self.moves.astype(jnp.int32)
        if line:
            pl.when(self.has_up)(lambda: signal(self.up))
            pl.when(self.has_down)(lambda: signal(self.down))
            count = count + self.has_up.astype(jnp.int32) + self.has_down.astype(jnp.int32)
        pl.semaphore_wait(barrier, count)

    def take(self, count=1):
        first = self.used
        self.used += count
        assert self.used <= self.send_sems.shape[0], self.used
        return first

    def copy(self, sem, src, dst, to):
        return pltpu.make_async_remote_copy(
            src_ref=src,
            dst_ref=dst,
            send_sem=self.send_sems.at[sem],
            recv_sem=self.recv_sems.at[sem],
            device_id=to,
            device_id_type=MESH,
        )

    def new(self, src, dst, to):
        return self.copy(self.take(), src, dst, to)


def rms(values):
    return lax.rsqrt(jnp.mean(values * values, axis=-1, keepdims=True) + epsilon)


class PlaneGather:
    def __init__(self, net, src, out, split=None):
        rows = out.shape[1]
        split = rows // 2 if split is None else split
        self.net = net
        me, sx, sy = net.me, net.sx, net.sy
        self.sides, self.relays = [], []
        for first, size, near, far, s_near in (
            (split, rows - split, net.to_y, net.to_x, sy),
            (0, split, net.to_x, net.to_y, sx),
        ):
            if size:
                at = pl.ds(first, size)
                one = net.new(src.at[at], out.at[me, at], near)
                self.sides.append(one)
                self.relays.append((one, net.new(out.at[s_near, at], out.at[s_near, at], far)))
        self.rest = []
        for first, size, far in ((split, rows - split, net.to_x), (0, split, net.to_y)):
            if size:
                at = pl.ds(first, size)
                self.rest.append(net.new(src.at[at], out.at[me, at], far))

    def start(self):
        for cp in self.sides + self.rest:
            cp.start()

    def forward(self):
        for one, relay in self.relays:
            one.wait_recv()
            relay.start()

    def wait_sides(self):
        for cp in self.rest:
            cp.wait_recv()

    def wait_diagonal(self):
        for _, relay in self.relays:
            relay.wait_recv()

    def drain(self):
        for cp in self.sides + self.rest:
            cp.wait_send()
        for _, relay in self.relays:
            relay.wait_send()


class PlaneSum:
    def __init__(self, net, part, got, mid, split=None):
        rows = part.shape[1]
        split = rows // 2 if split is None else split
        self.net, self.part, self.got, self.mid = net, part, got, mid
        me, sx, sy, sd = net.me, net.sx, net.sy, net.sd
        self.ways = []
        for first, size, near, far, s_near, s_far in (
            (0, split, net.to_x, net.to_y, sx, sy),
            (split, rows - split, net.to_y, net.to_x, sy, sx),
        ):
            if size:
                at = pl.ds(first, size)
                self.ways.append(
                    (
                        at,
                        s_far,
                        net.new(part.at[sd, at], got.at[0, at], near),
                        net.new(part.at[s_near, at], got.at[1, at], near),
                        net.new(mid.at[at], got.at[2, at], far),
                    )
                )

    def start_diagonal(self):
        for _, _, diagonal, _, _ in self.ways:
            diagonal.start()

    def start_sides(self):
        for _, _, _, side, _ in self.ways:
            side.start()

    def forward(self):
        for at, s_far, diagonal, _, relay in self.ways:
            diagonal.wait_recv()
            self.mid[at] = (self.part[s_far, at].astype(F32) + self.got[0, at].astype(F32)).astype(
                BF
            )
            relay.start()

    def finish(self, use):
        for at, _, _, side, relay in self.ways:
            side.wait_recv()
            relay.wait_recv()
            use(
                at,
                self.part[self.net.me, at].astype(F32)
                + self.got[1, at].astype(F32)
                + self.got[2, at].astype(F32),
            )

    def drain(self):
        for _, _, diagonal, side, relay in self.ways:
            diagonal.wait_send()
            side.wait_send()
            relay.wait_send()


class Fetch:
    def __init__(self, net, src, out):
        self.net, self.src = net, src
        whole = len(out.shape) == len(src.shape)
        self.out = out if whole else out.at[net.me]
        self.cp = net.new(src, out if whole else out.at[net.mate_chunk], net.mate)

    def start(self):
        pl.when(self.net.moves)(self.cp.start)

        @pl.when(jnp.logical_not(self.net.moves))
        def _():
            self.out[...] = self.src[...]

    def wait(self):
        pl.when(self.net.moves)(self.cp.wait_recv)

    def drain(self):
        pl.when(self.net.moves)(self.cp.wait_send)


class LineSum:
    def __init__(self, net, tiles, src, mine, slots, deliver):
        self.net, self.tiles, self.src, self.mine = net, tiles, src, mine
        self.slots, self.deliver = slots, deliver
        self.sems = net.take(4 * tiles)
        self.root = net.depth // 2
        self.below = net.z < self.root
        self.above = net.z > self.root
        self.middle = net.z == self.root
        self.two_sided = self.root < net.depth - 1
        self.at_end = jnp.logical_or(net.z == 0, net.z == net.depth - 1)
        self.between = jnp.logical_not(jnp.logical_or(self.middle, self.at_end))

    def hop(self, kind, k):
        net, slots = self.net, self.slots
        src, dst, to = (
            (slots.at[1, k], slots.at[0, k], net.up),
            (slots.at[0, k], slots.at[1, k], net.down),
            (self.mine(k), self.mine(k), net.down),
            (self.mine(k), self.mine(k), net.up),
        )[kind]
        return net.copy(self.sems + kind * self.tiles + k, src, dst, to)

    def gather(self, k):
        net, slots = self.net, self.slots

        def send(kind, has_before):
            @pl.when(has_before)
            def _():
                self.hop(kind, k).wait_recv()
                total = self.src(k)[...].astype(F32) + slots[kind, k].astype(F32)
                slots[1 - kind, k] = total.astype(slots.dtype)

            @pl.when(jnp.logical_not(has_before))
            def _():
                slots[1 - kind, k] = self.src(k)[...]

            self.hop(kind, k).start()

        pl.when(self.below)(lambda: send(0, net.has_down))
        pl.when(self.above)(lambda: send(1, net.has_up))

    def finish(self, k):
        net, slots = self.net, self.slots

        @pl.when(self.middle)
        def _():
            self.hop(0, k).wait_recv()
            total = self.src(k)[...].astype(F32) + slots[0, k].astype(F32)
            if self.two_sided:
                self.hop(1, k).wait_recv()
                total = total + slots[1, k].astype(F32)
            self.mine(k)[...] = total.astype(slots.dtype)
            self.hop(2, k).start()
            if self.two_sided:
                self.hop(3, k).start()

        @pl.when(self.below)
        def _():
            self.hop(2, k).wait_recv()
            pl.when(net.has_down)(lambda: self.hop(2, k).start())

        @pl.when(self.above)
        def _():
            self.hop(3, k).wait_recv()
            pl.when(net.has_up)(lambda: self.hop(3, k).start())

        self.deliver(k)

    def drain(self, k):
        net = self.net
        pl.when(self.below)(lambda: self.hop(0, k).wait_send())
        pl.when(self.above)(lambda: self.hop(1, k).wait_send())
        sends_down = jnp.logical_and(net.has_down, jnp.logical_not(self.above))
        sends_up = jnp.logical_and(net.has_up, jnp.logical_not(self.below))
        pl.when(sends_down)(lambda: self.hop(2, k).wait_send())
        pl.when(sends_up)(lambda: self.hop(3, k).wait_send())


def within(k, first, last):
    return jnp.logical_and(k >= first, k < last)


class Pump:
    def __init__(self, lines, lags=(1, 3, 5, 7), placed=None):
        self.lines = lines
        self.total = sum(line.tiles for line in lines)
        self.gather_lag, self.middle_lag, self.between_lag, self.end_lag = lags
        self.placed = placed

    def each(self, s, run):
        if isinstance(s, int):
            for line in self.lines:
                if 0 <= s < line.tiles:
                    run(line, s)
                s -= line.tiles
            return
        first = 0
        for line in self.lines:
            pl.when(within(s, first, first + line.tiles))(
                lambda line=line, first=first: run(line, s - first)
            )
            first += line.tiles

    def step(self, p, before=None):
        line = self.lines[0]

        @pl.when(line.between)
        def _():
            if before is not None:
                before(p - self.gather_lag)
            self.each(p - self.gather_lag, lambda ln, k: ln.gather(k))
            self.each(p - self.between_lag, lambda ln, k: ln.finish(k))

        @pl.when(line.middle)
        def _():
            if before is not None:
                before(p - self.middle_lag)
            self.each(p - self.middle_lag, lambda ln, k: ln.finish(k))

        @pl.when(line.at_end)
        def _():
            self.each(p - self.end_lag, lambda ln, k: ln.finish(k))

    def steps(self):
        return self.total + max(self.gather_lag, self.middle_lag, self.between_lag, self.end_lag)


def any_spec():
    return pl.BlockSpec(memory_space=pl.ANY)


def vmem_spec():
    return pl.BlockSpec(memory_space=pltpu.VMEM)


def params(cid, mib=60):
    return pltpu.CompilerParams(
        collective_id=cid, has_side_effects=True, vmem_limit_bytes=mib * 2**20
    )


def enter(tok, cot, pos, gains, wq, wk, wv, wg, wu):
    rows = tok.shape[0]
    d_rows = wq.shape[0]
    half = 4 * rows
    unit = wg.shape[1] // 4
    n_sems = 48

    def kernel(
        tok_ref,
        cot_ref,
        pos_in,
        attn_ref,
        mlp_ref,
        query_ref,
        key_ref,
        wq_ref,
        wk_ref,
        wv_ref,
        wg_ref,
        wu_ref,
        x_own,
        n1,
        raw_ref,
        table,
        core,
        wall,
        gains_ref,
        cot_own,
        wgu,
        wq_s,
        wk_s,
        wv_s,
        wg_s,
        wu_s,
        wloc,
        wloc2,
        toks,
        pos_ref,
        gain_ref,
        poss,
        heads,
        gslots,
        ssem,
        rsem,
        lsem,
    ):
        net = Net(ssem, rsem)
        y, c = net.y, net.c
        f = 2 * y + c
        fy = 2 * (1 - y) + c
        loads = [
            pltpu.make_async_copy(a, b, lsem.at[k])
            for k, (a, b) in enumerate(
                ((wq_ref, wq_s), (wk_ref, wk_s), (wv_ref, wv_s), (wg_ref, wg_s), (wu_ref, wu_s))
            )
        ]
        for cp in loads:
            cp.start()
        for h in range(rows // 128):
            pos_ref[8 * h : 8 * h + 1, :] = pos_in[0:1, h * 128 : (h + 1) * 128].astype(F32)
        gain_ref[...] = jnp.zeros_like(gain_ref)
        at = pl.ds(pl.multiple_of(f * d_rows, d_rows), d_rows)
        gain_ref[0:1, at] = attn_ref[...]
        gain_ref[1:2, at] = mlp_ref[...]
        for row, ref in ((2, query_ref), (3, key_ref)):
            n = ref.shape[1]
            wide = jnp.concatenate([ref[...], jnp.zeros((1, HD - n), F32)], axis=-1)
            wide = pltpu.roll(jnp.broadcast_to(wide, (8, HD)), f * n, 1)
            gain_ref[row : row + 1, 0:HD] = wide[0:1]
        net.greet(False, mate=True)
        fetch, pos_fetch = Fetch(net, tok_ref, toks), Fetch(net, pos_ref, poss)
        cot_fetch = Fetch(net, cot_ref, cot_own)
        fetch.start()
        pos_fetch.start()
        g_core = net.new(gain_ref, gslots.at[f], net.to_core)
        g_y = net.new(gain_ref, gslots.at[f], net.to_y)
        g_relay = net.new(gslots.at[fy], gslots.at[fy], net.to_core)
        g_core.start()
        g_y.start()
        gslots[f] = gain_ref[...]
        for cp in loads[:3]:
            cp.wait()
        for t in range(4):
            at = t * 4 * HD
            wloc[t, :, 0 : 4 * HD] = wq_s[:, at : at + 4 * HD].astype(BF)
            at = t * 2 * HD
            wloc[t, :, 4 * HD : 6 * HD] = wk_s[:, at : at + 2 * HD].astype(BF)
            wloc[t, :, 6 * HD : 8 * HD] = wv_s[:, at : at + 2 * HD].astype(BF)
        w_y = net.new(wloc.at[net.sy], wall.at[f], net.to_y)
        w_core = net.new(wloc.at[net.me], wall.at[f], net.to_core)
        w_relay = net.new(wall.at[fy], wall.at[fy], net.to_core)
        w_y.start()
        w_core.start()
        wall[f] = wloc[net.me]
        pos_fetch.wait()
        pos_gather = PlaneGather(net, poss.at[net.me], poss)
        pos_gather.start()
        fetch.wait()
        gather = PlaneGather(net, toks.at[net.me], toks, rows // 4)
        gather.start()
        cot_fetch.start()
        pos_gather.forward()
        for cp in loads[3:]:
            cp.wait()
        for t in range(4):
            at = t * unit
            wloc2[t, :, 0:unit] = wg_s[:, at : at + unit].astype(BF)
            wloc2[t, :, unit : 2 * unit] = wu_s[:, at : at + unit].astype(BF)
        gu_y = net.new(wloc2.at[net.sy], wgu.at[f], net.to_y)
        gu_core = net.new(wloc2.at[net.me], wgu.at[f], net.to_core)
        gu_relay = net.new(wgu.at[fy], wgu.at[fy], net.to_core)
        gu_y.start()
        gu_core.start()
        wgu[f] = wloc2[net.me]
        gather.forward()
        g_y.wait_recv()
        g_relay.start()
        w_y.wait_recv()
        w_relay.start()
        g_core.wait_recv()
        g_relay.wait_recv()
        w_core.wait_recv()
        w_relay.wait_recv()
        index = lax.broadcasted_iota(jnp.int32, (8, HD // 2), 1).astype(F32)
        frequency = jnp.exp(index * (-2.0 * math.log(theta_base) / HD))[0:1]
        full = gslots[0] + gslots[1] + gslots[2] + gslots[3]
        gains_ref[...] = full
        attn_gain, q_gain, k_gain = full[0:1, :], full[2:3, 0:HD], full[3:4, 0:HD]
        pos_gather.wait_sides()
        pos_gather.wait_diagonal()
        x_own[...] = toks[net.me]
        swaps = net.take(4)

        def swap(k):
            at = pl.ds(pl.multiple_of(k * rows, rows), rows)
            return net.copy(swaps + k, heads.at[1 - c, at], core.at[c, at], net.to_core)

        @pl.loop(0, 4)
        def _(n):
            pl.when(n == 1)(gather.wait_sides)
            pl.when(n == 3)(gather.wait_diagonal)
            k = jnp.where(
                n == 0, net.me, jnp.where(n == 1, net.sx, jnp.where(n == 2, net.sy, net.sd))
            )
            at = pl.ds(pl.multiple_of(k * rows, rows), rows)
            flat = toks[k].astype(F32)
            normed = (flat * rms(flat) * attn_gain).astype(BF)
            n1[at, :] = normed
            raw = dot_nn(normed[:, 0:d_rows], wall[0])
            for g in range(1, 4):
                raw = raw + dot_nn(normed[:, g * d_rows : (g + 1) * d_rows], wall[g])
            raw_ref[at, :] = raw[:, 0 : 6 * HD]
            place = jnp.transpose(poss[k])
            angles = jnp.concatenate(
                [place[:, 8 * h : 8 * h + 1] * frequency for h in range(rows // 128)],
                axis=0,
            )
            cosine, sine = jnp.cos(angles), jnp.sin(angles)
            table[at, :] = jnp.concatenate([cosine, sine], axis=-1)
            cosine = jnp.concatenate([cosine, cosine], axis=-1)
            sine = jnp.concatenate([-sine, sine], axis=-1)
            for h in range(6):
                u = raw[:, h * HD : (h + 1) * HD]
                unit = u * rms(u) * (q_gain if h < 4 else k_gain)
                turned = unit * cosine + pltpu.roll(unit, HD // 2, 1) * sine
                g, lane = (h // 2, (h % 2) * HD) if h < 4 else (h - 4, 2 * HD)
                heads[g, at, lane : lane + HD] = turned.astype(BF)
            for g in range(2):
                v = raw[:, (6 + g) * HD : (7 + g) * HD]
                heads[g, at, 3 * HD : 4 * HD] = v.astype(BF)
            swap(k).start()
            core[c, at] = heads[c, at]

        gu_y.wait_recv()
        gu_relay.start()
        for k in range(4):
            swap(k).wait()
        cot_fetch.wait()
        gu_core.wait_recv()
        gu_relay.wait_recv()
        for cp in (g_core, g_y, g_relay, w_core, w_y, w_relay, gu_core, gu_y, gu_relay):
            cp.wait_send()
        for item in (fetch, pos_fetch, cot_fetch, gather, pos_gather):
            item.drain()

    vm = vmem_spec()
    return pl.pallas_call(
        kernel,
        name="enter",
        out_shape=[
            shape((rows, D), BF),
            shape((half, D), BF),
            shape((half, 6 * HD), F32),
            shape((half, HD), F32),
            shape((2, half, 4 * HD), BF),
            shape((4, d_rows, 8 * HD), BF),
            shape((8, D), F32),
            shape((rows, D), BF),
            shape((4, d_rows, 2 * unit), BF),
        ],
        in_specs=[vm] * 7 + [any_spec()] * 5,
        out_specs=[vm] * 9,
        scratch_shapes=[
            pltpu.VMEM(wq.shape, F32),
            pltpu.VMEM(wk.shape, F32),
            pltpu.VMEM(wv.shape, F32),
            pltpu.VMEM(wg.shape, F32),
            pltpu.VMEM(wu.shape, F32),
            pltpu.VMEM((4, d_rows, 8 * HD), BF),
            pltpu.VMEM((4, d_rows, 2 * unit), BF),
            pltpu.VMEM((4, rows, D), BF),
            pltpu.VMEM((16, 128), F32),
            pltpu.VMEM((8, D), F32),
            pltpu.VMEM((4, 16, 128), F32),
            pltpu.VMEM((2, half, 4 * HD), BF),
            pltpu.VMEM((4, 8, D), F32),
            pltpu.SemaphoreType.DMA((n_sems,)),
            pltpu.SemaphoreType.DMA((n_sems,)),
            pltpu.SemaphoreType.DMA((5,)),
        ],
        compiler_params=params(0),
        cost_estimate=pl.CostEstimate(
            flops=2 * half * D * 8 * HD, bytes_accessed=16 * 2**20, transcendentals=0
        ),
    )(tok, cot, pos, *gains, wq, wk, wv, wg, wu)


def attend(block_map, inverse, core, cot, wo, wd):
    half = core.shape[1]
    length = 2 * half
    tiles = length // QT
    blocks = QT // BLK
    n_blocks = length // BLK
    factor = HD ** (-0.5) * LOG2E
    n_sems = 16
    rows = cot.shape[0]

    def kernel(
        bm,
        inv,
        x_ref,
        cot_ref,
        wo_ref,
        wd_ref,
        att,
        mixed,
        lse_ref,
        cots,
        wo_out,
        wd_out,
        q_s,
        k_s,
        v_s,
        o_s,
        wo_s,
        wd_s,
        ssem,
        rsem,
        lsem,
    ):
        net = Net(ssem, rsem)
        x, c = net.x, net.c
        loads = [
            pltpu.make_async_copy(a, b, lsem.at[k])
            for k, (a, b) in enumerate(((wo_ref, wo_s), (wd_ref, wd_s)))
        ]
        for cp in loads:
            cp.start()
        net.greet(False)
        gather = PlaneGather(net, cot_ref, cots)
        gather.start()
        o_core = net.new(wo_out, wo_out, net.to_core)
        d_core = net.new(wd_out, wd_out, net.to_core)
        own = c == x

        @pl.loop(0, tiles)
        def _(i):
            for h in range(blocks):
                block = x_ref[inv[i * blocks + h]]
                at = pl.multiple_of(i * QT, QT) + h * BLK
                q_s[i, pl.ds(h * BLK, BLK), :] = block[:, 0:HD]
                q_s[i, pl.ds(QT + h * BLK, BLK), :] = block[:, HD : 2 * HD]
                k_s[pl.ds(at, BLK), :] = block[:, 2 * HD : 3 * HD]
                v_s[pl.ds(at, BLK), 0:HD] = block[:, 3 * HD : 4 * HD]

        v_s[:, HD : 2 * HD] = jnp.ones((length, HD), BF)
        for cp in loads:
            cp.wait()

        @pl.when(own)
        def _():
            wo_out[...] = wo_s[...].astype(BF)
            wd_out[...] = wd_s[...].astype(BF)
            o_core.start()
            d_core.start()

        q_row = lax.broadcasted_iota(jnp.int32, (2 * QT, QT), 0)
        k_row = lax.broadcasted_iota(jnp.int32, (2 * QT, QT), 1)
        allowed = jnp.where(q_row >= QT, q_row - QT, q_row) >= k_row

        def tile(i):
            q = q_s[i]
            acc = None
            for j in range(i + 1):
                at = slice(j * QT, (j + 1) * QT)
                scores = dot_nt(q, k_s[at, :]) * factor
                if j == i:
                    scores = jnp.where(allowed, scores, NEG)
                add = dot_nn(jnp.exp2(scores).astype(BF), v_s[at, :])
                acc = add if acc is None else acc + add
            total = acc[:, HD:]
            out = acc[:, :HD] / total
            lse_ref[i] = jnp.log2(jnp.transpose(total)[0:8, :])
            for h in range(blocks):
                for u in range(2):
                    o_s[i * blocks + h, :, u * HD : (u + 1) * HD] = out[
                        u * QT + h * BLK : u * QT + (h + 1) * BLK
                    ].astype(BF)

        for i in range(tiles):
            tile(i)
            if i == tiles - 2:
                gather.forward()

        cots[net.me] = cot_ref[...]
        swap = net.take(1)

        @pl.loop(0, n_blocks)
        def _(s):
            mixed[pl.ds(pl.multiple_of(s * BLK, BLK), BLK), :] = o_s[bm[s]]

        away = mixed.at[pl.ds(pl.multiple_of((1 - c) * half, half), half)]
        o_swap = net.copy(swap, away, att.at[c], net.to_core)
        o_swap.start()
        att[c] = mixed[pl.ds(pl.multiple_of(c * half, half), half), :]
        pl.when(jnp.logical_not(own))(lambda: o_core.wait_recv())
        pl.when(jnp.logical_not(own))(lambda: d_core.wait_recv())
        gather.wait_sides()
        gather.wait_diagonal()
        o_swap.wait()
        gather.drain()
        pl.when(own)(lambda: o_core.wait_send())
        pl.when(own)(lambda: d_core.wait_send())

    vm = vmem_spec()
    smem = pl.BlockSpec(memory_space=pltpu.SMEM)
    return pl.pallas_call(
        kernel,
        name="attend",
        out_shape=[
            shape((2, half, 2 * HD), BF),
            shape((length, 2 * HD), BF),
            shape((tiles, 8, 2 * QT), F32),
            shape((4, rows, D), BF),
            shape(wo.shape, BF),
            shape(wd.shape, BF),
        ],
        in_specs=[smem, smem, vm, vm] + [any_spec()] * 2,
        out_specs=[vm] * 6,
        scratch_shapes=[
            pltpu.VMEM((tiles, 2 * QT, HD), BF),
            pltpu.VMEM((length, HD), BF),
            pltpu.VMEM((length, 2 * HD), BF),
            pltpu.VMEM((n_blocks, BLK, 2 * HD), BF),
            pltpu.VMEM(wo.shape, F32),
            pltpu.VMEM(wd.shape, F32),
            pltpu.SemaphoreType.DMA((n_sems,)),
            pltpu.SemaphoreType.DMA((n_sems,)),
            pltpu.SemaphoreType.DMA((2,)),
        ],
        compiler_params=params(1),
        cost_estimate=pl.CostEstimate(
            flops=2 * 2 * 2 * length * length * HD, bytes_accessed=16 * 2**20, transcendentals=0
        ),
    )(block_map, inverse, core.reshape(n_blocks, BLK, 4 * HD), cot, wo, wd)


def feed_forward(att, x_own, wo, wgu, wd, cots, cot_own, gains):
    half = att.shape[1]
    rows = half // 4
    unit = wd.shape[0]
    d_rows = wgu.shape[1]
    d_tiles = unit // 2 // SMALL
    n_sems = 48 + 4 * d_tiles

    def kernel(
        att_ref,
        x_ref,
        wo_ref,
        wgu_ref,
        wd_ref,
        dy_ref,
        cot_ref,
        gain_ref,
        core,
        middle,
        dmiddle,
        result_part,
        sum_gu,
        sum_o,
        total_d,
        mlp_gain_part,
        part,
        got,
        mid,
        n2,
        hid,
        dgu,
        got2,
        mid2,
        dmb,
        gm,
        w_gu,
        got_gu,
        w_d,
        got_d,
        w_o,
        got_o,
        sum_d,
        d_slots,
        ssem,
        rsem,
    ):
        net = Net(ssem, rsem)
        c, me, sx, sy, sd = net.c, net.me, net.sx, net.sy, net.sd
        mlp_gain = gain_ref[1:2, :]
        net.greet()
        out_sum = PlaneSum(net, part, got, mid)

        def chunk(k):
            return pl.ds(pl.multiple_of(k * rows, rows), rows)

        def project(k):
            part[k] = (
                dot_nn(att_ref[0, chunk(k)], wo_ref[0 : 2 * HD, :])
                + dot_nn(att_ref[1, chunk(k)], wo_ref[2 * HD : 4 * HD, :])
            ).astype(BF)

        project(sd)
        out_sum.start_diagonal()
        project(sx)
        project(sy)
        out_sum.start_sides()
        project(me)
        out_sum.forward()

        def add_residual(at, total):
            value = x_ref[at].astype(F32) + total
            middle[at] = value
            n2[me, at] = (value * rms(value) * mlp_gain).astype(BF)

        out_sum.finish(add_residual)
        gather = PlaneGather(net, n2.at[me], n2)
        gather.start()

        def forward_back(k):
            rows_k = n2[k]
            gate_up = dot_nn(rows_k[:, 0:d_rows], wgu_ref[0])
            for g in range(1, 4):
                gate_up = gate_up + dot_nn(rows_k[:, g * d_rows : (g + 1) * d_rows], wgu_ref[g])
            gate, upward = gate_up[:, 0:unit], gate_up[:, unit : 2 * unit]
            sigmoid = 1.0 / (1.0 + jnp.exp(-gate))
            silu = gate * sigmoid
            hid[k] = (silu * upward).astype(BF)
            dh = dot_nt(dy_ref[k], wd_ref[...])
            dgu[k, :, 0:unit] = (
                dh * upward * sigmoid * (1.0 + gate * (1.0 - sigmoid))
            ).astype(BF)
            dgu[k, :, unit : 2 * unit] = (dh * silu).astype(BF)
            grads = dgu[k]
            for g in range(4):
                part[k, :, g * d_rows : (g + 1) * d_rows] = dot_nt(grads, wgu_ref[g]).astype(BF)

        out_sum.drain()
        forward_back(me)
        gather.forward()
        gather.wait_sides()
        back_sum = PlaneSum(net, part, got2, mid2)

        @pl.loop(0, 2)
        def _(n):
            forward_back(jnp.where(n == 0, sx, sy))

        back_sum.start_sides()
        gather.wait_diagonal()
        forward_back(sd)
        back_sum.start_diagonal()

        gu_sem = net.take(2)
        d_sem = net.take(1)
        o_sem = net.take(1)

        def gu_copy(n):
            return net.copy(gu_sem + n, w_gu.at[n], got_gu.at[n], net.to_core)

        d_copy = net.copy(d_sem, w_d, got_d, net.to_core)
        o_copy = net.copy(o_sem, w_o, got_o, net.to_core)
        all_dgu = dgu.shape[2]
        unit_half = unit // 2

        def down(core_of):
            at = pl.ds(pl.multiple_of(core_of * unit_half, unit_half), unit_half)
            return dot_tn(hid[:, :, at].reshape(half, unit_half), dy_ref[...].reshape(half, D))

        line = LineSum(
            net,
            d_tiles,
            lambda k: sum_d.at[pl.ds(pl.multiple_of(k * SMALL, SMALL), SMALL)],
            lambda k: total_d.at[pl.ds(pl.multiple_of(k * SMALL, SMALL), SMALL)],
            d_slots,
            lambda k: None,
        )
        pump = Pump([line], (0, 2, 5, 7))

        w_d[...] = down(1 - c).astype(BF)
        d_copy.start()
        value = down(c)
        d_copy.wait_recv()
        sum_d[...] = (value + got_d[...].astype(F32)).astype(BF)

        @pl.when(line.at_end)
        def _():
            @pl.loop(0, d_tiles)
            def _(k):
                line.gather(k)

        @pl.loop(0, 4)
        def _(k):
            result_part[k] = dot_nn(hid[k], wd_ref[...]).astype(BF)

        back_sum.forward()
        pump.step(0)

        def slab(n, core_of):
            f = 2 * n + core_of
            at = pl.ds(pl.multiple_of(f * d_rows, d_rows), d_rows)
            return dot_tn(n2[:, :, at].reshape(half, d_rows), dgu[...].reshape(half, all_dgu))

        for n in range(2):
            w_gu[n] = slab(n, 1 - c).astype(BF)
            gu_copy(n).start()
            pump.step(1 + n)

        def back_through_norm(at, dn2):
            value = middle[at]
            scale = rms(value)
            w2 = dn2 * mlp_gain
            grad = cot_ref[at].astype(F32) + norm_back(w2, value, scale)
            dmiddle[at] = grad
            dmb[me, at] = grad.astype(BF)
            first = dn2.shape[0] // 8
            folded = jnp.sum((dn2 * value * scale).reshape(first, 8, D), axis=0)
            mlp_gain_part[...] += folded

        mlp_gain_part[...] = jnp.zeros_like(mlp_gain_part)
        back_sum.finish(back_through_norm)
        gather2 = PlaneGather(net, dmb.at[me], dmb)
        gather2.start()
        swap_sem = net.take(4)

        def swap(k):
            return net.copy(
                swap_sem + k, gm.at[1 - c, chunk(k)], core.at[c, chunk(k)], net.to_core
            )

        def grad_mixed(k):
            value = dot_nt(dmb[k], wo_ref[...]).astype(BF)
            gm[0, chunk(k)] = value[:, 0 : 2 * HD]
            gm[1, chunk(k)] = value[:, 2 * HD : 4 * HD]
            swap(k).start()
            core[c, chunk(k)] = gm[c, chunk(k)]

        pump.step(3)
        pump.step(4)
        grad_mixed(me)
        pump.step(5)
        for n in range(2):
            value = slab(n, c)
            gu_copy(n).wait_recv()
            sum_gu[n] = (value + got_gu[n].astype(F32)).astype(BF)
            pump.step(6 + n)

        gather2.forward()
        for n in range(8, 11):
            pump.step(n)
        gather2.wait_sides()

        @pl.loop(0, 2)
        def _(n):
            grad_mixed(jnp.where(n == 0, sx, sy))

        for n in range(11, 14):
            pump.step(n)
        gather2.wait_diagonal()
        grad_mixed(sd)

        def out_grad(g):
            return dot_tn(att_ref[g], dmb[...].reshape(half, D))

        w_o[...] = out_grad(1 - c).astype(BF)
        o_copy.start()
        value = out_grad(c)
        o_copy.wait_recv()
        sum_o[...] = (value + got_o[...].astype(F32)).astype(BF)
        @pl.loop(14, pump.steps())
        def _(p):
            pump.step(p)

        @pl.loop(0, d_tiles)
        def _(k):
            line.drain(k)

        for k in range(4):
            swap(k).wait()
        for n in range(2):
            gu_copy(n).wait_send()
        d_copy.wait_send()
        o_copy.wait_send()
        gather.drain()
        gather2.drain()
        back_sum.drain()

    vm = vmem_spec()
    return pl.pallas_call(
        kernel,
        name="feed_forward",
        out_shape=[
            shape((2, half, 2 * HD), BF),
            shape((rows, D), F32),
            shape((rows, D), F32),
            shape((4, rows, D), BF),
            shape((2, d_rows, 2 * unit), BF),
            shape((2 * HD, D), BF),
            shape((unit // 2, D), BF),
            shape((8, D), F32),
        ],
        in_specs=[vm] * 8,
        out_specs=[vm] * 8,
        scratch_shapes=[
            pltpu.VMEM((4, rows, D), BF),
            pltpu.VMEM((3, rows, D), BF),
            pltpu.VMEM((rows, D), BF),
            pltpu.VMEM((4, rows, D), BF),
            pltpu.VMEM((4, rows, unit), BF),
            pltpu.VMEM((4, rows, 2 * unit), BF),
            pltpu.VMEM((3, rows, D), BF),
            pltpu.VMEM((rows, D), BF),
            pltpu.VMEM((4, rows, D), BF),
            pltpu.VMEM((2, half, 2 * HD), BF),
            pltpu.VMEM((2, d_rows, 2 * unit), BF),
            pltpu.VMEM((2, d_rows, 2 * unit), BF),
            pltpu.VMEM((unit // 2, D), BF),
            pltpu.VMEM((unit // 2, D), BF),
            pltpu.VMEM((2 * HD, D), BF),
            pltpu.VMEM((2 * HD, D), BF),
            pltpu.VMEM((unit // 2, D), BF),
            pltpu.VMEM((2, d_tiles, SMALL, D), BF),
            pltpu.SemaphoreType.DMA((n_sems,)),
            pltpu.SemaphoreType.DMA((n_sems,)),
        ],
        compiler_params=params(2, 62),
        cost_estimate=pl.CostEstimate(
            flops=24 * half * D * unit, bytes_accessed=32 * 2**20, transcendentals=0
        ),
    )(att, x_own, wo, wgu, wd, cots, cot_own, gains)


def finish_back(
    block_map,
    inverse,
    core,
    mixed,
    grad,
    lse,
    sum_o,
    total_d,
    sum_gu,
    result_part,
    middle,
    raw,
    table,
    n1,
    wall,
    x_own,
    dmiddle,
    gains,
    mlp_gain_part,
):
    half = core.shape[1]
    length = 2 * half
    blocks = QT // BLK
    n_blocks = length // BLK
    wide = 2 * QT
    tiles = length // wide
    scale = HD ** (-0.5)
    factor = scale * LOG2E
    rows = middle.shape[0]
    d_rows = wall.shape[1]
    gu_cols = sum_gu.shape[2]
    unit = gu_cols // 2
    o_tiles = sum_o.shape[0] // SMALL
    per = d_rows // SMALL
    w_tiles = 2 * per
    n_sems = 7 * o_tiles + 10 * w_tiles + 90

    def kernel(
        bm,
        inv,
        core_hbm,
        mixed_hbm,
        grad_hbm,
        lse_ref,
        o_part,
        d_ref,
        gu_ref,
        rp_hbm,
        mid_hbm,
        raw_hbm,
        table_hbm,
        n1_hbm,
        wall_hbm,
        x_hbm,
        dmid_hbm,
        gain_ref,
        mlp_ref,
        result,
        input_out,
        o_final,
        d_final,
        out_q,
        out_k,
        out_v,
        out_g,
        out_u,
        gain_out,
        dq,
        d_s,
        result_part_s,
        part,
        res,
        got,
        mid,
        grad_in,
        got2,
        mid2,
        o_slots,
        o_sum,
        gu_rows,
        gu_slots,
        gu_mine,
        gu_other,
        w_out,
        w_got,
        w_sum,
        w_rows,
        w_slots,
        w_mine,
        w_other,
        g_sum,
        g_got,
        g_slots,
        g_mine,
        acc,
        ssem,
        rsem,
        lsem,
    ):
        net = Net(ssem, rsem)
        z, x, y, c = net.z, net.x, net.y, net.c
        load_part = pltpu.make_async_copy(rp_hbm, result_part_s, lsem.at[0])
        load_part.start()
        net.greet(True, True, mate=True)
        total = PlaneSum(net, result_part_s, got, mid, rows // 4)
        total2 = PlaneSum(net, part, got2, mid2, rows // 4)
        gu_y = net.new(gu_ref.at[1 - y], gu_rows.at[1], net.to_y)
        home = Fetch(net, res, result)
        home2 = Fetch(net, grad_in, input_out)
        swap = net.new(
            d_s.at[pl.ds(pl.multiple_of((1 - c) * half, half), half)], dq.at[c], net.to_core
        )
        x_sem = net.take(2 * o_tiles)
        chip_sem = net.take(o_tiles)
        owner = device(z, 1 - x, y, x)
        owns = c == x

        def cross(k, h):
            return net.copy(x_sem + h * o_tiles + k, o_sum.at[k], o_final.at[h, k], owner)

        def chip(k, h):
            return net.copy(chip_sem + k, o_sum.at[k], o_final.at[h, k], net.to_core)

        def deliver(k):
            cross(k, c).start()

            @pl.when(owns)
            def _():
                o_final[c, k] = o_sum[k]

            pl.when(jnp.logical_not(owns))(lambda: chip(k, c).start())

        d_x = [net.new(d_ref, d_final.at[h], owner) for h in range(2)]
        d_chip = net.new(d_ref, d_final.at[c], net.to_core)
        gx_sem = net.take(w_tiles)
        wx_sem = net.take(w_tiles)

        def gu_cross(k):
            return net.copy(gx_sem + k, gu_mine.at[k], gu_other.at[k], net.to_x)

        def w_cross(k):
            return net.copy(wx_sem + k, w_mine.at[k], w_other.at[k], net.to_x)

        def row_tile(ref):
            def at(k):
                first = pl.multiple_of(lax.rem(k, per) * SMALL, SMALL)
                return ref.at[lax.div(k, per), pl.ds(first, SMALL)]

            return at

        o_line = LineSum(
            net,
            o_tiles,
            lambda k: o_part.at[pl.ds(pl.multiple_of(k * SMALL, SMALL), SMALL)],
            lambda k: o_sum.at[k],
            o_slots,
            deliver,
        )
        gu_line = LineSum(
            net,
            w_tiles,
            row_tile(gu_rows),
            lambda k: gu_mine.at[k],
            gu_slots,
            lambda k: gu_cross(k).start(),
        )
        w_line = LineSum(
            net,
            w_tiles,
            row_tile(w_rows),
            lambda k: w_mine.at[k],
            w_slots,
            lambda k: w_cross(k).start(),
        )
        g_line = LineSum(
            net, 1, lambda k: g_sum.at[0], lambda k: g_mine.at[0], g_slots, lambda k: None
        )
        pump = Pump([o_line, gu_line, w_line], (1, 3, 5, 7))
        gu_first, w_first = o_tiles, o_tiles + w_tiles

        def rows_come(s):
            if isinstance(s, int):
                if s == gu_first + per:
                    gu_y.wait_recv()
                if s == w_first + per:
                    w_y.wait_recv()
            else:
                pl.when(s == gu_first + per)(gu_y.wait_recv)
                pl.when(s == w_first + per)(w_y.wait_recv)

        w_y = net.new(w_sum, w_rows.at[1], net.to_y)
        state = [0]

        def pump_on(count=1):
            for _ in range(count):
                pump.step(state[0], rows_come)
                state[0] += 1

        def ends(line, first, last):
            @pl.when(line.at_end)
            def _():
                @pl.loop(first, last)
                def _(k):
                    line.gather(k)

        gu_y.start()
        ends(o_line, 0, o_tiles)
        load_part.wait()
        total.start_diagonal()
        total.start_sides()
        gu_rows[0] = gu_ref[y]
        ends(gu_line, 0, per)
        for h in range(2):
            pl.when(c == h)(d_x[h].start)
        pl.when(jnp.logical_not(owns))(d_chip.start)

        d_keep = pltpu.make_async_copy(d_ref, d_final.at[c], lsem.at[11])
        pl.when(owns)(d_keep.start)
        def attention(x_s, o_s, g_in, q_s, g_s, k_s, v_s, delta_s):
            loads = [
                pltpu.make_async_copy(a, b, lsem.at[1 + n])
                for n, (a, b) in enumerate(((core_hbm, x_s), (mixed_hbm, o_s), (grad_hbm, g_in)))
            ]
            for cp in loads:
                cp.start()
            for cp in loads:
                cp.wait()
            for i in range(2 * tiles):
                for h in range(blocks):
                    s = inv[i * blocks + h]
                    block, out, grad_ = x_s[s], o_s[s], g_in[s]
                    at = slice((i * blocks + h) * BLK, (i * blocks + h + 1) * BLK)
                    for u in range(2):
                        first = (i % 2) * 2 * QT + u * QT + h * BLK
                        to = slice(first, first + BLK)
                        lanes = slice(u * HD, (u + 1) * HD)
                        q_s[i // 2, to, :] = block[:, lanes]
                        g_s[i // 2, to, :] = grad_[:, lanes]
                        product = grad_[:, lanes].astype(F32) * out[:, lanes].astype(F32)
                        delta_s[i // 2, :, to] = jnp.broadcast_to(
                            jnp.sum(jnp.transpose(product), axis=0, keepdims=True), (8, BLK)
                        )
                    k_s[at, :] = block[:, 2 * HD : 3 * HD]
                    v_s[at, :] = block[:, 3 * HD : 4 * HD]
                if i % 3 == 1:
                    pump_on()

            k_row = lax.broadcasted_iota(jnp.int32, (wide, 2 * wide), 0)
            q_row = lax.broadcasted_iota(jnp.int32, (wide, 2 * wide), 1)
            q_row = lax.shift_right_logical(q_row, 9) * QT + lax.bitwise_and(q_row, QT - 1)
            allowed = q_row >= k_row
            dq_t = [None] * tiles
            for j in range(tiles):
                at = slice(j * wide, (j + 1) * wide)
                k, v = k_s[at, :], v_s[at, :]
                k_t = jnp.transpose(k)
                dk = dv = None
                for i in range(j, tiles):
                    q, g = q_s[i], g_s[i]
                    shift = jnp.concatenate(
                        [lse_ref[2 * i, 0:1, :], lse_ref[2 * i + 1, 0:1, :]], 1
                    )
                    scores = dot_nt(k, q) * factor - shift
                    if i == j:
                        scores = jnp.where(allowed, scores, NEG)
                    p = jnp.exp2(scores)
                    ds = (p * (dot_nt(v, g) - delta_s[i, 0:1, :])).astype(BF)
                    add = dot_nn(k_t, ds)
                    dq_t[i] = add if dq_t[i] is None else dq_t[i] + add
                    add_k, add_v = dot_nn(ds, q), dot_nn(p.astype(BF), g)
                    dk = add_k if dk is None else dk + add_k
                    dv = add_v if dv is None else dv + add_v
                    pump_on()
                for h in range(wide // BLK):
                    part_ = slice(h * BLK, (h + 1) * BLK)
                    b = j * (wide // BLK) + h
                    x_s[b, :, 2 * HD : 3 * HD] = (dk[part_] * scale).astype(BF)
                    x_s[b, :, 3 * HD : 4 * HD] = dv[part_].astype(BF)
                dq_j = jnp.transpose(dq_t[j]) * scale
                for e in range(2):
                    for u in range(2):
                        for h in range(blocks):
                            first = e * 2 * QT + u * QT + h * BLK
                            x_s[(2 * j + e) * blocks + h, :, u * HD : (u + 1) * HD] = dq_j[
                                first : first + BLK
                            ].astype(BF)

            @pl.loop(0, n_blocks)
            def _(s):
                d_s[pl.ds(pl.multiple_of(s * BLK, BLK), BLK), :] = x_s[bm[s]]

        pl.run_scoped(
            attention,
            pltpu.VMEM((n_blocks, BLK, 4 * HD), BF),
            pltpu.VMEM((n_blocks, BLK, 2 * HD), BF),
            pltpu.VMEM((n_blocks, BLK, 2 * HD), BF),
            pltpu.VMEM((tiles, 2 * wide, HD), BF),
            pltpu.VMEM((tiles, 2 * wide, HD), BF),
            pltpu.VMEM((length, HD), BF),
            pltpu.VMEM((length, HD), BF),
            pltpu.VMEM((tiles, 8, 2 * wide), F32),
        )
        swap.start()
        dq[c] = d_s[pl.ds(pl.multiple_of(c * half, half), half), :]

        @pl.when(gu_line.at_end)
        def _():
            gu_y.wait_recv()

        ends(gu_line, per, w_tiles)
        pump_on()

        def norms(raw_ref, table_ref, n1_ref, wall_ref, x_ref, dmid_ref, mid_ref, dcat):
            loads = [
                pltpu.make_async_copy(a, b, lsem.at[4 + n])
                for n, (a, b) in enumerate(
                    (
                        (raw_hbm, raw_ref),
                        (table_hbm, table_ref),
                        (n1_hbm, n1_ref),
                        (wall_hbm, wall_ref),
                        (x_hbm, x_ref),
                        (dmid_hbm, dmid_ref),
                        (mid_hbm, mid_ref),
                    )
                )
            ]
            for cp in loads:
                cp.start()
            swap.wait_recv()
            for cp in loads:
                cp.wait()
            attn_gain, q_gain, k_gain = gain_ref[0:1, :], gain_ref[2:3, 0:HD], gain_ref[3:4, 0:HD]
            acc[...] = jnp.zeros_like(acc)

            def fold(v):
                return jnp.sum(v.reshape(v.shape[0] // 8, 8, v.shape[1]), axis=0)

            def chunk(k):
                at = pl.ds(pl.multiple_of(k * rows, rows), rows)
                half_w = HD // 2
                cosine, sine = table_ref[at, 0:half_w], table_ref[at, half_w:HD]
                cosine = jnp.concatenate([cosine, cosine], axis=-1)
                sine = jnp.concatenate([-sine, sine], axis=-1)
                for h in range(6):
                    g, lane = (h // 2, (h % 2) * HD) if h < 4 else (h - 4, 2 * HD)
                    gain = q_gain if h < 4 else k_gain
                    grad_ = dq[g, at, lane : lane + HD].astype(F32)
                    du = grad_ * cosine - pltpu.roll(grad_, half_w, 1) * sine
                    u = raw_ref[at, h * HD : (h + 1) * HD]
                    size = rms(u)
                    lanes = slice(0, HD) if h < 4 else slice(HD, 2 * HD)
                    acc[2, :, lanes] += fold(du * u * size)
                    dcat[at, h * HD : (h + 1) * HD] = norm_back(du * gain, u, size).astype(BF)
                for g in range(2):
                    dcat[at, (6 + g) * HD : (7 + g) * HD] = dq[g, at, 3 * HD : 4 * HD]

            def project(k):
                d = dcat[pl.ds(pl.multiple_of(k * rows, rows), rows), :]
                for g in range(4):
                    part[k, :, g * d_rows : (g + 1) * d_rows] = dot_nt(d, wall_ref[g]).astype(BF)

            def add(at, value):
                res[at] = (mid_ref[at] + value).astype(BF)

            chunk(net.sd)
            pump_on()
            project(net.sd)
            total2.start_diagonal()
            pump_on()
            total.forward()
            for k in (net.sx, net.sy):
                chunk(k)
                pump_on()
                project(k)
                pump_on()
            total2.start_sides()
            chunk(net.me)
            pump_on()
            project(net.me)
            total2.forward()
            pump_on()

            def slab(n, core_of):
                f = 2 * n + core_of
                at = pl.ds(pl.multiple_of(f * d_rows, d_rows), d_rows)
                return dot_tn(n1_ref[:, at], dcat[...])

            w_sem = net.take(2)

            def w_copy(n):
                return net.copy(w_sem + n, w_out.at[n], w_got.at[n], net.to_core)

            for n in range(2):
                w_out[n] = slab(n, 1 - c).astype(BF)
                w_copy(n).start()
                pump_on()
            total.finish(add)
            home.start()
            value = slab(1 - y, c)
            w_copy(1 - y).wait_recv()
            w_sum[...] = (value + w_got[1 - y].astype(F32)).astype(BF)
            w_y.start()
            pump_on()
            value = slab(y, c)
            w_copy(y).wait_recv()
            w_rows[0] = (value + w_got[y].astype(F32)).astype(BF)
            ends(w_line, 0, per)
            pump_on()

            def back_through_norm(at, dn1):
                value = x_ref[at].astype(F32)
                size = rms(value)
                acc[0] += fold(dn1 * value * size)
                grad_in[at] = (dmid_ref[at] + norm_back(dn1 * attn_gain, value, size)).astype(BF)

            total2.finish(back_through_norm)
            for n in range(2):
                w_copy(n).wait_send()

        pl.run_scoped(
            norms,
            pltpu.VMEM(raw.shape, F32),
            pltpu.VMEM(table.shape, F32),
            pltpu.VMEM(n1.shape, BF),
            pltpu.VMEM(wall.shape, BF),
            pltpu.VMEM((rows, D), BF),
            pltpu.VMEM((rows, D), F32),
            pltpu.VMEM((rows, D), F32),
            pltpu.VMEM((half, 8 * HD), BF),
        )
        home2.start()
        pump_on()

        def place(k, slots, copies, outs, widths):
            copies(k).wait_recv()
            row_half = jnp.where(k < per, y, 1 - y)
            at = pl.ds(pl.multiple_of(lax.rem(k, per) * SMALL, SMALL), SMALL)
            for tile, x_of in zip(slots, (x, 1 - x)):
                quarter = 2 * row_half + x_of
                first = 0
                for out, width in zip(outs, widths):
                    lanes = pl.ds(pl.multiple_of(quarter * width, width), width)
                    out[at, lanes] = tile[k, :, first : first + width]
                    first += width

        def place_gu(k):
            place(k, (gu_mine, gu_other), gu_cross, (out_g, out_u), (unit, unit))

        def place_w(k):
            place(k, (w_mine, w_other), w_cross, (out_q, out_k, out_v), (4 * HD, 2 * HD, 2 * HD))

        acc[1] = mlp_ref[...]
        for row in range(3):
            g_sum[0, row : row + 1, :] = jnp.sum(acc[row], axis=0, keepdims=True)
        g_sum[0, 3:8, :] = jnp.zeros((5, D), F32)
        for n, to in enumerate((net.to_core, net.to_y, net.to_x)):
            cp = net.new(g_sum.at[0], g_got.at[n], to)
            cp.start()
            pump_on()
            cp.wait()
            g_sum[0] = g_sum[0] + g_got[n]
        g_line.gather(0)

        @pl.when(w_line.at_end)
        def _():
            w_y.wait_recv()

        ends(w_line, per, w_tiles)
        so_far = state[0]
        place_lag = 14

        @pl.loop(0, so_far - place_lag - gu_first)
        def _(k):
            place_gu(k)

        @pl.loop(so_far, pump.steps())
        def _(p):
            pump.step(p, rows_come)
            q = p - place_lag
            pl.when(within(q, gu_first, w_first))(lambda: place_gu(q - gu_first))
            pl.when(within(q, w_first, w_first + w_tiles))(lambda: place_w(q - w_first))

        g_line.finish(0)
        gain_out[...] = g_mine[0]

        @pl.loop(pump.steps() - place_lag - w_first, w_tiles)
        def _(k):
            place_w(k)

        @pl.loop(0, o_tiles)
        def _(k):
            @pl.when(owns)
            def _():
                chip(k, 1 - c).wait_recv()

            @pl.when(jnp.logical_not(owns))
            def _():
                for h in range(2):
                    cross(k, h).wait_recv()
                chip(k, c).wait_send()

            cross(k, c).wait_send()
            o_line.drain(k)

        @pl.when(owns)
        def _():
            d_chip.wait_recv()
            d_keep.wait()

        @pl.when(jnp.logical_not(owns))
        def _():
            for h in range(2):
                d_x[h].wait_recv()
            d_chip.wait_send()

        for h in range(2):
            pl.when(c == h)(d_x[h].wait_send)

        @pl.loop(0, w_tiles)
        def _(k):
            gu_line.drain(k)
            w_line.drain(k)
            gu_cross(k).wait_send()
            w_cross(k).wait_send()

        g_line.drain(0)
        gu_y.wait_send()
        w_y.wait_send()
        swap.wait_send()
        total.drain()
        total2.drain()
        for item in (home, home2):
            item.wait()
            item.drain()

    vm = vmem_spec()
    hbm = any_spec()
    smem = pl.BlockSpec(memory_space=pltpu.SMEM)
    chunk_ = pltpu.VMEM((rows, D), BF)
    four = pltpu.VMEM((4, rows, D), BF)
    three = pltpu.VMEM((3, rows, D), BF)
    gu_tiles = pltpu.VMEM((w_tiles, SMALL, gu_cols), BF)
    gu_pairs = pltpu.VMEM((2, w_tiles, SMALL, gu_cols), BF)
    qkv_tiles = pltpu.VMEM((w_tiles, SMALL, 8 * HD), BF)
    qkv_pairs = pltpu.VMEM((2, w_tiles, SMALL, 8 * HD), BF)
    g_tile = pltpu.VMEM((1, 8, D), F32)
    slabs = pltpu.VMEM((2, d_rows, 8 * HD), BF)
    return pl.pallas_call(
        kernel,
        name="finish_back",
        out_shape=[
            shape((rows, D), BF),
            shape((rows, D), BF),
            shape((2, o_tiles, SMALL, D), BF),
            shape((2,) + total_d.shape, BF),
            shape((d_rows, 16 * HD), BF),
            shape((d_rows, 8 * HD), BF),
            shape((d_rows, 8 * HD), BF),
            shape((d_rows, 4 * unit), BF),
            shape((d_rows, 4 * unit), BF),
            shape((8, D), F32),
        ],
        in_specs=[smem, smem] + [hbm] * 3 + [vm] * 4 + [hbm] * 8 + [vm] * 2,
        out_specs=[vm] * 3 + [hbm] + [vm] * 6,
        scratch_shapes=[
            pltpu.VMEM((2, half, 4 * HD), BF),
            pltpu.VMEM((length, 4 * HD), BF),
            four,
            four,
            chunk_,
            three,
            chunk_,
            chunk_,
            three,
            chunk_,
            pltpu.VMEM((2, o_tiles, SMALL, D), BF),
            pltpu.VMEM((o_tiles, SMALL, D), BF),
            pltpu.VMEM(sum_gu.shape, BF),
            gu_pairs,
            gu_tiles,
            gu_tiles,
            slabs,
            slabs,
            pltpu.VMEM((d_rows, 8 * HD), BF),
            slabs,
            qkv_pairs,
            qkv_tiles,
            qkv_tiles,
            g_tile,
            pltpu.VMEM((3, 8, D), F32),
            pltpu.VMEM((2, 1, 8, D), F32),
            g_tile,
            pltpu.VMEM((3, 8, D), F32),
            pltpu.SemaphoreType.DMA((n_sems,)),
            pltpu.SemaphoreType.DMA((n_sems,)),
            pltpu.SemaphoreType.DMA((12,)),
        ],
        compiler_params=params(3, 63),
        cost_estimate=pl.CostEstimate(
            flops=5 * 2 * 2 * length * length * HD, bytes_accessed=32 * 2**20, transcendentals=0
        ),
    )(
        block_map,
        inverse,
        core.reshape(n_blocks, BLK, 4 * HD),
        mixed.reshape(n_blocks, BLK, 2 * HD),
        grad.reshape(n_blocks, BLK, 2 * HD),
        lse,
        sum_o,
        total_d,
        sum_gu,
        result_part,
        middle,
        raw,
        table,
        n1,
        wall,
        x_own,
        dmiddle,
        gains,
        mlp_gain_part,
    )


def widen(arrays, gain_sums, parts, steps=8):
    n = len(arrays)
    d_part, h_part = D // parts, HD // parts

    def kernel(*refs):
        for a, b in zip(refs[:n], refs[n + 1 : 2 * n + 1]):
            b[...] = a[...].astype(F32)
        sums = refs[n]
        attn, mlp, query, key = refs[2 * n + 1 :]

        @pl.when(pl.program_id(0) == 0)
        def _():
            f = lax.axis_index("fsdp")
            at = pl.ds(pl.multiple_of(f * d_part, d_part), d_part)
            attn[...] = sums[0:1, at]
            mlp[...] = sums[1:2, at]
            for out, first in ((query, 0), (key, HD)):
                turned = pltpu.roll(sums[0:8, first : first + HD], HD - f * h_part, 1)
                out[...] = turned[2:3, 0:h_part]

    def spec(a):
        return pl.BlockSpec((a.shape[0] // steps, a.shape[1]), lambda i: (i, 0))

    def whole(dims):
        return pl.BlockSpec(dims, lambda i: (0, 0))

    small = [(1, d_part), (1, d_part), (1, h_part), (1, h_part)]
    return pl.pallas_call(
        kernel,
        name="widen",
        grid=(steps,),
        out_shape=[shape(a.shape, F32) for a in arrays] + [shape(s, F32) for s in small],
        in_specs=[spec(a) for a in arrays] + [whole(gain_sums.shape)],
        out_specs=[spec(a) for a in arrays] + [whole(s) for s in small],
        compiler_params=pltpu.CompilerParams(vmem_limit_bytes=62 * 2**20),
    )(*arrays, gain_sums)


def plane_body(
    tokens,
    cotangent,
    block_map,
    positions,
    attn_gain,
    query_weight,
    key_weight,
    value_weight,
    query_gain,
    key_gain,
    out_weight,
    mlp_gain,
    gate_weight,
    up_weight,
    down_weight,
):
    rows = tokens.shape[1]
    parts = lax.axis_size("fsdp")
    flat_map = block_map.reshape(-1)
    n_blocks = flat_map.shape[0]
    order = jnp.arange(n_blocks, dtype=jnp.int32)
    inverse = jnp.sum(
        jnp.where(flat_map[None, :] == order[:, None], order[None, :], 0), axis=1
    ).astype(jnp.int32)
    x_own, n1, raw, table, core, wall, gains, cot_own, wgu = enter(
        tokens.reshape(rows, D),
        cotangent.reshape(rows, D),
        positions,
        [g.reshape(1, -1) for g in (attn_gain, mlp_gain, query_gain, key_gain)],
        query_weight,
        key_weight,
        value_weight,
        gate_weight,
        up_weight,
    )
    att, mixed, lse, cots, wo, wd = attend(
        flat_map, inverse, core, cot_own, out_weight, down_weight
    )
    grad, middle, dmiddle, result_part, sum_gu, sum_o, total_d, mlp_gain_part = feed_forward(
        att, x_own, wo, wgu, wd, cots, cot_own, gains
    )
    (
        result,
        input_grad,
        grad_o,
        grad_d,
        grad_q,
        grad_k,
        grad_v,
        grad_g,
        grad_u,
        gain_sums,
    ) = finish_back(
        flat_map,
        inverse,
        core,
        mixed,
        grad,
        lse,
        sum_o,
        total_d,
        sum_gu,
        result_part,
        middle,
        raw,
        table,
        n1,
        wall,
        x_own,
        dmiddle,
        gains,
        mlp_gain_part,
    )

    (
        result,
        input_grad,
        grad_q,
        grad_k,
        grad_v,
        grad_o,
        grad_g,
        grad_u,
        grad_d,
        *gain_grads,
    ) = widen(
        [
            result,
            input_grad,
            grad_q,
            grad_k,
            grad_v,
            grad_o.reshape(out_weight.shape),
            grad_g,
            grad_u,
            grad_d.reshape(down_weight.shape),
        ],
        gain_sums,
        parts,
    )
    attn_grad, mlp_grad, query_grad, key_grad = [g.reshape(-1) for g in gain_grads]
    return (
        result.reshape(tokens.shape),
        input_grad.reshape(tokens.shape),
        attn_grad,
        grad_q,
        grad_k,
        grad_v,
        query_grad,
        key_grad,
        grad_o,
        mlp_grad,
        grad_g,
        grad_u,
        grad_d,
    )


def solution(mesh):
    placed = (
        P("fsdp", "ctx", None),
        P("fsdp", "ctx", None),
        P(),
        P("fsdp", "ctx"),
        P("fsdp"),
        P("fsdp", None),
        P("fsdp", None),
        P("fsdp", None),
        P("fsdp"),
        P("fsdp"),
        P("fsdp", None),
        P("fsdp"),
        P("fsdp", None),
        P("fsdp", None),
        P("fsdp", None),
    )
    fits = mesh.shape["fsdp"] == 4 and mesh.shape["ctx"] == 8
    return jax.shard_map(
        plane_body if fits else body,
        mesh=mesh,
        in_specs=placed,
        out_specs=(
            P("fsdp", "ctx", None),
            P("fsdp", "ctx", None),
            P("fsdp"),
            P("fsdp", None),
            P("fsdp", None),
            P("fsdp", None),
            P("fsdp"),
            P("fsdp"),
            P("fsdp", None),
            P("fsdp"),
            P("fsdp", None),
            P("fsdp", None),
            P("fsdp", None),
        ),
        check_vma=False,
    )
```

```python
import math

import jax
import jax.numpy as jnp
from jax import lax
from jax.experimental import pallas as pl
from jax.experimental.pallas import tpu as pltpu
from jax.sharding import PartitionSpec as P

D = 1024
HQ = 16
HK = 8
HD = 128
BLK = 128


epsilon = 1e-06
theta_base = 1000000.0
masked_value = -1e30


def rms_scale(values):
    return lax.rsqrt(jnp.mean(values * values, axis=-1, keepdims=True) + epsilon)


def norm_back(upstream, values, scale):
    return scale * upstream - values * (scale * scale * scale) * jnp.mean(
        upstream * values, axis=-1, keepdims=True
    )


def rope_tables(positions, head_dim):
    frequency = jnp.exp(
        jnp.arange(0, head_dim, 2).astype(jnp.float32) * (-math.log(theta_base) / head_dim)
    )
    angles = positions.astype(jnp.float32)[..., None] * frequency
    angles = jnp.concatenate([angles, angles], axis=-1)
    return (jnp.cos(angles), jnp.sin(angles))


def rotate(values, cosine, sine_table):
    half_width = values.shape[-1] // 2
    turned = jnp.concatenate([-values[..., half_width:], values[..., :half_width]], axis=-1)
    return values * cosine + turned * sine_table


def unrotate(grads, cosine, sine_table):
    half_width = grads.shape[-1] // 2
    moved = grads * sine_table
    back_turn = jnp.concatenate([moved[..., half_width:], -moved[..., :half_width]], axis=-1)
    return grads * cosine + back_turn


def score_block(grouped, keys_head, allowed, scale):
    scores = (
        jnp.einsum("qgd,sd->gqs", grouped, keys_head, preferred_element_type=jnp.float32) * scale
    )
    return jnp.where(allowed, scores, masked_value)


def body(
    tokens,
    cotangent,
    block_map,
    positions,
    attn_gain,
    query_weight,
    key_weight,
    value_weight,
    query_gain,
    key_gain,
    out_weight,
    mlp_gain,
    gate_weight,
    up_weight,
    down_weight,
):
    seq_count = tokens.shape[0]
    seq_rows = tokens.shape[1]
    total_rows = seq_count * seq_rows
    groups = HQ // HK
    scale = HD ** (-0.5)
    attn_full, query_full, key_full, mlp_full = (
        lax.all_gather(attn_gain, "fsdp", axis=0, tiled=True),
        lax.all_gather(query_gain, "fsdp", axis=0, tiled=True),
        lax.all_gather(key_gain, "fsdp", axis=0, tiled=True),
        lax.all_gather(mlp_gain, "fsdp", axis=0, tiled=True),
    )
    query_w, key_w, value_w, out_w = (
        lax.all_gather(query_weight.astype(jnp.bfloat16), "fsdp", axis=0, tiled=True),
        lax.all_gather(key_weight.astype(jnp.bfloat16), "fsdp", axis=0, tiled=True),
        lax.all_gather(value_weight.astype(jnp.bfloat16), "fsdp", axis=0, tiled=True),
        lax.all_gather(out_weight.astype(jnp.bfloat16), "fsdp", axis=0, tiled=True),
    )
    flat = tokens.astype(jnp.float32).reshape(total_rows, D)
    scale_one = rms_scale(flat)
    normed = (flat * scale_one * attn_full).astype(jnp.bfloat16)
    query_raw = jnp.dot(normed, query_w, preferred_element_type=jnp.float32).reshape(
        total_rows, HQ, HD
    )
    key_raw = jnp.dot(normed, key_w, preferred_element_type=jnp.float32).reshape(total_rows, HK, HD)
    value_low = jnp.dot(normed, value_w, preferred_element_type=jnp.float32).astype(jnp.bfloat16)
    cosine, sine_table = rope_tables(positions.reshape(total_rows), HD)
    cosine = cosine[:, None, :]
    sine_table = sine_table[:, None, :]
    query_scale = rms_scale(query_raw)
    query_unit = query_raw * query_scale
    query_low = rotate(query_unit * query_full, cosine, sine_table).astype(jnp.bfloat16)
    key_scale = rms_scale(key_raw)
    key_unit = key_raw * key_scale
    key_low = rotate(key_unit * key_full, cosine, sine_table).astype(jnp.bfloat16)
    flat_map = block_map.reshape(-1)
    offsets = jnp.arange(BLK, dtype=jnp.int32)
    key_index = (flat_map[:, None] * BLK + offsets[None, :]).reshape(-1)
    own_blocks = lax.dynamic_slice_in_dim(flat_map, lax.axis_index("ctx") * 2, 2)
    query_index = (own_blocks[:, None] * BLK + offsets[None, :]).reshape(-1)
    allowed = query_index[:, None] >= key_index[None, :]
    query_seq = query_low.reshape(seq_count, seq_rows, HK, groups, HD)
    key_seq = key_low.reshape(seq_count, seq_rows, HK * HD)
    value_seq = value_low.reshape(seq_count, seq_rows, HK * HD)

    def forward_head(inputs):
        grouped, keys_head, values_head = inputs
        scores = score_block(grouped, keys_head, allowed, scale)
        row_max = jnp.max(scores, axis=-1, keepdims=True)
        exp_scores = jnp.exp(scores - row_max)
        row_total = jnp.sum(exp_scores, axis=-1, keepdims=True)
        prob_low = (exp_scores / row_total).astype(jnp.bfloat16)
        mixed = jnp.einsum("gqs,sd->qgd", prob_low, values_head, preferred_element_type=jnp.float32)
        return (mixed, row_max + jnp.log(row_total))

    seq_item = 0
    keys_all = lax.all_gather(key_seq[seq_item], "ctx", axis=0, tiled=True)
    values_all = lax.all_gather(value_seq[seq_item], "ctx", axis=0, tiled=True)
    keys_head = jnp.transpose(keys_all.reshape(-1, HK, HD), (1, 0, 2))
    values_head = jnp.transpose(values_all.reshape(-1, HK, HD), (1, 0, 2))
    grouped_head = jnp.transpose(query_seq[seq_item], (1, 0, 2, 3))
    mixed, lse = lax.map(forward_head, (grouped_head, keys_head, values_head))
    mixed_parts = jnp.transpose(mixed, (1, 0, 2, 3)).reshape(seq_rows, HQ * HD)
    lse_parts = [lse]
    gathered = [(grouped_head, keys_head, values_head)]
    attended = mixed_parts.astype(jnp.bfloat16)
    middle = flat + jnp.dot(attended, out_w, preferred_element_type=jnp.float32)
    gate_w, up_w, down_w = (
        lax.all_gather(gate_weight.astype(jnp.bfloat16), "fsdp", axis=0, tiled=True),
        lax.all_gather(up_weight.astype(jnp.bfloat16), "fsdp", axis=0, tiled=True),
        lax.all_gather(down_weight.astype(jnp.bfloat16), "fsdp", axis=0, tiled=True),
    )
    scale_two = rms_scale(middle)
    normed_two = (middle * scale_two * mlp_full).astype(jnp.bfloat16)
    gate = jnp.dot(normed_two, gate_w, preferred_element_type=jnp.float32)
    upward = jnp.dot(normed_two, up_w, preferred_element_type=jnp.float32)
    sigmoid_gate = jax.nn.sigmoid(gate)
    silu_gate = gate * sigmoid_gate
    hidden = (silu_gate * upward).astype(jnp.bfloat16)
    result = middle + jnp.dot(hidden, down_w, preferred_element_type=jnp.float32)
    query_back, key_back, value_back, out_back = (
        lax.all_gather(query_weight.astype(jnp.bfloat16), "fsdp", axis=0, tiled=True),
        lax.all_gather(key_weight.astype(jnp.bfloat16), "fsdp", axis=0, tiled=True),
        lax.all_gather(value_weight.astype(jnp.bfloat16), "fsdp", axis=0, tiled=True),
        lax.all_gather(out_weight.astype(jnp.bfloat16), "fsdp", axis=0, tiled=True),
    )
    gate_back, up_back, down_back = (
        lax.all_gather(gate_weight.astype(jnp.bfloat16), "fsdp", axis=0, tiled=True),
        lax.all_gather(up_weight.astype(jnp.bfloat16), "fsdp", axis=0, tiled=True),
        lax.all_gather(down_weight.astype(jnp.bfloat16), "fsdp", axis=0, tiled=True),
    )
    grad_out = cotangent.astype(jnp.float32).reshape(total_rows, D)
    grad_branch = grad_out.astype(jnp.bfloat16)
    down_grad = jnp.einsum("nf,nd->fd", hidden, grad_branch, preferred_element_type=jnp.float32)
    grad_hidden = jnp.einsum(
        "nd,fd->nf", grad_branch, down_back, preferred_element_type=jnp.float32
    )
    grad_gate = (grad_hidden * upward * sigmoid_gate * (1.0 + gate * (1.0 - sigmoid_gate))).astype(
        jnp.bfloat16
    )
    grad_up = (grad_hidden * silu_gate).astype(jnp.bfloat16)
    gate_grad = jnp.einsum("nd,nf->df", normed_two, grad_gate, preferred_element_type=jnp.float32)
    up_grad = jnp.einsum("nd,nf->df", normed_two, grad_up, preferred_element_type=jnp.float32)
    grad_normed_two = jnp.einsum(
        "nf,df->nd", grad_gate, gate_back, preferred_element_type=jnp.float32
    ) + jnp.einsum("nf,df->nd", grad_up, up_back, preferred_element_type=jnp.float32)
    mlp_local = jnp.sum(grad_normed_two * middle * scale_two, axis=0)
    grad_middle = grad_out + norm_back(grad_normed_two * mlp_full, middle, scale_two)
    grad_attn_low = grad_middle.astype(jnp.bfloat16)
    out_grad = jnp.einsum("nq,nd->qd", attended, grad_attn_low, preferred_element_type=jnp.float32)
    grad_mixed = jnp.einsum(
        "nd,qd->nq", grad_attn_low, out_back, preferred_element_type=jnp.float32
    ).astype(jnp.bfloat16)
    grad_mixed_seq = grad_mixed.reshape(seq_count, seq_rows, HK, groups, HD)

    def backward_head(inputs):
        grouped, keys_head, values_head, grad_head, lse = inputs
        scores = score_block(grouped, keys_head, allowed, scale)
        prob_full = jnp.exp(scores - lse)
        grad_prob = jnp.einsum(
            "qgd,sd->gqs", grad_head, values_head, preferred_element_type=jnp.float32
        )
        delta_row = jnp.sum(prob_full * grad_prob, axis=-1, keepdims=True)
        grad_scores = (prob_full * (grad_prob - delta_row)).astype(jnp.bfloat16)
        grad_query_head = (
            jnp.einsum("gqs,sd->qgd", grad_scores, keys_head, preferred_element_type=jnp.float32)
            * scale
        )
        grad_key_head = (
            jnp.einsum("gqs,qgd->sd", grad_scores, grouped, preferred_element_type=jnp.float32)
            * scale
        )
        grad_value_head = jnp.einsum(
            "gqs,qgd->sd",
            prob_full.astype(jnp.bfloat16),
            grad_head,
            preferred_element_type=jnp.float32,
        )
        return (grad_query_head, grad_key_head, grad_value_head)

    seq_item = 0
    grouped_head, keys_head, values_head = gathered[seq_item]
    grad_head = jnp.transpose(grad_mixed_seq[seq_item], (1, 0, 2, 3))
    grad_query_head, grad_key_head, grad_value_head = lax.map(
        backward_head, (grouped_head, keys_head, values_head, grad_head, lse_parts[seq_item])
    )
    grad_query_parts = jnp.transpose(grad_query_head, (1, 0, 2, 3)).reshape(seq_rows, HQ, HD)
    grad_keys_all = jnp.transpose(grad_key_head, (1, 0, 2)).reshape(-1, HK * HD)
    grad_values_all = jnp.transpose(grad_value_head, (1, 0, 2)).reshape(-1, HK * HD)
    grad_key_own = lax.psum_scatter(
        grad_keys_all.astype(jnp.bfloat16), "ctx", scatter_dimension=0, tiled=True
    ).astype(jnp.float32)
    grad_value_own = lax.psum_scatter(
        grad_values_all.astype(jnp.bfloat16), "ctx", scatter_dimension=0, tiled=True
    )
    grad_key = grad_key_own.reshape(total_rows, HK, HD)
    grad_query_unit = unrotate(grad_query_parts, cosine, sine_table)
    qgain_local = jnp.sum(grad_query_unit * query_unit, axis=(0, 1))
    grad_query_low = (
        norm_back(grad_query_unit * query_full, query_raw, query_scale)
        .astype(jnp.bfloat16)
        .reshape(total_rows, HQ * HD)
    )
    grad_key_unit = unrotate(grad_key, cosine, sine_table)
    kgain_local = jnp.sum(grad_key_unit * key_unit, axis=(0, 1))
    grad_key_low = (
        norm_back(grad_key_unit * key_full, key_raw, key_scale)
        .astype(jnp.bfloat16)
        .reshape(total_rows, HK * HD)
    )
    query_grad = jnp.einsum("nd,nc->dc", normed, grad_query_low, preferred_element_type=jnp.float32)
    key_grad = jnp.einsum("nd,nc->dc", normed, grad_key_low, preferred_element_type=jnp.float32)
    value_grad = jnp.einsum("nd,nc->dc", normed, grad_value_own, preferred_element_type=jnp.float32)
    grad_normed = jnp.einsum(
        "nc,dc->nd", grad_query_low, query_back, preferred_element_type=jnp.float32
    )
    grad_normed = grad_normed + jnp.einsum(
        "nc,dc->nd", grad_key_low, key_back, preferred_element_type=jnp.float32
    )
    grad_normed = grad_normed + jnp.einsum(
        "nc,dc->nd", grad_value_own, value_back, preferred_element_type=jnp.float32
    )
    attn_local = jnp.sum(grad_normed * flat * scale_one, axis=0)
    input_grad = grad_middle + norm_back(grad_normed * attn_full, flat, scale_one)
    shares = (
        lax.psum_scatter(
            attn_local.astype(jnp.bfloat16), "fsdp", scatter_dimension=0, tiled=True
        ).astype(jnp.float32),
        lax.psum_scatter(
            query_grad.astype(jnp.bfloat16), "fsdp", scatter_dimension=0, tiled=True
        ).astype(jnp.float32),
        lax.psum_scatter(
            key_grad.astype(jnp.bfloat16), "fsdp", scatter_dimension=0, tiled=True
        ).astype(jnp.float32),
        lax.psum_scatter(
            value_grad.astype(jnp.bfloat16), "fsdp", scatter_dimension=0, tiled=True
        ).astype(jnp.float32),
        lax.psum_scatter(
            qgain_local.astype(jnp.bfloat16), "fsdp", scatter_dimension=0, tiled=True
        ).astype(jnp.float32),
        lax.psum_scatter(
            kgain_local.astype(jnp.bfloat16), "fsdp", scatter_dimension=0, tiled=True
        ).astype(jnp.float32),
        lax.psum_scatter(
            out_grad.astype(jnp.bfloat16), "fsdp", scatter_dimension=0, tiled=True
        ).astype(jnp.float32),
        lax.psum_scatter(
            mlp_local.astype(jnp.bfloat16), "fsdp", scatter_dimension=0, tiled=True
        ).astype(jnp.float32),
        lax.psum_scatter(
            gate_grad.astype(jnp.bfloat16), "fsdp", scatter_dimension=0, tiled=True
        ).astype(jnp.float32),
        lax.psum_scatter(
            up_grad.astype(jnp.bfloat16), "fsdp", scatter_dimension=0, tiled=True
        ).astype(jnp.float32),
        lax.psum_scatter(
            down_grad.astype(jnp.bfloat16), "fsdp", scatter_dimension=0, tiled=True
        ).astype(jnp.float32),
    )
    summed = (
        lax.psum(shares[0].astype(jnp.bfloat16), "ctx").astype(jnp.float32),
        lax.psum(shares[1].astype(jnp.bfloat16), "ctx").astype(jnp.float32),
        lax.psum(shares[2].astype(jnp.bfloat16), "ctx").astype(jnp.float32),
        lax.psum(shares[3].astype(jnp.bfloat16), "ctx").astype(jnp.float32),
        lax.psum(shares[4].astype(jnp.bfloat16), "ctx").astype(jnp.float32),
        lax.psum(shares[5].astype(jnp.bfloat16), "ctx").astype(jnp.float32),
        lax.psum(shares[6].astype(jnp.bfloat16), "ctx").astype(jnp.float32),
        lax.psum(shares[7].astype(jnp.bfloat16), "ctx").astype(jnp.float32),
        lax.psum(shares[8].astype(jnp.bfloat16), "ctx").astype(jnp.float32),
        lax.psum(shares[9].astype(jnp.bfloat16), "ctx").astype(jnp.float32),
        lax.psum(shares[10].astype(jnp.bfloat16), "ctx").astype(jnp.float32),
    )
    return (
        result.reshape(tokens.shape),
        input_grad.reshape(tokens.shape),
        summed[0],
        summed[1],
        summed[2],
        summed[3],
        summed[4],
        summed[5],
        summed[6],
        summed[7],
        summed[8],
        summed[9],
        summed[10],
    )


MESH = pl.DeviceIdType.MESH
BF = jnp.bfloat16
F32 = jnp.float32
LOG2E = math.log2(math.e)
QT = 256
NEG = -1e30
SMALL = 32


def shape(dims, dtype):
    return jax.ShapeDtypeStruct(dims, dtype)


def dot_nn(a, b):
    return jnp.dot(a, b, preferred_element_type=F32)


def dot_nt(a, b):
    return lax.dot_general(a, b, (((1,), (1,)), ((), ())), preferred_element_type=F32)


def dot_tn(a, b):
    return lax.dot_general(a, b, (((0,), (0,)), ((), ())), preferred_element_type=F32)


def device(z, x, y, c):
    return (z * 2 + x, y * 2 + c)


def coords():
    a = lax.axis_index("ctx")
    f = lax.axis_index("fsdp")
    return lax.div(a, 2), lax.rem(a, 2), lax.div(f, 2), lax.rem(f, 2)


class Net:
    def __init__(self, send_sems, recv_sems):
        self.z, self.x, self.y, self.c = z, x, y, c = coords()
        self.depth = lax.axis_size("ctx") // 2
        self.to_x = device(z, 1 - x, y, c)
        self.to_y = device(z, x, 1 - y, c)
        self.to_core = device(z, x, y, 1 - c)
        self.to_x_other = device(z, 1 - x, y, 1 - c)
        self.up = device(z + 1, x, y, c)
        self.down = device(z - 1, x, y, c)
        self.mate = device(2 * c + y, x, lax.rem(z, 2), lax.div(z, 2))
        self.moves = z != 2 * c + y
        self.mate_chunk = 2 * lax.rem(z, 2) + x
        self.has_up = z < self.depth - 1
        self.has_down = z > 0
        self.send_sems, self.recv_sems = send_sems, recv_sems
        self.used = 0
        self.me = 2 * y + x
        self.sx = 2 * y + 1 - x
        self.sy = 2 * (1 - y) + x
        self.sd = 2 * (1 - y) + 1 - x

    def greet(self, line=True, owners=False, mate=False):
        barrier = pltpu.get_barrier_semaphore()

        def signal(to):
            pl.semaphore_signal(barrier, inc=1, device_id=to, device_id_type=MESH)

        for to in (self.to_x, self.to_y, self.to_core):
            signal(to)
        count = 3
        if owners:
            signal(self.to_x_other)
            count = count + 1
        if mate:
            pl.when(self.moves)(lambda: signal(self.mate))
            count = count + self.moves.astype(jnp.int32)
        if line:
            pl.when(self.has_up)(lambda: signal(self.up))
            pl.when(self.has_down)(lambda: signal(self.down))
            count = count + self.has_up.astype(jnp.int32) + self.has_down.astype(jnp.int32)
        pl.semaphore_wait(barrier, count)

    def take(self, count=1):
        first = self.used
        self.used += count
        assert self.used <= self.send_sems.shape[0], self.used
        return first

    def copy(self, sem, src, dst, to):
        return pltpu.make_async_remote_copy(
            src_ref=src,
            dst_ref=dst,
            send_sem=self.send_sems.at[sem],
            recv_sem=self.recv_sems.at[sem],
            device_id=to,
            device_id_type=MESH,
        )

    def new(self, src, dst, to):
        return self.copy(self.take(), src, dst, to)


def rms(values):
    return lax.rsqrt(jnp.mean(values * values, axis=-1, keepdims=True) + epsilon)


class PlaneGather:
    def __init__(self, net, src, out, split=None):
        rows = out.shape[1]
        split = rows // 2 if split is None else split
        self.net = net
        me, sx, sy = net.me, net.sx, net.sy
        self.sides, self.relays = [], []
        for first, size, near, far, s_near in (
            (split, rows - split, net.to_y, net.to_x, sy),
            (0, split, net.to_x, net.to_y, sx),
        ):
            if size:
                at = pl.ds(first, size)
                one = net.new(src.at[at], out.at[me, at], near)
                self.sides.append(one)
                self.relays.append((one, net.new(out.at[s_near, at], out.at[s_near, at], far)))
        self.rest = []
        for first, size, far in ((split, rows - split, net.to_x), (0, split, net.to_y)):
            if size:
                at = pl.ds(first, size)
                self.rest.append(net.new(src.at[at], out.at[me, at], far))

    def start(self):
        for cp in self.sides + self.rest:
            cp.start()

    def forward(self):
        for one, relay in self.relays:
            one.wait_recv()
            relay.start()

    def wait_sides(self):
        for cp in self.rest:
            cp.wait_recv()

    def wait_diagonal(self):
        for _, relay in self.relays:
            relay.wait_recv()

    def drain(self):
        for cp in self.sides + self.rest:
            cp.wait_send()
        for _, relay in self.relays:
            relay.wait_send()


class PlaneSum:
    def __init__(self, net, part, got, mid, split=None):
        rows = part.shape[1]
        split = rows // 2 if split is None else split
        self.net, self.part, self.got, self.mid = net, part, got, mid
        me, sx, sy, sd = net.me, net.sx, net.sy, net.sd
        self.ways = []
        for first, size, near, far, s_near, s_far in (
            (0, split, net.to_x, net.to_y, sx, sy),
            (split, rows - split, net.to_y, net.to_x, sy, sx),
        ):
            if size:
                at = pl.ds(first, size)
                self.ways.append(
                    (
                        at,
                        s_far,
                        net.new(part.at[sd, at], got.at[0, at], near),
                        net.new(part.at[s_near, at], got.at[1, at], near),
                        net.new(mid.at[at], got.at[2, at], far),
                    )
                )

    def start_diagonal(self):
        for _, _, diagonal, _, _ in self.ways:
            diagonal.start()

    def start_sides(self):
        for _, _, _, side, _ in self.ways:
            side.start()

    def forward(self):
        for at, s_far, diagonal, _, relay in self.ways:
            diagonal.wait_recv()
            self.mid[at] = (self.part[s_far, at].astype(F32) + self.got[0, at].astype(F32)).astype(
                BF
            )
            relay.start()

    def finish(self, use):
        for at, _, _, side, relay in self.ways:
            side.wait_recv()
            relay.wait_recv()
            use(
                at,
                self.part[self.net.me, at].astype(F32)
                + self.got[1, at].astype(F32)
                + self.got[2, at].astype(F32),
            )

    def drain(self):
        for _, _, diagonal, side, relay in self.ways:
            diagonal.wait_send()
            side.wait_send()
            relay.wait_send()


class Fetch:
    def __init__(self, net, src, out):
        self.net, self.src = net, src
        whole = len(out.shape) == len(src.shape)
        self.out = out if whole else out.at[net.me]
        self.cp = net.new(src, out if whole else out.at[net.mate_chunk], net.mate)

    def start(self):
        pl.when(self.net.moves)(self.cp.start)

        @pl.when(jnp.logical_not(self.net.moves))
        def _():
            self.out[...] = self.src[...]

    def wait(self):
        pl.when(self.net.moves)(self.cp.wait_recv)

    def drain(self):
        pl.when(self.net.moves)(self.cp.wait_send)


class LineSum:
    def __init__(self, net, tiles, src, mine, slots, deliver):
        self.net, self.tiles, self.src, self.mine = net, tiles, src, mine
        self.slots, self.deliver = slots, deliver
        self.sems = net.take(4 * tiles)
        self.root = net.depth // 2
        self.below = net.z < self.root
        self.above = net.z > self.root
        self.middle = net.z == self.root
        self.two_sided = self.root < net.depth - 1
        self.at_end = jnp.logical_or(net.z == 0, net.z == net.depth - 1)
        self.between = jnp.logical_not(jnp.logical_or(self.middle, self.at_end))

    def hop(self, kind, k):
        net, slots = self.net, self.slots
        src, dst, to = (
            (slots.at[1, k], slots.at[0, k], net.up),
            (slots.at[0, k], slots.at[1, k], net.down),
            (self.mine(k), self.mine(k), net.down),
            (self.mine(k), self.mine(k), net.up),
        )[kind]
        return net.copy(self.sems + kind * self.tiles + k, src, dst, to)

    def gather(self, k):
        net, slots = self.net, self.slots

        def send(kind, has_before):
            @pl.when(has_before)
            def _():
                self.hop(kind, k).wait_recv()
                total = self.src(k)[...].astype(F32) + slots[kind, k].astype(F32)
                slots[1 - kind, k] = total.astype(slots.dtype)

            @pl.when(jnp.logical_not(has_before))
            def _():
                slots[1 - kind, k] = self.src(k)[...]

            self.hop(kind, k).start()

        pl.when(self.below)(lambda: send(0, net.has_down))
        pl.when(self.above)(lambda: send(1, net.has_up))

    def finish(self, k):
        net, slots = self.net, self.slots

        @pl.when(self.middle)
        def _():
            self.hop(0, k).wait_recv()
            total = self.src(k)[...].astype(F32) + slots[0, k].astype(F32)
            if self.two_sided:
                self.hop(1, k).wait_recv()
                total = total + slots[1, k].astype(F32)
            self.mine(k)[...] = total.astype(slots.dtype)
            self.hop(2, k).start()
            if self.two_sided:
                self.hop(3, k).start()

        @pl.when(self.below)
        def _():
            self.hop(2, k).wait_recv()
            pl.when(net.has_down)(lambda: self.hop(2, k).start())

        @pl.when(self.above)
        def _():
            self.hop(3, k).wait_recv()
            pl.when(net.has_up)(lambda: self.hop(3, k).start())

        self.deliver(k)

    def drain(self, k):
        net = self.net
        pl.when(self.below)(lambda: self.hop(0, k).wait_send())
        pl.when(self.above)(lambda: self.hop(1, k).wait_send())
        sends_down = jnp.logical_and(net.has_down, jnp.logical_not(self.above))
        sends_up = jnp.logical_and(net.has_up, jnp.logical_not(self.below))
        pl.when(sends_down)(lambda: self.hop(2, k).wait_send())
        pl.when(sends_up)(lambda: self.hop(3, k).wait_send())


def within(k, first, last):
    return jnp.logical_and(k >= first, k < last)


class Pump:
    def __init__(self, lines, lags=(1, 3, 5, 7), placed=None):
        self.lines = lines
        self.total = sum(line.tiles for line in lines)
        self.gather_lag, self.middle_lag, self.between_lag, self.end_lag = lags
        self.placed = placed

    def each(self, s, run):
        if isinstance(s, int):
            for line in self.lines:
                if 0 <= s < line.tiles:
                    run(line, s)
                s -= line.tiles
            return
        first = 0
        for line in self.lines:
            pl.when(within(s, first, first + line.tiles))(
                lambda line=line, first=first: run(line, s - first)
            )
            first += line.tiles

    def step(self, p, before=None):
        line = self.lines[0]

        @pl.when(line.between)
        def _():
            if before is not None:
                before(p - self.gather_lag)
            self.each(p - self.gather_lag, lambda ln, k: ln.gather(k))
            self.each(p - self.between_lag, lambda ln, k: ln.finish(k))

        @pl.when(line.middle)
        def _():
            if before is not None:
                before(p - self.middle_lag)
            self.each(p - self.middle_lag, lambda ln, k: ln.finish(k))

        @pl.when(line.at_end)
        def _():
            self.each(p - self.end_lag, lambda ln, k: ln.finish(k))

    def steps(self):
        return self.total + max(self.gather_lag, self.middle_lag, self.between_lag, self.end_lag)


def any_spec():
    return pl.BlockSpec(memory_space=pl.ANY)


def vmem_spec():
    return pl.BlockSpec(memory_space=pltpu.VMEM)


def params(cid, mib=60):
    return pltpu.CompilerParams(
        collective_id=cid, has_side_effects=True, vmem_limit_bytes=mib * 2**20
    )


def enter(tok, cot, pos, gains, wq, wk, wv, wg, wu):
    rows = tok.shape[0]
    d_rows = wq.shape[0]
    half = 4 * rows
    unit = wg.shape[1] // 4
    n_sems = 48

    def kernel(
        tok_ref,
        cot_ref,
        pos_in,
        attn_ref,
        mlp_ref,
        query_ref,
        key_ref,
        wq_ref,
        wk_ref,
        wv_ref,
        wg_ref,
        wu_ref,
        x_own,
        n1,
        raw_ref,
        table,
        core,
        wall,
        gains_ref,
        cot_own,
        wgu,
        wq_s,
        wk_s,
        wv_s,
        wg_s,
        wu_s,
        wloc,
        wloc2,
        toks,
        pos_ref,
        gain_ref,
        poss,
        heads,
        gslots,
        ssem,
        rsem,
        lsem,
    ):
        net = Net(ssem, rsem)
        y, c = net.y, net.c
        f = 2 * y + c
        fy = 2 * (1 - y) + c
        loads = [
            pltpu.make_async_copy(a, b, lsem.at[k])
            for k, (a, b) in enumerate(
                ((wq_ref, wq_s), (wk_ref, wk_s), (wv_ref, wv_s), (wg_ref, wg_s), (wu_ref, wu_s))
            )
        ]
        for cp in loads:
            cp.start()
        for h in range(rows // 128):
            pos_ref[8 * h : 8 * h + 1, :] = pos_in[0:1, h * 128 : (h + 1) * 128].astype(F32)
        gain_ref[...] = jnp.zeros_like(gain_ref)
        at = pl.ds(pl.multiple_of(f * d_rows, d_rows), d_rows)
        gain_ref[0:1, at] = attn_ref[...]
        gain_ref[1:2, at] = mlp_ref[...]
        for row, ref in ((2, query_ref), (3, key_ref)):
            n = ref.shape[1]
            wide = jnp.concatenate([ref[...], jnp.zeros((1, HD - n), F32)], axis=-1)
            wide = pltpu.roll(jnp.broadcast_to(wide, (8, HD)), f * n, 1)
            gain_ref[row : row + 1, 0:HD] = wide[0:1]
        net.greet(False, mate=True)
        fetch, pos_fetch = Fetch(net, tok_ref, toks), Fetch(net, pos_ref, poss)
        cot_fetch = Fetch(net, cot_ref, cot_own)
        fetch.start()
        pos_fetch.start()
        g_core = net.new(gain_ref, gslots.at[f], net.to_core)
        g_y = net.new(gain_ref, gslots.at[f], net.to_y)
        g_relay = net.new(gslots.at[fy], gslots.at[fy], net.to_core)
        g_core.start()
        g_y.start()
        gslots[f] = gain_ref[...]
        for cp in loads[:3]:
            cp.wait()
        for t in range(4):
            at = t * 4 * HD
            wloc[t, :, 0 : 4 * HD] = wq_s[:, at : at + 4 * HD].astype(BF)
            at = t * 2 * HD
            wloc[t, :, 4 * HD : 6 * HD] = wk_s[:, at : at + 2 * HD].astype(BF)
            wloc[t, :, 6 * HD : 8 * HD] = wv_s[:, at : at + 2 * HD].astype(BF)
        w_y = net.new(wloc.at[net.sy], wall.at[f], net.to_y)
        w_core = net.new(wloc.at[net.me], wall.at[f], net.to_core)
        w_relay = net.new(wall.at[fy], wall.at[fy], net.to_core)
        w_y.start()
        w_core.start()
        wall[f] = wloc[net.me]
        pos_fetch.wait()
        pos_gather = PlaneGather(net, poss.at[net.me], poss)
        pos_gather.start()
        fetch.wait()
        gather = PlaneGather(net, toks.at[net.me], toks, 0)
        gather.start()
        cot_fetch.start()
        pos_gather.forward()
        for cp in loads[3:]:
            cp.wait()
        for t in range(4):
            at = t * unit
            wloc2[t, :, 0:unit] = wg_s[:, at : at + unit].astype(BF)
            wloc2[t, :, unit : 2 * unit] = wu_s[:, at : at + unit].astype(BF)
        gu_y = net.new(wloc2.at[net.sy], wgu.at[f], net.to_y)
        gu_core = net.new(wloc2.at[net.me], wgu.at[f], net.to_core)
        gu_relay = net.new(wgu.at[fy], wgu.at[fy], net.to_core)
        gu_y.start()
        gu_core.start()
        wgu[f] = wloc2[net.me]
        gather.forward()
        g_y.wait_recv()
        g_relay.start()
        w_y.wait_recv()
        w_relay.start()
        g_core.wait_recv()
        g_relay.wait_recv()
        w_core.wait_recv()
        w_relay.wait_recv()
        index = lax.broadcasted_iota(jnp.int32, (8, HD // 2), 1).astype(F32)
        frequency = jnp.exp(index * (-2.0 * math.log(theta_base) / HD))[0:1]
        full = gslots[0] + gslots[1] + gslots[2] + gslots[3]
        gains_ref[...] = full
        attn_gain, q_gain, k_gain = full[0:1, :], full[2:3, 0:HD], full[3:4, 0:HD]
        pos_gather.wait_sides()
        pos_gather.wait_diagonal()
        x_own[...] = toks[net.me]
        swaps = net.take(4)

        def swap(k):
            at = pl.ds(pl.multiple_of(k * rows, rows), rows)
            return net.copy(swaps + k, heads.at[1 - c, at], core.at[c, at], net.to_core)

        @pl.loop(0, 4)
        def _(n):
            pl.when(n == 1)(gather.wait_sides)
            pl.when(n == 3)(gather.wait_diagonal)
            k = jnp.where(
                n == 0, net.me, jnp.where(n == 1, net.sx, jnp.where(n == 2, net.sy, net.sd))
            )
            at = pl.ds(pl.multiple_of(k * rows, rows), rows)
            flat = toks[k].astype(F32)
            normed = (flat * rms(flat) * attn_gain).astype(BF)
            n1[at, :] = normed
            raw = dot_nn(normed[:, 0:d_rows], wall[0])
            for g in range(1, 4):
                raw = raw + dot_nn(normed[:, g * d_rows : (g + 1) * d_rows], wall[g])
            raw_ref[at, :] = raw[:, 0 : 6 * HD]
            place = jnp.transpose(poss[k])
            angles = jnp.concatenate(
                [place[:, 8 * h : 8 * h + 1] * frequency for h in range(rows // 128)],
                axis=0,
            )
            cosine, sine = jnp.cos(angles), jnp.sin(angles)
            table[at, :] = jnp.concatenate([cosine, sine], axis=-1)
            cosine = jnp.concatenate([cosine, cosine], axis=-1)
            sine = jnp.concatenate([-sine, sine], axis=-1)
            for h in range(6):
                u = raw[:, h * HD : (h + 1) * HD]
                unit = u * rms(u) * (q_gain if h < 4 else k_gain)
                turned = unit * cosine + pltpu.roll(unit, HD // 2, 1) * sine
                g, lane = (h // 2, (h % 2) * HD) if h < 4 else (h - 4, 2 * HD)
                heads[g, at, lane : lane + HD] = turned.astype(BF)
            for g in range(2):
                v = raw[:, (6 + g) * HD : (7 + g) * HD]
                heads[g, at, 3 * HD : 4 * HD] = v.astype(BF)
            swap(k).start()
            core[c, at] = heads[c, at]

        gu_y.wait_recv()
        gu_relay.start()
        for k in range(4):
            swap(k).wait()
        cot_fetch.wait()
        gu_core.wait_recv()
        gu_relay.wait_recv()
        for cp in (g_core, g_y, g_relay, w_core, w_y, w_relay, gu_core, gu_y, gu_relay):
            cp.wait_send()
        for item in (fetch, pos_fetch, cot_fetch, gather, pos_gather):
            item.drain()

    vm = vmem_spec()
    return pl.pallas_call(
        kernel,
        name="enter",
        out_shape=[
            shape((rows, D), BF),
            shape((half, D), BF),
            shape((half, 6 * HD), F32),
            shape((half, HD), F32),
            shape((2, half, 4 * HD), BF),
            shape((4, d_rows, 8 * HD), BF),
            shape((8, D), F32),
            shape((rows, D), BF),
            shape((4, d_rows, 2 * unit), BF),
        ],
        in_specs=[vm] * 7 + [any_spec()] * 5,
        out_specs=[vm] * 9,
        scratch_shapes=[
            pltpu.VMEM(wq.shape, F32),
            pltpu.VMEM(wk.shape, F32),
            pltpu.VMEM(wv.shape, F32),
            pltpu.VMEM(wg.shape, F32),
            pltpu.VMEM(wu.shape, F32),
            pltpu.VMEM((4, d_rows, 8 * HD), BF),
            pltpu.VMEM((4, d_rows, 2 * unit), BF),
            pltpu.VMEM((4, rows, D), BF),
            pltpu.VMEM((16, 128), F32),
            pltpu.VMEM((8, D), F32),
            pltpu.VMEM((4, 16, 128), F32),
            pltpu.VMEM((2, half, 4 * HD), BF),
            pltpu.VMEM((4, 8, D), F32),
            pltpu.SemaphoreType.DMA((n_sems,)),
            pltpu.SemaphoreType.DMA((n_sems,)),
            pltpu.SemaphoreType.DMA((5,)),
        ],
        compiler_params=params(0),
        cost_estimate=pl.CostEstimate(
            flops=2 * half * D * 8 * HD, bytes_accessed=16 * 2**20, transcendentals=0
        ),
    )(tok, cot, pos, *gains, wq, wk, wv, wg, wu)


def attend(block_map, inverse, core, cot, wo, wd):
    half = core.shape[1]
    length = 2 * half
    tiles = length // QT
    blocks = QT // BLK
    n_blocks = length // BLK
    factor = HD ** (-0.5) * LOG2E
    n_sems = 16
    rows = cot.shape[0]

    def kernel(
        bm,
        inv,
        x_ref,
        cot_ref,
        wo_ref,
        wd_ref,
        att,
        mixed,
        lse_ref,
        cots,
        wo_out,
        wd_out,
        q_s,
        k_s,
        v_s,
        o_s,
        wo_s,
        wd_s,
        ssem,
        rsem,
        lsem,
    ):
        net = Net(ssem, rsem)
        x, c = net.x, net.c
        loads = [
            pltpu.make_async_copy(a, b, lsem.at[k])
            for k, (a, b) in enumerate(((wo_ref, wo_s), (wd_ref, wd_s)))
        ]
        for cp in loads:
            cp.start()
        net.greet(False)
        gather = PlaneGather(net, cot_ref, cots)
        gather.start()
        o_core = net.new(wo_out, wo_out, net.to_core)
        d_core = net.new(wd_out, wd_out, net.to_core)
        own = c == x

        @pl.loop(0, tiles)
        def _(i):
            for h in range(blocks):
                block = x_ref[inv[i * blocks + h]]
                at = pl.multiple_of(i * QT, QT) + h * BLK
                q_s[i, pl.ds(h * BLK, BLK), :] = block[:, 0:HD]
                q_s[i, pl.ds(QT + h * BLK, BLK), :] = block[:, HD : 2 * HD]
                k_s[pl.ds(at, BLK), :] = block[:, 2 * HD : 3 * HD]
                v_s[pl.ds(at, BLK), 0:HD] = block[:, 3 * HD : 4 * HD]

        v_s[:, HD : 2 * HD] = jnp.ones((length, HD), BF)
        for cp in loads:
            cp.wait()

        @pl.when(own)
        def _():
            wo_out[...] = wo_s[...].astype(BF)
            wd_out[...] = wd_s[...].astype(BF)
            o_core.start()
            d_core.start()

        q_row = lax.broadcasted_iota(jnp.int32, (2 * QT, QT), 0)
        k_row = lax.broadcasted_iota(jnp.int32, (2 * QT, QT), 1)
        allowed = jnp.where(q_row >= QT, q_row - QT, q_row) >= k_row

        def tile(i):
            q = q_s[i]
            acc = None
            for j in range(i + 1):
                at = slice(j * QT, (j + 1) * QT)
                scores = dot_nt(q, k_s[at, :]) * factor
                if j == i:
                    scores = jnp.where(allowed, scores, NEG)
                add = dot_nn(jnp.exp2(scores).astype(BF), v_s[at, :])
                acc = add if acc is None else acc + add
            total = acc[:, HD:]
            out = acc[:, :HD] / total
            lse_ref[i] = jnp.log2(jnp.transpose(total)[0:8, :])
            for h in range(blocks):
                for u in range(2):
                    o_s[i * blocks + h, :, u * HD : (u + 1) * HD] = out[
                        u * QT + h * BLK : u * QT + (h + 1) * BLK
                    ].astype(BF)

        for i in range(tiles):
            tile(i)
            if i == tiles - 2:
                gather.forward()

        cots[net.me] = cot_ref[...]
        swap = net.take(1)

        @pl.loop(0, n_blocks)
        def _(s):
            mixed[pl.ds(pl.multiple_of(s * BLK, BLK), BLK), :] = o_s[bm[s]]

        away = mixed.at[pl.ds(pl.multiple_of((1 - c) * half, half), half)]
        o_swap = net.copy(swap, away, att.at[c], net.to_core)
        o_swap.start()
        att[c] = mixed[pl.ds(pl.multiple_of(c * half, half), half), :]
        pl.when(jnp.logical_not(own))(lambda: o_core.wait_recv())
        pl.when(jnp.logical_not(own))(lambda: d_core.wait_recv())
        gather.wait_sides()
        gather.wait_diagonal()
        o_swap.wait()
        gather.drain()
        pl.when(own)(lambda: o_core.wait_send())
        pl.when(own)(lambda: d_core.wait_send())

    vm = vmem_spec()
    smem = pl.BlockSpec(memory_space=pltpu.SMEM)
    return pl.pallas_call(
        kernel,
        name="attend",
        out_shape=[
            shape((2, half, 2 * HD), BF),
            shape((length, 2 * HD), BF),
            shape((tiles, 8, 2 * QT), F32),
            shape((4, rows, D), BF),
            shape(wo.shape, BF),
            shape(wd.shape, BF),
        ],
        in_specs=[smem, smem, vm, vm] + [any_spec()] * 2,
        out_specs=[vm] * 6,
        scratch_shapes=[
            pltpu.VMEM((tiles, 2 * QT, HD), BF),
            pltpu.VMEM((length, HD), BF),
            pltpu.VMEM((length, 2 * HD), BF),
            pltpu.VMEM((n_blocks, BLK, 2 * HD), BF),
            pltpu.VMEM(wo.shape, F32),
            pltpu.VMEM(wd.shape, F32),
            pltpu.SemaphoreType.DMA((n_sems,)),
            pltpu.SemaphoreType.DMA((n_sems,)),
            pltpu.SemaphoreType.DMA((2,)),
        ],
        compiler_params=params(1),
        cost_estimate=pl.CostEstimate(
            flops=2 * 2 * 2 * length * length * HD, bytes_accessed=16 * 2**20, transcendentals=0
        ),
    )(block_map, inverse, core.reshape(n_blocks, BLK, 4 * HD), cot, wo, wd)


def feed_forward(att, x_own, wo, wgu, wd, cots, cot_own, gains):
    half = att.shape[1]
    rows = half // 4
    unit = wd.shape[0]
    d_rows = wgu.shape[1]
    d_tiles = unit // 2 // SMALL
    n_sems = 48 + 4 * d_tiles

    def kernel(
        att_ref,
        x_ref,
        wo_ref,
        wgu_ref,
        wd_ref,
        dy_ref,
        cot_ref,
        gain_ref,
        core,
        middle,
        dmiddle,
        result_part,
        sum_gu,
        sum_o,
        total_d,
        mlp_gain_part,
        part,
        got,
        mid,
        n2,
        hid,
        dgu,
        got2,
        mid2,
        dmb,
        gm,
        w_gu,
        got_gu,
        w_d,
        got_d,
        w_o,
        got_o,
        sum_d,
        d_slots,
        ssem,
        rsem,
    ):
        net = Net(ssem, rsem)
        c, me, sx, sy, sd = net.c, net.me, net.sx, net.sy, net.sd
        mlp_gain = gain_ref[1:2, :]
        net.greet()
        out_sum = PlaneSum(net, part, got, mid)

        def chunk(k):
            return pl.ds(pl.multiple_of(k * rows, rows), rows)

        def project(k):
            part[k] = (
                dot_nn(att_ref[0, chunk(k)], wo_ref[0 : 2 * HD, :])
                + dot_nn(att_ref[1, chunk(k)], wo_ref[2 * HD : 4 * HD, :])
            ).astype(BF)

        project(sd)
        out_sum.start_diagonal()
        project(sx)
        project(sy)
        out_sum.start_sides()
        project(me)
        out_sum.forward()

        def add_residual(at, total):
            value = x_ref[at].astype(F32) + total
            middle[at] = value
            n2[me, at] = (value * rms(value) * mlp_gain).astype(BF)

        out_sum.finish(add_residual)
        gather = PlaneGather(net, n2.at[me], n2)
        gather.start()

        def forward_back(k):
            rows_k = n2[k]
            gate_up = dot_nn(rows_k[:, 0:d_rows], wgu_ref[0])
            for g in range(1, 4):
                gate_up = gate_up + dot_nn(rows_k[:, g * d_rows : (g + 1) * d_rows], wgu_ref[g])
            gate, upward = gate_up[:, 0:unit], gate_up[:, unit : 2 * unit]
            sigmoid = 1.0 / (1.0 + jnp.exp(-gate))
            silu = gate * sigmoid
            hid[k] = (silu * upward).astype(BF)
            dh = dot_nt(dy_ref[k], wd_ref[...])
            dgu[k, :, 0:unit] = (
                dh * upward * sigmoid * (1.0 + gate * (1.0 - sigmoid))
            ).astype(BF)
            dgu[k, :, unit : 2 * unit] = (dh * silu).astype(BF)
            grads = dgu[k]
            for g in range(4):
                part[k, :, g * d_rows : (g + 1) * d_rows] = dot_nt(grads, wgu_ref[g]).astype(BF)

        out_sum.drain()
        forward_back(me)
        gather.forward()
        gather.wait_sides()
        back_sum = PlaneSum(net, part, got2, mid2)

        @pl.loop(0, 2)
        def _(n):
            forward_back(jnp.where(n == 0, sx, sy))

        back_sum.start_sides()
        gather.wait_diagonal()
        forward_back(sd)
        back_sum.start_diagonal()

        gu_sem = net.take(2)
        d_sem = net.take(1)
        o_sem = net.take(1)

        def gu_copy(n):
            return net.copy(gu_sem + n, w_gu.at[n], got_gu.at[n], net.to_core)

        d_copy = net.copy(d_sem, w_d, got_d, net.to_core)
        o_copy = net.copy(o_sem, w_o, got_o, net.to_core)
        all_dgu = dgu.shape[2]
        unit_half = unit // 2

        def down(core_of):
            at = pl.ds(pl.multiple_of(core_of * unit_half, unit_half), unit_half)
            return dot_tn(hid[:, :, at].reshape(half, unit_half), dy_ref[...].reshape(half, D))

        line = LineSum(
            net,
            d_tiles,
            lambda k: sum_d.at[pl.ds(pl.multiple_of(k * SMALL, SMALL), SMALL)],
            lambda k: total_d.at[pl.ds(pl.multiple_of(k * SMALL, SMALL), SMALL)],
            d_slots,
            lambda k: None,
        )
        pump = Pump([line], (0, 2, 5, 7))

        w_d[...] = down(1 - c).astype(BF)
        d_copy.start()
        value = down(c)
        d_copy.wait_recv()
        sum_d[...] = (value + got_d[...].astype(F32)).astype(BF)

        @pl.when(line.at_end)
        def _():
            @pl.loop(0, d_tiles)
            def _(k):
                line.gather(k)

        @pl.loop(0, 4)
        def _(k):
            result_part[k] = dot_nn(hid[k], wd_ref[...]).astype(BF)

        back_sum.forward()
        pump.step(0)

        def slab(n, core_of):
            f = 2 * n + core_of
            at = pl.ds(pl.multiple_of(f * d_rows, d_rows), d_rows)
            return dot_tn(n2[:, :, at].reshape(half, d_rows), dgu[...].reshape(half, all_dgu))

        for n in range(2):
            w_gu[n] = slab(n, 1 - c).astype(BF)
            gu_copy(n).start()
            pump.step(1 + n)

        def back_through_norm(at, dn2):
            value = middle[at]
            scale = rms(value)
            w2 = dn2 * mlp_gain
            grad = cot_ref[at].astype(F32) + norm_back(w2, value, scale)
            dmiddle[at] = grad
            dmb[me, at] = grad.astype(BF)
            first = dn2.shape[0] // 8
            folded = jnp.sum((dn2 * value * scale).reshape(first, 8, D), axis=0)
            mlp_gain_part[...] += folded

        mlp_gain_part[...] = jnp.zeros_like(mlp_gain_part)
        back_sum.finish(back_through_norm)
        gather2 = PlaneGather(net, dmb.at[me], dmb)
        gather2.start()
        swap_sem = net.take(4)

        def swap(k):
            return net.copy(
                swap_sem + k, gm.at[1 - c, chunk(k)], core.at[c, chunk(k)], net.to_core
            )

        def grad_mixed(k):
            value = dot_nt(dmb[k], wo_ref[...]).astype(BF)
            gm[0, chunk(k)] = value[:, 0 : 2 * HD]
            gm[1, chunk(k)] = value[:, 2 * HD : 4 * HD]
            swap(k).start()
            core[c, chunk(k)] = gm[c, chunk(k)]

        pump.step(3)
        pump.step(4)
        grad_mixed(me)
        pump.step(5)
        for n in range(2):
            value = slab(n, c)
            gu_copy(n).wait_recv()
            sum_gu[n] = (value + got_gu[n].astype(F32)).astype(BF)
            pump.step(6 + n)

        gather2.forward()
        for n in range(8, 11):
            pump.step(n)
        gather2.wait_sides()

        @pl.loop(0, 2)
        def _(n):
            grad_mixed(jnp.where(n == 0, sx, sy))

        for n in range(11, 14):
            pump.step(n)
        gather2.wait_diagonal()
        grad_mixed(sd)

        def out_grad(g):
            return dot_tn(att_ref[g], dmb[...].reshape(half, D))

        w_o[...] = out_grad(1 - c).astype(BF)
        o_copy.start()
        value = out_grad(c)
        o_copy.wait_recv()
        sum_o[...] = (value + got_o[...].astype(F32)).astype(BF)
        @pl.loop(14, pump.steps())
        def _(p):
            pump.step(p)

        @pl.loop(0, d_tiles)
        def _(k):
            line.drain(k)

        for k in range(4):
            swap(k).wait()
        for n in range(2):
            gu_copy(n).wait_send()
        d_copy.wait_send()
        o_copy.wait_send()
        gather.drain()
        gather2.drain()
        back_sum.drain()

    vm = vmem_spec()
    return pl.pallas_call(
        kernel,
        name="feed_forward",
        out_shape=[
            shape((2, half, 2 * HD), BF),
            shape((rows, D), F32),
            shape((rows, D), F32),
            shape((4, rows, D), BF),
            shape((2, d_rows, 2 * unit), BF),
            shape((2 * HD, D), BF),
            shape((unit // 2, D), BF),
            shape((8, D), F32),
        ],
        in_specs=[vm] * 8,
        out_specs=[vm] * 8,
        scratch_shapes=[
            pltpu.VMEM((4, rows, D), BF),
            pltpu.VMEM((3, rows, D), BF),
            pltpu.VMEM((rows, D), BF),
            pltpu.VMEM((4, rows, D), BF),
            pltpu.VMEM((4, rows, unit), BF),
            pltpu.VMEM((4, rows, 2 * unit), BF),
            pltpu.VMEM((3, rows, D), BF),
            pltpu.VMEM((rows, D), BF),
            pltpu.VMEM((4, rows, D), BF),
            pltpu.VMEM((2, half, 2 * HD), BF),
            pltpu.VMEM((2, d_rows, 2 * unit), BF),
            pltpu.VMEM((2, d_rows, 2 * unit), BF),
            pltpu.VMEM((unit // 2, D), BF),
            pltpu.VMEM((unit // 2, D), BF),
            pltpu.VMEM((2 * HD, D), BF),
            pltpu.VMEM((2 * HD, D), BF),
            pltpu.VMEM((unit // 2, D), BF),
            pltpu.VMEM((2, d_tiles, SMALL, D), BF),
            pltpu.SemaphoreType.DMA((n_sems,)),
            pltpu.SemaphoreType.DMA((n_sems,)),
        ],
        compiler_params=params(2, 62),
        cost_estimate=pl.CostEstimate(
            flops=24 * half * D * unit, bytes_accessed=32 * 2**20, transcendentals=0
        ),
    )(att, x_own, wo, wgu, wd, cots, cot_own, gains)


def finish_back(
    block_map,
    inverse,
    core,
    mixed,
    grad,
    lse,
    sum_o,
    total_d,
    sum_gu,
    result_part,
    middle,
    raw,
    table,
    n1,
    wall,
    x_own,
    dmiddle,
    gains,
    mlp_gain_part,
):
    half = core.shape[1]
    length = 2 * half
    blocks = QT // BLK
    n_blocks = length // BLK
    wide = 2 * QT
    tiles = length // wide
    scale = HD ** (-0.5)
    factor = scale * LOG2E
    rows = middle.shape[0]
    d_rows = wall.shape[1]
    gu_cols = sum_gu.shape[2]
    unit = gu_cols // 2
    o_tiles = sum_o.shape[0] // SMALL
    per = d_rows // SMALL
    w_tiles = 2 * per
    n_sems = 7 * o_tiles + 10 * w_tiles + 90

    def kernel(
        bm,
        inv,
        core_hbm,
        mixed_hbm,
        grad_hbm,
        lse_ref,
        o_part,
        d_ref,
        gu_ref,
        rp_hbm,
        mid_hbm,
        raw_hbm,
        table_hbm,
        n1_hbm,
        wall_hbm,
        x_hbm,
        dmid_hbm,
        gain_ref,
        mlp_ref,
        result,
        input_out,
        o_final,
        d_final,
        out_q,
        out_k,
        out_v,
        out_g,
        out_u,
        gain_out,
        dq,
        d_s,
        result_part_s,
        part,
        res,
        got,
        mid,
        grad_in,
        got2,
        mid2,
        o_slots,
        o_sum,
        gu_rows,
        gu_slots,
        gu_mine,
        gu_other,
        w_out,
        w_got,
        w_sum,
        w_rows,
        w_slots,
        w_mine,
        w_other,
        g_sum,
        g_got,
        g_slots,
        g_mine,
        acc,
        ssem,
        rsem,
        lsem,
    ):
        net = Net(ssem, rsem)
        z, x, y, c = net.z, net.x, net.y, net.c
        load_part = pltpu.make_async_copy(rp_hbm, result_part_s, lsem.at[0])
        load_part.start()
        net.greet(True, True, mate=True)
        total = PlaneSum(net, result_part_s, got, mid, rows // 4)
        total2 = PlaneSum(net, part, got2, mid2, rows // 4)
        gu_y = net.new(gu_ref.at[1 - y], gu_rows.at[1], net.to_y)
        home = Fetch(net, res, result)
        home2 = Fetch(net, grad_in, input_out)
        swap = net.new(
            d_s.at[pl.ds(pl.multiple_of((1 - c) * half, half), half)], dq.at[c], net.to_core
        )
        x_sem = net.take(2 * o_tiles)
        chip_sem = net.take(o_tiles)
        owner = device(z, 1 - x, y, x)
        owns = c == x

        def cross(k, h):
            return net.copy(x_sem + h * o_tiles + k, o_sum.at[k], o_final.at[h, k], owner)

        def chip(k, h):
            return net.copy(chip_sem + k, o_sum.at[k], o_final.at[h, k], net.to_core)

        def deliver(k):
            cross(k, c).start()

            @pl.when(owns)
            def _():
                o_final[c, k] = o_sum[k]

            pl.when(jnp.logical_not(owns))(lambda: chip(k, c).start())

        d_x = [net.new(d_ref, d_final.at[h], owner) for h in range(2)]
        d_chip = net.new(d_ref, d_final.at[c], net.to_core)
        gx_sem = net.take(w_tiles)
        wx_sem = net.take(w_tiles)

        def gu_cross(k):
            return net.copy(gx_sem + k, gu_mine.at[k], gu_other.at[k], net.to_x)

        def w_cross(k):
            return net.copy(wx_sem + k, w_mine.at[k], w_other.at[k], net.to_x)

        def row_tile(ref):
            def at(k):
                first = pl.multiple_of(lax.rem(k, per) * SMALL, SMALL)
                return ref.at[lax.div(k, per), pl.ds(first, SMALL)]

            return at

        o_line = LineSum(
            net,
            o_tiles,
            lambda k: o_part.at[pl.ds(pl.multiple_of(k * SMALL, SMALL), SMALL)],
            lambda k: o_sum.at[k],
            o_slots,
            deliver,
        )
        gu_line = LineSum(
            net,
            w_tiles,
            row_tile(gu_rows),
            lambda k: gu_mine.at[k],
            gu_slots,
            lambda k: gu_cross(k).start(),
        )
        w_line = LineSum(
            net,
            w_tiles,
            row_tile(w_rows),
            lambda k: w_mine.at[k],
            w_slots,
            lambda k: w_cross(k).start(),
        )
        g_line = LineSum(
            net, 1, lambda k: g_sum.at[0], lambda k: g_mine.at[0], g_slots, lambda k: None
        )
        pump = Pump([o_line, gu_line, w_line], (1, 4, 7, 10))
        gu_first, w_first = o_tiles, o_tiles + w_tiles

        def rows_come(s):
            if isinstance(s, int):
                if s == gu_first + per:
                    gu_y.wait_recv()
                if s == w_first + per:
                    w_y.wait_recv()
            else:
                pl.when(s == gu_first + per)(gu_y.wait_recv)
                pl.when(s == w_first + per)(w_y.wait_recv)

        w_y = net.new(w_sum, w_rows.at[1], net.to_y)
        state = [0]

        def pump_on(count=1):
            for _ in range(count):
                pump.step(state[0], rows_come)
                state[0] += 1

        def ends(line, first, last):
            @pl.when(line.at_end)
            def _():
                @pl.loop(first, last)
                def _(k):
                    line.gather(k)

        gu_y.start()
        ends(o_line, 0, o_tiles)
        load_part.wait()
        total.start_diagonal()
        total.start_sides()
        gu_rows[0] = gu_ref[y]
        ends(gu_line, 0, per)
        for h in range(2):
            pl.when(c == h)(d_x[h].start)
        pl.when(jnp.logical_not(owns))(d_chip.start)

        d_keep = pltpu.make_async_copy(d_ref, d_final.at[c], lsem.at[11])
        pl.when(owns)(d_keep.start)
        def attention(x_s, o_s, g_in, q_s, g_s, k_s, v_s, delta_s):
            loads = [
                pltpu.make_async_copy(a, b, lsem.at[1 + n])
                for n, (a, b) in enumerate(((core_hbm, x_s), (mixed_hbm, o_s), (grad_hbm, g_in)))
            ]
            for cp in loads:
                cp.start()
            for cp in loads:
                cp.wait()
            for i in range(2 * tiles):
                for h in range(blocks):
                    s = inv[i * blocks + h]
                    block, out, grad_ = x_s[s], o_s[s], g_in[s]
                    at = slice((i * blocks + h) * BLK, (i * blocks + h + 1) * BLK)
                    for u in range(2):
                        first = (i % 2) * 2 * QT + u * QT + h * BLK
                        to = slice(first, first + BLK)
                        lanes = slice(u * HD, (u + 1) * HD)
                        q_s[i // 2, to, :] = block[:, lanes]
                        g_s[i // 2, to, :] = grad_[:, lanes]
                        product = grad_[:, lanes].astype(F32) * out[:, lanes].astype(F32)
                        delta_s[i // 2, :, to] = jnp.broadcast_to(
                            jnp.sum(jnp.transpose(product), axis=0, keepdims=True), (8, BLK)
                        )
                    k_s[at, :] = block[:, 2 * HD : 3 * HD]
                    v_s[at, :] = block[:, 3 * HD : 4 * HD]
                if i % 3 == 1:
                    pump_on()

            k_row = lax.broadcasted_iota(jnp.int32, (wide, 2 * wide), 0)
            q_row = lax.broadcasted_iota(jnp.int32, (wide, 2 * wide), 1)
            q_row = lax.shift_right_logical(q_row, 9) * QT + lax.bitwise_and(q_row, QT - 1)
            allowed = q_row >= k_row
            dq_t = [None] * tiles
            for j in range(tiles):
                at = slice(j * wide, (j + 1) * wide)
                k, v = k_s[at, :], v_s[at, :]
                k_t = jnp.transpose(k)
                dk = dv = None
                for i in range(j, tiles):
                    q, g = q_s[i], g_s[i]
                    shift = jnp.concatenate(
                        [lse_ref[2 * i, 0:1, :], lse_ref[2 * i + 1, 0:1, :]], 1
                    )
                    scores = dot_nt(k, q) * factor - shift
                    if i == j:
                        scores = jnp.where(allowed, scores, NEG)
                    p = jnp.exp2(scores)
                    ds = (p * (dot_nt(v, g) - delta_s[i, 0:1, :])).astype(BF)
                    add = dot_nn(k_t, ds)
                    dq_t[i] = add if dq_t[i] is None else dq_t[i] + add
                    add_k, add_v = dot_nn(ds, q), dot_nn(p.astype(BF), g)
                    dk = add_k if dk is None else dk + add_k
                    dv = add_v if dv is None else dv + add_v
                    pump_on()
                for h in range(wide // BLK):
                    part_ = slice(h * BLK, (h + 1) * BLK)
                    b = j * (wide // BLK) + h
                    x_s[b, :, 2 * HD : 3 * HD] = (dk[part_] * scale).astype(BF)
                    x_s[b, :, 3 * HD : 4 * HD] = dv[part_].astype(BF)
                dq_j = jnp.transpose(dq_t[j]) * scale
                for e in range(2):
                    for u in range(2):
                        for h in range(blocks):
                            first = e * 2 * QT + u * QT + h * BLK
                            x_s[(2 * j + e) * blocks + h, :, u * HD : (u + 1) * HD] = dq_j[
                                first : first + BLK
                            ].astype(BF)

            @pl.loop(0, n_blocks)
            def _(s):
                d_s[pl.ds(pl.multiple_of(s * BLK, BLK), BLK), :] = x_s[bm[s]]

        pl.run_scoped(
            attention,
            pltpu.VMEM((n_blocks, BLK, 4 * HD), BF),
            pltpu.VMEM((n_blocks, BLK, 2 * HD), BF),
            pltpu.VMEM((n_blocks, BLK, 2 * HD), BF),
            pltpu.VMEM((tiles, 2 * wide, HD), BF),
            pltpu.VMEM((tiles, 2 * wide, HD), BF),
            pltpu.VMEM((length, HD), BF),
            pltpu.VMEM((length, HD), BF),
            pltpu.VMEM((tiles, 8, 2 * wide), F32),
        )
        swap.start()
        dq[c] = d_s[pl.ds(pl.multiple_of(c * half, half), half), :]

        @pl.when(gu_line.at_end)
        def _():
            gu_y.wait_recv()

        ends(gu_line, per, w_tiles)
        pump_on()

        def norms(raw_ref, table_ref, n1_ref, wall_ref, x_ref, dmid_ref, mid_ref, dcat):
            loads = [
                pltpu.make_async_copy(a, b, lsem.at[4 + n])
                for n, (a, b) in enumerate(
                    (
                        (raw_hbm, raw_ref),
                        (table_hbm, table_ref),
                        (n1_hbm, n1_ref),
                        (wall_hbm, wall_ref),
                        (x_hbm, x_ref),
                        (dmid_hbm, dmid_ref),
                        (mid_hbm, mid_ref),
                    )
                )
            ]
            for cp in loads:
                cp.start()
            swap.wait_recv()
            for cp in loads:
                cp.wait()
            attn_gain, q_gain, k_gain = gain_ref[0:1, :], gain_ref[2:3, 0:HD], gain_ref[3:4, 0:HD]
            acc[...] = jnp.zeros_like(acc)

            def fold(v):
                return jnp.sum(v.reshape(v.shape[0] // 8, 8, v.shape[1]), axis=0)

            def chunk(k):
                at = pl.ds(pl.multiple_of(k * rows, rows), rows)
                half_w = HD // 2
                cosine, sine = table_ref[at, 0:half_w], table_ref[at, half_w:HD]
                cosine = jnp.concatenate([cosine, cosine], axis=-1)
                sine = jnp.concatenate([-sine, sine], axis=-1)
                for h in range(6):
                    g, lane = (h // 2, (h % 2) * HD) if h < 4 else (h - 4, 2 * HD)
                    gain = q_gain if h < 4 else k_gain
                    grad_ = dq[g, at, lane : lane + HD].astype(F32)
                    du = grad_ * cosine - pltpu.roll(grad_, half_w, 1) * sine
                    u = raw_ref[at, h * HD : (h + 1) * HD]
                    size = rms(u)
                    lanes = slice(0, HD) if h < 4 else slice(HD, 2 * HD)
                    acc[2, :, lanes] += fold(du * u * size)
                    dcat[at, h * HD : (h + 1) * HD] = norm_back(du * gain, u, size).astype(BF)
                for g in range(2):
                    dcat[at, (6 + g) * HD : (7 + g) * HD] = dq[g, at, 3 * HD : 4 * HD]

            def project(k):
                d = dcat[pl.ds(pl.multiple_of(k * rows, rows), rows), :]
                for g in range(4):
                    part[k, :, g * d_rows : (g + 1) * d_rows] = dot_nt(d, wall_ref[g]).astype(BF)

            def add(at, value):
                res[at] = (mid_ref[at] + value).astype(BF)

            chunk(net.sd)
            pump_on()
            project(net.sd)
            total2.start_diagonal()
            pump_on()
            total.forward()
            for k in (net.sx, net.sy):
                chunk(k)
                pump_on()
                project(k)
                pump_on()
            total2.start_sides()
            chunk(net.me)
            pump_on()
            project(net.me)
            total2.forward()
            pump_on()

            def slab(n, core_of):
                f = 2 * n + core_of
                at = pl.ds(pl.multiple_of(f * d_rows, d_rows), d_rows)
                return dot_tn(n1_ref[:, at], dcat[...])

            w_sem = net.take(2)

            def w_copy(n):
                return net.copy(w_sem + n, w_out.at[n], w_got.at[n], net.to_core)

            for n in range(2):
                w_out[n] = slab(n, 1 - c).astype(BF)
                w_copy(n).start()
                pump_on()
            total.finish(add)
            home.start()
            value = slab(1 - y, c)
            w_copy(1 - y).wait_recv()
            w_sum[...] = (value + w_got[1 - y].astype(F32)).astype(BF)
            w_y.start()
            pump_on()
            value = slab(y, c)
            w_copy(y).wait_recv()
            w_rows[0] = (value + w_got[y].astype(F32)).astype(BF)
            ends(w_line, 0, per)
            pump_on()

            def back_through_norm(at, dn1):
                value = x_ref[at].astype(F32)
                size = rms(value)
                acc[0] += fold(dn1 * value * size)
                grad_in[at] = (dmid_ref[at] + norm_back(dn1 * attn_gain, value, size)).astype(BF)

            total2.finish(back_through_norm)
            for n in range(2):
                w_copy(n).wait_send()

        pl.run_scoped(
            norms,
            pltpu.VMEM(raw.shape, F32),
            pltpu.VMEM(table.shape, F32),
            pltpu.VMEM(n1.shape, BF),
            pltpu.VMEM(wall.shape, BF),
            pltpu.VMEM((rows, D), BF),
            pltpu.VMEM((rows, D), F32),
            pltpu.VMEM((rows, D), F32),
            pltpu.VMEM((half, 8 * HD), BF),
        )
        home2.start()
        pump_on()

        def place(k, slots, copies, outs, widths):
            copies(k).wait_recv()
            row_half = jnp.where(k < per, y, 1 - y)
            at = pl.ds(pl.multiple_of(lax.rem(k, per) * SMALL, SMALL), SMALL)
            for tile, x_of in zip(slots, (x, 1 - x)):
                quarter = 2 * row_half + x_of
                first = 0
                for out, width in zip(outs, widths):
                    lanes = pl.ds(pl.multiple_of(quarter * width, width), width)
                    out[at, lanes] = tile[k, :, first : first + width]
                    first += width

        def place_gu(k):
            place(k, (gu_mine, gu_other), gu_cross, (out_g, out_u), (unit, unit))

        def place_w(k):
            place(k, (w_mine, w_other), w_cross, (out_q, out_k, out_v), (4 * HD, 2 * HD, 2 * HD))

        acc[1] = mlp_ref[...]
        for row in range(3):
            g_sum[0, row : row + 1, :] = jnp.sum(acc[row], axis=0, keepdims=True)
        g_sum[0, 3:8, :] = jnp.zeros((5, D), F32)
        for n, to in enumerate((net.to_core, net.to_y, net.to_x)):
            cp = net.new(g_sum.at[0], g_got.at[n], to)
            cp.start()
            pump_on()
            cp.wait()
            g_sum[0] = g_sum[0] + g_got[n]
        g_line.gather(0)

        @pl.when(w_line.at_end)
        def _():
            w_y.wait_recv()

        ends(w_line, per, w_tiles)
        so_far = state[0]
        place_lag = 14

        @pl.loop(0, so_far - place_lag - gu_first)
        def _(k):
            place_gu(k)

        @pl.loop(so_far, pump.steps())
        def _(p):
            pump.step(p, rows_come)
            q = p - place_lag
            pl.when(within(q, gu_first, w_first))(lambda: place_gu(q - gu_first))
            pl.when(within(q, w_first, w_first + w_tiles))(lambda: place_w(q - w_first))

        g_line.finish(0)
        gain_out[...] = g_mine[0]

        @pl.loop(pump.steps() - place_lag - w_first, w_tiles)
        def _(k):
            place_w(k)

        @pl.loop(0, o_tiles)
        def _(k):
            @pl.when(owns)
            def _():
                chip(k, 1 - c).wait_recv()

            @pl.when(jnp.logical_not(owns))
            def _():
                for h in range(2):
                    cross(k, h).wait_recv()
                chip(k, c).wait_send()

            cross(k, c).wait_send()
            o_line.drain(k)

        @pl.when(owns)
        def _():
            d_chip.wait_recv()
            d_keep.wait()

        @pl.when(jnp.logical_not(owns))
        def _():
            for h in range(2):
                d_x[h].wait_recv()
            d_chip.wait_send()

        for h in range(2):
            pl.when(c == h)(d_x[h].wait_send)

        @pl.loop(0, w_tiles)
        def _(k):
            gu_line.drain(k)
            w_line.drain(k)
            gu_cross(k).wait_send()
            w_cross(k).wait_send()

        g_line.drain(0)
        gu_y.wait_send()
        w_y.wait_send()
        swap.wait_send()
        total.drain()
        total2.drain()
        for item in (home, home2):
            item.wait()
            item.drain()

    vm = vmem_spec()
    hbm = any_spec()
    smem = pl.BlockSpec(memory_space=pltpu.SMEM)
    chunk_ = pltpu.VMEM((rows, D), BF)
    four = pltpu.VMEM((4, rows, D), BF)
    three = pltpu.VMEM((3, rows, D), BF)
    gu_tiles = pltpu.VMEM((w_tiles, SMALL, gu_cols), BF)
    gu_pairs = pltpu.VMEM((2, w_tiles, SMALL, gu_cols), BF)
    qkv_tiles = pltpu.VMEM((w_tiles, SMALL, 8 * HD), BF)
    qkv_pairs = pltpu.VMEM((2, w_tiles, SMALL, 8 * HD), BF)
    g_tile = pltpu.VMEM((1, 8, D), F32)
    slabs = pltpu.VMEM((2, d_rows, 8 * HD), BF)
    return pl.pallas_call(
        kernel,
        name="finish_back",
        out_shape=[
            shape((rows, D), BF),
            shape((rows, D), BF),
            shape((2, o_tiles, SMALL, D), BF),
            shape((2,) + total_d.shape, BF),
            shape((d_rows, 16 * HD), BF),
            shape((d_rows, 8 * HD), BF),
            shape((d_rows, 8 * HD), BF),
            shape((d_rows, 4 * unit), BF),
            shape((d_rows, 4 * unit), BF),
            shape((8, D), F32),
        ],
        in_specs=[smem, smem] + [hbm] * 3 + [vm] * 4 + [hbm] * 8 + [vm] * 2,
        out_specs=[vm] * 3 + [hbm] + [vm] * 6,
        scratch_shapes=[
            pltpu.VMEM((2, half, 4 * HD), BF),
            pltpu.VMEM((length, 4 * HD), BF),
            four,
            four,
            chunk_,
            three,
            chunk_,
            chunk_,
            three,
            chunk_,
            pltpu.VMEM((2, o_tiles, SMALL, D), BF),
            pltpu.VMEM((o_tiles, SMALL, D), BF),
            pltpu.VMEM(sum_gu.shape, BF),
            gu_pairs,
            gu_tiles,
            gu_tiles,
            slabs,
            slabs,
            pltpu.VMEM((d_rows, 8 * HD), BF),
            slabs,
            qkv_pairs,
            qkv_tiles,
            qkv_tiles,
            g_tile,
            pltpu.VMEM((3, 8, D), F32),
            pltpu.VMEM((2, 1, 8, D), F32),
            g_tile,
            pltpu.VMEM((3, 8, D), F32),
            pltpu.SemaphoreType.DMA((n_sems,)),
            pltpu.SemaphoreType.DMA((n_sems,)),
            pltpu.SemaphoreType.DMA((12,)),
        ],
        compiler_params=params(3, 63),
        cost_estimate=pl.CostEstimate(
            flops=5 * 2 * 2 * length * length * HD, bytes_accessed=32 * 2**20, transcendentals=0
        ),
    )(
        block_map,
        inverse,
        core.reshape(n_blocks, BLK, 4 * HD),
        mixed.reshape(n_blocks, BLK, 2 * HD),
        grad.reshape(n_blocks, BLK, 2 * HD),
        lse,
        sum_o,
        total_d,
        sum_gu,
        result_part,
        middle,
        raw,
        table,
        n1,
        wall,
        x_own,
        dmiddle,
        gains,
        mlp_gain_part,
    )


def widen(arrays, gain_sums, parts, steps=4):
    n = len(arrays)
    d_part, h_part = D // parts, HD // parts

    def kernel(*refs):
        for a, b in zip(refs[:n], refs[n + 1 : 2 * n + 1]):
            b[...] = a[...].astype(F32)
        sums = refs[n]
        attn, mlp, query, key = refs[2 * n + 1 :]

        @pl.when(pl.program_id(0) == 0)
        def _():
            f = lax.axis_index("fsdp")
            at = pl.ds(pl.multiple_of(f * d_part, d_part), d_part)
            attn[...] = sums[0:1, at]
            mlp[...] = sums[1:2, at]
            for out, first in ((query, 0), (key, HD)):
                turned = pltpu.roll(sums[0:8, first : first + HD], HD - f * h_part, 1)
                out[...] = turned[2:3, 0:h_part]

    def spec(a):
        return pl.BlockSpec((a.shape[0] // steps, a.shape[1]), lambda i: (i, 0))

    def whole(dims):
        return pl.BlockSpec(dims, lambda i: (0, 0))

    small = [(1, d_part), (1, d_part), (1, h_part), (1, h_part)]
    return pl.pallas_call(
        kernel,
        name="widen",
        grid=(steps,),
        out_shape=[shape(a.shape, F32) for a in arrays] + [shape(s, F32) for s in small],
        in_specs=[spec(a) for a in arrays] + [whole(gain_sums.shape)],
        out_specs=[spec(a) for a in arrays] + [whole(s) for s in small],
        compiler_params=pltpu.CompilerParams(vmem_limit_bytes=62 * 2**20),
    )(*arrays, gain_sums)


def plane_body(
    tokens,
    cotangent,
    block_map,
    positions,
    attn_gain,
    query_weight,
    key_weight,
    value_weight,
    query_gain,
    key_gain,
    out_weight,
    mlp_gain,
    gate_weight,
    up_weight,
    down_weight,
):
    rows = tokens.shape[1]
    parts = lax.axis_size("fsdp")
    flat_map = block_map.reshape(-1)
    n_blocks = flat_map.shape[0]
    order = jnp.arange(n_blocks, dtype=jnp.int32)
    inverse = jnp.sum(
        jnp.where(flat_map[None, :] == order[:, None], order[None, :], 0), axis=1
    ).astype(jnp.int32)
    x_own, n1, raw, table, core, wall, gains, cot_own, wgu = enter(
        tokens.reshape(rows, D),
        cotangent.reshape(rows, D),
        positions,
        [g.reshape(1, -1) for g in (attn_gain, mlp_gain, query_gain, key_gain)],
        query_weight,
        key_weight,
        value_weight,
        gate_weight,
        up_weight,
    )
    att, mixed, lse, cots, wo, wd = attend(
        flat_map, inverse, core, cot_own, out_weight, down_weight
    )
    grad, middle, dmiddle, result_part, sum_gu, sum_o, total_d, mlp_gain_part = feed_forward(
        att, x_own, wo, wgu, wd, cots, cot_own, gains
    )
    (
        result,
        input_grad,
        grad_o,
        grad_d,
        grad_q,
        grad_k,
        grad_v,
        grad_g,
        grad_u,
        gain_sums,
    ) = finish_back(
        flat_map,
        inverse,
        core,
        mixed,
        grad,
        lse,
        sum_o,
        total_d,
        sum_gu,
        result_part,
        middle,
        raw,
        table,
        n1,
        wall,
        x_own,
        dmiddle,
        gains,
        mlp_gain_part,
    )

    (
        result,
        input_grad,
        grad_q,
        grad_k,
        grad_v,
        grad_o,
        grad_g,
        grad_u,
        grad_d,
        *gain_grads,
    ) = widen(
        [
            result,
            input_grad,
            grad_q,
            grad_k,
            grad_v,
            grad_o.reshape(out_weight.shape),
            grad_g,
            grad_u,
            grad_d.reshape(down_weight.shape),
        ],
        gain_sums,
        parts,
    )
    attn_grad, mlp_grad, query_grad, key_grad = [g.reshape(-1) for g in gain_grads]
    return (
        result.reshape(tokens.shape),
        input_grad.reshape(tokens.shape),
        attn_grad,
        grad_q,
        grad_k,
        grad_v,
        query_grad,
        key_grad,
        grad_o,
        mlp_grad,
        grad_g,
        grad_u,
        grad_d,
    )


def solution(mesh):
    placed = (
        P("fsdp", "ctx", None),
        P("fsdp", "ctx", None),
        P(),
        P("fsdp", "ctx"),
        P("fsdp"),
        P("fsdp", None),
        P("fsdp", None),
        P("fsdp", None),
        P("fsdp"),
        P("fsdp"),
        P("fsdp", None),
        P("fsdp"),
        P("fsdp", None),
        P("fsdp", None),
        P("fsdp", None),
    )
    fits = mesh.shape["fsdp"] == 4 and mesh.shape["ctx"] == 8
    return jax.shard_map(
        plane_body if fits else body,
        mesh=mesh,
        in_specs=placed,
        out_specs=(
            P("fsdp", "ctx", None),
            P("fsdp", "ctx", None),
            P("fsdp"),
            P("fsdp", None),
            P("fsdp", None),
            P("fsdp", None),
            P("fsdp"),
            P("fsdp"),
            P("fsdp", None),
            P("fsdp"),
            P("fsdp", None),
            P("fsdp", None),
            P("fsdp", None),
        ),
        check_vma=False,
    )
```
